32 devices in a mesh: pts: 8 (over z, y), head: 4 (over x, core).
Axes of the slice: x: 2, y: 2, z: 4, core: 2. Of those that a mesh axis runs over, the one named last changes fastest.
Arguments:
- tokens: bfloat16 [65536, 256], P(('pts', 'head'))
- cotangent: bfloat16 [65536, 256], P(('pts', 'head')), may hold values from -6 to 6
- segment_ids: int32 [65536], P('pts'), may hold values from 0 to 23, as said below
- owner: int32 [176], replicated, may hold values from 0 to 7, as said below
- w_fx: bfloat16 [2, 256, 256], P(None, None, 'head'), may hold values from -0.375 to 0.375
- w_mid: bfloat16 [2, 256, 256], P(None, None, 'head'), may hold values from -0.375 to 0.375
- w_out: bfloat16 [2, 256, 256], P(None, 'head'), may hold values from -0.375 to 0.375
- w_up: bfloat16 [2, 256, 1024], replicated, may hold values from -0.375 to 0.375
- w_down: bfloat16 [2, 1024, 256], replicated, may hold values from -0.375 to 0.375
- small_master: float32 [2, 6144], replicated
- small_first: float32 [2, 6144], replicated, may hold values from -48 to 48
- small_second: float32 [2, 6144], replicated, may hold values from 170.3936 to 1245.184
- master_table: float32 [352, 8192], P('pts', 'head'), may hold values from -0.75 to 0.75
- first_table: float32 [352, 8192], P('pts', 'head'), may hold values from -48 to 48
- second_table: float32 [352, 8192], P('pts', 'head'), may hold values from 170.3936 to 1245.184
Outputs:
- layer_out: bfloat16 [65536, 256], P(('pts', 'head'))
- input_grad: float32 [65536, 256], P(('pts', 'head'))
- new_master: float32 [352, 8192], P('pts', 'head')
- new_first: float32 [352, 8192], P('pts', 'head')
- new_second: float32 [352, 8192], P('pts', 'head')
- fresh_copies: bfloat16 [176, 8192], P(None, 'head')
- small_new: float32 [2, 6144], replicated
- small_first_new: float32 [2, 6144], replicated
- small_second_new: float32 [2, 6144], replicated
The draws below stay inside these ranges and needn't reach their ends.
Inputs may be any that keep to these rules, and one draw needn't show every extreme that they name: `segment_ids`: ids never fall along the points; each of the 24 meshes has points, the largest exactly 5461. `owner`: no index owns more than 44 blocks, and one owns exactly 44.
All inputs are finite; a program needn't handle non-finite values.
Results may differ from the reference program's by a relative error of at most 0.025.
Values may be sent and summed in bfloat16 or wider, within the bound.
A program may use at most 192 MiB of HBM per device.

```python
import math
import jax
import jax.numpy as jnp
from jax import lax

D = 256
HEADS = 8
DH = 32
SLICES = 64
FF = 1024
LAYERS = 2
MESHES = 24
BLOCK = 2048
STEP = 10
TOKENS = 65536
MOST = 5461
NBLK = 176
CAP = 44
SMALL = 6144
N_PTS = 8
N_HEAD = 4


def mesh_lengths(key):
    heavy_key, share_key = jax.random.split(jax.random.fold_in(key, 7))
    heavy = jax.random.randint(heavy_key, (), 0, MESHES)
    places = jnp.arange(MESHES)
    shares_raw = jax.random.randint(share_key, (MESHES,), 800, 1201)
    shares_raw = jnp.where(places == heavy, 0, shares_raw)
    remaining = TOKENS - MOST
    shares = shares_raw * remaining // jnp.sum(shares_raw)
    spare = remaining - jnp.sum(shares)
    first_other = jnp.where(heavy == 0, 1, 0)
    shares = shares + jnp.where(places == first_other, spare, 0)
    return jnp.where(places == heavy, MOST, shares).astype(jnp.int32)


def mesh_ids(key):
    ends = jnp.cumsum(mesh_lengths(key))
    spots = jnp.arange(TOKENS)
    return jnp.sum((spots[:, None] >= ends[None, :]).astype(jnp.int32), axis=1).astype(jnp.int32)


def draw_segment_ids(key, part):
    return mesh_ids(key)


def draw_tokens(key, part):
    lengths = mesh_lengths(key)
    ends = jnp.cumsum(lengths)
    ids = mesh_ids(key)
    starts = (ends - lengths)[ids]
    place_in = (jnp.arange(TOKENS) - starts).astype(jnp.float32) / lengths[ids].astype(jnp.float32)
    noise_key, common_key, slope_key = jax.random.split(jax.random.fold_in(key, 11), 3)
    noise = jax.random.normal(noise_key, (TOKENS, D))
    common = jax.random.normal(common_key, (MESHES, D))
    slope = jax.random.normal(slope_key, (MESHES, D))
    values = 0.7 * noise + common[ids] + (2.0 * place_in[:, None] - 1.0) * slope[ids]
    return values.astype(jnp.bfloat16)


def draw_owner(key, part):
    order_key, device_key = jax.random.split(jax.random.fold_in(key, 23))
    order = jax.random.permutation(order_key, NBLK)
    devices = jax.random.permutation(device_key, N_PTS)
    turns = jnp.arange(NBLK)
    others = devices[1 + jnp.maximum(turns - CAP, 0) % (N_PTS - 1)]
    chosen = jnp.where(turns < CAP, devices[0], others).astype(jnp.int32)
    return jnp.zeros((NBLK,), jnp.int32).at[order].set(chosen)


def draw_small_master(key, part):
    columns = jnp.arange(SMALL)[None, :]
    base = jax.random.normal(jax.random.fold_in(key, 31), (LAYERS, SMALL))
    edge_slice = DH * SLICES
    edge_attend = edge_slice + 3 * DH * DH
    is_gain = (columns - edge_attend) // D % 2 == 0
    values = jnp.where(columns < edge_slice, base * (2.0 / math.sqrt(DH)), jnp.where(columns < edge_attend, base * (2.5 / math.sqrt(DH)), jnp.where(is_gain, 1.0 + 0.3 * jnp.tanh(base), 0.3 * base)))
    return values.astype(jnp.float32)


def steps_of(stream_key, dims, cuts, smallest, top_value):
    def one(dim, parts):
        steps = jax.random.uniform(jax.random.fold_in(jax.random.fold_in(stream_key, 6), dim), (parts,), jnp.float32, smallest / len(cuts), top_value / len(cuts))
        return jnp.repeat(jnp.exp(steps), dims[dim] // parts).reshape((-1,) + (1,) * (len(dims) - dim - 1))

    level = one(*cuts[0])
    for cut in cuts[1:]:
        level = level * one(*cut)
    return level


def bell_draw(rng, extent, scale, bound, shards=(), dtype=jnp.bfloat16):
    entries = jax.random.normal(rng, extent, jnp.float32) * scale
    if len(shards) > 0:
        entries = steps_of(rng, extent, shards, -0.22, 0.18) * entries
    return jnp.clip(entries, min=-bound, max=bound).astype(dtype)


def setup_inputs(seed: int = 0) -> dict:
    seeds = jax.random.split(jax.random.key(seed), 16)
    return {
        "tokens": draw_tokens(jax.random.fold_in(seeds[15], 71), 0),
        "cotangent": bell_draw(seeds[1], (TOKENS, D), 1.0, 6.0, ((0, 32),)),
        "segment_ids": draw_segment_ids(jax.random.fold_in(seeds[15], 71), 0),
        "owner": draw_owner(jax.random.fold_in(seeds[15], 71), 0),
        "w_fx": bell_draw(seeds[4], (LAYERS, D, HEADS * DH), D ** -0.5, 0.375, ((2, 4),)),
        "w_mid": bell_draw(seeds[5], (LAYERS, D, HEADS * DH), D ** -0.5, 0.375, ((2, 4),)),
        "w_out": bell_draw(seeds[6], (LAYERS, HEADS * DH, D), (HEADS * DH) ** -0.5, 0.375, ((1, 4),)),
        "w_up": bell_draw(seeds[7], (LAYERS, D, FF), D ** -0.5, 0.375),
        "w_down": bell_draw(seeds[8], (LAYERS, FF, D), (FF // 4) ** -0.5, 0.375),
        "small_master": draw_small_master(jax.random.fold_in(seeds[15], 71), 0),
        "small_first": bell_draw(seeds[10], (LAYERS, SMALL), (0.033 * TOKENS ** 0.5), 48.0, (), jnp.float32),
        "small_second": jnp.clip(jnp.exp(jax.random.uniform(seeds[11], (LAYERS, SMALL), jnp.float32, math.log(170.3936), math.log(1245.184))), 170.3936, 1245.184),
        "master_table": bell_draw(seeds[12], (N_PTS * CAP, N_HEAD * BLOCK), 0.05, 0.75, ((0, 8), (1, 4)), jnp.float32),
        "first_table": bell_draw(seeds[13], (N_PTS * CAP, N_HEAD * BLOCK), (0.033 * TOKENS ** 0.5), 48.0, ((0, 8), (1, 4)), jnp.float32),
        "second_table": jnp.clip(jnp.exp(math.log(1245.184) - 1.9889275 * jax.random.uniform(seeds[14], (N_PTS * CAP, N_HEAD * BLOCK), jnp.float32) ** steps_of(seeds[14], (N_PTS * CAP, N_HEAD * BLOCK), ((0, 8), (1, 4)), -0.2, 0.2)), 170.3936, 1245.184),
    }


@jax.custom_vjp
def low(v):
    return lax.optimization_barrier(v.astype(jnp.bfloat16)).astype(jnp.float32)

@jax.custom_vjp
def low_back(v):
    return v

def low_keep(v):
    return (low(v), None)

def low_pass(kept, grad):
    return (grad,)

def back_keep(v):
    return (v, None)

def back_low(kept, grad):
    return (low(grad),)
low.defvjp(low_keep, low_pass)
low_back.defvjp(back_keep, back_low)
HIGH = lax.Precision.HIGHEST
norm_eps = 1e-05
beta_one = 0.9
beta_two = 0.95
adam_eps = 1e-08
decay_rate = 0.1
rate_large = 0.1
rate_small = 0.75

def both_ways(v):
    return low(low_back(v))

def layer_norm(values, gain, shift):
    center = lax.optimization_barrier(jnp.mean(values, axis=-1, keepdims=True))
    spread = values - center
    scale = lax.rsqrt(lax.optimization_barrier(jnp.mean(spread * spread, axis=-1, keepdims=True)) + norm_eps)
    return spread * scale * gain + shift

def split_small(vector):
    first_edge = DH * SLICES
    second_edge = first_edge + 3 * DH * DH
    return (vector[:first_edge].reshape(DH, SLICES), vector[first_edge:second_edge].reshape(3, DH, DH), vector[second_edge:].reshape(4, D))

def attend(summed, counted, wqkv):
    slice_tok = summed / counted[..., None]
    queries = jnp.einsum('mhgc,cd->mhgd', slice_tok, wqkv[0], precision=HIGH)
    keyset = jnp.einsum('mhgc,cd->mhgd', slice_tok, wqkv[1], precision=HIGH)
    valueset = jnp.einsum('mhgc,cd->mhgd', slice_tok, wqkv[2], precision=HIGH)
    scores = jnp.einsum('mhgd,mhkd->mhgk', queries, keyset, precision=HIGH) * (1.0 / math.sqrt(DH))
    attn_prob = jax.nn.softmax(scores, axis=-1)
    return jnp.einsum('mhgk,mhkd->mhgd', attn_prob, valueset, precision=HIGH)

def adam_update(master, grad, first, second, rate):
    new_first = beta_one * first + (1.0 - beta_one) * grad
    new_second = beta_two * second + (1.0 - beta_two) * grad * grad
    fix_one = 1.0 - beta_one ** STEP
    fix_two = 1.0 - beta_two ** STEP
    direction = new_first / fix_one / (jnp.sqrt(new_second / fix_two) + adam_eps)
    return (master - rate * (direction + decay_rate * master), new_first, new_second)

def forward(points, w_fx, w_mid, w_out, w_up, w_down, small, onehot):
    block_rows = math.gcd(TOKENS, 4096)
    block_count = TOKENS // block_rows
    hot_blocks = onehot.reshape(block_count, block_rows, MESHES)
    for layer in range(LAYERS):
        wslice, wqkv, norms = split_small(small[layer])
        wslice_r = low(wslice)

        def project(row_part):
            normed = low(layer_norm(row_part, norms[0], norms[1]))
            feats = both_ways(jnp.dot(normed, w_fx[layer], precision=HIGH))
            middle = both_ways(jnp.dot(normed, w_mid[layer], precision=HIGH))
            logits = low_back(jnp.einsum('nhc,cg->nhg', middle.reshape(-1, HEADS, DH), wslice_r, precision=HIGH))
            return (feats.reshape(-1, HEADS, DH), low(jax.nn.softmax(logits, axis=-1)))
        feats, weights = lax.map(jax.checkpoint(project), points.reshape(block_count, block_rows, D))

        def add_block(carry, blk):
            hot_blk, feat_blk, weight_blk = blk
            mixed = hot_blk[:, :, None, None] * weight_blk[:, None]
            part_sum = jnp.einsum('nmhg,nhc->mhgc', mixed, feat_blk, precision=HIGH)
            return ((carry[0] + part_sum, carry[1] + lax.optimization_barrier(jnp.sum(mixed, axis=0))), None)
        start_sum = (jnp.zeros((MESHES, HEADS, SLICES, DH), jnp.float32), jnp.zeros((MESHES, HEADS, SLICES), jnp.float32))
        (summed, counted), _ = lax.scan(jax.checkpoint(add_block), start_sum, (hot_blocks, feats, weights))
        attended = low(attend(low_back(summed), counted, wqkv))

        def finish(blk):
            row_part, hot_blk, weight_blk = blk
            mixed = hot_blk[:, :, None, None] * weight_blk[:, None]
            spread_out = both_ways(jnp.einsum('nmhg,mhgc->nhc', mixed, attended, precision=HIGH).reshape(-1, HEADS * DH))
            middle = row_part + low_back(jnp.dot(spread_out, w_out[layer], precision=HIGH))
            normed_two = low(layer_norm(middle, norms[2], norms[3]))
            hidden = low_back(jnp.dot(normed_two, w_up[layer], precision=HIGH))
            active = low(jax.nn.gelu(hidden))
            return middle + low_back(jnp.dot(active, w_down[layer], precision=HIGH))
        points = lax.map(jax.checkpoint(finish), (points.reshape(block_count, block_rows, D), hot_blocks, weights)).reshape(TOKENS, D)
    return points

def reference(tokens, cotangent, segment_ids, owner, w_fx, w_mid, w_out, w_up, w_down, small_master, small_first, small_second, master_table, first_table, second_table):
    onehot = (segment_ids[:, None] == jnp.arange(MESHES)[None, :]).astype(jnp.float32)

    def run(points, wa, wb, wc, wd, we, small):
        return forward(points, wa, wb, wc, wd, we, small, onehot)
    result, back = jax.vjp(run, tokens.astype(jnp.float32), w_fx.astype(jnp.float32), w_mid.astype(jnp.float32), w_out.astype(jnp.float32), w_up.astype(jnp.float32), w_down.astype(jnp.float32), small_master)
    g_in, g_fx, g_mid, g_out, g_up, g_down, g_small = back(cotangent.astype(jnp.float32))
    in_dev = HEADS * DH // N_HEAD
    ff_dev = FF // N_HEAD

    def by_columns(grad, width):
        return grad.reshape(LAYERS, D, N_HEAD, width).transpose(0, 2, 1, 3).reshape(LAYERS, N_HEAD, D * width)
    pieces = [by_columns(g_fx, in_dev), by_columns(g_mid, in_dev), g_out.reshape(LAYERS, N_HEAD, in_dev * D), by_columns(g_up, ff_dev), g_down.reshape(LAYERS, N_HEAD, ff_dev, D).transpose(0, 1, 3, 2).reshape(LAYERS, N_HEAD, D * ff_dev)]
    flat = jnp.concatenate(pieces, axis=2).transpose(1, 0, 2).reshape(N_HEAD, NBLK, BLOCK)
    flat = flat.transpose(1, 0, 2).reshape(NBLK, N_HEAD * BLOCK)
    block_ids = jnp.arange(NBLK)
    same_owner = (owner[:, None] == owner[None, :]) & (block_ids[None, :] < block_ids[:, None])
    slot = lax.optimization_barrier(jnp.sum(same_owner.astype(jnp.int32), axis=1)).astype(jnp.int32)
    table_row = (owner * CAP + slot).astype(jnp.int32)
    place = (jnp.arange(N_PTS * CAP)[:, None] == table_row[None, :]).astype(jnp.float32)
    grad_table = jnp.dot(place, flat, precision=HIGH)
    filled = lax.optimization_barrier(jnp.sum(place, axis=1))[:, None] > 0.5
    upd_master, upd_first, upd_second = adam_update(master_table, grad_table, first_table, second_table, rate_large)
    new_master = jnp.where(filled, upd_master, master_table)
    new_first = jnp.where(filled, upd_first, first_table)
    new_second = jnp.where(filled, upd_second, second_table)
    fresh = jnp.dot(place.T, new_master, precision=HIGH).astype(jnp.bfloat16)
    small_new, small_first_new, small_second_new = adam_update(small_master, g_small, small_first, small_second, rate_small)
    return (result.astype(jnp.bfloat16), g_in, new_master, new_first, new_second, fresh, small_new, small_first_new, small_second_new)
```

```python
import functools
import math

import jax
import jax.numpy as jnp
from jax import lax
from jax.experimental import pallas as pl
from jax.experimental.pallas import tpu as pltpu
from jax.sharding import PartitionSpec as P

D = 256
HEADS = 8
DH = 32
SLICES = 64
HS = HEADS * SLICES
FF = 1024
MESHES = 24
BLOCK = 2048
STEP = 10
LARGEST = 12
EDGE = 80
VMEM_BYTES = 58 << 20

MESH = pl.DeviceIdType.MESH
HIGH = lax.Precision.HIGHEST
norm_eps = 1e-05
beta_one = 0.9
beta_two = 0.95
adam_eps = 1e-08
decay_rate = 0.1
rate_large = 0.1
rate_small = 0.75
f32 = jnp.float32
b16 = jnp.bfloat16


def nn(a, b, precision=None):
    return lax.dot_general(
        a, b, (((1,), (0,)), ((), ())), preferred_element_type=f32, precision=precision
    )


def nt(a, b, precision=None):
    return lax.dot_general(
        a, b, (((1,), (1,)), ((), ())), preferred_element_type=f32, precision=precision
    )


def tn(a, b, precision=None):
    return lax.dot_general(
        a, b, (((0,), (0,)), ((), ())), preferred_element_type=f32, precision=precision
    )


def iota(shape, axis):
    return lax.broadcasted_iota(jnp.int32, shape, axis)


def pick_diag(full, per_head):
    lane_head = iota((SLICES, full.shape[1]), 1) // per_head
    total = jnp.where(lane_head == 0, full[:SLICES], 0.0)
    for head in range(1, HEADS):
        total = total + jnp.where(
            lane_head == head, full[head * SLICES : (head + 1) * SLICES], 0.0
        )
    return total


def spread_diag(small):
    lane_head = iota((SLICES, D), 1) // DH
    return jnp.concatenate(
        [jnp.where(lane_head == head, small, jnp.zeros_like(small)) for head in range(HEADS)],
        axis=0,
    )


def repeat_rows(width):
    return (iota((D, width), 0) % width == iota((D, width), 1)).astype(f32)


def slice_repeat():
    return (iota((SLICES, HS), 1) % SLICES == iota((SLICES, HS), 0)).astype(f32)


def same_head(rows_per, cols_per, shape):
    return (iota(shape, 0) // rows_per) == (iota(shape, 1) // cols_per)


def weights_kernel(n_head, wfx_ref, wmid_ref, wout_ref, ws_ref, wqkv_ref, out_ref, wsb_ref, wqb_ref, send_sem, recv_sem):
    me = lax.axis_index("head")
    barrier = pltpu.get_barrier_semaphore()
    for step in range(1, n_head):
        pl.semaphore_signal(
            barrier, inc=1, device_id={"head": lax.rem(me + step, n_head)}, device_id_type=MESH
        )
    layers = wfx_ref.shape[0]
    for layer in range(layers):
        out_ref[me, layer, 0] = wfx_ref[layer].astype(f32).T.astype(b16)
        out_ref[me, layer, 1] = wmid_ref[layer].astype(f32).T.astype(b16)
        out_ref[me, layer, 2] = wout_ref[layer]
    pl.semaphore_wait(barrier, n_head - 1)
    copies = []
    for step in range(1, n_head):
        peer = lax.rem(me + step, n_head)
        copy = pltpu.make_async_remote_copy(
            src_ref=out_ref.at[me],
            dst_ref=out_ref.at[me],
            send_sem=send_sem.at[step - 1],
            recv_sem=recv_sem.at[step - 1],
            device_id={"head": peer},
            device_id_type=MESH,
        )
        copy.start()
        copies.append(copy)
    left = repeat_rows(DH)
    right = slice_repeat()
    for layer in range(layers):
        tiled = nn(nn(left, ws_ref[layer], HIGH), right, HIGH)
        wsb_ref[layer] = jnp.where(same_head(DH, SLICES, (D, HS)), tiled, 0.0).astype(b16)
        for part in range(3):
            square = nt(nn(left, wqkv_ref[layer, part], HIGH), left, HIGH)
            wqb_ref[layer, :, part * D : (part + 1) * D] = jnp.where(
                same_head(DH, DH, (D, D)), square, 0.0
            )
    for copy in copies:
        copy.wait()


def gather_weights(n_head, w_fx, w_mid, w_out, ws, wqkv):
    layers, _, part = w_fx.shape
    return pl.pallas_call(
        functools.partial(weights_kernel, n_head),
        out_shape=(
            jax.ShapeDtypeStruct((n_head, layers, 3, part, D), b16),
            jax.ShapeDtypeStruct((layers, D, HS), b16),
            jax.ShapeDtypeStruct((layers, D, 3 * D), f32),
        ),
        in_specs=[pl.BlockSpec(memory_space=pltpu.VMEM)] * 5,
        out_specs=[pl.BlockSpec(memory_space=pltpu.VMEM)] * 3,
        scratch_shapes=[
            pltpu.SemaphoreType.DMA((n_head - 1,)),
            pltpu.SemaphoreType.DMA((n_head - 1,)),
        ],
        compiler_params=pltpu.CompilerParams(
            collective_id=0, has_side_effects=True, vmem_limit_bytes=VMEM_BYTES
        ),
        name="gather_weights",
    )(w_fx, w_mid, w_out, ws, wqkv)


def edge_kernel(sizes, window, edge_ref, out_ref, send_sem, recv_sem):
    n_pts, n_head = sizes
    total = n_pts * n_head
    me = lax.axis_index("pts") * n_head + lax.axis_index("head")

    def place(shift):
        other = lax.rem(me + (shift + total), total)
        return (other // n_head, lax.rem(other, n_head))

    barrier = pltpu.get_barrier_semaphore()
    for step in range(1, window + 1):
        for shift in (step, -step):
            pl.semaphore_signal(barrier, inc=1, device_id=place(shift), device_id_type=MESH)
    pl.semaphore_wait(barrier, 2 * window)
    copies = []
    for step in range(1, window + 1):
        for side, shift in ((1, step), (0, -step)):
            slot = step - 1 if side == 1 else window + step - 1
            copy = pltpu.make_async_remote_copy(
                src_ref=edge_ref.at[side],
                dst_ref=out_ref.at[slot],
                send_sem=send_sem.at[slot],
                recv_sem=recv_sem.at[slot],
                device_id=place(shift),
                device_id_type=MESH,
            )
            copy.start()
            copies.append(copy)
    for copy in copies:
        copy.wait()


def swap_edges(sizes, window, edge, collective_id):
    _, rows, width = edge.shape
    return pl.pallas_call(
        functools.partial(edge_kernel, sizes, window),
        out_shape=jax.ShapeDtypeStruct((2 * window, rows, width), b16),
        in_specs=[pl.BlockSpec(memory_space=pltpu.VMEM)],
        out_specs=pl.BlockSpec(memory_space=pltpu.VMEM),
        scratch_shapes=[
            pltpu.SemaphoreType.DMA((2 * window,)),
            pltpu.SemaphoreType.DMA((2 * window,)),
        ],
        compiler_params=pltpu.CompilerParams(
            collective_id=collective_id, has_side_effects=True, vmem_limit_bytes=VMEM_BYTES
        ),
        name="swap_edges",
    )(edge)


def norm_stats(values):
    center = jnp.mean(values, axis=0, keepdims=True)
    spread = values - center
    scale = lax.rsqrt(jnp.mean(spread * spread, axis=0, keepdims=True) + norm_eps)
    return (spread * scale, scale)


def norm_back(grad_out, scaled, scale, gain):
    inner = grad_out * gain
    return scale * (
        inner
        - jnp.mean(inner, axis=0, keepdims=True)
        - scaled * jnp.mean(inner * scaled, axis=0, keepdims=True)
    )


def group_sum(values):
    return jnp.sum(values.reshape(HEADS, SLICES, values.shape[1]), axis=1, keepdims=True)


def fold_lanes(values):
    total = values[:, :128]
    for start in range(128, values.shape[1], 128):
        total = total + values[:, start : start + 128]
    return total


def tile_mask(scal, mesh, tile, width):
    spot = iota((1, width), 1) + tile * width
    return (spot >= scal[mesh]) & (spot < scal[mesh + 1])


def tile_range(scal, tile):
    base = MESHES + 1
    return (scal[base + 2 * tile], scal[base + 2 * tile + 1])


def front_tile(scal, tile, x, wfm, wsb, norms, vh_ref, rs_ref, u_ref, f_ref, m_ref, p_ref, sums):
    width = x.shape[1]
    scaled, scale = norm_stats(x)
    vh_ref[...] = scaled.astype(b16)
    rs_ref[...] = jnp.broadcast_to(scale, (8, width))
    normed = (scaled * norms[:, 0:1] + norms[:, 1:2]).astype(b16)
    u_ref[...] = normed
    joint = nn(wfm, normed)
    feats = joint[:D].astype(b16)
    middle = joint[D:].astype(b16)
    f_ref[...] = feats
    m_ref[...] = middle
    logits = tn(wsb, middle).reshape(HEADS, SLICES, width)
    top = jnp.max(logits, axis=1, keepdims=True)
    expo = jnp.exp(logits - top)
    weights = expo / jnp.sum(expo, axis=1, keepdims=True)
    weights_r = weights.reshape(HS, width).astype(b16)
    p_ref[...] = weights_r
    low, high = tile_range(scal, tile)

    def add(mesh, carry):
        keep = tile_mask(scal, mesh, tile, width).astype(b16)
        wide = jnp.concatenate(
            [feats * keep, jnp.broadcast_to(keep, (128, width))], axis=0
        )
        full = nt(weights_r, wide)
        sums[mesh, :, :D] += pick_diag(full[:, :D], DH)
        sums[mesh, :, D:] += pick_diag(full[:, D:], 16)
        return carry

    lax.fori_loop(low, high + 1, add, 0)


def write_edges(scal, tiles, sums, edge_ref):
    first = tile_range(scal, 0)[0]
    last = tile_range(scal, tiles - 1)[1]
    for side, mesh in ((0, first), (1, last)):
        edge_ref[side, :SLICES] = sums[mesh].astype(b16)
        edge_ref[side, SLICES:] = jnp.full(
            (EDGE - SLICES, sums.shape[2]), mesh.astype(f32), f32
        ).astype(b16)


def add_edges(own, mesh, recv_ref):
    total = own
    wanted = mesh.astype(f32)
    for slot in range(recv_ref.shape[0]):
        match = recv_ref[slot, SLICES : SLICES + 1].astype(f32) == wanted
        total = total + jnp.where(match, recv_ref[slot, :SLICES].astype(f32), 0.0)
    return total


def attend_parts(total, wqb):
    expand = (iota((128, D), 0) == 16 * (iota((128, D), 1) // DH)).astype(f32)
    count = nn(total[:, D:], expand, HIGH)
    slice_tok = total[:, :D] / count
    triple = nn(slice_tok, wqb, HIGH)
    queries, keyset, valueset = triple[:, :D], triple[:, D : 2 * D], triple[:, 2 * D :]
    key_wide = spread_diag(keyset)
    value_wide = spread_diag(valueset)
    scores = (nt(key_wide, queries, HIGH) * (1.0 / math.sqrt(DH))).reshape(HEADS, SLICES, SLICES)
    expo = jnp.exp(scores - jnp.max(scores, axis=1, keepdims=True))
    prob = (expo / jnp.sum(expo, axis=1, keepdims=True)).reshape(HS, SLICES)
    return (slice_tok, count, queries, key_wide, value_wide, prob)


def attend_all(scal, tiles, sums, recv_ref, wqb, total_ref, attended_ref, wide_ref):
    first = tile_range(scal, 0)[0]
    last = tile_range(scal, tiles - 1)[1]

    def one(mesh, carry):
        total = add_edges(sums[mesh], mesh, recv_ref)
        total_ref[mesh] = total
        _, _, _, _, value_wide, prob = attend_parts(total, wqb)
        attended = tn(prob, value_wide, HIGH).astype(b16)
        attended_ref[mesh] = attended
        wide_ref[mesh] = spread_diag(attended)
        return carry

    lax.fori_loop(first, last + 1, one, 0)


def spread_tile(scal, tile, wide_ref, p_ref, spread):
    low, high = tile_range(scal, tile)
    weights_r = p_ref[...]
    width = weights_r.shape[1]

    def one(mesh, carry):
        keep = tile_mask(scal, mesh, tile, width)
        spread[...] = jnp.where(keep, tn(wide_ref[mesh], weights_r), spread[...])
        return carry

    lax.fori_loop(low, high + 1, one, 0)
    return spread[...].astype(b16)


GELU_A = math.sqrt(2.0 / math.pi)
GELU_B = 0.044715


def gelu_pair(hidden):
    square = hidden * hidden
    bend = jnp.tanh(hidden * (GELU_A + (GELU_A * GELU_B) * square))
    half = 0.5 + 0.5 * bend
    value = hidden * half
    slope = half + (0.5 * hidden) * (1.0 - bend * bend) * (
        GELU_A + (3.0 * GELU_A * GELU_B) * square
    )
    return (value, slope)


CHUNK = 256


def mlp_back_tile(scal, tile, grad, slopes, actives, scaled_two, scale_two, normed_two_r, spread_r,
                  weights_r, wout, wup, wdown, norms, d2_ref, de_ref, sums,
                  gup, gdown, gout, gnorm):
    width = grad.shape[1]
    grad_r = grad.astype(b16)
    grad_normed = jnp.zeros((D, width), f32)
    for start in range(0, FF, CHUNK):
        part = slice(start, start + CHUNK)
        back = (slopes(part) * nn(wdown[part], grad_r)).astype(b16)
        gup[:, part] += nt(normed_two_r, back)
        gdown[:, part] += nt(grad_r, actives(part))
        grad_normed = grad_normed + nn(wup[:, part], back)
    gnorm[2] += fold_lanes(grad_normed * scaled_two)
    gnorm[3] += fold_lanes(grad_normed)
    grad_middle = grad + norm_back(grad_normed, scaled_two, scale_two, norms[:, 2:3])
    d2_ref[...] = grad_middle
    branch_r = grad_middle.astype(b16)
    gout[...] += nt(spread_r, branch_r)
    spread_grad = nn(wout, branch_r).astype(b16)
    de_ref[...] = spread_grad
    low, high = tile_range(scal, tile)

    def add(mesh, carry):
        keep = tile_mask(scal, mesh, tile, width).astype(b16)
        sums[mesh] += pick_diag(nt(weights_r, spread_grad * keep), DH)
        return carry

    lax.fori_loop(low, high + 1, add, 0)


def attend_back_all(scal, tiles, sums, recv_ref, total_ref, attended_ref, wqb, both, dcount, gqkv):
    first = tile_range(scal, 0)[0]
    last = tile_range(scal, tiles - 1)[1]
    root = 1.0 / math.sqrt(DH)

    def one(mesh, carry):
        grad = add_edges(sums[mesh], mesh, recv_ref)
        slice_tok, count, queries, key_wide, value_wide, prob = attend_parts(total_ref[mesh], wqb)
        grad_prob = nt(value_wide, grad, HIGH)
        inner = prob * grad_prob
        mixed = group_sum(inner)
        grad_scores = root * (
            inner
            - (prob.reshape(HEADS, SLICES, SLICES) * mixed).reshape(HS, SLICES)
        )
        grad_q = tn(grad_scores, key_wide, HIGH)
        grad_k = pick_diag(nn(grad_scores, queries, HIGH), DH)
        grad_v = pick_diag(nn(prob, grad, HIGH), DH)
        triple = jnp.concatenate([grad_q, grad_k, grad_v], axis=1)
        grad_tok = nt(triple, wqb, HIGH)
        grad_sum = grad_tok / count
        both[mesh, :, :D] = spread_diag(attended_ref[mesh])
        both[mesh, :, D:] = spread_diag(grad_sum.astype(b16))
        grad_count = spread_diag(-(grad_sum * slice_tok))
        dcount[mesh] = jnp.broadcast_to(jnp.sum(grad_count, axis=1, keepdims=True), (HS, 128))
        seen = (recv_ref[0, SLICES : SLICES + 1, :1].astype(f32) == mesh.astype(f32)).astype(f32)
        gqkv[...] += tn(slice_tok, triple, HIGH) * (1.0 - seen)
        return carry

    lax.fori_loop(first, last + 1, one, 0)


def attend_back_tile(scal, tile, both, dcount, de_ref, f_ref, m_ref, p_ref, u_ref, vh_ref, rs_ref,
                     d2_ref, wfm, wsb, norms, grad_p, grad_f, gfm, gws, gnorm):
    low, high = tile_range(scal, tile)
    weights_r = p_ref[...]
    width = weights_r.shape[1]
    pair = jnp.concatenate([de_ref[...], f_ref[...]], axis=0)

    def one(mesh, carry):
        keep = tile_mask(scal, mesh, tile, width)
        back = nn(both[mesh], pair) + dcount[mesh][:, :1]
        grad_p[...] = jnp.where(keep, back, grad_p[...])
        grad_f[...] = jnp.where(keep, tn(both[mesh, :, D:], weights_r), grad_f[...])
        return carry

    lax.fori_loop(low, high + 1, one, 0)
    weights = weights_r.astype(f32)
    inner = weights * grad_p[...]
    mixed = group_sum(inner)
    grad_logits = (
        inner - (weights.reshape(HEADS, SLICES, width) * mixed).reshape(HS, width)
    ).astype(b16)
    gws[...] += nt(m_ref[...], grad_logits)
    grad_m = nn(wsb, grad_logits).astype(b16)
    grad_fm = jnp.concatenate([grad_f[...].astype(b16), grad_m], axis=0)
    gfm[...] += nt(u_ref[...], grad_fm)
    grad_normed = tn(wfm, grad_fm)
    scaled = vh_ref[...].astype(f32)
    gnorm[0] += fold_lanes(grad_normed * scaled)
    gnorm[1] += fold_lanes(grad_normed)
    return d2_ref[...] + norm_back(grad_normed, scaled, rs_ref[:1], norms[:, 0:1])


def fold_small(gws_ref, gqkv_ref, gws_out, gqkv_out):
    left = repeat_rows(DH)
    kept = jnp.where(same_head(DH, SLICES, (D, HS)), gws_ref[...], 0.0)
    gws_out[...] = nt(tn(left, kept, HIGH), slice_repeat(), HIGH)
    for part in range(3):
        square = jnp.where(
            same_head(DH, DH, (D, D)), gqkv_ref[:, part * D : (part + 1) * D], 0.0
        )
        gqkv_out[part] = nn(tn(left, square, HIGH), left, HIGH)


def norm_columns(gnorm, rows, out_ref):
    lane = iota((D, 128), 1)
    total = jnp.zeros((D, 128), f32)
    for row in rows:
        total = total + jnp.where(lane == row, jnp.sum(gnorm[row], axis=1, keepdims=True), 0.0)
    out_ref[...] = total


def first_kernel(tiles, scal, tok_ref, wfm_ref, wsb_ref, norm_ref,
                 xt_ref, vh_ref, rs_ref, u_ref, f_ref, m_ref, p_ref, sums, edge_ref):
    tile = pl.program_id(0)

    @pl.when(tile == 0)
    def _():
        sums[...] = jnp.zeros_like(sums)

    x = tok_ref[...].astype(f32).T
    xt_ref[...] = x.astype(b16)
    front_tile(scal, tile, x, wfm_ref[...], wsb_ref[...], norm_ref[...],
               vh_ref, rs_ref, u_ref, f_ref, m_ref, p_ref, sums)

    @pl.when(tile == tiles - 1)
    def _():
        write_edges(scal, tiles, sums, edge_ref)


def second_kernel(tiles, scal, xt_ref, p0_ref, sums0, recv_ref, wout_ref, wup_ref, wdown_ref, wqb_ref, norm0_ref,
                  wfm_ref, wsb_ref, norm1_ref,
                  e_ref, vh2_ref, rs2_ref, u2_ref, gp_ref, z_ref, att_ref, total_ref,
                  x1_ref, vh_ref, rs_ref, u_ref, f_ref, m_ref, p_ref, sums, edge_ref,
                  wide, spread):
    tile = pl.program_id(0)

    @pl.when(tile == 0)
    def _():
        sums[...] = jnp.zeros_like(sums)
        attend_all(scal, tiles, sums0, recv_ref, wqb_ref[...], total_ref, att_ref, wide)

    norms = norm0_ref[...]
    spread_r = spread_tile(scal, tile, wide, p0_ref, spread)
    e_ref[...] = spread_r
    middle = xt_ref[...].astype(f32) + tn(wout_ref[...], spread_r)
    scaled_two, scale_two = norm_stats(middle)
    vh2_ref[...] = scaled_two.astype(b16)
    rs2_ref[...] = jnp.broadcast_to(scale_two, rs2_ref.shape)
    normed_two_r = (scaled_two * norms[:, 2:3] + norms[:, 3:4]).astype(b16)
    u2_ref[...] = normed_two_r
    x = middle
    for start in range(0, FF, CHUNK):
        part = slice(start, start + CHUNK)
        active, slope = gelu_pair(tn(wup_ref[:, part], normed_two_r))
        active_r = active.astype(b16)
        z_ref[part] = active_r
        gp_ref[part] = slope.astype(b16)
        x = x + tn(wdown_ref[part], active_r)
    x1_ref[...] = x
    front_tile(scal, tile, x, wfm_ref[...], wsb_ref[...], norm1_ref[...],
               vh_ref, rs_ref, u_ref, f_ref, m_ref, p_ref, sums)

    @pl.when(tile == tiles - 1)
    def _():
        write_edges(scal, tiles, sums, edge_ref)


def third_kernel(tiles, scal, x1_ref, p_ref, sums1, recv_ref, cot_ref, wout_ref, wup_ref, wdown_ref, wqb_ref, norm_ref,
                 out_ref, d2_ref, de_ref, att_ref, total_ref, sums, edge_ref,
                 gup_ref, gdown_ref, gout_ref, gn_ref,
                 wide, spread, gnorm, slope_s, active_s):
    tile = pl.program_id(0)

    @pl.when(tile == 0)
    def _():
        sums[...] = jnp.zeros_like(sums)
        gup_ref[...] = jnp.zeros_like(gup_ref)
        gdown_ref[...] = jnp.zeros_like(gdown_ref)
        gout_ref[...] = jnp.zeros_like(gout_ref)
        gnorm[...] = jnp.zeros_like(gnorm)
        attend_all(scal, tiles, sums1, recv_ref, wqb_ref[...], total_ref, att_ref, wide)

    norms = norm_ref[...]
    spread_r = spread_tile(scal, tile, wide, p_ref, spread)
    middle = x1_ref[...] + tn(wout_ref[...], spread_r)
    scaled_two, scale_two = norm_stats(middle)
    normed_two_r = (scaled_two * norms[:, 2:3] + norms[:, 3:4]).astype(b16)
    x = middle
    for start in range(0, FF, CHUNK):
        part = slice(start, start + CHUNK)
        active, slope = gelu_pair(tn(wup_ref[:, part], normed_two_r))
        active_r = active.astype(b16)
        active_s[part] = active_r
        slope_s[part] = slope
        x = x + tn(wdown_ref[part], active_r)
    out_ref[...] = x.T.astype(b16)
    grad = cot_ref[...].astype(f32).T
    mlp_back_tile(scal, tile, grad, lambda part: slope_s[part], lambda part: active_s[part],
                  scaled_two, scale_two, normed_two_r, spread_r, p_ref[...],
                  wout_ref[...], wup_ref, wdown_ref, norms, d2_ref, de_ref, sums,
                  gup_ref, gdown_ref, gout_ref, gnorm)

    @pl.when(tile == tiles - 1)
    def _():
        write_edges(scal, tiles, sums, edge_ref)
        norm_columns(gnorm, (2, 3), gn_ref)


def fourth_kernel(tiles, scal, sums1, recv_ref, att_ref, total_ref, de1_ref, f_ref, m_ref, p1_ref, u_ref, vh_ref, rs_ref, d21_ref,
                  wfm_ref, wsb_ref, wqb_ref, norm1_ref,
                  gp_ref, z_ref, vh2_ref, rs2_ref, u2_ref, e_ref, p0_ref, wout_ref, wup_ref, wdown_ref, norm0_ref,
                  gfm_ref, gws_out, gqkv_out, d2_ref, de_ref, sums, edge_ref, gup_ref, gdown_ref, gout_ref, gn1_ref, gn0_ref,
                  both, dcount, grad_p, grad_f, gws, gqkv, gnorm):
    tile = pl.program_id(0)

    @pl.when(tile == 0)
    def _():
        for ref in (sums, gfm_ref, gws, gqkv, gup_ref, gdown_ref, gout_ref, gnorm):
            ref[...] = jnp.zeros_like(ref)
        attend_back_all(scal, tiles, sums1, recv_ref, total_ref, att_ref, wqb_ref[...], both, dcount, gqkv)

    grad = attend_back_tile(scal, tile, both, dcount, de1_ref, f_ref, m_ref, p1_ref, u_ref, vh_ref, rs_ref,
                            d21_ref, wfm_ref[...], wsb_ref[...], norm1_ref[...], grad_p, grad_f, gfm_ref, gws, gnorm)
    mlp_back_tile(scal, tile, grad, lambda part: gp_ref[part].astype(f32), lambda part: z_ref[part],
                  vh2_ref[...].astype(f32), rs2_ref[:1], u2_ref[...], e_ref[...], p0_ref[...],
                  wout_ref[...], wup_ref, wdown_ref, norm0_ref[...], d2_ref, de_ref, sums,
                  gup_ref, gdown_ref, gout_ref, gnorm)

    @pl.when(tile == tiles - 1)
    def _():
        write_edges(scal, tiles, sums, edge_ref)
        norm_columns(gnorm, (0, 1), gn1_ref)
        norm_columns(gnorm, (2, 3), gn0_ref)
        fold_small(gws, gqkv, gws_out, gqkv_out)


def fifth_kernel(tiles, scal, sums0, recv_ref, att_ref, total_ref, de_ref, f_ref, m_ref, p_ref, u_ref, vh_ref, rs_ref, d2_ref,
                 wfm_ref, wsb_ref, wqb_ref, norm_ref,
                 gin_ref, gfm_ref, gws_out, gqkv_out, gn_ref,
                 both, dcount, grad_p, grad_f, gws, gqkv, gnorm):
    tile = pl.program_id(0)

    @pl.when(tile == 0)
    def _():
        for ref in (gfm_ref, gws, gqkv, gnorm):
            ref[...] = jnp.zeros_like(ref)
        attend_back_all(scal, tiles, sums0, recv_ref, total_ref, att_ref, wqb_ref[...], both, dcount, gqkv)

    grad = attend_back_tile(scal, tile, both, dcount, de_ref, f_ref, m_ref, p_ref, u_ref, vh_ref, rs_ref,
                            d2_ref, wfm_ref[...], wsb_ref[...], norm_ref[...], grad_p, grad_f, gfm_ref, gws, gnorm)
    gin_ref[...] = grad.T

    @pl.when(tile == tiles - 1)
    def _():
        norm_columns(gnorm, (0, 1), gn_ref)
        fold_small(gws, gqkv, gws_out, gqkv_out)


class Args:
    def __init__(self, rows, width):
        self.rows, self.width = rows, width
        self.operands, self.in_specs, self.outs, self.out_specs = [], [], [], []

    def cols(self, *arrays):
        for array in arrays:
            self.operands.append(array)
            self.in_specs.append(
                pl.BlockSpec((array.shape[0], self.width), lambda tile, scal: (0, tile))
            )

    def points(self, *arrays):
        for array in arrays:
            self.operands.append(array)
            self.in_specs.append(
                pl.BlockSpec((self.width, array.shape[1]), lambda tile, scal: (tile, 0))
            )

    def whole(self, *arrays):
        for array in arrays:
            rank = array.ndim
            self.operands.append(array)
            self.in_specs.append(
                pl.BlockSpec(array.shape, lambda tile, scal, rank=rank: (0,) * rank)
            )

    def out_cols(self, *pairs):
        for height, dtype in pairs:
            self.outs.append(jax.ShapeDtypeStruct((height, self.rows), dtype))
            self.out_specs.append(
                pl.BlockSpec((height, self.width), lambda tile, scal: (0, tile))
            )

    def out_points(self, *dtypes):
        for dtype in dtypes:
            self.outs.append(jax.ShapeDtypeStruct((self.rows, D), dtype))
            self.out_specs.append(pl.BlockSpec((self.width, D), lambda tile, scal: (tile, 0)))

    def out_whole(self, *pairs):
        for shape, dtype in pairs:
            rank = len(shape)
            self.outs.append(jax.ShapeDtypeStruct(shape, dtype))
            self.out_specs.append(
                pl.BlockSpec(shape, lambda tile, scal, rank=rank: (0,) * rank)
            )

    def call(self, body, scal, scratch, name):
        tiles = self.rows // self.width
        return pl.pallas_call(
            functools.partial(body, tiles),
            grid_spec=pltpu.PrefetchScalarGridSpec(
                num_scalar_prefetch=1,
                grid=(tiles,),
                in_specs=self.in_specs,
                out_specs=self.out_specs,
                scratch_shapes=scratch,
            ),
            out_shape=self.outs,
            compiler_params=pltpu.CompilerParams(
                dimension_semantics=("arbitrary",), vmem_limit_bytes=VMEM_BYTES
            ),
            name=name,
        )(scal, *self.operands)


def adam_update(master, grad, first, second, rate):
    new_first = beta_one * first + (1.0 - beta_one) * grad
    new_second = beta_two * second + (1.0 - beta_two) * grad * grad
    fix_one = 1.0 - beta_one**STEP
    fix_two = 1.0 - beta_two**STEP
    direction = new_first / fix_one / (jnp.sqrt(new_second / fix_two) + adam_eps)
    return (master - rate * (direction + decay_rate * master), new_first, new_second)


def flat_blocks(n_head, gfm, gout, gup, gdown):
    def columns(grad):
        width = grad.shape[1] // n_head
        return grad.reshape(D, n_head, width).transpose(1, 0, 2).reshape(n_head, -1)

    return jnp.concatenate(
        [
            columns(gfm[:, :D]),
            columns(gfm[:, D:]),
            gout.reshape(n_head, -1),
            columns(gup),
            columns(gdown),
        ],
        axis=1,
    ).reshape(n_head, -1, BLOCK)


def on_device(
    sizes,
    tokens,
    cotangent,
    segment_ids,
    owner,
    w_fx,
    w_mid,
    w_out,
    w_up,
    w_down,
    small_master,
    small_first,
    small_second,
    master_table,
    first_table,
    second_table,
):
    n_pts, n_head = sizes
    rows = tokens.shape[0]
    width = min(512, rows)
    tiles = rows // width
    most = rows * n_pts * n_head // LARGEST
    window = (rows - 1 + most - 1) // rows
    layers = w_fx.shape[0]

    ids = lax.dynamic_slice_in_dim(segment_ids, lax.axis_index("head") * rows, rows, 0)
    bounds = jnp.sum(
        (ids[None, :] < jnp.arange(MESHES + 1, dtype=jnp.int32)[:, None]).astype(jnp.int32), axis=1
    )
    tile_ids = ids.reshape(tiles, width)
    ranges = jnp.stack([tile_ids[:, 0], tile_ids[:, -1]], axis=1).reshape(-1)
    scal = jnp.concatenate([bounds, ranges]).astype(jnp.int32)

    edge_ws = DH * SLICES
    edge_qkv = edge_ws + 3 * DH * DH
    ws = small_master[:, :edge_ws].reshape(layers, DH, SLICES).astype(b16).astype(f32)
    wqkv = small_master[:, edge_ws:edge_qkv].reshape(layers, 3, DH, DH)
    norms = small_master[:, edge_qkv:].reshape(layers, 4, D).transpose(0, 2, 1)
    norms = jnp.pad(norms, ((0, 0), (0, 0), (0, 124)))

    gathered, wsb, wqb = gather_weights(n_head, w_fx, w_mid, w_out, ws, wqkv)
    full = gathered.transpose(1, 2, 0, 3, 4).reshape(layers, 3 * D, D)
    wfm = full[:, : 2 * D]
    wout = full[:, 2 * D :]

    sums_shape = (MESHES, SLICES, D + 128)
    grad_sums_shape = (MESHES, SLICES, D)
    front_cols = ((D, b16), (8, f32), (D, b16), (D, b16), (D, b16), (HS, b16))
    wide_scratch = [pltpu.VMEM((MESHES, HS, D), b16), pltpu.VMEM((D, width), f32)]

    args = Args(rows, width)
    args.points(tokens)
    args.whole(wfm[0], wsb[0], norms[0])
    args.out_cols((D, b16), *front_cols)
    args.out_whole((sums_shape, f32), ((2, EDGE, D + 128), b16))
    xt0, vh0, rs0, u0, f0, m0, p0, sums0, edge = args.call(first_kernel, scal, [], "first")
    recv = swap_edges(sizes, window, edge, 1)

    args = Args(rows, width)
    args.cols(xt0, p0)
    args.whole(sums0, recv, wout[0], w_up[0], w_down[0], wqb[0], norms[0], wfm[1], wsb[1], norms[1])
    args.out_cols((D, b16), (D, b16), (8, f32), (D, b16), (FF, b16), (FF, b16))
    args.out_whole((grad_sums_shape, b16), (sums_shape, f32))
    args.out_cols((D, f32), *front_cols)
    args.out_whole((sums_shape, f32), ((2, EDGE, D + 128), b16))
    (e0, vh20, rs20, u20, gp0, z0, att0, total0, x1, vh1, rs1, u1, f1, m1, p1, sums1, edge) = args.call(
        second_kernel, scal, wide_scratch, "second"
    )
    recv = swap_edges(sizes, window, edge, 1)

    args = Args(rows, width)
    args.cols(x1, p1)
    args.whole(sums1, recv)
    args.points(cotangent)
    args.whole(wout[1], w_up[1], w_down[1], wqb[1], norms[1])
    args.out_points(b16)
    args.out_cols((D, f32), (D, b16))
    args.out_whole((grad_sums_shape, b16), (sums_shape, f32), (grad_sums_shape, f32), ((2, EDGE, D), b16))
    args.out_whole(((D, FF), f32), ((D, FF), f32), ((D, D), f32), ((D, 128), f32))
    (layer_out, d21, de1, att1, total1, dsums1, edge, gup1, gdown1, gout1, gn1b) = args.call(
        third_kernel,
        scal,
        wide_scratch
        + [pltpu.VMEM((4, D, 128), f32), pltpu.VMEM((FF, width), f32), pltpu.VMEM((FF, width), b16)],
        "third",
    )
    recv = swap_edges(sizes, window, edge, 2)

    back_scratch = [
        pltpu.VMEM((MESHES, HS, 2 * D), b16),
        pltpu.VMEM((MESHES, HS, 128), f32),
        pltpu.VMEM((HS, width), f32),
        pltpu.VMEM((D, width), f32),
        pltpu.VMEM((D, HS), f32),
        pltpu.VMEM((D, 3 * D), f32),
        pltpu.VMEM((4, D, 128), f32),
    ]
    small_outs = (((DH, SLICES), f32), ((3, DH, DH), f32))

    args = Args(rows, width)
    args.whole(dsums1, recv, att1, total1)
    args.cols(de1, f1, m1, p1, u1, vh1, rs1, d21)
    args.whole(wfm[1], wsb[1], wqb[1], norms[1])
    args.cols(gp0, z0, vh20, rs20, u20, e0, p0)
    args.whole(wout[0], w_up[0], w_down[0], norms[0])
    args.out_whole(((D, 2 * D), f32), *small_outs)
    args.out_cols((D, f32), (D, b16))
    args.out_whole((grad_sums_shape, f32), ((2, EDGE, D), b16))
    args.out_whole(((D, FF), f32), ((D, FF), f32), ((D, D), f32), ((D, 128), f32), ((D, 128), f32))
    (gfm1, gws1, gqkv1, d20, de0, dsums0, edge, gup0, gdown0, gout0, gn1a, gn0b) = args.call(
        fourth_kernel, scal, back_scratch, "fourth"
    )
    recv = swap_edges(sizes, window, edge, 2)

    args = Args(rows, width)
    args.whole(dsums0, recv, att0, total0)
    args.cols(de0, f0, m0, p0, u0, vh0, rs0, d20)
    args.whole(wfm[0], wsb[0], wqb[0], norms[0])
    args.out_points(f32)
    args.out_whole(((D, 2 * D), f32), *small_outs, ((D, 128), f32))
    input_grad, gfm0, gws0, gqkv0, gn0a = args.call(fifth_kernel, scal, back_scratch, "fifth")

    def small_grads(gws, gqkv, front, back):
        return jnp.concatenate(
            [
                gws.reshape(-1),
                gqkv.reshape(-1),
                jnp.concatenate([front[:, :2], back[:, 2:4]], axis=1).T.reshape(-1),
            ]
        )

    small_total = lax.psum(
        jnp.stack([small_grads(gws0, gqkv0, gn0a, gn0b), small_grads(gws1, gqkv1, gn1a, gn1b)]),
        ("pts", "head"),
    )
    totals = []
    for parts in ((gfm0, gout0, gup0, gdown0), (gfm1, gout1, gup1, gdown1)):
        flat = flat_blocks(n_head, *[part.astype(b16) for part in parts])
        mine = lax.psum_scatter(flat, "head", scatter_dimension=0, tiled=True)
        totals.append(lax.psum(mine.reshape(-1, BLOCK), "pts"))
    total_grad = jnp.concatenate(totals, axis=0).astype(f32)

    block_total = total_grad.shape[0]
    cap = master_table.shape[0]
    my_index = lax.axis_index("pts")
    block_ids = jnp.arange(block_total)
    same_owner = (owner[:, None] == owner[None, :]) & (block_ids[None, :] < block_ids[:, None])
    slot = jnp.sum(same_owner.astype(jnp.int32), axis=1)
    table_row = owner * cap + slot
    place_all = (jnp.arange(n_pts * cap)[:, None] == table_row[None, :]).astype(f32)
    mine_place = lax.dynamic_slice_in_dim(place_all, my_index * cap, cap, 0)
    own_grad = jnp.dot(mine_place, total_grad, precision=HIGH)
    filled = jnp.sum(mine_place, axis=1)[:, None] > 0.5
    upd_master, upd_first, upd_second = adam_update(
        master_table, own_grad, first_table, second_table, rate_large
    )
    new_master = jnp.where(filled, upd_master, master_table)
    new_first = jnp.where(filled, upd_first, first_table)
    new_second = jnp.where(filled, upd_second, second_table)
    collected = lax.all_gather(new_master.astype(b16), "pts", axis=0, tiled=True)
    pick_back = (table_row[:, None] == jnp.arange(n_pts * cap)[None, :]).astype(b16)
    fresh = jnp.dot(pick_back, collected, preferred_element_type=f32).astype(b16)
    small_new, small_first_new, small_second_new = adam_update(
        small_master, small_total, small_first, small_second, rate_small
    )
    return (
        layer_out,
        input_grad,
        new_master,
        new_first,
        new_second,
        fresh,
        small_new,
        small_first_new,
        small_second_new,
    )


def solution(mesh):
    sizes = (mesh.shape["pts"], mesh.shape["head"])
    return jax.shard_map(
        functools.partial(on_device, sizes),
        mesh=mesh,
        in_specs=(
            P(("pts", "head"), None),
            P(("pts", "head"), None),
            P("pts"),
            P(),
            P(None, None, "head"),
            P(None, None, "head"),
            P(None, "head", None),
            P(),
            P(),
            P(),
            P(),
            P(),
            P("pts", "head"),
            P("pts", "head"),
            P("pts", "head"),
        ),
        out_specs=(
            P(("pts", "head"), None),
            P(("pts", "head"), None),
            P("pts", "head"),
            P("pts", "head"),
            P("pts", "head"),
            P(None, "head"),
            P(),
            P(),
            P(),
        ),
        check_vma=False,
    )
```

```python
import functools
import math

import jax
import jax.numpy as jnp
from jax import lax
from jax.experimental import pallas as pl
from jax.experimental.pallas import tpu as pltpu
from jax.sharding import PartitionSpec as P

D = 256
HEADS = 8
DH = 32
SLICES = 64
HS = HEADS * SLICES
FF = 1024
MESHES = 24
BLOCK = 2048
SMALL = 6144
STEP = 10
LARGEST = 12
EDGE = 80
VMEM_BYTES = 58 << 20

MESH = pl.DeviceIdType.MESH
HIGH = lax.Precision.HIGHEST
norm_eps = 1e-05
beta_one = 0.9
beta_two = 0.95
adam_eps = 1e-08
decay_rate = 0.1
rate_large = 0.1
rate_small = 0.75
f32 = jnp.float32
b16 = jnp.bfloat16


def nn(a, b, precision=None):
    return lax.dot_general(
        a, b, (((1,), (0,)), ((), ())), preferred_element_type=f32, precision=precision
    )


def nt(a, b, precision=None):
    return lax.dot_general(
        a, b, (((1,), (1,)), ((), ())), preferred_element_type=f32, precision=precision
    )


def tn(a, b, precision=None):
    return lax.dot_general(
        a, b, (((0,), (0,)), ((), ())), preferred_element_type=f32, precision=precision
    )


def iota(shape, axis):
    return lax.broadcasted_iota(jnp.int32, shape, axis)


def pick_diag(full, per_head):
    lane_head = iota((SLICES, full.shape[1]), 1) // per_head
    total = jnp.where(lane_head == 0, full[:SLICES], 0.0)
    for head in range(1, HEADS):
        total = total + jnp.where(
            lane_head == head, full[head * SLICES : (head + 1) * SLICES], 0.0
        )
    return total


def spread_diag(small):
    lane_head = iota((SLICES, D), 1) // DH
    return jnp.concatenate(
        [jnp.where(lane_head == head, small, jnp.zeros_like(small)) for head in range(HEADS)],
        axis=0,
    )


def repeat_rows(width):
    return (iota((D, width), 0) % width == iota((D, width), 1)).astype(f32)


def slice_repeat():
    return (iota((SLICES, HS), 1) % SLICES == iota((SLICES, HS), 0)).astype(f32)


def same_head(rows_per, cols_per, shape):
    return (iota(shape, 0) // rows_per) == (iota(shape, 1) // cols_per)


def start_gather(n_head, picks, send_sem, recv_sem):
    me = lax.axis_index("head")
    copies = []
    for index, ref in enumerate(picks):
        for step in range(1, n_head):
            copy = pltpu.make_async_remote_copy(
                src_ref=ref.at[:, me],
                dst_ref=ref.at[:, me],
                send_sem=send_sem.at[index, step - 1],
                recv_sem=recv_sem.at[index, step - 1],
                device_id={"head": lax.rem(me + step, n_head)},
                device_id_type=MESH,
            )
            copy.start()
            copies.append(copy)
    return copies


def unroll_slices(row_of, out):
    lane = iota((1, 128), 1)
    for pair in range(DH // 2):
        row = row_of(pair)
        out[2 * pair : 2 * pair + 1] = jnp.where(lane < SLICES, row, 0.0)
        out[2 * pair + 1 : 2 * pair + 2] = jnp.where(
            lane < SLICES, pltpu.roll(row, 128 - SLICES, 1), 0.0
        )


def opening_kernel(n_head, tiles, ids_ref, wfx_ref, wmid_ref, sm_ref,
                   out_ref, wsb_ref, norm_ref, scal_ref, send_sem, recv_sem, slices_s, norm_s):
    me = lax.axis_index("head")
    barrier = pltpu.get_barrier_semaphore()
    for step in range(1, n_head):
        pl.semaphore_signal(
            barrier, inc=1, device_id={"head": lax.rem(me + step, n_head)}, device_id_type=MESH
        )
    out_ref[0, me] = wfx_ref[0]
    out_ref[1, me] = wmid_ref[0]
    pl.semaphore_wait(barrier, n_head - 1)
    copies = start_gather(n_head, [out_ref], send_sem, recv_sem)
    layers = sm_ref.shape[0]
    left = repeat_rows(DH)
    right = (iota((128, HS), 1) % SLICES == iota((128, HS), 0)).astype(b16)
    for layer in range(layers):
        unroll_slices(lambda pair: sm_ref[layer : layer + 1, 128 * pair : 128 * pair + 128], slices_s)
        wide = nn(slices_s[...].astype(b16), right)
        tiled = jnp.concatenate([wide] * HEADS, axis=0)
        wsb_ref[layer] = jnp.where(same_head(DH, SLICES, (D, HS)), tiled, 0.0).astype(b16)
        norm_s[...] = jnp.zeros_like(norm_s)
        for row in range(4):
            start = SMALL - 4 * D + row * D
            norm_s[row : row + 1] = sm_ref[layer : layer + 1, start : start + D]
        norm_ref[layer] = norm_s[...].T
    rows = ids_ref.shape[0] // n_head
    ids = ids_ref[pl.ds(pl.multiple_of(me * rows, rows), rows), :]
    for mesh in range(MESHES + 1):
        scal_ref[mesh] = jnp.sum((ids < mesh).astype(jnp.int32))
    deep = rows // tiles
    for tile in range(tiles):
        part = ids[tile * deep : (tile + 1) * deep]
        scal_ref[MESHES + 1 + 2 * tile] = jnp.min(part)
        scal_ref[MESHES + 2 + 2 * tile] = jnp.max(part)
    for copy in copies:
        copy.wait()


def opening(n_head, tiles, ids, w_fx, w_mid, small):
    layers, part, _ = w_fx.shape
    vmem = pl.BlockSpec(memory_space=pltpu.VMEM)
    return pl.pallas_call(
        functools.partial(opening_kernel, n_head, tiles),
        out_shape=(
            jax.ShapeDtypeStruct((2, n_head, part, D), b16),
            jax.ShapeDtypeStruct((layers, D, HS), b16),
            jax.ShapeDtypeStruct((layers, D, 128), f32),
            jax.ShapeDtypeStruct((MESHES + 1 + 2 * tiles,), jnp.int32),
        ),
        in_specs=[vmem] * 4,
        out_specs=[vmem] * 3 + [pl.BlockSpec(memory_space=pltpu.SMEM)],
        scratch_shapes=[
            pltpu.SemaphoreType.DMA((1, n_head - 1)),
            pltpu.SemaphoreType.DMA((1, n_head - 1)),
            pltpu.VMEM((DH, 128), f32),
            pltpu.VMEM((128, D), f32),
        ],
        compiler_params=pltpu.CompilerParams(
            collective_id=0, has_side_effects=True, vmem_limit_bytes=VMEM_BYTES
        ),
        name="opening",
    )(ids, w_fx, w_mid, small)


def place_of(sizes, shift):
    n_pts, n_head = sizes
    total = n_pts * n_head
    me = lax.axis_index("pts") * n_head + lax.axis_index("head")
    other = lax.rem(me + (shift + total), total)
    return (other // n_head, lax.rem(other, n_head))


def greet(sizes, window):
    barrier = pltpu.get_barrier_semaphore()
    for step in range(1, window + 1):
        for shift in (step, -step):
            pl.semaphore_signal(barrier, inc=1, device_id=place_of(sizes, shift), device_id_type=MESH)
    return barrier


def start_edges(sizes, window, edge_ref, out_ref, send_sem, recv_sem):
    copies = []
    for step in range(1, window + 1):
        for side, shift in ((1, step), (0, -step)):
            slot = step - 1 if side == 1 else window + step - 1
            copy = pltpu.make_async_remote_copy(
                src_ref=edge_ref.at[side],
                dst_ref=out_ref.at[slot],
                send_sem=send_sem.at[slot],
                recv_sem=recv_sem.at[slot],
                device_id=place_of(sizes, shift),
                device_id_type=MESH,
            )
            copy.start()
            copies.append(copy)
    return copies


def edge_kernel(sizes, window, edge_ref, out_ref, send_sem, recv_sem):
    barrier = greet(sizes, window)
    pl.semaphore_wait(barrier, 2 * window)
    for copy in start_edges(sizes, window, edge_ref, out_ref, send_sem, recv_sem):
        copy.wait()


def edge_weights_kernel(sizes, window, edge_ref, wfx_ref, wmid_ref, wout_ref, sm_ref,
                        out_ref, wa_ref, wb_ref, wqb_ref,
                        send_sem, recv_sem, wsend_sem, wrecv_sem, square_s):
    n_head = sizes[1]
    me = lax.axis_index("head")
    barrier = greet(sizes, window)
    for step in range(1, n_head):
        pl.semaphore_signal(
            barrier, inc=1, device_id={"head": lax.rem(me + step, n_head)}, device_id_type=MESH
        )
    layers = wout_ref.shape[0]
    wa_ref[0, me] = wfx_ref[1]
    wa_ref[1, me] = wmid_ref[1]
    for layer in range(layers):
        wb_ref[layer, me] = wout_ref[layer]
    pl.semaphore_wait(barrier, 2 * window + n_head - 1)
    copies = start_edges(sizes, window, edge_ref, out_ref, send_sem, recv_sem)
    copies += start_gather(n_head, [wb_ref, wa_ref], wsend_sem, wrecv_sem)
    left = repeat_rows(DH)
    lane = iota((1, 128), 1)
    for layer in range(layers):
        for part in range(3):
            start = DH * SLICES + part * DH * DH
            for group in range(DH // 4):
                row = sm_ref[layer : layer + 1, start + 128 * group : start + 128 * group + 128]
                for inner in range(4):
                    moved = row if inner == 0 else pltpu.roll(row, 128 - DH * inner, 1)
                    square_s[4 * group + inner : 4 * group + inner + 1] = jnp.where(
                        lane < DH, moved, 0.0
                    )
            pick = (iota((D, 128), 0) % DH == iota((D, 128), 1)).astype(f32)
            square = nt(nn(left, square_s[...], HIGH), pick, HIGH)
            wqb_ref[layer, :, part * D : (part + 1) * D] = jnp.where(
                same_head(DH, DH, (D, D)), square, 0.0
            )
    for copy in copies:
        copy.wait()


def edge_call(window, collective_id, rows, width, body, extra, outs, scratch, name):
    vmem = pl.BlockSpec(memory_space=pltpu.VMEM)
    outs = [jax.ShapeDtypeStruct((2 * window, rows, width), b16)] + outs
    return pl.pallas_call(
        body,
        out_shape=outs,
        in_specs=[vmem] * (1 + extra),
        out_specs=[vmem] * len(outs),
        scratch_shapes=[
            pltpu.SemaphoreType.DMA((2 * window,)),
            pltpu.SemaphoreType.DMA((2 * window,)),
        ]
        + scratch,
        compiler_params=pltpu.CompilerParams(
            collective_id=collective_id, has_side_effects=True, vmem_limit_bytes=VMEM_BYTES
        ),
        name=name,
    )


def swap_edges(sizes, window, edge, collective_id):
    _, rows, width = edge.shape
    return edge_call(
        window, collective_id, rows, width,
        functools.partial(edge_kernel, sizes, window), 0, [], [], "swap_edges",
    )(edge)[0]


def swap_edges_weights(sizes, window, edge, w_fx, w_mid, w_out, small, collective_id):
    _, rows, width = edge.shape
    n_head = sizes[1]
    layers, part, _ = w_fx.shape
    return edge_call(
        window, collective_id, rows, width,
        functools.partial(edge_weights_kernel, sizes, window), 4,
        [
            jax.ShapeDtypeStruct((2, n_head, part, D), b16),
            jax.ShapeDtypeStruct((layers, n_head, part, D), b16),
            jax.ShapeDtypeStruct((layers, D, 3 * D), f32),
        ],
        [
            pltpu.SemaphoreType.DMA((2, n_head - 1)),
            pltpu.SemaphoreType.DMA((2, n_head - 1)),
            pltpu.VMEM((DH, 128), f32),
        ],
        "swap_edges_weights",
    )(edge, w_fx, w_mid, w_out, small)


def norm_stats(values):
    center = jnp.mean(values, axis=0, keepdims=True)
    spread = values - center
    scale = lax.rsqrt(jnp.mean(spread * spread, axis=0, keepdims=True) + norm_eps)
    return (spread * scale, scale)


def norm_back(grad_out, scaled, scale, gain):
    inner = grad_out * gain
    return scale * (
        inner
        - jnp.mean(inner, axis=0, keepdims=True)
        - scaled * jnp.mean(inner * scaled, axis=0, keepdims=True)
    )


def group_sum(values):
    return jnp.sum(values.reshape(HEADS, SLICES, values.shape[1]), axis=1, keepdims=True)


def fold_lanes(values):
    total = values[:, :128]
    for start in range(128, values.shape[1], 128):
        total = total + values[:, start : start + 128]
    return total


def tile_mask(scal, mesh, tile, width):
    spot = iota((1, width), 1) + tile * width
    return (spot >= scal[mesh]) & (spot < scal[mesh + 1])


def tile_range(scal, tile):
    base = MESHES + 1
    return (scal[base + 2 * tile], scal[base + 2 * tile + 1])


def front_tile(scal, tile, x, wfm, wsb, norms, vh_ref, rs_ref, u_ref, f_ref, m_ref, p_ref, sums):
    width = x.shape[1]
    scaled, scale = norm_stats(x)
    vh_ref[...] = scaled.astype(b16)
    rs_ref[...] = jnp.broadcast_to(scale, (8, width))
    normed = (scaled * norms[:, 0:1] + norms[:, 1:2]).astype(b16)
    u_ref[...] = normed
    joint = nn(wfm, normed)
    feats = joint[:D].astype(b16)
    middle = joint[D:].astype(b16)
    f_ref[...] = feats
    m_ref[...] = middle
    logits = tn(wsb, middle).reshape(HEADS, SLICES, width)
    top = jnp.max(logits, axis=1, keepdims=True)
    expo = jnp.exp(logits - top)
    weights = expo / jnp.sum(expo, axis=1, keepdims=True)
    weights_r = weights.reshape(HS, width).astype(b16)
    p_ref[...] = weights_r
    low, high = tile_range(scal, tile)

    def add(mesh, carry):
        keep = tile_mask(scal, mesh, tile, width).astype(b16)
        wide = jnp.concatenate(
            [feats * keep, jnp.broadcast_to(keep, (128, width))], axis=0
        )
        full = nt(weights_r, wide)
        sums[mesh, :, :D] += pick_diag(full[:, :D], DH)
        sums[mesh, :, D:] += pick_diag(full[:, D:], 16)
        return carry

    lax.fori_loop(low, high + 1, add, 0)


def write_edges(scal, tiles, sums, edge_ref):
    first = tile_range(scal, 0)[0]
    last = tile_range(scal, tiles - 1)[1]
    for side, mesh in ((0, first), (1, last)):
        edge_ref[side, :SLICES] = sums[mesh].astype(b16)
        edge_ref[side, SLICES:] = jnp.full(
            (EDGE - SLICES, sums.shape[2]), mesh.astype(f32), f32
        ).astype(b16)


def add_edges(own, mesh, recv_ref):
    total = own
    wanted = mesh.astype(f32)
    for slot in range(recv_ref.shape[0]):
        match = recv_ref[slot, SLICES : SLICES + 1].astype(f32) == wanted
        total = total + jnp.where(match, recv_ref[slot, :SLICES].astype(f32), 0.0)
    return total


def attend_parts(total, wqb):
    expand = (iota((128, D), 0) == 16 * (iota((128, D), 1) // DH)).astype(f32)
    count = nn(total[:, D:], expand, HIGH)
    slice_tok = total[:, :D] / count
    triple = nn(slice_tok, wqb, HIGH)
    queries, keyset, valueset = triple[:, :D], triple[:, D : 2 * D], triple[:, 2 * D :]
    key_wide = spread_diag(keyset)
    value_wide = spread_diag(valueset)
    scores = (nt(key_wide, queries, HIGH) * (1.0 / math.sqrt(DH))).reshape(HEADS, SLICES, SLICES)
    expo = jnp.exp(scores - jnp.max(scores, axis=1, keepdims=True))
    prob = (expo / jnp.sum(expo, axis=1, keepdims=True)).reshape(HS, SLICES)
    return (slice_tok, count, queries, key_wide, value_wide, prob)


def attend_all(scal, tiles, sums, recv_ref, wqb, total_ref, attended_ref, wide_ref):
    first = tile_range(scal, 0)[0]
    last = tile_range(scal, tiles - 1)[1]

    def one(mesh, carry):
        total = add_edges(sums[mesh], mesh, recv_ref)
        total_ref[mesh] = total
        _, _, _, _, value_wide, prob = attend_parts(total, wqb)
        attended = tn(prob, value_wide, HIGH).astype(b16)
        attended_ref[mesh] = attended
        wide_ref[mesh] = spread_diag(attended)
        return carry

    lax.fori_loop(first, last + 1, one, 0)


def spread_tile(scal, tile, wide_ref, p_ref, spread):
    low, high = tile_range(scal, tile)
    weights_r = p_ref[...]
    width = weights_r.shape[1]

    def one(mesh, carry):
        keep = tile_mask(scal, mesh, tile, width)
        spread[...] = jnp.where(keep, tn(wide_ref[mesh], weights_r), spread[...])
        return carry

    lax.fori_loop(low, high + 1, one, 0)
    return spread[...].astype(b16)


GELU_A = math.sqrt(2.0 / math.pi)
GELU_B = 0.044715


def gelu_pair(hidden):
    square = hidden * hidden
    bend = jnp.tanh(hidden * (GELU_A + (GELU_A * GELU_B) * square))
    half = 0.5 + 0.5 * bend
    value = hidden * half
    slope = half + (0.5 * hidden) * (1.0 - bend * bend) * (
        GELU_A + (3.0 * GELU_A * GELU_B) * square
    )
    return (value, slope)


CHUNK = 256


def mlp_back_tile(scal, tile, grad, slopes, actives, scaled_two, scale_two, normed_two_r, spread_r,
                  weights_r, wout, wup, wdown, norms, d2_ref, de_ref, sums,
                  gup, gdown, gout, gnorm):
    width = grad.shape[1]
    grad_r = grad.astype(b16)
    grad_normed = jnp.zeros((D, width), f32)
    for start in range(0, FF, CHUNK):
        part = slice(start, start + CHUNK)
        back = (slopes(part) * nn(wdown[part], grad_r)).astype(b16)
        gup[:, part] += nt(normed_two_r, back)
        gdown[:, part] += nt(grad_r, actives(part))
        grad_normed = grad_normed + nn(wup[:, part], back)
    gnorm[2] += fold_lanes(grad_normed * scaled_two)
    gnorm[3] += fold_lanes(grad_normed)
    grad_middle = grad + norm_back(grad_normed, scaled_two, scale_two, norms[:, 2:3])
    d2_ref[...] = grad_middle
    branch_r = grad_middle.astype(b16)
    gout[...] += nt(spread_r, branch_r)
    spread_grad = nn(wout, branch_r).astype(b16)
    de_ref[...] = spread_grad
    low, high = tile_range(scal, tile)

    def add(mesh, carry):
        keep = tile_mask(scal, mesh, tile, width).astype(b16)
        sums[mesh] += pick_diag(nt(weights_r, spread_grad * keep), DH)
        return carry

    lax.fori_loop(low, high + 1, add, 0)


def attend_back_all(scal, tiles, sums, recv_ref, total_ref, attended_ref, wqb, both, dcount, gqkv):
    first = tile_range(scal, 0)[0]
    last = tile_range(scal, tiles - 1)[1]
    root = 1.0 / math.sqrt(DH)

    def one(mesh, carry):
        grad = add_edges(sums[mesh], mesh, recv_ref)
        slice_tok, count, queries, key_wide, value_wide, prob = attend_parts(total_ref[mesh], wqb)
        grad_prob = nt(value_wide, grad, HIGH)
        inner = prob * grad_prob
        mixed = group_sum(inner)
        grad_scores = root * (
            inner
            - (prob.reshape(HEADS, SLICES, SLICES) * mixed).reshape(HS, SLICES)
        )
        grad_q = tn(grad_scores, key_wide, HIGH)
        grad_k = pick_diag(nn(grad_scores, queries, HIGH), DH)
        grad_v = pick_diag(nn(prob, grad, HIGH), DH)
        triple = jnp.concatenate([grad_q, grad_k, grad_v], axis=1)
        grad_tok = nt(triple, wqb, HIGH)
        grad_sum = grad_tok / count
        both[mesh, :, :D] = spread_diag(attended_ref[mesh])
        both[mesh, :, D:] = spread_diag(grad_sum.astype(b16))
        grad_count = spread_diag(-(grad_sum * slice_tok))
        dcount[mesh] = jnp.broadcast_to(jnp.sum(grad_count, axis=1, keepdims=True), (HS, 128))
        seen = (recv_ref[0, SLICES : SLICES + 1, :1].astype(f32) == mesh.astype(f32)).astype(f32)
        gqkv[...] += tn(slice_tok, triple, HIGH) * (1.0 - seen)
        return carry

    lax.fori_loop(first, last + 1, one, 0)


def attend_back_tile(scal, tile, both, dcount, de_ref, f_ref, m_ref, p_ref, u_ref, vh_ref, rs_ref,
                     d2_ref, wfm, wsb, norms, grad_p, grad_f, gfm, gws, gnorm):
    low, high = tile_range(scal, tile)
    weights_r = p_ref[...]
    width = weights_r.shape[1]
    pair = jnp.concatenate([de_ref[...], f_ref[...]], axis=0)

    def one(mesh, carry):
        keep = tile_mask(scal, mesh, tile, width)
        back = nn(both[mesh], pair) + dcount[mesh][:, :1]
        grad_p[...] = jnp.where(keep, back, grad_p[...])
        grad_f[...] = jnp.where(keep, tn(both[mesh, :, D:], weights_r), grad_f[...])
        return carry

    lax.fori_loop(low, high + 1, one, 0)
    weights = weights_r.astype(f32)
    inner = weights * grad_p[...]
    mixed = group_sum(inner)
    grad_logits = (
        inner - (weights.reshape(HEADS, SLICES, width) * mixed).reshape(HS, width)
    ).astype(b16)
    gws[...] += nt(m_ref[...], grad_logits)
    grad_m = nn(wsb, grad_logits).astype(b16)
    grad_fm = jnp.concatenate([grad_f[...].astype(b16), grad_m], axis=0)
    gfm[...] += nt(u_ref[...], grad_fm)
    grad_normed = tn(wfm, grad_fm)
    scaled = vh_ref[...].astype(f32)
    gnorm[0] += fold_lanes(grad_normed * scaled)
    gnorm[1] += fold_lanes(grad_normed)
    return d2_ref[...] + norm_back(grad_normed, scaled, rs_ref[:1], norms[:, 0:1])


def small_rows(base, gws, gqkv, scratch, out_ref):
    lane = iota((1, 128), 1)
    left = repeat_rows(DH)
    fold = (iota((128, HS), 1) % SLICES == iota((128, HS), 0)).astype(f32)
    kept = jnp.where(same_head(DH, SLICES, (D, HS)), gws[...], 0.0)
    scratch[...] = nt(tn(left, kept, HIGH), fold, HIGH)
    even = scratch[pl.ds(0, DH // 2, stride=2), :]
    odd = scratch[pl.ds(1, DH // 2, stride=2), :]
    out_ref[base : base + DH // 2] = jnp.where(lane < SLICES, even, pltpu.roll(odd, SLICES, 1))
    fold = (iota((D, 128), 0) % DH == iota((D, 128), 1)).astype(f32)
    for part in range(3):
        square = jnp.where(same_head(DH, DH, (D, D)), gqkv[:, part * D : (part + 1) * D], 0.0)
        scratch[...] = nn(tn(left, square, HIGH), fold, HIGH)
        total = scratch[pl.ds(0, DH // 4, stride=4), :]
        for inner in range(1, 4):
            total = total + pltpu.roll(scratch[pl.ds(inner, DH // 4, stride=4), :], DH * inner, 1)
        start = base + DH // 2 + part * (DH // 4)
        out_ref[start : start + DH // 4] = total


NORM_ROW = (SMALL - 4 * D) // 128
LAYER_ROWS = SMALL // 128


def norm_rows(gnorm, index, out_ref, base):
    lane = iota((D, 128), 1)
    total = jnp.zeros((D, 128), f32)
    for column, row in enumerate(index):
        total = total + jnp.where(lane == column, jnp.sum(gnorm[row], axis=1, keepdims=True), 0.0)
    flat = total.T
    for column in range(len(index)):
        for half in range(D // 128):
            place = base + column * (D // 128) + half
            out_ref[place : place + 1] = flat[column : column + 1, 128 * half : 128 * half + 128]


def pack_front(gfm, head):
    lane = iota((D, 128), 1)
    start = (head // 2) * 128
    feats, middle = gfm[:, start : start + 128], gfm[:, D + start : D + start + 128]
    if head % 2 == 0:
        return jnp.where(lane < 64, feats, pltpu.roll(middle, 64, 1))
    return jnp.where(lane < 64, pltpu.roll(feats, 64, 1), middle)


def pack_rest(gout, gup, gdown, out_ref, base, n_head):
    for head in range(n_head):
        deep, wide = D // n_head, FF // n_head
        out_ref[head, base : base + deep] = gout[head * deep : (head + 1) * deep].astype(b16)
        start = base + deep
        out_ref[head, start : start + D] = gup[:, head * wide : (head + 1) * wide].astype(b16)
        out_ref[head, start + D : start + 2 * D] = gdown[:, head * wide : (head + 1) * wide].astype(b16)


def first_kernel(tiles, scal, tok_ref, wfm_ref, wsb_ref, norm_ref,
                 xt_ref, vh_ref, rs_ref, u_ref, f_ref, m_ref, p_ref, sums, edge_ref):
    tile = pl.program_id(0)

    @pl.when(tile == 0)
    def _():
        sums[...] = jnp.zeros_like(sums)

    x = tok_ref[...].astype(f32).T
    xt_ref[...] = x.astype(b16)
    front_tile(scal, tile, x, wfm_ref[...], wsb_ref[...], norm_ref[...],
               vh_ref, rs_ref, u_ref, f_ref, m_ref, p_ref, sums)

    @pl.when(tile == tiles - 1)
    def _():
        write_edges(scal, tiles, sums, edge_ref)


def second_kernel(tiles, scal, xt_ref, p0_ref, sums0, recv_ref, wout_ref, wup_ref, wdown_ref, wqb_ref, norm0_ref,
                  wfm_ref, wsb_ref, norm1_ref,
                  e_ref, vh2_ref, rs2_ref, u2_ref, gp_ref, z_ref, att_ref, total_ref,
                  x1_ref, vh_ref, rs_ref, u_ref, f_ref, m_ref, p_ref, sums, edge_ref,
                  wide, spread):
    tile = pl.program_id(0)

    @pl.when(tile == 0)
    def _():
        sums[...] = jnp.zeros_like(sums)
        attend_all(scal, tiles, sums0, recv_ref, wqb_ref[...], total_ref, att_ref, wide)

    norms = norm0_ref[...]
    spread_r = spread_tile(scal, tile, wide, p0_ref, spread)
    e_ref[...] = spread_r
    middle = xt_ref[...].astype(f32) + tn(wout_ref[...], spread_r)
    scaled_two, scale_two = norm_stats(middle)
    vh2_ref[...] = scaled_two.astype(b16)
    rs2_ref[...] = jnp.broadcast_to(scale_two, rs2_ref.shape)
    normed_two_r = (scaled_two * norms[:, 2:3] + norms[:, 3:4]).astype(b16)
    u2_ref[...] = normed_two_r
    x = middle
    for start in range(0, FF, CHUNK):
        part = slice(start, start + CHUNK)
        active, slope = gelu_pair(tn(wup_ref[:, part], normed_two_r))
        active_r = active.astype(b16)
        z_ref[part] = active_r
        gp_ref[part] = slope.astype(b16)
        x = x + tn(wdown_ref[part], active_r)
    x1_ref[...] = x
    front_tile(scal, tile, x, wfm_ref[...], wsb_ref[...], norm1_ref[...],
               vh_ref, rs_ref, u_ref, f_ref, m_ref, p_ref, sums)

    @pl.when(tile == tiles - 1)
    def _():
        write_edges(scal, tiles, sums, edge_ref)


def third_kernel(n_head, packed, tiles, scal, x1_ref, p_ref, sums1, recv_ref, cot_ref, wout_ref, wup_ref, wdown_ref, wqb_ref, norm_ref,
                 out_ref, d2_ref, de_ref, att_ref, total_ref, sums, edge_ref,
                 gn_ref, *rest):
    grad_outs, (wide, spread, gnorm, slope_s, active_s, gup, gdown, gout) = rest[:-8], rest[-8:]
    tile = pl.program_id(0)

    @pl.when(tile == 0)
    def _():
        sums[...] = jnp.zeros_like(sums)
        gup[...] = jnp.zeros_like(gup)
        gdown[...] = jnp.zeros_like(gdown)
        gout[...] = jnp.zeros_like(gout)
        gnorm[...] = jnp.zeros_like(gnorm)
        attend_all(scal, tiles, sums1, recv_ref, wqb_ref[...], total_ref, att_ref, wide)

    norms = norm_ref[...]
    spread_r = spread_tile(scal, tile, wide, p_ref, spread)
    middle = x1_ref[...] + tn(wout_ref[...], spread_r)
    scaled_two, scale_two = norm_stats(middle)
    normed_two_r = (scaled_two * norms[:, 2:3] + norms[:, 3:4]).astype(b16)
    x = middle
    for start in range(0, FF, CHUNK):
        part = slice(start, start + CHUNK)
        active, slope = gelu_pair(tn(wup_ref[:, part], normed_two_r))
        active_r = active.astype(b16)
        active_s[part] = active_r
        slope_s[part] = slope
        x = x + tn(wdown_ref[part], active_r)
    out_ref[...] = x.T.astype(b16)
    grad = cot_ref[...].astype(f32).T
    mlp_back_tile(scal, tile, grad, lambda part: slope_s[part], lambda part: active_s[part],
                  scaled_two, scale_two, normed_two_r, spread_r, p_ref[...],
                  wout_ref[...], wup_ref, wdown_ref, norms, d2_ref, de_ref, sums,
                  gup, gdown, gout, gnorm)

    @pl.when(tile == tiles - 1)
    def _():
        write_edges(scal, tiles, sums, edge_ref)
        norm_rows(gnorm, (2, 3), gn_ref, 0)
        if packed:
            pack_rest(gout, gup, gdown, grad_outs[0], 0, n_head)
        else:
            for ref, total in zip(grad_outs, (gup, gdown, gout)):
                ref[...] = total[...].astype(b16)


def fourth_kernel(n_head, packed, tiles, scal, sums1, recv_ref, att_ref, total_ref, de1_ref, f_ref, m_ref, p1_ref, u_ref, vh_ref, rs_ref, d21_ref,
                  wfm_ref, wsb_ref, wqb_ref, norm1_ref,
                  gp_ref, z_ref, vh2_ref, rs2_ref, u2_ref, e_ref, p0_ref, wout_ref, wup_ref, wdown_ref, norm0_ref, gn1b_ref,
                  d2_ref, de_ref, sums, edge_ref, small_ref, gn0_ref, *rest):
    grad_outs = rest[:-12]
    both, dcount, grad_p, grad_f, gws, gqkv, gnorm, fold_s, gfm, gup, gdown, gout = rest[-12:]
    tile = pl.program_id(0)

    @pl.when(tile == 0)
    def _():
        for ref in (sums, gfm, gws, gqkv, gup, gdown, gout, gnorm):
            ref[...] = jnp.zeros_like(ref)
        attend_back_all(scal, tiles, sums1, recv_ref, total_ref, att_ref, wqb_ref[...], both, dcount, gqkv)

    grad = attend_back_tile(scal, tile, both, dcount, de1_ref, f_ref, m_ref, p1_ref, u_ref, vh_ref, rs_ref,
                            d21_ref, wfm_ref[...], wsb_ref[...], norm1_ref[...], grad_p, grad_f, gfm, gws, gnorm)
    mlp_back_tile(scal, tile, grad, lambda part: gp_ref[part].astype(f32), lambda part: z_ref[part],
                  vh2_ref[...].astype(f32), rs2_ref[:1], u2_ref[...], e_ref[...], p0_ref[...],
                  wout_ref[...], wup_ref, wdown_ref, norm0_ref[...], d2_ref, de_ref, sums,
                  gup, gdown, gout, gnorm)

    @pl.when(tile == tiles - 1)
    def _():
        write_edges(scal, tiles, sums, edge_ref)
        small_rows(0, gws, gqkv, fold_s, small_ref)
        norm_rows(gnorm, (0, 1), small_ref, NORM_ROW)
        small_ref[NORM_ROW + 4 :] = gn1b_ref[...]
        norm_rows(gnorm, (2, 3), gn0_ref, 0)
        if packed:
            for head in range(n_head):
                front = pack_front(gfm, head).astype(b16)
                grad_outs[0][head, : D // 2, :128] = front[: D // 2]
                grad_outs[0][head, : D // 2, 128:] = front[D // 2 :]
            pack_rest(gout, gup, gdown, grad_outs[0], D // 2, n_head)
        else:
            for ref, total in zip(grad_outs, (gfm, gup, gdown, gout)):
                ref[...] = total[...].astype(b16)


def fifth_kernel(n_head, packed, tiles, scal, sums0, recv_ref, att_ref, total_ref, de_ref, f_ref, m_ref, p_ref, u_ref, vh_ref, rs_ref, d2_ref,
                 wfm_ref, wsb_ref, wqb_ref, norm_ref, gn0b_ref, small1_ref,
                 gin_ref, small_ref, front_ref,
                 both, dcount, grad_p, grad_f, gws, gqkv, gnorm, fold_s, gfm):
    tile = pl.program_id(0)

    @pl.when(tile == 0)
    def _():
        for ref in (gfm, gws, gqkv, gnorm):
            ref[...] = jnp.zeros_like(ref)
        attend_back_all(scal, tiles, sums0, recv_ref, total_ref, att_ref, wqb_ref[...], both, dcount, gqkv)

    grad = attend_back_tile(scal, tile, both, dcount, de_ref, f_ref, m_ref, p_ref, u_ref, vh_ref, rs_ref,
                            d2_ref, wfm_ref[...], wsb_ref[...], norm_ref[...], grad_p, grad_f, gfm, gws, gnorm)
    gin_ref[...] = grad.T

    @pl.when(tile == tiles - 1)
    def _():
        small_rows(0, gws, gqkv, fold_s, small_ref)
        norm_rows(gnorm, (0, 1), small_ref, NORM_ROW)
        small_ref[NORM_ROW + 4 : LAYER_ROWS] = gn0b_ref[...]
        small_ref[LAYER_ROWS:] = small1_ref[...]
        if packed:
            for head in range(n_head):
                front_ref[head] = pack_front(gfm, head).astype(b16)
        else:
            front_ref[...] = gfm[...].astype(b16)


def total_kernel(sizes, gb_ref, gc_ref, gs_ref, tb_ref, tc_ref, ts_ref,
                 rb, rc, rs, b_send, b_recv, c_send, c_recv, s_send, s_recv,
                 b_send2, b_recv2, c_send2, c_recv2, s_send2, s_recv2):
    n_pts, n_head = sizes
    total = n_pts * n_head
    pts, head = lax.axis_index("pts"), lax.axis_index("head")
    me = pts * n_head + head
    c_rows = D // n_pts
    b_rows = gb_ref.shape[0] // (n_pts // 2)
    chunks = gs_ref.shape[0] // 8

    def device(index):
        return (index // n_head, lax.rem(index, n_head))

    def copy(src, dst, send, recv, to):
        return pltpu.make_async_remote_copy(
            src_ref=src, dst_ref=dst, send_sem=send, recv_sem=recv, device_id=to, device_id_type=MESH
        )

    def b_part(ref, index):
        return ref.at[
            pl.ds(pl.multiple_of((index // 2) * b_rows, 16), b_rows),
            pl.ds(pl.multiple_of(lax.rem(index, 2) * 128, 128), 128),
        ]

    def c_part(ref, index):
        return ref.at[pl.ds(pl.multiple_of(index * c_rows, c_rows), c_rows), :]

    def s_part(ref, index):
        return ref.at[pl.ds(pl.multiple_of(index * 8, 8), 8), :]

    def c_copy(step):
        peer = lax.rem(me + step, total)
        other, lane = device(peer)
        return copy(c_part(gc_ref.at[lane], other), rc.at[step - 1], c_send.at[step - 1], c_recv.at[step - 1], (other, lane))

    def s_copy(step):
        peer = lax.rem(me + step, total)
        part = jnp.minimum(peer, chunks - 1)
        return peer, copy(s_part(gs_ref, part), rs.at[step - 1], s_send.at[step - 1], s_recv.at[step - 1], device(peer))

    def b_copy(step):
        other = lax.rem(pts + step, n_pts)
        return copy(b_part(gb_ref, other), rb.at[step - 1], b_send.at[step - 1], b_recv.at[step - 1], (other, head))

    def b_share(step):
        other = lax.rem(pts + step, n_pts)
        return copy(b_part(tb_ref, pts), b_part(tb_ref, pts), b_send2.at[step - 1], b_recv2.at[step - 1], (other, head))

    def c_share(step):
        other = lax.rem(pts + step, n_pts)
        return copy(c_part(tc_ref, pts), c_part(tc_ref, pts), c_send2.at[step - 1], c_recv2.at[step - 1], (other, head))

    mine = jnp.minimum(me, chunks - 1)

    def s_share(step):
        peer = lax.rem(me + step, total)
        return copy(s_part(ts_ref, mine), s_part(ts_ref, mine), s_send2.at[step - 1], s_recv2.at[step - 1], device(peer))

    barrier = pltpu.get_barrier_semaphore()

    def hello(step, carry):
        pl.semaphore_signal(barrier, inc=1, device_id=device(lax.rem(me + step, total)), device_id_type=MESH)
        return carry

    def loop(count, body):
        def run(step, carry):
            body(step)
            return carry

        lax.fori_loop(1, count, run, 0)

    lax.fori_loop(1, total, hello, 0)
    pl.semaphore_wait(barrier, total - 1)

    def send_first(step):
        c_copy(step).start()
        peer, small = s_copy(step)

        @pl.when(peer < chunks)
        def _():
            small.start()

    loop(total, send_first)
    loop(n_pts, lambda step: b_copy(step).start())

    def wait_c(step):
        c_copy(step).wait()
        peer, small = s_copy(step)

        @pl.when(peer < chunks)
        def _():
            small.wait_send()

        @pl.when(me < chunks)
        def _():
            small.wait_recv()

    loop(total, wait_c)
    acc = gc_ref[head, pl.ds(pl.multiple_of(pts * c_rows, c_rows), c_rows), :].astype(f32)
    tc_ref[pl.ds(pl.multiple_of(pts * c_rows, c_rows), c_rows), :] = lax.fori_loop(
        0, total - 1, lambda i, acc: acc + rc[i].astype(f32), acc
    ).astype(b16)
    loop(n_pts, lambda step: c_share(step).start())

    @pl.when(me < chunks)
    def _():
        acc = gs_ref[pl.ds(pl.multiple_of(mine * 8, 8), 8), :]
        ts_ref[pl.ds(pl.multiple_of(mine * 8, 8), 8), :] = lax.fori_loop(
            0, total - 1, lambda i, acc: acc + rs[i], acc
        )
        loop(total, lambda step: s_share(step).start())

    loop(n_pts, lambda step: b_copy(step).wait())
    rows, lanes = (
        pl.ds(pl.multiple_of((pts // 2) * b_rows, 16), b_rows),
        pl.ds(pl.multiple_of(lax.rem(pts, 2) * 128, 128), 128),
    )
    acc = gb_ref[rows, lanes].astype(f32)
    for index in range(n_pts - 1):
        acc = acc + rb[index].astype(f32)
    tb_ref[rows, lanes] = acc.astype(b16)
    loop(n_pts, lambda step: b_share(step).start())
    loop(n_pts, lambda step: c_share(step).wait())

    def wait_s(step):
        peer = lax.rem(me + total - step, total)
        share = s_share(step)

        @pl.when(peer < chunks)
        def _():
            share.wait_recv()

        @pl.when(me < chunks)
        def _():
            share.wait_send()

    loop(total, wait_s)
    loop(n_pts, lambda step: b_share(step).wait())


def total_gradients(sizes, gb, gc, gs):
    n_pts, n_head = sizes
    total = n_pts * n_head
    vmem = pl.BlockSpec(memory_space=pltpu.VMEM)
    dma = pltpu.SemaphoreType.DMA
    return pl.pallas_call(
        functools.partial(total_kernel, sizes),
        out_shape=(
            jax.ShapeDtypeStruct(gb.shape, b16),
            jax.ShapeDtypeStruct(gc.shape[1:], b16),
            jax.ShapeDtypeStruct(gs.shape, f32),
        ),
        in_specs=[vmem] * 3,
        out_specs=[vmem] * 3,
        scratch_shapes=[
            pltpu.VMEM((n_pts - 1, gb.shape[0] // (n_pts // 2), 128), b16),
            pltpu.VMEM((total - 1, D // n_pts, 128), b16),
            pltpu.VMEM((total - 1, 8, 128), f32),
        ]
        + [dma((n_pts - 1,))] * 2
        + [dma((total - 1,))] * 4
        + [dma((n_pts - 1,))] * 4
        + [dma((total - 1,))] * 2,
        compiler_params=pltpu.CompilerParams(
            collective_id=3, has_side_effects=True, vmem_limit_bytes=VMEM_BYTES
        ),
        name="total_gradients",
    )(gb, gc, gs)


def update_kernel(ta_ref, tb_ref, tc_ref, ts_ref, row_ref, sel_ref, m_ref, v_ref, w_ref, sm_ref, sv_ref, sw_ref,
                  nm_ref, nv_ref, nw_ref, fresh_ref, om_ref, ov_ref, ow_ref, wide, tall, front, flat):
    lane = iota((8, 128), 1)

    def place_front(base):
        for pair in range(16):
            first = front[pl.ds(2 * pair, 8, stride=32), :]
            second = front[pl.ds(2 * pair + 1, 8, stride=32), :]
            columns = slice(128 * pair, 128 * pair + 128)
            wide[base : base + 8, columns] = jnp.where(lane < 64, first, pltpu.roll(second, 64, 1))
            wide[base + 8 : base + 16, columns] = jnp.where(lane < 64, pltpu.roll(first, 64, 1), second)

    def place_rest(base):
        for part in range(8):
            for half in range(2):
                wide[base : base + 72, 256 * part + 128 * half : 256 * part + 128 * half + 128] = tall[
                    half, pl.ds(part, 72, stride=8), :
                ]

    def fill(value):
        for half in range(2):
            tall[half] = value[:, 128 * half : 128 * half + 128].astype(f32)

    front[...] = tc_ref[...].astype(f32)
    place_front(0)
    fill(tb_ref[D // 2 :])
    place_rest(16)
    front[: D // 2] = tb_ref[: D // 2, :128].astype(f32)
    front[D // 2 :] = tb_ref[: D // 2, 128:].astype(f32)
    place_front(88)
    fill(ta_ref[...])
    place_rest(104)

    cap, blocks = m_ref.shape[0], wide.shape[0]
    mine = (iota((cap, blocks), 0) == row_ref[:1, :blocks]).astype(f32)
    filled = jnp.sum(mine, axis=1, keepdims=True) > 0.5
    mine = mine.astype(b16)
    step = 512
    for start in range(0, BLOCK, step):
        part = slice(start, start + step)
        grad = wide[:, part]
        own = nn(mine, grad.astype(b16))
        old = (m_ref[:, part], v_ref[:, part], w_ref[:, part])
        new = adam_update(old[0], own, old[1], old[2], rate_large)
        for ref, before, after in zip((nm_ref, nv_ref, nw_ref), old, new):
            ref[:, part] = jnp.where(filled, after, before)
        picked = [
            sel_ref[:, which * BLOCK + start : which * BLOCK + start + step].astype(f32)
            for which in range(3)
        ]
        fresh_ref[:, part] = adam_update(picked[0], grad, picked[1], picked[2], rate_large)[0].astype(b16)
    for layer in range(2):
        for row in range(LAYER_ROWS):
            flat[layer : layer + 1, 128 * row : 128 * row + 128] = ts_ref[
                layer * LAYER_ROWS + row : layer * LAYER_ROWS + row + 1, :
            ]
    new = adam_update(sm_ref[...], flat[:2], sv_ref[...], sw_ref[...], rate_small)
    for ref, value in zip((om_ref, ov_ref, ow_ref), new):
        ref[...] = value


def update(ta, tb, tc, ts, row, sel, tables, smalls):
    vmem = pl.BlockSpec(memory_space=pltpu.VMEM)
    blocks = sel.shape[0]
    operands = (ta, tb, tc, ts, row, sel, *tables, *smalls)
    outs = [jax.ShapeDtypeStruct(table.shape, f32) for table in tables]
    outs.append(jax.ShapeDtypeStruct((blocks, BLOCK), b16))
    outs += [jax.ShapeDtypeStruct(small.shape, f32) for small in smalls]
    return pl.pallas_call(
        update_kernel,
        out_shape=outs,
        in_specs=[vmem] * len(operands),
        out_specs=[vmem] * len(outs),
        scratch_shapes=[
            pltpu.VMEM((blocks, BLOCK), f32),
            pltpu.VMEM((2, ta.shape[0], 128), f32),
            pltpu.VMEM((D, 128), f32),
            pltpu.VMEM((8, SMALL), f32),
        ],
        compiler_params=pltpu.CompilerParams(vmem_limit_bytes=VMEM_BYTES),
        name="update",
    )(*operands)


class Args:
    def __init__(self, rows, width):
        self.rows, self.width = rows, width
        self.operands, self.in_specs, self.outs, self.out_specs = [], [], [], []

    def cols(self, *arrays):
        for array in arrays:
            self.operands.append(array)
            self.in_specs.append(
                pl.BlockSpec((array.shape[0], self.width), lambda tile, scal: (0, tile))
            )

    def points(self, *arrays):
        for array in arrays:
            self.operands.append(array)
            self.in_specs.append(
                pl.BlockSpec((self.width, array.shape[1]), lambda tile, scal: (tile, 0))
            )

    def whole(self, *arrays):
        for array in arrays:
            rank = array.ndim
            self.operands.append(array)
            self.in_specs.append(
                pl.BlockSpec(array.shape, lambda tile, scal, rank=rank: (0,) * rank)
            )

    def layer(self, index, *arrays):
        for array in arrays:
            self.operands.append(array)
            self.in_specs.append(
                pl.BlockSpec((None,) + array.shape[1:], lambda tile, scal: (index, 0, 0))
            )

    def out_cols(self, *pairs):
        for height, dtype in pairs:
            self.outs.append(jax.ShapeDtypeStruct((height, self.rows), dtype))
            self.out_specs.append(
                pl.BlockSpec((height, self.width), lambda tile, scal: (0, tile))
            )

    def out_points(self, *dtypes):
        for dtype in dtypes:
            self.outs.append(jax.ShapeDtypeStruct((self.rows, D), dtype))
            self.out_specs.append(pl.BlockSpec((self.width, D), lambda tile, scal: (tile, 0)))

    def out_whole(self, *pairs):
        for shape, dtype in pairs:
            rank = len(shape)
            self.outs.append(jax.ShapeDtypeStruct(shape, dtype))
            self.out_specs.append(
                pl.BlockSpec(shape, lambda tile, scal, rank=rank: (0,) * rank)
            )

    def call(self, body, scal, scratch, name):
        tiles = self.rows // self.width
        return pl.pallas_call(
            functools.partial(body, tiles),
            grid_spec=pltpu.PrefetchScalarGridSpec(
                num_scalar_prefetch=1,
                grid=(tiles,),
                in_specs=self.in_specs,
                out_specs=self.out_specs,
                scratch_shapes=scratch,
            ),
            out_shape=self.outs,
            compiler_params=pltpu.CompilerParams(
                dimension_semantics=("arbitrary",), vmem_limit_bytes=VMEM_BYTES
            ),
            name=name,
        )(scal, *self.operands)


def adam_update(master, grad, first, second, rate):
    new_first = beta_one * first + (1.0 - beta_one) * grad
    new_second = beta_two * second + (1.0 - beta_two) * grad * grad
    fix_one = 1.0 - beta_one**STEP
    fix_two = 1.0 - beta_two**STEP
    direction = new_first / fix_one / (jnp.sqrt(new_second / fix_two) + adam_eps)
    return (master - rate * (direction + decay_rate * master), new_first, new_second)


def flat_blocks(n_head, gfm, gout, gup, gdown):
    def columns(grad):
        width = grad.shape[1] // n_head
        return grad.reshape(D, n_head, width).transpose(1, 0, 2).reshape(n_head, -1)

    return jnp.concatenate(
        [
            columns(gfm[:, :D]),
            columns(gfm[:, D:]),
            gout.reshape(n_head, -1),
            columns(gup),
            columns(gdown),
        ],
        axis=1,
    ).reshape(n_head, -1, BLOCK)


def on_device(
    sizes,
    tokens,
    cotangent,
    segment_ids,
    owner,
    w_fx,
    w_mid,
    w_out,
    w_up,
    w_down,
    small_master,
    small_first,
    small_second,
    master_table,
    first_table,
    second_table,
):
    n_pts, n_head = sizes
    rows = tokens.shape[0]
    width = min(512, rows)
    tiles = rows // width
    most = rows * n_pts * n_head // LARGEST
    window = (rows - 1 + most - 1) // rows
    layers = w_fx.shape[0]
    packed = (n_pts, n_head) == (8, 4)

    ids = segment_ids.reshape(-1, 128)
    w_fx = w_fx.transpose(0, 2, 1)
    w_mid = w_mid.transpose(0, 2, 1)
    gathered, wsb, norms, scal = opening(n_head, tiles, ids, w_fx, w_mid, small_master)
    wfm0 = gathered.reshape(2 * D, D)

    block_total = owner.shape[0]
    cap = master_table.shape[0]
    my_index = lax.axis_index("pts")
    block_ids = jnp.arange(block_total)
    same_owner = (owner[:, None] == owner[None, :]) & (block_ids[None, :] < block_ids[:, None])
    slot = jnp.sum(same_owner.astype(jnp.int32), axis=1)

    sums_shape = (MESHES, SLICES, D + 128)
    grad_sums_shape = (MESHES, SLICES, D)
    front_cols = ((D, b16), (8, f32), (D, b16), (D, b16), (D, b16), (HS, b16))
    wide_scratch = [pltpu.VMEM((MESHES, HS, D), b16), pltpu.VMEM((D, width), f32)]

    args = Args(rows, width)
    args.points(tokens)
    args.whole(wfm0)
    args.layer(0, wsb, norms)
    args.out_cols((D, b16), *front_cols)
    args.out_whole((sums_shape, f32), ((2, EDGE, D + 128), b16))
    xt0, vh0, rs0, u0, f0, m0, p0, sums0, edge = args.call(first_kernel, scal, [], "first")
    recv, wfm1, wout, wqb = swap_edges_weights(
        sizes, window, edge, w_fx, w_mid, w_out, small_master, 1
    )
    wfm1 = wfm1.reshape(2 * D, D)
    wout = wout.reshape(layers, D, D)

    args = Args(rows, width)
    args.cols(xt0, p0)
    args.whole(sums0, recv)
    args.layer(0, wout, w_up, w_down, wqb, norms)
    args.whole(wfm1)
    args.layer(1, wsb, norms)
    args.out_cols((D, b16), (D, b16), (8, f32), (D, b16), (FF, b16), (FF, b16))
    args.out_whole((grad_sums_shape, b16), (sums_shape, f32))
    args.out_cols((D, f32), *front_cols)
    args.out_whole((sums_shape, f32), ((2, EDGE, D + 128), b16))
    (e0, vh20, rs20, u20, gp0, z0, att0, total0, x1, vh1, rs1, u1, f1, m1, p1, sums1, edge) = args.call(
        second_kernel, scal, wide_scratch, "second"
    )
    recv = swap_edges(sizes, window, edge, 4)

    grad_scratch = [pltpu.VMEM((D, FF), f32), pltpu.VMEM((D, FF), f32), pltpu.VMEM((D, D), f32)]
    rest_rows = D // n_head + 2 * D

    args = Args(rows, width)
    args.cols(x1, p1)
    args.whole(sums1, recv)
    args.points(cotangent)
    args.layer(1, wout, w_up, w_down, wqb, norms)
    args.out_points(b16)
    args.out_cols((D, f32), (D, b16))
    args.out_whole((grad_sums_shape, b16), (sums_shape, f32), (grad_sums_shape, f32), ((2, EDGE, D), b16))
    args.out_whole(((4, 128), f32))
    if packed:
        args.out_whole(((n_head, rest_rows, D), b16))
    else:
        args.out_whole(((D, FF), b16), ((D, FF), b16), ((D, D), b16))
    (layer_out, d21, de1, att1, total1, dsums1, edge, gn1b, *grads_a) = args.call(
        functools.partial(third_kernel, n_head, packed),
        scal,
        wide_scratch
        + [pltpu.VMEM((4, D, 128), f32), pltpu.VMEM((FF, width), f32), pltpu.VMEM((FF, width), b16)]
        + grad_scratch,
        "third",
    )
    recv = swap_edges(sizes, window, edge, 2)

    back_scratch = [
        pltpu.VMEM((MESHES, HS, 2 * D), b16),
        pltpu.VMEM((MESHES, HS, 128), f32),
        pltpu.VMEM((HS, width), f32),
        pltpu.VMEM((D, width), f32),
        pltpu.VMEM((D, HS), f32),
        pltpu.VMEM((D, 3 * D), f32),
        pltpu.VMEM((4, D, 128), f32),
        pltpu.VMEM((DH, 128), f32),
        pltpu.VMEM((D, 2 * D), f32),
    ]

    args = Args(rows, width)
    args.whole(dsums1, recv, att1, total1)
    args.cols(de1, f1, m1, p1, u1, vh1, rs1, d21)
    args.whole(wfm1)
    args.layer(1, wsb, wqb, norms)
    args.cols(gp0, z0, vh20, rs20, u20, e0, p0)
    args.layer(0, wout, w_up, w_down, norms)
    args.whole(gn1b)
    args.out_cols((D, f32), (D, b16))
    args.out_whole((grad_sums_shape, f32), ((2, EDGE, D), b16), ((LAYER_ROWS, 128), f32), ((4, 128), f32))
    if packed:
        args.out_whole(((n_head, D // 2 + rest_rows, D), b16))
    else:
        args.out_whole(((D, 2 * D), b16), ((D, FF), b16), ((D, FF), b16), ((D, D), b16))
    (d20, de0, dsums0, edge, small1, gn0b, *grads_b) = args.call(
        functools.partial(fourth_kernel, n_head, packed), scal, back_scratch + grad_scratch, "fourth"
    )
    recv = swap_edges(sizes, window, edge, 2)

    args = Args(rows, width)
    args.whole(dsums0, recv, att0, total0)
    args.cols(de0, f0, m0, p0, u0, vh0, rs0, d20)
    args.whole(wfm0)
    args.layer(0, wsb, wqb, norms)
    args.whole(gn0b, small1)
    args.out_points(f32)
    args.out_whole(((2 * LAYER_ROWS, 128), f32))
    args.out_whole(((n_head, D, 128), b16) if packed else ((D, 2 * D), b16))
    input_grad, small, front = args.call(
        functools.partial(fifth_kernel, n_head, packed), scal, back_scratch, "fifth"
    )

    tables = (master_table, first_table, second_table)
    smalls = (small_master, small_first, small_second)
    if packed:
        deep = -(-cap // 16) * 16
        mine = jnp.pad(
            jnp.concatenate([table.astype(b16) for table in tables], axis=1), ((0, deep - cap), (0, 0))
        )
        collected = lax.all_gather(mine, "pts", axis=0, tiled=True)
        pick = (owner * deep + slot)[:, None] == jnp.arange(n_pts * deep)[None, :]
        chosen = jnp.dot(pick.astype(b16), collected, preferred_element_type=f32).astype(b16)
        row = jnp.where(owner == my_index, slot, -1)
        row = jnp.broadcast_to(jnp.pad(row, (0, 256 - block_total), constant_values=-1)[None, :], (8, 256))
        total_a = lax.psum(
            lax.psum_scatter(grads_a[0], "head", scatter_dimension=0, tiled=True)[0], "pts"
        )
        mine_b = lax.psum_scatter(grads_b[0], "head", scatter_dimension=0, tiled=True)[0]
        total_b, total_c, total_s = total_gradients(sizes, mine_b, front, small)
        outs = update(total_a, total_b, total_c, total_s, row, chosen, tables, smalls)
        return (layer_out, input_grad, *outs)

    gup1, gdown1, gout1 = grads_a
    gfm1, gup0, gdown0, gout0 = grads_b
    small_total = lax.psum(small, ("pts", "head")).reshape(layers, -1)
    totals = []
    for parts in ((front, gout0, gup0, gdown0), (gfm1, gout1, gup1, gdown1)):
        blocks = lax.psum_scatter(
            flat_blocks(n_head, *parts), "head", scatter_dimension=0, tiled=True
        )
        totals.append(lax.psum(blocks.reshape(-1, BLOCK), "pts"))
    total_grad = jnp.concatenate(totals, axis=0).astype(f32)
    table_row = owner * cap + slot
    place_all = (jnp.arange(n_pts * cap)[:, None] == table_row[None, :]).astype(f32)
    mine_place = lax.dynamic_slice_in_dim(place_all, my_index * cap, cap, 0)
    own_grad = jnp.dot(mine_place, total_grad, precision=HIGH)
    filled = jnp.sum(mine_place, axis=1)[:, None] > 0.5
    updated = adam_update(master_table, own_grad, first_table, second_table, rate_large)
    new_tables = [jnp.where(filled, new, old) for new, old in zip(updated, tables)]
    collected = lax.all_gather(new_tables[0].astype(b16), "pts", axis=0, tiled=True)
    pick_back = (table_row[:, None] == jnp.arange(n_pts * cap)[None, :]).astype(b16)
    fresh = jnp.dot(pick_back, collected, preferred_element_type=f32).astype(b16)
    small_outs = adam_update(small_master, small_total, small_first, small_second, rate_small)
    return (layer_out, input_grad, *new_tables, fresh, *small_outs)


def solution(mesh):
    sizes = (mesh.shape["pts"], mesh.shape["head"])
    return jax.shard_map(
        functools.partial(on_device, sizes),
        mesh=mesh,
        in_specs=(
            P(("pts", "head"), None),
            P(("pts", "head"), None),
            P("pts"),
            P(),
            P(None, None, "head"),
            P(None, None, "head"),
            P(None, "head", None),
            P(),
            P(),
            P(),
            P(),
            P(),
            P("pts", "head"),
            P("pts", "head"),
            P("pts", "head"),
        ),
        out_specs=(
            P(("pts", "head"), None),
            P(("pts", "head"), None),
            P("pts", "head"),
            P("pts", "head"),
            P("pts", "head"),
            P(None, "head"),
            P(),
            P(),
            P(),
        ),
        check_vma=False,
    )
```

```python
import functools
import math

import jax
import jax.numpy as jnp
from jax import lax
from jax.experimental import pallas as pl
from jax.experimental.pallas import tpu as pltpu
from jax.sharding import PartitionSpec as P

D = 256
HEADS = 8
DH = 32
SLICES = 64
HS = HEADS * SLICES
FF = 1024
MESHES = 24
BLOCK = 2048
SMALL = 6144
STEP = 10
LARGEST = 12
EDGE = 80
VMEM_BYTES = 58 << 20

MESH = pl.DeviceIdType.MESH
HIGH = lax.Precision.HIGHEST
norm_eps = 1e-05
beta_one = 0.9
beta_two = 0.95
adam_eps = 1e-08
decay_rate = 0.1
rate_large = 0.1
rate_small = 0.75
f32 = jnp.float32
b16 = jnp.bfloat16


def nn(a, b, precision=None):
    return lax.dot_general(
        a, b, (((1,), (0,)), ((), ())), preferred_element_type=f32, precision=precision
    )


def nt(a, b, precision=None):
    return lax.dot_general(
        a, b, (((1,), (1,)), ((), ())), preferred_element_type=f32, precision=precision
    )


def tn(a, b, precision=None):
    return lax.dot_general(
        a, b, (((0,), (0,)), ((), ())), preferred_element_type=f32, precision=precision
    )


def iota(shape, axis):
    return lax.broadcasted_iota(jnp.int32, shape, axis)


def pick_diag(full, per_head):
    lane_head = iota((SLICES, full.shape[1]), 1) // per_head
    total = jnp.where(lane_head == 0, full[:SLICES], 0.0)
    for head in range(1, HEADS):
        total = total + jnp.where(
            lane_head == head, full[head * SLICES : (head + 1) * SLICES], 0.0
        )
    return total


def spread_diag(small):
    lane_head = iota((SLICES, D), 1) // DH
    return jnp.concatenate(
        [jnp.where(lane_head == head, small, jnp.zeros_like(small)) for head in range(HEADS)],
        axis=0,
    )


def repeat_rows(width):
    return (iota((D, width), 0) % width == iota((D, width), 1)).astype(f32)


def slice_repeat():
    return (iota((SLICES, HS), 1) % SLICES == iota((SLICES, HS), 0)).astype(f32)


def same_head(rows_per, cols_per, shape):
    return (iota(shape, 0) // rows_per) == (iota(shape, 1) // cols_per)


def start_gather(n_head, picks, send_sem, recv_sem):
    me = lax.axis_index("head")
    copies = []
    for index, ref in enumerate(picks):
        for step in range(1, n_head):
            copy = pltpu.make_async_remote_copy(
                src_ref=ref.at[:, me],
                dst_ref=ref.at[:, me],
                send_sem=send_sem.at[index, step - 1],
                recv_sem=recv_sem.at[index, step - 1],
                device_id={"head": lax.rem(me + step, n_head)},
                device_id_type=MESH,
            )
            copy.start()
            copies.append(copy)
    return copies


def unroll_slices(row_of, out):
    lane = iota((1, 128), 1)
    for pair in range(DH // 2):
        row = row_of(pair)
        out[2 * pair : 2 * pair + 1] = jnp.where(lane < SLICES, row, 0.0)
        out[2 * pair + 1 : 2 * pair + 2] = jnp.where(
            lane < SLICES, pltpu.roll(row, 128 - SLICES, 1), 0.0
        )


def opening_kernel(n_head, tiles, ids_ref, wfx_ref, wmid_ref, sm_ref,
                   out_ref, wsb_ref, norm_ref, scal_ref, send_sem, recv_sem, slices_s, norm_s):
    me = lax.axis_index("head")
    barrier = pltpu.get_barrier_semaphore()
    for step in range(1, n_head):
        pl.semaphore_signal(
            barrier, inc=1, device_id={"head": lax.rem(me + step, n_head)}, device_id_type=MESH
        )
    out_ref[0, me] = wfx_ref[0]
    out_ref[1, me] = wmid_ref[0]
    pl.semaphore_wait(barrier, n_head - 1)
    copies = start_gather(n_head, [out_ref], send_sem, recv_sem)
    layers = sm_ref.shape[0]
    left = repeat_rows(DH)
    right = (iota((128, HS), 1) % SLICES == iota((128, HS), 0)).astype(b16)
    for layer in range(layers):
        unroll_slices(lambda pair: sm_ref[layer : layer + 1, 128 * pair : 128 * pair + 128], slices_s)
        wide = nn(slices_s[...].astype(b16), right)
        tiled = jnp.concatenate([wide] * HEADS, axis=0)
        wsb_ref[layer] = jnp.where(same_head(DH, SLICES, (D, HS)), tiled, 0.0).astype(b16)
        norm_s[...] = jnp.zeros_like(norm_s)
        for row in range(4):
            start = SMALL - 4 * D + row * D
            norm_s[row : row + 1] = sm_ref[layer : layer + 1, start : start + D]
        norm_ref[layer] = norm_s[...].T
    rows = ids_ref.shape[0] // n_head
    ids = ids_ref[pl.ds(pl.multiple_of(me * rows, rows), rows), :]
    for mesh in range(MESHES + 1):
        scal_ref[mesh] = jnp.sum((ids < mesh).astype(jnp.int32))
    deep = rows // tiles
    for tile in range(tiles):
        part = ids[tile * deep : (tile + 1) * deep]
        scal_ref[MESHES + 1 + 2 * tile] = jnp.min(part)
        scal_ref[MESHES + 2 + 2 * tile] = jnp.max(part)
    for copy in copies:
        copy.wait()


def opening(n_head, tiles, ids, w_fx, w_mid, small):
    layers, part, _ = w_fx.shape
    vmem = pl.BlockSpec(memory_space=pltpu.VMEM)
    return pl.pallas_call(
        functools.partial(opening_kernel, n_head, tiles),
        out_shape=(
            jax.ShapeDtypeStruct((2, n_head, part, D), b16),
            jax.ShapeDtypeStruct((layers, D, HS), b16),
            jax.ShapeDtypeStruct((layers, D, 128), f32),
            jax.ShapeDtypeStruct((MESHES + 1 + 2 * tiles,), jnp.int32),
        ),
        in_specs=[vmem] * 4,
        out_specs=[vmem] * 3 + [pl.BlockSpec(memory_space=pltpu.SMEM)],
        scratch_shapes=[
            pltpu.SemaphoreType.DMA((1, n_head - 1)),
            pltpu.SemaphoreType.DMA((1, n_head - 1)),
            pltpu.VMEM((DH, 128), f32),
            pltpu.VMEM((128, D), f32),
        ],
        compiler_params=pltpu.CompilerParams(
            collective_id=0, has_side_effects=True, vmem_limit_bytes=VMEM_BYTES
        ),
        name="opening",
    )(ids, w_fx, w_mid, small)


def place_of(sizes, shift):
    n_pts, n_head = sizes
    total = n_pts * n_head
    me = lax.axis_index("pts") * n_head + lax.axis_index("head")
    other = lax.rem(me + (shift + total), total)
    return (other // n_head, lax.rem(other, n_head))


def greet(sizes, window):
    barrier = pltpu.get_barrier_semaphore()
    for step in range(1, window + 1):
        for shift in (step, -step):
            pl.semaphore_signal(barrier, inc=1, device_id=place_of(sizes, shift), device_id_type=MESH)
    return barrier


def start_edges(sizes, window, edge_ref, out_ref, send_sem, recv_sem):
    copies = []
    for step in range(1, window + 1):
        for side, shift in ((1, step), (0, -step)):
            slot = step - 1 if side == 1 else window + step - 1
            copy = pltpu.make_async_remote_copy(
                src_ref=edge_ref.at[side],
                dst_ref=out_ref.at[slot],
                send_sem=send_sem.at[slot],
                recv_sem=recv_sem.at[slot],
                device_id=place_of(sizes, shift),
                device_id_type=MESH,
            )
            copy.start()
            copies.append(copy)
    return copies


def edge_kernel(sizes, window, edge_ref, out_ref, send_sem, recv_sem):
    barrier = greet(sizes, window)
    pl.semaphore_wait(barrier, 2 * window)
    for copy in start_edges(sizes, window, edge_ref, out_ref, send_sem, recv_sem):
        copy.wait()


def edge_weights_kernel(sizes, window, edge_ref, wfx_ref, wmid_ref, wout_ref, sm_ref,
                        out_ref, wa_ref, wb_ref, wqb_ref,
                        send_sem, recv_sem, wsend_sem, wrecv_sem, square_s):
    n_head = sizes[1]
    me = lax.axis_index("head")
    barrier = greet(sizes, window)
    for step in range(1, n_head):
        pl.semaphore_signal(
            barrier, inc=1, device_id={"head": lax.rem(me + step, n_head)}, device_id_type=MESH
        )
    layers = wout_ref.shape[0]
    wa_ref[0, me] = wfx_ref[1]
    wa_ref[1, me] = wmid_ref[1]
    for layer in range(layers):
        wb_ref[layer, me] = wout_ref[layer]
    pl.semaphore_wait(barrier, 2 * window + n_head - 1)
    copies = start_edges(sizes, window, edge_ref, out_ref, send_sem, recv_sem)
    copies += start_gather(n_head, [wb_ref, wa_ref], wsend_sem, wrecv_sem)
    left = repeat_rows(DH)
    lane = iota((1, 128), 1)
    for layer in range(layers):
        for part in range(3):
            start = DH * SLICES + part * DH * DH
            for group in range(DH // 4):
                row = sm_ref[layer : layer + 1, start + 128 * group : start + 128 * group + 128]
                for inner in range(4):
                    moved = row if inner == 0 else pltpu.roll(row, 128 - DH * inner, 1)
                    square_s[4 * group + inner : 4 * group + inner + 1] = jnp.where(
                        lane < DH, moved, 0.0
                    )
            pick = (iota((D, 128), 0) % DH == iota((D, 128), 1)).astype(f32)
            square = nt(nn(left, square_s[...], HIGH), pick, HIGH)
            wqb_ref[layer, :, part * D : (part + 1) * D] = jnp.where(
                same_head(DH, DH, (D, D)), square, 0.0
            )
    for copy in copies:
        copy.wait()


def edge_pick_kernel(sizes, window, cap, edge_ref, owner_ref, tables_ref,
                     out_ref, chosen_ref, row_ref, send_sem, recv_sem, tables_s, local_sem):
    barrier = greet(sizes, window)
    load = pltpu.make_async_copy(tables_ref, tables_s, local_sem)
    load.start()
    pl.semaphore_wait(barrier, 2 * window)
    copies = start_edges(sizes, window, edge_ref, out_ref, send_sem, recv_sem)
    blocks = owner_ref.shape[1]
    deep = tables_s.shape[0] // sizes[0]
    across = jnp.broadcast_to(owner_ref[...].astype(f32), (blocks, blocks))
    down = across.T
    low, high = iota((blocks, blocks), 0), iota((blocks, blocks), 1)
    same = across == down
    slot_down = jnp.sum(jnp.where(same & (high < low), 1.0, 0.0), axis=1, keepdims=True)
    slot_across = jnp.sum(jnp.where(same & (low < high), 1.0, 0.0), axis=0, keepdims=True)
    mine = owner_ref[...] == lax.axis_index("pts")
    row_ref[...] = jnp.broadcast_to(
        jnp.where(mine, slot_across.astype(jnp.int32), -1), row_ref.shape
    )
    target = (down[:, :1] * deep + slot_down).astype(jnp.int32)
    pick = (iota((blocks, tables_s.shape[0]), 1) == target).astype(b16)
    load.wait()
    step = 1024

    def choose(part, carry):
        lanes = pl.ds(pl.multiple_of(part * step, step), step)
        chosen_ref[:, lanes] = nn(pick, tables_s[:, lanes]).astype(b16)
        return carry

    lax.fori_loop(0, tables_s.shape[1] // step, choose, 0)
    for copy in copies:
        copy.wait()


def swap_edges_pick(sizes, window, cap, edge, owner, tables, collective_id):
    _, rows, width = edge.shape
    blocks = owner.shape[1]
    vmem = pl.BlockSpec(memory_space=pltpu.VMEM)
    return pl.pallas_call(
        functools.partial(edge_pick_kernel, sizes, window, cap),
        out_shape=(
            jax.ShapeDtypeStruct((2 * window, rows, width), b16),
            jax.ShapeDtypeStruct((blocks, tables.shape[1]), b16),
            jax.ShapeDtypeStruct((8, blocks), jnp.int32),
        ),
        in_specs=[vmem, vmem, pl.BlockSpec(memory_space=pl.ANY)],
        out_specs=[vmem] * 3,
        scratch_shapes=[
            pltpu.SemaphoreType.DMA((2 * window,)),
            pltpu.SemaphoreType.DMA((2 * window,)),
            pltpu.VMEM(tables.shape, b16),
            pltpu.SemaphoreType.DMA,
        ],
        compiler_params=pltpu.CompilerParams(
            collective_id=collective_id, has_side_effects=True, vmem_limit_bytes=VMEM_BYTES
        ),
        name="swap_edges_pick",
    )(edge, owner, tables)


def edge_call(window, collective_id, rows, width, body, extra, outs, scratch, name):
    vmem = pl.BlockSpec(memory_space=pltpu.VMEM)
    outs = [jax.ShapeDtypeStruct((2 * window, rows, width), b16)] + outs
    return pl.pallas_call(
        body,
        out_shape=outs,
        in_specs=[vmem] * (1 + extra),
        out_specs=[vmem] * len(outs),
        scratch_shapes=[
            pltpu.SemaphoreType.DMA((2 * window,)),
            pltpu.SemaphoreType.DMA((2 * window,)),
        ]
        + scratch,
        compiler_params=pltpu.CompilerParams(
            collective_id=collective_id, has_side_effects=True, vmem_limit_bytes=VMEM_BYTES
        ),
        name=name,
    )


def swap_edges(sizes, window, edge, collective_id):
    _, rows, width = edge.shape
    return edge_call(
        window, collective_id, rows, width,
        functools.partial(edge_kernel, sizes, window), 0, [], [], "swap_edges",
    )(edge)[0]


def swap_edges_weights(sizes, window, edge, w_fx, w_mid, w_out, small, collective_id):
    _, rows, width = edge.shape
    n_head = sizes[1]
    layers, part, _ = w_fx.shape
    return edge_call(
        window, collective_id, rows, width,
        functools.partial(edge_weights_kernel, sizes, window), 4,
        [
            jax.ShapeDtypeStruct((2, n_head, part, D), b16),
            jax.ShapeDtypeStruct((layers, n_head, part, D), b16),
            jax.ShapeDtypeStruct((layers, D, 3 * D), f32),
        ],
        [
            pltpu.SemaphoreType.DMA((2, n_head - 1)),
            pltpu.SemaphoreType.DMA((2, n_head - 1)),
            pltpu.VMEM((DH, 128), f32),
        ],
        "swap_edges_weights",
    )(edge, w_fx, w_mid, w_out, small)


def norm_stats(values):
    center = jnp.mean(values, axis=0, keepdims=True)
    spread = values - center
    scale = lax.rsqrt(jnp.mean(spread * spread, axis=0, keepdims=True) + norm_eps)
    return (spread * scale, scale)


def norm_back(grad_out, scaled, scale, gain):
    inner = grad_out * gain
    return scale * (
        inner
        - jnp.mean(inner, axis=0, keepdims=True)
        - scaled * jnp.mean(inner * scaled, axis=0, keepdims=True)
    )


def group_sum(values):
    return jnp.sum(values.reshape(HEADS, SLICES, values.shape[1]), axis=1, keepdims=True)


def fold_lanes(values):
    total = values[:, :128]
    for start in range(128, values.shape[1], 128):
        total = total + values[:, start : start + 128]
    return total


def tile_mask(scal, mesh, tile, width):
    spot = iota((1, width), 1) + tile * width
    return (spot >= scal[mesh]) & (spot < scal[mesh + 1])


def tile_range(scal, tile):
    base = MESHES + 1
    return (scal[base + 2 * tile], scal[base + 2 * tile + 1])


def front_tile(scal, tile, x, wfm, wsb, norms, vh_ref, rs_ref, u_ref, f_ref, m_ref, p_ref, sums):
    width = x.shape[1]
    scaled, scale = norm_stats(x)
    vh_ref[...] = scaled.astype(b16)
    rs_ref[...] = jnp.broadcast_to(scale, (8, width))
    normed = (scaled * norms[:, 0:1] + norms[:, 1:2]).astype(b16)
    u_ref[...] = normed
    joint = nn(wfm, normed)
    feats = joint[:D].astype(b16)
    middle = joint[D:].astype(b16)
    f_ref[...] = feats
    m_ref[...] = middle
    logits = tn(wsb, middle).reshape(HEADS, SLICES, width)
    top = jnp.max(logits, axis=1, keepdims=True)
    expo = jnp.exp(logits - top)
    weights = expo / jnp.sum(expo, axis=1, keepdims=True)
    weights_r = weights.reshape(HS, width).astype(b16)
    p_ref[...] = weights_r
    low, high = tile_range(scal, tile)

    def add(mesh, carry):
        keep = tile_mask(scal, mesh, tile, width).astype(b16)
        wide = jnp.concatenate(
            [feats * keep, jnp.broadcast_to(keep, (128, width))], axis=0
        )
        full = nt(weights_r, wide)
        sums[mesh, :, :D] += pick_diag(full[:, :D], DH)
        sums[mesh, :, D:] += pick_diag(full[:, D:], 16)
        return carry

    lax.fori_loop(low, high + 1, add, 0)


def write_edges(scal, tiles, sums, edge_ref):
    first = tile_range(scal, 0)[0]
    last = tile_range(scal, tiles - 1)[1]
    extra = EDGE - SLICES
    for side, mesh in ((0, first), (1, last)):
        edge_ref[side, :SLICES] = sums[mesh, :, :D].astype(b16)
        rows = jnp.zeros((extra, D), f32)
        if sums.shape[2] > D:
            counts = jnp.concatenate(
                [sums[mesh, :, D:], jnp.zeros((D - SLICES, 128), f32)], axis=0
            )
            pick = (iota((extra, 128), 1) == 16 * iota((extra, 128), 0)).astype(f32)
            rows = nt(pick, counts, HIGH)
        edge_ref[side, SLICES:] = jnp.where(
            iota((extra, D), 0) >= HEADS, mesh.astype(f32), rows
        ).astype(b16)


def add_edges(own, mesh, recv_ref):
    wanted = mesh.astype(f32)
    total = jnp.zeros((EDGE, D), f32)
    for slot in range(recv_ref.shape[0]):
        match = recv_ref[slot, SLICES + HEADS : SLICES + HEADS + 1].astype(f32) == wanted
        total = total + jnp.where(match, recv_ref[slot].astype(f32), 0.0)
    if own.shape[1] == D:
        return own + total[:SLICES]
    extra = EDGE - SLICES
    spread = (iota((extra, 128), 1) // 16 == iota((extra, 128), 0)).astype(f32)
    counts = tn(total[SLICES:, :SLICES], spread, HIGH)
    return own + jnp.concatenate([total[:SLICES], counts], axis=1)


def attend_parts(total, wqb):
    expand = (iota((128, D), 0) == 16 * (iota((128, D), 1) // DH)).astype(f32)
    count = nn(total[:, D:], expand, HIGH)
    slice_tok = total[:, :D] / count
    triple = nn(slice_tok, wqb, HIGH)
    queries, keyset, valueset = triple[:, :D], triple[:, D : 2 * D], triple[:, 2 * D :]
    key_wide = spread_diag(keyset)
    value_wide = spread_diag(valueset)
    scores = (nt(key_wide, queries, HIGH) * (1.0 / math.sqrt(DH))).reshape(HEADS, SLICES, SLICES)
    expo = jnp.exp(scores - jnp.max(scores, axis=1, keepdims=True))
    prob = (expo / jnp.sum(expo, axis=1, keepdims=True)).reshape(HS, SLICES)
    return (slice_tok, count, queries, key_wide, value_wide, prob)


def attend_all(scal, tiles, sums, recv_ref, wqb, total_ref, attended_ref, wide_ref):
    first = tile_range(scal, 0)[0]
    last = tile_range(scal, tiles - 1)[1]

    def one(mesh, carry):
        total = add_edges(sums[mesh], mesh, recv_ref)
        total_ref[mesh] = total
        _, _, _, _, value_wide, prob = attend_parts(total, wqb)
        attended = tn(prob, value_wide, HIGH).astype(b16)
        attended_ref[mesh] = attended
        wide_ref[mesh] = spread_diag(attended)
        return carry

    lax.fori_loop(first, last + 1, one, 0)


def spread_tile(scal, tile, wide_ref, p_ref, spread):
    low, high = tile_range(scal, tile)
    weights_r = p_ref[...]
    width = weights_r.shape[1]

    def one(mesh, carry):
        keep = tile_mask(scal, mesh, tile, width)
        spread[...] = jnp.where(keep, tn(wide_ref[mesh], weights_r), spread[...])
        return carry

    lax.fori_loop(low, high + 1, one, 0)
    return spread[...].astype(b16)


GELU_A = math.sqrt(2.0 / math.pi)
GELU_B = 0.044715


def gelu_pair(hidden):
    square = hidden * hidden
    bend = jnp.tanh(hidden * (GELU_A + (GELU_A * GELU_B) * square))
    half = 0.5 + 0.5 * bend
    value = hidden * half
    slope = half + (0.5 * hidden) * (1.0 - bend * bend) * (
        GELU_A + (3.0 * GELU_A * GELU_B) * square
    )
    return (value, slope)


CHUNK = 256


def mlp_back_tile(scal, tile, grad, slopes, actives, scaled_two, scale_two, normed_two_r, spread_r,
                  weights_r, wout, wup, wdown, norms, d2_ref, de_ref, sums,
                  gup, gdown, gout, gnorm):
    width = grad.shape[1]
    grad_r = grad.astype(b16)
    grad_normed = jnp.zeros((D, width), f32)
    for start in range(0, FF, CHUNK):
        part = slice(start, start + CHUNK)
        back = (slopes(part) * nn(wdown[part], grad_r)).astype(b16)
        gup[:, part] += nt(normed_two_r, back)
        gdown[:, part] += nt(grad_r, actives(part))
        grad_normed = grad_normed + nn(wup[:, part], back)
    gnorm[2] += fold_lanes(grad_normed * scaled_two)
    gnorm[3] += fold_lanes(grad_normed)
    grad_middle = grad + norm_back(grad_normed, scaled_two, scale_two, norms[:, 2:3])
    d2_ref[...] = grad_middle
    branch_r = grad_middle.astype(b16)
    gout[...] += nt(spread_r, branch_r)
    spread_grad = nn(wout, branch_r).astype(b16)
    de_ref[...] = spread_grad
    low, high = tile_range(scal, tile)

    def add(mesh, carry):
        keep = tile_mask(scal, mesh, tile, width).astype(b16)
        sums[mesh] += pick_diag(nt(weights_r, spread_grad * keep), DH)
        return carry

    lax.fori_loop(low, high + 1, add, 0)


def attend_back_all(scal, tiles, sums, recv_ref, total_ref, attended_ref, wqb, both, dcount, gqkv):
    first = tile_range(scal, 0)[0]
    last = tile_range(scal, tiles - 1)[1]
    root = 1.0 / math.sqrt(DH)

    def one(mesh, carry):
        grad = add_edges(sums[mesh], mesh, recv_ref)
        slice_tok, count, queries, key_wide, value_wide, prob = attend_parts(total_ref[mesh], wqb)
        grad_prob = nt(value_wide, grad, HIGH)
        inner = prob * grad_prob
        mixed = group_sum(inner)
        grad_scores = root * (
            inner
            - (prob.reshape(HEADS, SLICES, SLICES) * mixed).reshape(HS, SLICES)
        )
        grad_q = tn(grad_scores, key_wide, HIGH)
        grad_k = pick_diag(nn(grad_scores, queries, HIGH), DH)
        grad_v = pick_diag(nn(prob, grad, HIGH), DH)
        triple = jnp.concatenate([grad_q, grad_k, grad_v], axis=1)
        grad_tok = nt(triple, wqb, HIGH)
        grad_sum = grad_tok / count
        both[mesh, :, :D] = spread_diag(attended_ref[mesh])
        both[mesh, :, D:] = spread_diag(grad_sum.astype(b16))
        grad_count = spread_diag(-(grad_sum * slice_tok))
        dcount[mesh] = jnp.broadcast_to(jnp.sum(grad_count, axis=1, keepdims=True), (HS, 128))
        seen = (recv_ref[0, SLICES + HEADS : SLICES + HEADS + 1, :1].astype(f32) == mesh.astype(f32)).astype(f32)
        gqkv[...] += tn(slice_tok, triple, HIGH) * (1.0 - seen)
        return carry

    lax.fori_loop(first, last + 1, one, 0)


def attend_back_tile(scal, tile, both, dcount, de_ref, f_ref, m_ref, p_ref, u_ref, vh_ref, rs_ref,
                     d2_ref, wfm, wsb, norms, grad_p, grad_f, gfm, gws, gnorm):
    low, high = tile_range(scal, tile)
    weights_r = p_ref[...]
    width = weights_r.shape[1]
    pair = jnp.concatenate([de_ref[...], f_ref[...]], axis=0)

    def one(mesh, carry):
        keep = tile_mask(scal, mesh, tile, width)
        back = nn(both[mesh], pair) + dcount[mesh][:, :1]
        grad_p[...] = jnp.where(keep, back, grad_p[...])
        grad_f[...] = jnp.where(keep, tn(both[mesh, :, D:], weights_r), grad_f[...])
        return carry

    lax.fori_loop(low, high + 1, one, 0)
    weights = weights_r.astype(f32)
    inner = weights * grad_p[...]
    mixed = group_sum(inner)
    grad_logits = (
        inner - (weights.reshape(HEADS, SLICES, width) * mixed).reshape(HS, width)
    ).astype(b16)
    gws[...] += nt(m_ref[...], grad_logits)
    grad_m = nn(wsb, grad_logits).astype(b16)
    grad_fm = jnp.concatenate([grad_f[...].astype(b16), grad_m], axis=0)
    gfm[...] += nt(u_ref[...], grad_fm)
    grad_normed = tn(wfm, grad_fm)
    scaled = vh_ref[...].astype(f32)
    gnorm[0] += fold_lanes(grad_normed * scaled)
    gnorm[1] += fold_lanes(grad_normed)
    return d2_ref[...] + norm_back(grad_normed, scaled, rs_ref[:1], norms[:, 0:1])


def small_rows(base, gws, gqkv, scratch, out_ref):
    lane = iota((1, 128), 1)
    left = repeat_rows(DH)
    fold = (iota((128, HS), 1) % SLICES == iota((128, HS), 0)).astype(f32)
    kept = jnp.where(same_head(DH, SLICES, (D, HS)), gws[...], 0.0)
    scratch[...] = nt(tn(left, kept, HIGH), fold, HIGH)
    even = scratch[pl.ds(0, DH // 2, stride=2), :]
    odd = scratch[pl.ds(1, DH // 2, stride=2), :]
    out_ref[base : base + DH // 2] = jnp.where(lane < SLICES, even, pltpu.roll(odd, SLICES, 1))
    fold = (iota((D, 128), 0) % DH == iota((D, 128), 1)).astype(f32)
    for part in range(3):
        square = jnp.where(same_head(DH, DH, (D, D)), gqkv[:, part * D : (part + 1) * D], 0.0)
        scratch[...] = nn(tn(left, square, HIGH), fold, HIGH)
        total = scratch[pl.ds(0, DH // 4, stride=4), :]
        for inner in range(1, 4):
            total = total + pltpu.roll(scratch[pl.ds(inner, DH // 4, stride=4), :], DH * inner, 1)
        start = base + DH // 2 + part * (DH // 4)
        out_ref[start : start + DH // 4] = total


NORM_ROW = (SMALL - 4 * D) // 128
LAYER_ROWS = SMALL // 128


def norm_rows(gnorm, index, out_ref, base):
    lane = iota((D, 128), 1)
    total = jnp.zeros((D, 128), f32)
    for column, row in enumerate(index):
        total = total + jnp.where(lane == column, jnp.sum(gnorm[row], axis=1, keepdims=True), 0.0)
    flat = total.T
    for column in range(len(index)):
        for half in range(D // 128):
            place = base + column * (D // 128) + half
            out_ref[place : place + 1] = flat[column : column + 1, 128 * half : 128 * half + 128]


def pack_front(gfm, head):
    lane = iota((D, 128), 1)
    start = (head // 2) * 128
    feats, middle = gfm[:, start : start + 128], gfm[:, D + start : D + start + 128]
    if head % 2 == 0:
        return jnp.where(lane < 64, feats, pltpu.roll(middle, 64, 1))
    return jnp.where(lane < 64, pltpu.roll(feats, 64, 1), middle)


def pack_rest(gout, gup, gdown, out_ref, base, n_head):
    for head in range(n_head):
        deep, wide = D // n_head, FF // n_head
        out_ref[head, base : base + deep] = gout[head * deep : (head + 1) * deep].astype(b16)
        start = base + deep
        out_ref[head, start : start + D] = gup[:, head * wide : (head + 1) * wide].astype(b16)
        out_ref[head, start + D : start + 2 * D] = gdown[:, head * wide : (head + 1) * wide].astype(b16)


def first_kernel(tiles, scal, tok_ref, wfm_ref, wsb_ref, norm_ref,
                 xt_ref, vh_ref, rs_ref, u_ref, f_ref, m_ref, p_ref, sums, edge_ref):
    tile = pl.program_id(0)

    @pl.when(tile == 0)
    def _():
        sums[...] = jnp.zeros_like(sums)

    x = tok_ref[...].astype(f32).T
    xt_ref[...] = x.astype(b16)
    front_tile(scal, tile, x, wfm_ref[...], wsb_ref[...], norm_ref[...],
               vh_ref, rs_ref, u_ref, f_ref, m_ref, p_ref, sums)

    @pl.when(tile == tiles - 1)
    def _():
        write_edges(scal, tiles, sums, edge_ref)


def second_kernel(tiles, scal, xt_ref, p0_ref, sums0, recv_ref, wout_ref, wup_ref, wdown_ref, wqb_ref, norm0_ref,
                  wfm_ref, wsb_ref, norm1_ref,
                  e_ref, vh2_ref, rs2_ref, u2_ref, gp_ref, z_ref, att_ref, total_ref,
                  x1_ref, vh_ref, rs_ref, u_ref, f_ref, m_ref, p_ref, sums, edge_ref,
                  wide, spread):
    tile = pl.program_id(0)

    @pl.when(tile == 0)
    def _():
        sums[...] = jnp.zeros_like(sums)
        attend_all(scal, tiles, sums0, recv_ref, wqb_ref[...], total_ref, att_ref, wide)

    norms = norm0_ref[...]
    spread_r = spread_tile(scal, tile, wide, p0_ref, spread)
    e_ref[...] = spread_r
    middle = xt_ref[...].astype(f32) + tn(wout_ref[...], spread_r)
    scaled_two, scale_two = norm_stats(middle)
    vh2_ref[...] = scaled_two.astype(b16)
    rs2_ref[...] = jnp.broadcast_to(scale_two, rs2_ref.shape)
    normed_two_r = (scaled_two * norms[:, 2:3] + norms[:, 3:4]).astype(b16)
    u2_ref[...] = normed_two_r
    x = middle
    for start in range(0, FF, CHUNK):
        part = slice(start, start + CHUNK)
        active, slope = gelu_pair(tn(wup_ref[:, part], normed_two_r))
        active_r = active.astype(b16)
        z_ref[part] = active_r
        gp_ref[part] = slope.astype(b16)
        x = x + tn(wdown_ref[part], active_r)
    x1_ref[...] = x
    front_tile(scal, tile, x, wfm_ref[...], wsb_ref[...], norm1_ref[...],
               vh_ref, rs_ref, u_ref, f_ref, m_ref, p_ref, sums)

    @pl.when(tile == tiles - 1)
    def _():
        write_edges(scal, tiles, sums, edge_ref)


def third_kernel(n_head, packed, tiles, scal, x1_ref, p_ref, sums1, recv_ref, cot_ref, wout_ref, wup_ref, wdown_ref, wqb_ref, norm_ref,
                 out_ref, d2_ref, de_ref, att_ref, total_ref, sums, edge_ref,
                 gn_ref, *rest):
    grad_outs, (wide, spread, gnorm, slope_s, active_s, gup, gdown, gout) = rest[:-8], rest[-8:]
    tile = pl.program_id(0)

    @pl.when(tile == 0)
    def _():
        sums[...] = jnp.zeros_like(sums)
        gup[...] = jnp.zeros_like(gup)
        gdown[...] = jnp.zeros_like(gdown)
        gout[...] = jnp.zeros_like(gout)
        gnorm[...] = jnp.zeros_like(gnorm)
        attend_all(scal, tiles, sums1, recv_ref, wqb_ref[...], total_ref, att_ref, wide)

    norms = norm_ref[...]
    spread_r = spread_tile(scal, tile, wide, p_ref, spread)
    middle = x1_ref[...] + tn(wout_ref[...], spread_r)
    scaled_two, scale_two = norm_stats(middle)
    normed_two_r = (scaled_two * norms[:, 2:3] + norms[:, 3:4]).astype(b16)
    x = middle
    for start in range(0, FF, CHUNK):
        part = slice(start, start + CHUNK)
        active, slope = gelu_pair(tn(wup_ref[:, part], normed_two_r))
        active_r = active.astype(b16)
        active_s[part] = active_r
        slope_s[part] = slope
        x = x + tn(wdown_ref[part], active_r)
    out_ref[...] = x.T.astype(b16)
    grad = cot_ref[...].astype(f32).T
    mlp_back_tile(scal, tile, grad, lambda part: slope_s[part], lambda part: active_s[part],
                  scaled_two, scale_two, normed_two_r, spread_r, p_ref[...],
                  wout_ref[...], wup_ref, wdown_ref, norms, d2_ref, de_ref, sums,
                  gup, gdown, gout, gnorm)

    @pl.when(tile == tiles - 1)
    def _():
        write_edges(scal, tiles, sums, edge_ref)
        norm_rows(gnorm, (2, 3), gn_ref, 0)
        if packed:
            pack_rest(gout, gup, gdown, grad_outs[0], 0, n_head)
        else:
            for ref, total in zip(grad_outs, (gup, gdown, gout)):
                ref[...] = total[...].astype(b16)


def fourth_kernel(n_head, packed, tiles, scal, sums1, recv_ref, att_ref, total_ref, de1_ref, f_ref, m_ref, p1_ref, u_ref, vh_ref, rs_ref, d21_ref,
                  wfm_ref, wsb_ref, wqb_ref, norm1_ref,
                  gp_ref, z_ref, vh2_ref, rs2_ref, u2_ref, e_ref, p0_ref, wout_ref, wup_ref, wdown_ref, norm0_ref, gn1b_ref,
                  d2_ref, de_ref, sums, edge_ref, small_ref, gn0_ref, *rest):
    grad_outs = rest[:-12]
    both, dcount, grad_p, grad_f, gws, gqkv, gnorm, fold_s, gfm, gup, gdown, gout = rest[-12:]
    tile = pl.program_id(0)

    @pl.when(tile == 0)
    def _():
        for ref in (sums, gfm, gws, gqkv, gup, gdown, gout, gnorm):
            ref[...] = jnp.zeros_like(ref)
        attend_back_all(scal, tiles, sums1, recv_ref, total_ref, att_ref, wqb_ref[...], both, dcount, gqkv)

    grad = attend_back_tile(scal, tile, both, dcount, de1_ref, f_ref, m_ref, p1_ref, u_ref, vh_ref, rs_ref,
                            d21_ref, wfm_ref[...], wsb_ref[...], norm1_ref[...], grad_p, grad_f, gfm, gws, gnorm)
    mlp_back_tile(scal, tile, grad, lambda part: gp_ref[part].astype(f32), lambda part: z_ref[part],
                  vh2_ref[...].astype(f32), rs2_ref[:1], u2_ref[...], e_ref[...], p0_ref[...],
                  wout_ref[...], wup_ref, wdown_ref, norm0_ref[...], d2_ref, de_ref, sums,
                  gup, gdown, gout, gnorm)

    @pl.when(tile == tiles - 1)
    def _():
        write_edges(scal, tiles, sums, edge_ref)
        small_rows(0, gws, gqkv, fold_s, small_ref)
        norm_rows(gnorm, (0, 1), small_ref, NORM_ROW)
        small_ref[NORM_ROW + 4 :] = gn1b_ref[...]
        norm_rows(gnorm, (2, 3), gn0_ref, 0)
        if packed:
            for head in range(n_head):
                front = pack_front(gfm, head).astype(b16)
                grad_outs[0][head, : D // 2, :128] = front[: D // 2]
                grad_outs[0][head, : D // 2, 128:] = front[D // 2 :]
            pack_rest(gout, gup, gdown, grad_outs[0], D // 2, n_head)
        else:
            for ref, total in zip(grad_outs, (gfm, gup, gdown, gout)):
                ref[...] = total[...].astype(b16)


def fifth_kernel(n_head, packed, tiles, scal, sums0, recv_ref, att_ref, total_ref, de_ref, f_ref, m_ref, p_ref, u_ref, vh_ref, rs_ref, d2_ref,
                 wfm_ref, wsb_ref, wqb_ref, norm_ref, gn0b_ref, small1_ref,
                 gin_ref, small_ref, front_ref,
                 both, dcount, grad_p, grad_f, gws, gqkv, gnorm, fold_s, gfm):
    tile = pl.program_id(0)

    @pl.when(tile == 0)
    def _():
        for ref in (gfm, gws, gqkv, gnorm):
            ref[...] = jnp.zeros_like(ref)
        attend_back_all(scal, tiles, sums0, recv_ref, total_ref, att_ref, wqb_ref[...], both, dcount, gqkv)

    grad = attend_back_tile(scal, tile, both, dcount, de_ref, f_ref, m_ref, p_ref, u_ref, vh_ref, rs_ref,
                            d2_ref, wfm_ref[...], wsb_ref[...], norm_ref[...], grad_p, grad_f, gfm, gws, gnorm)
    gin_ref[...] = grad.T

    @pl.when(tile == tiles - 1)
    def _():
        small_rows(0, gws, gqkv, fold_s, small_ref)
        norm_rows(gnorm, (0, 1), small_ref, NORM_ROW)
        small_ref[NORM_ROW + 4 : LAYER_ROWS] = gn0b_ref[...]
        small_ref[LAYER_ROWS:] = small1_ref[...]
        if packed:
            for head in range(n_head):
                front_ref[head] = pack_front(gfm, head).astype(b16)
        else:
            front_ref[...] = gfm[...].astype(b16)


def total_kernel(sizes, gb_ref, gc_ref, gs_ref, tb_ref, tc_ref, ts_ref,
                 rb, rc, rs, b_send, b_recv, c_send, c_recv, s_send, s_recv,
                 b_send2, b_recv2, c_send2, c_recv2, s_send2, s_recv2):
    n_pts, n_head = sizes
    total = n_pts * n_head
    pts, head = lax.axis_index("pts"), lax.axis_index("head")
    me = pts * n_head + head
    c_rows = D // n_pts
    b_rows = gb_ref.shape[0] // (n_pts // 2)
    chunks = gs_ref.shape[0] // 8

    def device(index):
        return (index // n_head, lax.rem(index, n_head))

    def copy(src, dst, send, recv, to):
        return pltpu.make_async_remote_copy(
            src_ref=src, dst_ref=dst, send_sem=send, recv_sem=recv, device_id=to, device_id_type=MESH
        )

    def b_part(ref, index):
        return ref.at[
            pl.ds(pl.multiple_of((index // 2) * b_rows, 16), b_rows),
            pl.ds(pl.multiple_of(lax.rem(index, 2) * 128, 128), 128),
        ]

    def c_part(ref, index):
        return ref.at[pl.ds(pl.multiple_of(index * c_rows, c_rows), c_rows), :]

    def s_part(ref, index):
        return ref.at[pl.ds(pl.multiple_of(index * 8, 8), 8), :]

    def c_copy(step):
        peer = lax.rem(me + step, total)
        other, lane = device(peer)
        return copy(c_part(gc_ref.at[lane], other), rc.at[step - 1], c_send.at[step - 1], c_recv.at[step - 1], (other, lane))

    def s_copy(step):
        peer = lax.rem(me + step, total)
        part = jnp.minimum(peer, chunks - 1)
        return peer, copy(s_part(gs_ref, part), rs.at[step - 1], s_send.at[step - 1], s_recv.at[step - 1], device(peer))

    def b_copy(step):
        other = lax.rem(pts + step, n_pts)
        return copy(b_part(gb_ref, other), rb.at[step - 1], b_send.at[step - 1], b_recv.at[step - 1], (other, head))

    def b_share(step):
        other = lax.rem(pts + step, n_pts)
        return copy(b_part(tb_ref, pts), b_part(tb_ref, pts), b_send2.at[step - 1], b_recv2.at[step - 1], (other, head))

    def c_share(step):
        other = lax.rem(pts + step, n_pts)
        return copy(c_part(tc_ref, pts), c_part(tc_ref, pts), c_send2.at[step - 1], c_recv2.at[step - 1], (other, head))

    mine = jnp.minimum(me, chunks - 1)

    def s_share(step):
        peer = lax.rem(me + step, total)
        return copy(s_part(ts_ref, mine), s_part(ts_ref, mine), s_send2.at[step - 1], s_recv2.at[step - 1], device(peer))

    barrier = pltpu.get_barrier_semaphore()

    def hello(step, carry):
        pl.semaphore_signal(barrier, inc=1, device_id=device(lax.rem(me + step, total)), device_id_type=MESH)
        return carry

    def loop(count, body):
        def run(step, carry):
            body(step)
            return carry

        lax.fori_loop(1, count, run, 0)

    lax.fori_loop(1, total, hello, 0)
    pl.semaphore_wait(barrier, total - 1)

    def send_first(step):
        c_copy(step).start()
        peer, small = s_copy(step)

        @pl.when(peer < chunks)
        def _():
            small.start()

    loop(total, send_first)
    loop(n_pts, lambda step: b_copy(step).start())

    def wait_c(step):
        c_copy(step).wait()
        peer, small = s_copy(step)

        @pl.when(peer < chunks)
        def _():
            small.wait_send()

        @pl.when(me < chunks)
        def _():
            small.wait_recv()

    loop(total, wait_c)
    acc = gc_ref[head, pl.ds(pl.multiple_of(pts * c_rows, c_rows), c_rows), :].astype(f32)
    tc_ref[pl.ds(pl.multiple_of(pts * c_rows, c_rows), c_rows), :] = lax.fori_loop(
        0, total - 1, lambda i, acc: acc + rc[i].astype(f32), acc
    ).astype(b16)
    loop(n_pts, lambda step: c_share(step).start())

    @pl.when(me < chunks)
    def _():
        acc = gs_ref[pl.ds(pl.multiple_of(mine * 8, 8), 8), :]
        ts_ref[pl.ds(pl.multiple_of(mine * 8, 8), 8), :] = lax.fori_loop(
            0, total - 1, lambda i, acc: acc + rs[i], acc
        )
        loop(total, lambda step: s_share(step).start())

    loop(n_pts, lambda step: b_copy(step).wait())
    rows, lanes = (
        pl.ds(pl.multiple_of((pts // 2) * b_rows, 16), b_rows),
        pl.ds(pl.multiple_of(lax.rem(pts, 2) * 128, 128), 128),
    )
    acc = gb_ref[rows, lanes].astype(f32)
    for index in range(n_pts - 1):
        acc = acc + rb[index].astype(f32)
    tb_ref[rows, lanes] = acc.astype(b16)
    loop(n_pts, lambda step: b_share(step).start())
    loop(n_pts, lambda step: c_share(step).wait())

    def wait_s(step):
        peer = lax.rem(me + total - step, total)
        share = s_share(step)

        @pl.when(peer < chunks)
        def _():
            share.wait_recv()

        @pl.when(me < chunks)
        def _():
            share.wait_send()

    loop(total, wait_s)
    loop(n_pts, lambda step: b_share(step).wait())


def total_gradients(sizes, gb, gc, gs):
    n_pts, n_head = sizes
    total = n_pts * n_head
    vmem = pl.BlockSpec(memory_space=pltpu.VMEM)
    dma = pltpu.SemaphoreType.DMA
    return pl.pallas_call(
        functools.partial(total_kernel, sizes),
        out_shape=(
            jax.ShapeDtypeStruct(gb.shape, b16),
            jax.ShapeDtypeStruct(gc.shape[1:], b16),
            jax.ShapeDtypeStruct(gs.shape, f32),
        ),
        in_specs=[vmem] * 3,
        out_specs=[vmem] * 3,
        scratch_shapes=[
            pltpu.VMEM((n_pts - 1, gb.shape[0] // (n_pts // 2), 128), b16),
            pltpu.VMEM((total - 1, D // n_pts, 128), b16),
            pltpu.VMEM((total - 1, 8, 128), f32),
        ]
        + [dma((n_pts - 1,))] * 2
        + [dma((total - 1,))] * 4
        + [dma((n_pts - 1,))] * 4
        + [dma((total - 1,))] * 2,
        compiler_params=pltpu.CompilerParams(
            collective_id=3, has_side_effects=True, vmem_limit_bytes=VMEM_BYTES
        ),
        name="total_gradients",
    )(gb, gc, gs)


def update_kernel(ta_ref, tb_ref, tc_ref, ts_ref, row_ref, sel_ref, m_ref, v_ref, w_ref, sm_ref, sv_ref, sw_ref,
                  nm_ref, nv_ref, nw_ref, fresh_ref, om_ref, ov_ref, ow_ref, wide, tall, front, flat):
    lane = iota((8, 128), 1)

    def place_front(base):
        for pair in range(16):
            first = front[pl.ds(2 * pair, 8, stride=32), :]
            second = front[pl.ds(2 * pair + 1, 8, stride=32), :]
            columns = slice(128 * pair, 128 * pair + 128)
            wide[base : base + 8, columns] = jnp.where(lane < 64, first, pltpu.roll(second, 64, 1))
            wide[base + 8 : base + 16, columns] = jnp.where(lane < 64, pltpu.roll(first, 64, 1), second)

    def place_rest(base):
        for part in range(8):
            for half in range(2):
                wide[base : base + 72, 256 * part + 128 * half : 256 * part + 128 * half + 128] = tall[
                    half, pl.ds(part, 72, stride=8), :
                ]

    def fill(value):
        for half in range(2):
            tall[half] = value[:, 128 * half : 128 * half + 128].astype(f32)

    front[...] = tc_ref[...].astype(f32)
    place_front(0)
    fill(tb_ref[D // 2 :])
    place_rest(16)
    front[: D // 2] = tb_ref[: D // 2, :128].astype(f32)
    front[D // 2 :] = tb_ref[: D // 2, 128:].astype(f32)
    place_front(88)
    fill(ta_ref[...])
    place_rest(104)

    cap, blocks = m_ref.shape[0], wide.shape[0]
    mine = (iota((cap, blocks), 0) == row_ref[:1]).astype(f32)
    filled = jnp.sum(mine, axis=1, keepdims=True) > 0.5
    mine = mine.astype(b16)
    step = 512
    for start in range(0, BLOCK, step):
        part = slice(start, start + step)
        grad = wide[:, part]
        own = nn(mine, grad.astype(b16))
        old = (m_ref[:, part], v_ref[:, part], w_ref[:, part])
        new = adam_update(old[0], own, old[1], old[2], rate_large)
        for ref, before, after in zip((nm_ref, nv_ref, nw_ref), old, new):
            ref[:, part] = jnp.where(filled, after, before)
        picked = [
            sel_ref[:, which * BLOCK + start : which * BLOCK + start + step].astype(f32)
            for which in range(3)
        ]
        fresh_ref[:, part] = adam_update(picked[0], grad, picked[1], picked[2], rate_large)[0].astype(b16)
    for layer in range(2):
        for row in range(LAYER_ROWS):
            flat[layer : layer + 1, 128 * row : 128 * row + 128] = ts_ref[
                layer * LAYER_ROWS + row : layer * LAYER_ROWS + row + 1, :
            ]
    new = adam_update(sm_ref[...], flat[:2], sv_ref[...], sw_ref[...], rate_small)
    for ref, value in zip((om_ref, ov_ref, ow_ref), new):
        ref[...] = value


def update(ta, tb, tc, ts, row, sel, tables, smalls):
    vmem = pl.BlockSpec(memory_space=pltpu.VMEM)
    blocks = sel.shape[0]
    operands = (ta, tb, tc, ts, row, sel, *tables, *smalls)
    outs = [jax.ShapeDtypeStruct(table.shape, f32) for table in tables]
    outs.append(jax.ShapeDtypeStruct((blocks, BLOCK), b16))
    outs += [jax.ShapeDtypeStruct(small.shape, f32) for small in smalls]
    return pl.pallas_call(
        update_kernel,
        out_shape=outs,
        in_specs=[vmem] * len(operands),
        out_specs=[vmem] * len(outs),
        scratch_shapes=[
            pltpu.VMEM((blocks, BLOCK), f32),
            pltpu.VMEM((2, ta.shape[0], 128), f32),
            pltpu.VMEM((D, 128), f32),
            pltpu.VMEM((8, SMALL), f32),
        ],
        compiler_params=pltpu.CompilerParams(vmem_limit_bytes=VMEM_BYTES),
        name="update",
    )(*operands)


class Args:
    def __init__(self, rows, width):
        self.rows, self.width = rows, width
        self.operands, self.in_specs, self.outs, self.out_specs = [], [], [], []

    def cols(self, *arrays):
        for array in arrays:
            self.operands.append(array)
            self.in_specs.append(
                pl.BlockSpec((array.shape[0], self.width), lambda tile, scal: (0, tile))
            )

    def points(self, *arrays):
        for array in arrays:
            self.operands.append(array)
            self.in_specs.append(
                pl.BlockSpec((self.width, array.shape[1]), lambda tile, scal: (tile, 0))
            )

    def whole(self, *arrays):
        for array in arrays:
            rank = array.ndim
            self.operands.append(array)
            self.in_specs.append(
                pl.BlockSpec(array.shape, lambda tile, scal, rank=rank: (0,) * rank)
            )

    def layer(self, index, *arrays):
        for array in arrays:
            self.operands.append(array)
            self.in_specs.append(
                pl.BlockSpec((None,) + array.shape[1:], lambda tile, scal: (index, 0, 0))
            )

    def out_cols(self, *pairs):
        for height, dtype in pairs:
            self.outs.append(jax.ShapeDtypeStruct((height, self.rows), dtype))
            self.out_specs.append(
                pl.BlockSpec((height, self.width), lambda tile, scal: (0, tile))
            )

    def out_points(self, *dtypes):
        for dtype in dtypes:
            self.outs.append(jax.ShapeDtypeStruct((self.rows, D), dtype))
            self.out_specs.append(pl.BlockSpec((self.width, D), lambda tile, scal: (tile, 0)))

    def out_whole(self, *pairs):
        for shape, dtype in pairs:
            rank = len(shape)
            self.outs.append(jax.ShapeDtypeStruct(shape, dtype))
            self.out_specs.append(
                pl.BlockSpec(shape, lambda tile, scal, rank=rank: (0,) * rank)
            )

    def call(self, body, scal, scratch, name):
        tiles = self.rows // self.width
        return pl.pallas_call(
            functools.partial(body, tiles),
            grid_spec=pltpu.PrefetchScalarGridSpec(
                num_scalar_prefetch=1,
                grid=(tiles,),
                in_specs=self.in_specs,
                out_specs=self.out_specs,
                scratch_shapes=scratch,
            ),
            out_shape=self.outs,
            compiler_params=pltpu.CompilerParams(
                dimension_semantics=("arbitrary",), vmem_limit_bytes=VMEM_BYTES
            ),
            name=name,
        )(scal, *self.operands)


def adam_update(master, grad, first, second, rate):
    new_first = beta_one * first + (1.0 - beta_one) * grad
    new_second = beta_two * second + (1.0 - beta_two) * grad * grad
    fix_one = 1.0 - beta_one**STEP
    fix_two = 1.0 - beta_two**STEP
    direction = new_first / fix_one / (jnp.sqrt(new_second / fix_two) + adam_eps)
    return (master - rate * (direction + decay_rate * master), new_first, new_second)


def flat_blocks(n_head, gfm, gout, gup, gdown):
    def columns(grad):
        width = grad.shape[1] // n_head
        return grad.reshape(D, n_head, width).transpose(1, 0, 2).reshape(n_head, -1)

    return jnp.concatenate(
        [
            columns(gfm[:, :D]),
            columns(gfm[:, D:]),
            gout.reshape(n_head, -1),
            columns(gup),
            columns(gdown),
        ],
        axis=1,
    ).reshape(n_head, -1, BLOCK)


def on_device(
    sizes,
    tokens,
    cotangent,
    segment_ids,
    owner,
    w_fx,
    w_mid,
    w_out,
    w_up,
    w_down,
    small_master,
    small_first,
    small_second,
    master_table,
    first_table,
    second_table,
):
    n_pts, n_head = sizes
    rows = tokens.shape[0]
    width = min(512, rows)
    tiles = rows // width
    most = rows * n_pts * n_head // LARGEST
    window = (rows - 1 + most - 1) // rows
    layers = w_fx.shape[0]
    packed = (n_pts, n_head) == (8, 4)

    ids = segment_ids.reshape(-1, 128)
    w_fx = w_fx.transpose(0, 2, 1)
    w_mid = w_mid.transpose(0, 2, 1)
    gathered, wsb, norms, scal = opening(n_head, tiles, ids, w_fx, w_mid, small_master)
    wfm0 = gathered.reshape(2 * D, D)

    cap = master_table.shape[0]
    tables = (master_table, first_table, second_table)
    smalls = (small_master, small_first, small_second)
    if packed:
        deep = -(-cap // 16) * 16
        collected = lax.all_gather(
            jnp.pad(
                jnp.concatenate([table.astype(b16) for table in tables], axis=1),
                ((0, deep - cap), (0, 0)),
            ),
            "pts",
            axis=0,
            tiled=True,
        )

    sums_shape = (MESHES, SLICES, D + 128)
    grad_sums_shape = (MESHES, SLICES, D)
    front_cols = ((D, b16), (8, f32), (D, b16), (D, b16), (D, b16), (HS, b16))
    wide_scratch = [pltpu.VMEM((MESHES, HS, D), b16), pltpu.VMEM((D, width), f32)]

    args = Args(rows, width)
    args.points(tokens)
    args.whole(wfm0)
    args.layer(0, wsb, norms)
    args.out_cols((D, b16), *front_cols)
    args.out_whole((sums_shape, f32), ((2, EDGE, D), b16))
    xt0, vh0, rs0, u0, f0, m0, p0, sums0, edge = args.call(first_kernel, scal, [], "first")
    recv, wfm1, wout, wqb = swap_edges_weights(
        sizes, window, edge, w_fx, w_mid, w_out, small_master, 1
    )
    wfm1 = wfm1.reshape(2 * D, D)
    wout = wout.reshape(layers, D, D)

    args = Args(rows, width)
    args.cols(xt0, p0)
    args.whole(sums0, recv)
    args.layer(0, wout, w_up, w_down, wqb, norms)
    args.whole(wfm1)
    args.layer(1, wsb, norms)
    args.out_cols((D, b16), (D, b16), (8, f32), (D, b16), (FF, b16), (FF, b16))
    args.out_whole((grad_sums_shape, b16), (sums_shape, f32))
    args.out_cols((D, f32), *front_cols)
    args.out_whole((sums_shape, f32), ((2, EDGE, D), b16))
    (e0, vh20, rs20, u20, gp0, z0, att0, total0, x1, vh1, rs1, u1, f1, m1, p1, sums1, edge) = args.call(
        second_kernel, scal, wide_scratch, "second"
    )
    recv = swap_edges(sizes, window, edge, 4)

    grad_scratch = [pltpu.VMEM((D, FF), f32), pltpu.VMEM((D, FF), f32), pltpu.VMEM((D, D), f32)]
    rest_rows = D // n_head + 2 * D

    args = Args(rows, width)
    args.cols(x1, p1)
    args.whole(sums1, recv)
    args.points(cotangent)
    args.layer(1, wout, w_up, w_down, wqb, norms)
    args.out_points(b16)
    args.out_cols((D, f32), (D, b16))
    args.out_whole((grad_sums_shape, b16), (sums_shape, f32), (grad_sums_shape, f32), ((2, EDGE, D), b16))
    args.out_whole(((4, 128), f32))
    if packed:
        args.out_whole(((n_head, rest_rows, D), b16))
    else:
        args.out_whole(((D, FF), b16), ((D, FF), b16), ((D, D), b16))
    (layer_out, d21, de1, att1, total1, dsums1, edge, gn1b, *grads_a) = args.call(
        functools.partial(third_kernel, n_head, packed),
        scal,
        wide_scratch
        + [pltpu.VMEM((4, D, 128), f32), pltpu.VMEM((FF, width), f32), pltpu.VMEM((FF, width), b16)]
        + grad_scratch,
        "third",
    )
    if packed:
        recv, chosen, row = swap_edges_pick(
            sizes, window, cap, edge, owner.reshape(1, -1), collected, 2
        )
        part_a = lax.psum_scatter(grads_a[0], "head", scatter_dimension=0, tiled=True)[0]
    else:
        recv = swap_edges(sizes, window, edge, 4)

    back_scratch = [
        pltpu.VMEM((MESHES, HS, 2 * D), b16),
        pltpu.VMEM((MESHES, HS, 128), f32),
        pltpu.VMEM((HS, width), f32),
        pltpu.VMEM((D, width), f32),
        pltpu.VMEM((D, HS), f32),
        pltpu.VMEM((D, 3 * D), f32),
        pltpu.VMEM((4, D, 128), f32),
        pltpu.VMEM((DH, 128), f32),
        pltpu.VMEM((D, 2 * D), f32),
    ]

    args = Args(rows, width)
    args.whole(dsums1, recv, att1, total1)
    args.cols(de1, f1, m1, p1, u1, vh1, rs1, d21)
    args.whole(wfm1)
    args.layer(1, wsb, wqb, norms)
    args.cols(gp0, z0, vh20, rs20, u20, e0, p0)
    args.layer(0, wout, w_up, w_down, norms)
    args.whole(gn1b)
    args.out_cols((D, f32), (D, b16))
    args.out_whole((grad_sums_shape, f32), ((2, EDGE, D), b16), ((LAYER_ROWS, 128), f32), ((4, 128), f32))
    if packed:
        args.out_whole(((n_head, D // 2 + rest_rows, D), b16))
    else:
        args.out_whole(((D, 2 * D), b16), ((D, FF), b16), ((D, FF), b16), ((D, D), b16))
    (d20, de0, dsums0, edge, small1, gn0b, *grads_b) = args.call(
        functools.partial(fourth_kernel, n_head, packed), scal, back_scratch + grad_scratch, "fourth"
    )
    if packed:
        edge, part_a = lax.optimization_barrier((edge, part_a))
        total_a = lax.psum(part_a, "pts")
    recv = swap_edges(sizes, window, edge, 4)

    args = Args(rows, width)
    args.whole(dsums0, recv, att0, total0)
    args.cols(de0, f0, m0, p0, u0, vh0, rs0, d20)
    args.whole(wfm0)
    args.layer(0, wsb, wqb, norms)
    args.whole(gn0b, small1)
    args.out_points(f32)
    args.out_whole(((2 * LAYER_ROWS, 128), f32))
    args.out_whole(((n_head, D, 128), b16) if packed else ((D, 2 * D), b16))
    input_grad, small, front = args.call(
        functools.partial(fifth_kernel, n_head, packed), scal, back_scratch, "fifth"
    )

    if packed:
        mine_b = lax.psum_scatter(grads_b[0], "head", scatter_dimension=0, tiled=True)[0]
        total_b, total_c, total_s = total_gradients(sizes, mine_b, front, small)
        outs = update(total_a, total_b, total_c, total_s, row, chosen, tables, smalls)
        return (layer_out, input_grad, *outs)

    gup1, gdown1, gout1 = grads_a
    gfm1, gup0, gdown0, gout0 = grads_b
    small_total = lax.psum(small, ("pts", "head")).reshape(layers, -1)
    totals = []
    for parts in ((front, gout0, gup0, gdown0), (gfm1, gout1, gup1, gdown1)):
        blocks = lax.psum_scatter(
            flat_blocks(n_head, *parts), "head", scatter_dimension=0, tiled=True
        )
        totals.append(lax.psum(blocks.reshape(-1, BLOCK), "pts"))
    total_grad = jnp.concatenate(totals, axis=0).astype(f32)
    my_index = lax.axis_index("pts")
    block_ids = jnp.arange(owner.shape[0])
    same_owner = (owner[:, None] == owner[None, :]) & (block_ids[None, :] < block_ids[:, None])
    table_row = owner * cap + jnp.sum(same_owner.astype(jnp.int32), axis=1)
    place_all = (jnp.arange(n_pts * cap)[:, None] == table_row[None, :]).astype(f32)
    mine_place = lax.dynamic_slice_in_dim(place_all, my_index * cap, cap, 0)
    own_grad = jnp.dot(mine_place, total_grad, precision=HIGH)
    filled = jnp.sum(mine_place, axis=1)[:, None] > 0.5
    updated = adam_update(master_table, own_grad, first_table, second_table, rate_large)
    new_tables = [jnp.where(filled, new, old) for new, old in zip(updated, tables)]
    collected = lax.all_gather(new_tables[0].astype(b16), "pts", axis=0, tiled=True)
    pick_back = (table_row[:, None] == jnp.arange(n_pts * cap)[None, :]).astype(b16)
    fresh = jnp.dot(pick_back, collected, preferred_element_type=f32).astype(b16)
    small_outs = adam_update(small_master, small_total, small_first, small_second, rate_small)
    return (layer_out, input_grad, *new_tables, fresh, *small_outs)


def solution(mesh):
    sizes = (mesh.shape["pts"], mesh.shape["head"])
    return jax.shard_map(
        functools.partial(on_device, sizes),
        mesh=mesh,
        in_specs=(
            P(("pts", "head"), None),
            P(("pts", "head"), None),
            P("pts"),
            P(),
            P(None, None, "head"),
            P(None, None, "head"),
            P(None, "head", None),
            P(),
            P(),
            P(),
            P(),
            P(),
            P("pts", "head"),
            P("pts", "head"),
            P("pts", "head"),
        ),
        out_specs=(
            P(("pts", "head"), None),
            P(("pts", "head"), None),
            P("pts", "head"),
            P("pts", "head"),
            P("pts", "head"),
            P(None, "head"),
            P(),
            P(),
            P(),
        ),
        check_vma=False,
    )
```

```python
import functools
import math

import jax
import jax.numpy as jnp
from jax import lax
from jax.experimental import pallas as pl
from jax.experimental.pallas import tpu as pltpu
from jax.sharding import PartitionSpec as P

D = 256
HEADS = 8
DH = 32
SLICES = 64
HS = HEADS * SLICES
FF = 1024
MESHES = 24
BLOCK = 2048
SMALL = 6144
STEP = 10
LARGEST = 12
EDGE = 80
VMEM_BYTES = 58 << 20

MESH = pl.DeviceIdType.MESH
HIGH = lax.Precision.HIGHEST
norm_eps = 1e-05
beta_one = 0.9
beta_two = 0.95
adam_eps = 1e-08
decay_rate = 0.1
rate_large = 0.1
rate_small = 0.75
f32 = jnp.float32
b16 = jnp.bfloat16


def nn(a, b, precision=None):
    return lax.dot_general(
        a, b, (((1,), (0,)), ((), ())), preferred_element_type=f32, precision=precision
    )


def nt(a, b, precision=None):
    return lax.dot_general(
        a, b, (((1,), (1,)), ((), ())), preferred_element_type=f32, precision=precision
    )


def tn(a, b, precision=None):
    return lax.dot_general(
        a, b, (((0,), (0,)), ((), ())), preferred_element_type=f32, precision=precision
    )


def iota(shape, axis):
    return lax.broadcasted_iota(jnp.int32, shape, axis)


def pick_diag(full, per_head):
    lane_head = iota((SLICES, full.shape[1]), 1) // per_head
    total = jnp.where(lane_head == 0, full[:SLICES], 0.0)
    for head in range(1, HEADS):
        total = total + jnp.where(
            lane_head == head, full[head * SLICES : (head + 1) * SLICES], 0.0
        )
    return total


def spread_diag(small):
    lane_head = iota((SLICES, D), 1) // DH
    return jnp.concatenate(
        [jnp.where(lane_head == head, small, jnp.zeros_like(small)) for head in range(HEADS)],
        axis=0,
    )


def repeat_rows(width):
    return (iota((D, width), 0) % width == iota((D, width), 1)).astype(f32)


def slice_repeat():
    return (iota((SLICES, HS), 1) % SLICES == iota((SLICES, HS), 0)).astype(f32)


def same_head(rows_per, cols_per, shape):
    return (iota(shape, 0) // rows_per) == (iota(shape, 1) // cols_per)


def start_gather(n_head, picks, send_sem, recv_sem):
    me = lax.axis_index("head")
    copies = []
    for index, ref in enumerate(picks):
        for step in range(1, n_head):
            copy = pltpu.make_async_remote_copy(
                src_ref=ref.at[:, me],
                dst_ref=ref.at[:, me],
                send_sem=send_sem.at[index, step - 1],
                recv_sem=recv_sem.at[index, step - 1],
                device_id={"head": lax.rem(me + step, n_head)},
                device_id_type=MESH,
            )
            copy.start()
            copies.append(copy)
    return copies


def unroll_slices(row_of, out):
    lane = iota((1, 128), 1)
    for pair in range(DH // 2):
        row = row_of(pair)
        out[2 * pair : 2 * pair + 1] = jnp.where(lane < SLICES, row, 0.0)
        out[2 * pair + 1 : 2 * pair + 2] = jnp.where(
            lane < SLICES, pltpu.roll(row, 128 - SLICES, 1), 0.0
        )


def opening_kernel(n_head, tiles, ids_ref, wfx_ref, wmid_ref, sm_ref, m_ref, v_ref, w_ref,
                   out_ref, wsb_ref, norm_ref, scal_ref, tables_ref, send_sem, recv_sem, slices_s, norm_s):
    me = lax.axis_index("head")
    barrier = pltpu.get_barrier_semaphore()
    for step in range(1, n_head):
        pl.semaphore_signal(
            barrier, inc=1, device_id={"head": lax.rem(me + step, n_head)}, device_id_type=MESH
        )
    out_ref[0, me] = wfx_ref[0]
    out_ref[1, me] = wmid_ref[0]
    pl.semaphore_wait(barrier, n_head - 1)
    copies = start_gather(n_head, [out_ref], send_sem, recv_sem)
    layers = sm_ref.shape[0]
    cap, deep = m_ref.shape[0], tables_ref.shape[0]
    for which, ref in enumerate((m_ref, v_ref, w_ref)):
        value = ref[...]
        if deep > cap:
            value = jnp.concatenate([value, jnp.zeros((deep - cap, BLOCK), f32)], axis=0)
        tables_ref[:, which * BLOCK : (which + 1) * BLOCK] = value.astype(b16)
    right = (iota((128, HS), 1) % SLICES == iota((128, HS), 0)).astype(b16)
    for layer in range(layers):
        unroll_slices(lambda pair: sm_ref[layer : layer + 1, 128 * pair : 128 * pair + 128], slices_s)
        wide = nn(slices_s[...].astype(b16), right)
        tiled = jnp.concatenate([wide] * HEADS, axis=0)
        wsb_ref[layer] = jnp.where(same_head(DH, SLICES, (D, HS)), tiled, 0.0).astype(b16)
        norm_s[...] = jnp.zeros_like(norm_s)
        for row in range(4):
            start = SMALL - 4 * D + row * D
            norm_s[row : row + 1] = sm_ref[layer : layer + 1, start : start + D]
        norm_ref[layer] = norm_s[...].T
    rows = ids_ref.shape[0] // n_head
    ids = ids_ref[pl.ds(pl.multiple_of(me * rows, rows), rows), :]
    for mesh in range(MESHES + 1):
        scal_ref[mesh] = jnp.sum((ids < mesh).astype(jnp.int32))
    deep = rows // tiles
    for tile in range(tiles):
        part = ids[tile * deep : (tile + 1) * deep]
        scal_ref[MESHES + 1 + 2 * tile] = jnp.min(part)
        scal_ref[MESHES + 2 + 2 * tile] = jnp.max(part)
    for copy in copies:
        copy.wait()


def opening(n_head, tiles, ids, w_fx, w_mid, small, tables):
    layers, part, _ = w_fx.shape
    deep = -(-tables[0].shape[0] // 16) * 16
    vmem = pl.BlockSpec(memory_space=pltpu.VMEM)
    return pl.pallas_call(
        functools.partial(opening_kernel, n_head, tiles),
        out_shape=(
            jax.ShapeDtypeStruct((2, n_head, part, D), b16),
            jax.ShapeDtypeStruct((layers, D, HS), b16),
            jax.ShapeDtypeStruct((layers, D, 128), f32),
            jax.ShapeDtypeStruct((MESHES + 1 + 2 * tiles,), jnp.int32),
            jax.ShapeDtypeStruct((deep, 3 * BLOCK), b16),
        ),
        in_specs=[vmem] * 7,
        out_specs=[vmem] * 3 + [pl.BlockSpec(memory_space=pltpu.SMEM), vmem],
        scratch_shapes=[
            pltpu.SemaphoreType.DMA((1, n_head - 1)),
            pltpu.SemaphoreType.DMA((1, n_head - 1)),
            pltpu.VMEM((DH, 128), f32),
            pltpu.VMEM((128, D), f32),
        ],
        compiler_params=pltpu.CompilerParams(
            collective_id=0, has_side_effects=True, vmem_limit_bytes=VMEM_BYTES
        ),
        name="opening",
    )(ids, w_fx, w_mid, small, *tables)


def place_of(sizes, shift):
    n_pts, n_head = sizes
    total = n_pts * n_head
    me = lax.axis_index("pts") * n_head + lax.axis_index("head")
    other = lax.rem(me + (shift + total), total)
    return (other // n_head, lax.rem(other, n_head))


def greet(sizes, window):
    barrier = pltpu.get_barrier_semaphore()
    for step in range(1, window + 1):
        for shift in (step, -step):
            pl.semaphore_signal(barrier, inc=1, device_id=place_of(sizes, shift), device_id_type=MESH)
    return barrier


def start_edges(sizes, window, edge_ref, out_ref, send_sem, recv_sem):
    copies = []
    for step in range(1, window + 1):
        for side, shift in ((1, step), (0, -step)):
            slot = step - 1 if side == 1 else window + step - 1
            copy = pltpu.make_async_remote_copy(
                src_ref=edge_ref.at[side],
                dst_ref=out_ref.at[slot],
                send_sem=send_sem.at[slot],
                recv_sem=recv_sem.at[slot],
                device_id=place_of(sizes, shift),
                device_id_type=MESH,
            )
            copy.start()
            copies.append(copy)
    return copies


def edge_kernel(sizes, window, edge_ref, out_ref, send_sem, recv_sem):
    barrier = greet(sizes, window)
    pl.semaphore_wait(barrier, 2 * window)
    for copy in start_edges(sizes, window, edge_ref, out_ref, send_sem, recv_sem):
        copy.wait()


def edge_weights_kernel(sizes, window, layer, pieces, edge_ref, wfx_ref, wmid_ref, wout_ref, sm_ref,
                        out_ref, w_ref, wqb_ref,
                        send_sem, recv_sem, wsend_sem, wrecv_sem, square_s):
    n_head = sizes[1]
    me = lax.axis_index("head")
    barrier = greet(sizes, window)
    for step in range(1, n_head):
        pl.semaphore_signal(
            barrier, inc=1, device_id={"head": lax.rem(me + step, n_head)}, device_id_type=MESH
        )
    refs = (wfx_ref, wmid_ref, wout_ref)
    for index, (kind, which) in enumerate(pieces):
        w_ref[index, me] = refs[kind][which]
    pl.semaphore_wait(barrier, 2 * window + n_head - 1)
    copies = start_edges(sizes, window, edge_ref, out_ref, send_sem, recv_sem)
    copies += start_gather(n_head, [w_ref], wsend_sem, wrecv_sem)
    lane = iota((1, 128), 1)
    for part in range(3):
        start = DH * SLICES + part * DH * DH
        for group in range(DH // 4):
            row = sm_ref[layer : layer + 1, start + 128 * group : start + 128 * group + 128]
            for inner in range(4):
                moved = row if inner == 0 else pltpu.roll(row, 128 - DH * inner, 1)
                square_s[4 * group + inner : 4 * group + inner + 1] = jnp.where(
                    lane < DH, moved, 0.0
                )
        square = square_s[...]
        for turn in range(1, 128 // DH):
            square = square + pltpu.roll(square_s[...], DH * turn, 1)
        square = jnp.concatenate([square] * (D // 128), axis=1)
        square = jnp.concatenate([square] * HEADS, axis=0)
        wqb_ref[:, part * D : (part + 1) * D] = jnp.where(
            same_head(DH, DH, (D, D)), square, 0.0
        )
    for copy in copies:
        copy.wait()


def edge_pick_kernel(sizes, window, cap, edge_ref, owner_ref, tables_ref,
                     out_ref, chosen_ref, row_ref, send_sem, recv_sem, tables_s, local_sem):
    barrier = greet(sizes, window)
    load = pltpu.make_async_copy(tables_ref, tables_s, local_sem)
    load.start()
    pl.semaphore_wait(barrier, 2 * window)
    copies = start_edges(sizes, window, edge_ref, out_ref, send_sem, recv_sem)
    blocks = owner_ref.shape[1]
    deep = tables_s.shape[0] // sizes[0]
    across = jnp.broadcast_to(owner_ref[...].astype(f32), (blocks, blocks))
    down = across.T
    low, high = iota((blocks, blocks), 0), iota((blocks, blocks), 1)
    same = across == down
    slot_down = jnp.sum(jnp.where(same & (high < low), 1.0, 0.0), axis=1, keepdims=True)
    slot_across = jnp.sum(jnp.where(same & (low < high), 1.0, 0.0), axis=0, keepdims=True)
    mine = owner_ref[...] == lax.axis_index("pts")
    row_ref[...] = jnp.broadcast_to(
        jnp.where(mine, slot_across.astype(jnp.int32), -1), row_ref.shape
    )
    target = (down[:, :1] * deep + slot_down).astype(jnp.int32)
    pick = (iota((blocks, tables_s.shape[0]), 1) == target).astype(b16)
    load.wait()
    step = 1024

    def choose(part, carry):
        lanes = pl.ds(pl.multiple_of(part * step, step), step)
        chosen_ref[:, lanes] = nn(pick, tables_s[:, lanes]).astype(b16)
        return carry

    lax.fori_loop(0, tables_s.shape[1] // step, choose, 0)
    for copy in copies:
        copy.wait()


def swap_edges_pick(sizes, window, cap, edge, owner, tables, collective_id):
    _, rows, width = edge.shape
    blocks = owner.shape[1]
    vmem = pl.BlockSpec(memory_space=pltpu.VMEM)
    return pl.pallas_call(
        functools.partial(edge_pick_kernel, sizes, window, cap),
        out_shape=(
            jax.ShapeDtypeStruct((2 * window, rows, width), b16),
            jax.ShapeDtypeStruct((blocks, tables.shape[1]), b16),
            jax.ShapeDtypeStruct((8, blocks), jnp.int32),
        ),
        in_specs=[vmem, vmem, pl.BlockSpec(memory_space=pl.ANY)],
        out_specs=[vmem] * 3,
        scratch_shapes=[
            pltpu.SemaphoreType.DMA((2 * window,)),
            pltpu.SemaphoreType.DMA((2 * window,)),
            pltpu.VMEM(tables.shape, b16),
            pltpu.SemaphoreType.DMA,
        ],
        compiler_params=pltpu.CompilerParams(
            collective_id=collective_id, has_side_effects=True, vmem_limit_bytes=VMEM_BYTES
        ),
        name="swap_edges_pick",
    )(edge, owner, tables)


def edge_call(window, collective_id, rows, width, body, extra, outs, scratch, name):
    vmem = pl.BlockSpec(memory_space=pltpu.VMEM)
    outs = [jax.ShapeDtypeStruct((2 * window, rows, width), b16)] + outs
    return pl.pallas_call(
        body,
        out_shape=outs,
        in_specs=[vmem] * (1 + extra),
        out_specs=[vmem] * len(outs),
        scratch_shapes=[
            pltpu.SemaphoreType.DMA((2 * window,)),
            pltpu.SemaphoreType.DMA((2 * window,)),
        ]
        + scratch,
        compiler_params=pltpu.CompilerParams(
            collective_id=collective_id, has_side_effects=True, vmem_limit_bytes=VMEM_BYTES
        ),
        name=name,
    )


def swap_edges(sizes, window, edge, collective_id):
    _, rows, width = edge.shape
    return edge_call(
        window, collective_id, rows, width,
        functools.partial(edge_kernel, sizes, window), 0, [], [], "swap_edges",
    )(edge)[0]


def swap_edges_weights(sizes, window, layer, pieces, edge, w_fx, w_mid, w_out, small, collective_id):
    _, rows, width = edge.shape
    n_head = sizes[1]
    part = w_fx.shape[1]
    return edge_call(
        window, collective_id, rows, width,
        functools.partial(edge_weights_kernel, sizes, window, layer, pieces), 4,
        [
            jax.ShapeDtypeStruct((len(pieces), n_head, part, D), b16),
            jax.ShapeDtypeStruct((D, 3 * D), f32),
        ],
        [
            pltpu.SemaphoreType.DMA((1, n_head - 1)),
            pltpu.SemaphoreType.DMA((1, n_head - 1)),
            pltpu.VMEM((DH, 128), f32),
        ],
        "swap_edges_weights",
    )(edge, w_fx, w_mid, w_out, small)


def pts_copies(n_pts, source, target, send_sem, recv_sem):
    pts, head = lax.axis_index("pts"), lax.axis_index("head")
    copies = []
    for step in range(1, n_pts):
        peer = lax.rem(pts + step, n_pts)
        copies.append(
            pltpu.make_async_remote_copy(
                src_ref=source(step, peer),
                dst_ref=target(step, peer),
                send_sem=send_sem.at[step - 1],
                recv_sem=recv_sem.at[step - 1],
                device_id=(peer, head),
                device_id_type=MESH,
            )
        )
    return copies


def edge_sums_kernel(sizes, window, edge_ref, ga_ref, out_ref, ta_ref,
                     send_sem, recv_sem, a_send, a_recv, a_send2, a_recv2, got_a):
    n_pts, n_head = sizes
    pts, head = lax.axis_index("pts"), lax.axis_index("head")
    barrier = greet(sizes, window)
    for step in range(1, n_pts):
        pl.semaphore_signal(
            barrier, inc=1, device_id=(lax.rem(pts + step, n_pts), head), device_id_type=MESH
        )
    pl.semaphore_wait(barrier, 2 * window + n_pts - 1)
    edges = start_edges(sizes, window, edge_ref, out_ref, send_sem, recv_sem)
    gather = pts_copies(
        n_pts,
        lambda step, peer: ga_ref.at[peer],
        lambda step, peer: got_a.at[step - 1],
        a_send,
        a_recv,
    )
    for copy in gather:
        copy.start()
    for copy in gather:
        copy.wait()
    total = ga_ref[pts].astype(f32)
    for index in range(n_pts - 1):
        total = total + got_a[index].astype(f32)
    ta_ref[pts] = total.astype(b16)
    share = pts_copies(
        n_pts,
        lambda step, peer: ta_ref.at[pts],
        lambda step, peer: ta_ref.at[pts],
        a_send2,
        a_recv2,
    )
    for copy in share:
        copy.start()
    for copy in edges:
        copy.wait()
    for copy in share:
        copy.wait()


def swap_edges_sums(sizes, window, edge, ga, collective_id):
    _, rows, width = edge.shape
    n_pts = sizes[0]
    dma = pltpu.SemaphoreType.DMA
    return edge_call(
        window, collective_id, rows, width,
        functools.partial(edge_sums_kernel, sizes, window), 1,
        [jax.ShapeDtypeStruct(ga.shape, b16)],
        [dma((n_pts - 1,))] * 4 + [pltpu.VMEM((n_pts - 1,) + ga.shape[1:], b16)],
        "swap_edges_sums",
    )(edge, ga)


def norm_stats(values):
    center = jnp.mean(values, axis=0, keepdims=True)
    spread = values - center
    scale = lax.rsqrt(jnp.mean(spread * spread, axis=0, keepdims=True) + norm_eps)
    return (spread * scale, scale)


def norm_back(grad_out, scaled, scale, gain):
    inner = grad_out * gain
    return scale * (
        inner
        - jnp.mean(inner, axis=0, keepdims=True)
        - scaled * jnp.mean(inner * scaled, axis=0, keepdims=True)
    )


def group_sum(values):
    return jnp.sum(values.reshape(HEADS, SLICES, values.shape[1]), axis=1, keepdims=True)


def fold_lanes(values):
    total = values[:, :128]
    for start in range(128, values.shape[1], 128):
        total = total + values[:, start : start + 128]
    return total


def tile_mask(scal, mesh, tile, width):
    spot = iota((1, width), 1) + tile * width
    return (spot >= scal[mesh]) & (spot < scal[mesh + 1])


def tile_range(scal, tile):
    base = MESHES + 1
    return (scal[base + 2 * tile], scal[base + 2 * tile + 1])


def front_tile(scal, tile, x, wfm, wsb, norms, vh_ref, rs_ref, u_ref, f_ref, m_ref, p_ref, sums):
    width = x.shape[1]
    scaled, scale = norm_stats(x)
    vh_ref[...] = scaled.astype(b16)
    rs_ref[...] = jnp.broadcast_to(scale, (8, width))
    normed = (scaled * norms[:, 0:1] + norms[:, 1:2]).astype(b16)
    u_ref[...] = normed
    joint = nn(wfm, normed)
    feats = joint[:D].astype(b16)
    middle = joint[D:].astype(b16)
    f_ref[...] = feats
    m_ref[...] = middle
    logits = tn(wsb, middle).reshape(HEADS, SLICES, width)
    top = jnp.max(logits, axis=1, keepdims=True)
    expo = jnp.exp(logits - top)
    weights = expo / jnp.sum(expo, axis=1, keepdims=True)
    weights_r = weights.reshape(HS, width).astype(b16)
    p_ref[...] = weights_r
    low, high = tile_range(scal, tile)

    def add(mesh, carry):
        keep = tile_mask(scal, mesh, tile, width).astype(b16)
        wide = jnp.concatenate(
            [feats * keep, jnp.broadcast_to(keep, (128, width))], axis=0
        )
        full = nt(weights_r, wide)
        sums[mesh, :, :D] += pick_diag(full[:, :D], DH)
        sums[mesh, :, D:] += pick_diag(full[:, D:], 16)
        return carry

    lax.fori_loop(low, high + 1, add, 0)


def present(scal, tiles, body):
    def one(mesh, carry):
        body(mesh)
        return carry

    lax.fori_loop(tile_range(scal, 0)[0], tile_range(scal, tiles - 1)[1] + 1, one, 0)


def move_present(scal, tiles, source, target, sem):
    present(scal, tiles, lambda mesh: pltpu.make_async_copy(source.at[mesh], target.at[mesh], sem.at[mesh]).start())
    present(scal, tiles, lambda mesh: pltpu.make_async_copy(source.at[mesh], target.at[mesh], sem.at[mesh]).wait())


def clear_present(scal, tiles, sums):
    def clear(mesh):
        sums[mesh] = jnp.zeros(sums.shape[1:], f32)

    present(scal, tiles, clear)


def write_edges(scal, tiles, sums, edge_ref):
    first = tile_range(scal, 0)[0]
    last = tile_range(scal, tiles - 1)[1]
    extra = EDGE - SLICES
    for side, mesh in ((0, first), (1, last)):
        edge_ref[side, :SLICES] = sums[mesh, :, :D].astype(b16)
        rows = jnp.zeros((extra, D), f32)
        if sums.shape[2] > D:
            counts = jnp.concatenate(
                [sums[mesh, :, D:], jnp.zeros((D - SLICES, 128), f32)], axis=0
            )
            pick = (iota((extra, 128), 1) == 16 * iota((extra, 128), 0)).astype(f32)
            rows = nt(pick, counts, HIGH)
        edge_ref[side, SLICES:] = jnp.where(
            iota((extra, D), 0) >= HEADS, mesh.astype(f32), rows
        ).astype(b16)


def add_edges(own, mesh, recv_ref):
    wanted = mesh.astype(f32)
    total = jnp.zeros((EDGE, D), f32)
    for slot in range(recv_ref.shape[0]):
        match = recv_ref[slot, SLICES + HEADS : SLICES + HEADS + 1].astype(f32) == wanted
        total = total + jnp.where(match, recv_ref[slot].astype(f32), 0.0)
    if own.shape[1] == D:
        return own + total[:SLICES]
    extra = EDGE - SLICES
    spread = (iota((extra, 128), 1) // 16 == iota((extra, 128), 0)).astype(f32)
    counts = tn(total[SLICES:, :SLICES], spread, HIGH)
    return own + jnp.concatenate([total[:SLICES], counts], axis=1)


def attend_parts(total, wqb):
    expand = (iota((128, D), 0) == 16 * (iota((128, D), 1) // DH)).astype(f32)
    count = nn(total[:, D:], expand, HIGH)
    slice_tok = total[:, :D] / count
    triple = nn(slice_tok, wqb, HIGH)
    queries, keyset, valueset = triple[:, :D], triple[:, D : 2 * D], triple[:, 2 * D :]
    key_wide = spread_diag(keyset)
    value_wide = spread_diag(valueset)
    scores = (nt(key_wide, queries, HIGH) * (1.0 / math.sqrt(DH))).reshape(HEADS, SLICES, SLICES)
    expo = jnp.exp(scores - jnp.max(scores, axis=1, keepdims=True))
    prob = (expo / jnp.sum(expo, axis=1, keepdims=True)).reshape(HS, SLICES)
    return (slice_tok, count, queries, key_wide, value_wide, prob)


def attend_all(scal, tiles, sums, recv_ref, wqb, wide_ref):
    def one(mesh):
        total = add_edges(sums[mesh], mesh, recv_ref)
        _, _, _, _, value_wide, prob = attend_parts(total, wqb)
        wide_ref[mesh] = spread_diag(tn(prob, value_wide, HIGH).astype(b16))

    present(scal, tiles, one)


def spread_tile(scal, tile, wide_ref, p_ref, spread):
    low, high = tile_range(scal, tile)
    weights_r = p_ref[...]
    width = weights_r.shape[1]

    def one(mesh, carry):
        keep = tile_mask(scal, mesh, tile, width)
        spread[...] = jnp.where(keep, tn(wide_ref[mesh], weights_r), spread[...])
        return carry

    lax.fori_loop(low, high + 1, one, 0)
    return spread[...].astype(b16)


GELU_A = math.sqrt(2.0 / math.pi)
GELU_B = 0.044715


def gelu_pair(hidden):
    square = hidden * hidden
    bend = jnp.tanh(hidden * (GELU_A + (GELU_A * GELU_B) * square))
    half = 0.5 + 0.5 * bend
    value = hidden * half
    slope = half + (0.5 * hidden) * (1.0 - bend * bend) * (
        GELU_A + (3.0 * GELU_A * GELU_B) * square
    )
    return (value, slope)


CHUNK = 256


def mlp_back_tile(scal, tile, grad, slopes, actives, scaled_two, scale_two, normed_two_r, spread_r,
                  weights_r, wout, wup, wdown, norms, d2_ref, de_ref, sums,
                  gup, gdown, gout, gnorm):
    width = grad.shape[1]
    grad_r = grad.astype(b16)
    grad_normed = jnp.zeros((D, width), f32)
    for start in range(0, FF, CHUNK):
        part = slice(start, start + CHUNK)
        back = (slopes(part) * nn(wdown[part], grad_r)).astype(b16)
        gup[:, part] += nt(normed_two_r, back)
        gdown[:, part] += nt(grad_r, actives(part))
        grad_normed = grad_normed + nn(wup[:, part], back)
    gnorm[2] += fold_lanes(grad_normed * scaled_two)
    gnorm[3] += fold_lanes(grad_normed)
    grad_middle = grad + norm_back(grad_normed, scaled_two, scale_two, norms[:, 2:3])
    d2_ref[...] = grad_middle
    branch_r = grad_middle.astype(b16)
    gout[...] += nt(spread_r, branch_r)
    spread_grad = nn(wout, branch_r).astype(b16)
    de_ref[...] = spread_grad
    low, high = tile_range(scal, tile)

    def add(mesh, carry):
        keep = tile_mask(scal, mesh, tile, width).astype(b16)
        sums[mesh] += pick_diag(nt(weights_r, spread_grad * keep), DH)
        return carry

    lax.fori_loop(low, high + 1, add, 0)


def attend_back_all(scal, tiles, sums, recv_ref, grads, grad_recv_ref, wqb, both, dcount, gqkv):
    root = 1.0 / math.sqrt(DH)

    def one(mesh):
        grad = add_edges(grads[mesh], mesh, grad_recv_ref)
        total = add_edges(sums[mesh], mesh, recv_ref)
        slice_tok, count, queries, key_wide, value_wide, prob = attend_parts(total, wqb)
        grad_prob = nt(value_wide, grad, HIGH)
        inner = prob * grad_prob
        mixed = group_sum(inner)
        grad_scores = root * (
            inner
            - (prob.reshape(HEADS, SLICES, SLICES) * mixed).reshape(HS, SLICES)
        )
        grad_q = tn(grad_scores, key_wide, HIGH)
        grad_k = pick_diag(nn(grad_scores, queries, HIGH), DH)
        grad_v = pick_diag(nn(prob, grad, HIGH), DH)
        triple = jnp.concatenate([grad_q, grad_k, grad_v], axis=1)
        grad_tok = nt(triple, wqb, HIGH)
        grad_sum = grad_tok / count
        both[mesh, :, :D] = spread_diag(tn(prob, value_wide, HIGH).astype(b16))
        both[mesh, :, D:] = spread_diag(grad_sum.astype(b16))
        grad_count = spread_diag(-(grad_sum * slice_tok))
        dcount[mesh] = jnp.broadcast_to(jnp.sum(grad_count, axis=1, keepdims=True), (HS, 128))
        seen = (recv_ref[0, SLICES + HEADS : SLICES + HEADS + 1, :1].astype(f32) == mesh.astype(f32)).astype(f32)
        gqkv[...] += tn(slice_tok, triple, HIGH) * (1.0 - seen)

    present(scal, tiles, one)


def attend_back_tile(scal, tile, both, dcount, de_ref, f_ref, m_ref, p_ref, u_ref, vh_ref, rs_ref,
                     d2_ref, wfm, wsb, norms, grad_p, grad_f, gfm, gws, gnorm):
    low, high = tile_range(scal, tile)
    weights_r = p_ref[...]
    width = weights_r.shape[1]
    pair = jnp.concatenate([de_ref[...], f_ref[...]], axis=0)

    def one(mesh, carry):
        keep = tile_mask(scal, mesh, tile, width)
        back = nn(both[mesh], pair) + dcount[mesh][:, :1]
        grad_p[...] = jnp.where(keep, back, grad_p[...])
        grad_f[...] = jnp.where(keep, tn(both[mesh, :, D:], weights_r), grad_f[...])
        return carry

    lax.fori_loop(low, high + 1, one, 0)
    weights = weights_r.astype(f32)
    inner = weights * grad_p[...]
    mixed = group_sum(inner)
    grad_logits = (
        inner - (weights.reshape(HEADS, SLICES, width) * mixed).reshape(HS, width)
    ).astype(b16)
    gws[...] += nt(m_ref[...], grad_logits)
    grad_m = nn(wsb, grad_logits).astype(b16)
    grad_fm = jnp.concatenate([grad_f[...].astype(b16), grad_m], axis=0)
    gfm[...] += nt(u_ref[...], grad_fm)
    grad_normed = tn(wfm, grad_fm)
    scaled = vh_ref[...].astype(f32)
    gnorm[0] += fold_lanes(grad_normed * scaled)
    gnorm[1] += fold_lanes(grad_normed)
    return d2_ref[...] + norm_back(grad_normed, scaled, rs_ref[:1], norms[:, 0:1])


def small_rows(base, gws, gqkv, scratch, out_ref):
    lane = iota((1, 128), 1)
    left = repeat_rows(DH)
    fold = (iota((128, HS), 1) % SLICES == iota((128, HS), 0)).astype(f32)
    kept = jnp.where(same_head(DH, SLICES, (D, HS)), gws[...], 0.0)
    scratch[...] = nt(tn(left, kept, HIGH), fold, HIGH)
    even = scratch[pl.ds(0, DH // 2, stride=2), :]
    odd = scratch[pl.ds(1, DH // 2, stride=2), :]
    out_ref[base : base + DH // 2] = jnp.where(lane < SLICES, even, pltpu.roll(odd, SLICES, 1))
    fold = (iota((D, 128), 0) % DH == iota((D, 128), 1)).astype(f32)
    for part in range(3):
        square = jnp.where(same_head(DH, DH, (D, D)), gqkv[:, part * D : (part + 1) * D], 0.0)
        scratch[...] = nn(tn(left, square, HIGH), fold, HIGH)
        total = scratch[pl.ds(0, DH // 4, stride=4), :]
        for inner in range(1, 4):
            total = total + pltpu.roll(scratch[pl.ds(inner, DH // 4, stride=4), :], DH * inner, 1)
        start = base + DH // 2 + part * (DH // 4)
        out_ref[start : start + DH // 4] = total


NORM_ROW = (SMALL - 4 * D) // 128
LAYER_ROWS = SMALL // 128


def norm_rows(gnorm, index, out_ref, base):
    lane = iota((D, 128), 1)
    total = jnp.zeros((D, 128), f32)
    for column, row in enumerate(index):
        total = total + jnp.where(lane == column, jnp.sum(gnorm[row], axis=1, keepdims=True), 0.0)
    flat = total.T
    for column in range(len(index)):
        for half in range(D // 128):
            place = base + column * (D // 128) + half
            out_ref[place : place + 1] = flat[column : column + 1, 128 * half : 128 * half + 128]


def pack_front(gfm, head):
    lane = iota((D, 128), 1)
    start = (head // 2) * 128
    feats, middle = gfm[:, start : start + 128], gfm[:, D + start : D + start + 128]
    if head % 2 == 0:
        return jnp.where(lane < 64, feats, pltpu.roll(middle, 64, 1))
    return jnp.where(lane < 64, pltpu.roll(feats, 64, 1), middle)


def store_pieces(out_ref, head, base, value):
    size = out_ref.shape[2]
    done = 0
    while done < value.shape[0]:
        chunk, offset = divmod(base + done, size)
        count = min(size - offset, value.shape[0] - done)
        for half in range(2):
            out_ref[head, 2 * chunk + half, offset : offset + count] = value[
                done : done + count, 128 * half : 128 * half + 128
            ]
        done += count


def pack_rest(gout, gup, gdown, out_ref, base, n_head):
    for head in range(n_head):
        deep, wide = D // n_head, FF // n_head
        store_pieces(out_ref, head, base, gout[head * deep : (head + 1) * deep].astype(b16))
        start = base + deep
        store_pieces(out_ref, head, start, gup[:, head * wide : (head + 1) * wide].astype(b16))
        store_pieces(out_ref, head, start + D, gdown[:, head * wide : (head + 1) * wide].astype(b16))


def first_kernel(tiles, scal, tok_ref, wfm_ref, wsb_ref, norm_ref,
                 xt_ref, vh_ref, rs_ref, u_ref, f_ref, m_ref, p_ref, sums_hbm, edge_ref, sums, sem):
    tile = pl.program_id(0)

    @pl.when(tile == 0)
    def _():
        clear_present(scal, tiles, sums)

    x = tok_ref[...].astype(f32).T
    xt_ref[...] = x.astype(b16)
    front_tile(scal, tile, x, wfm_ref[...], wsb_ref[...], norm_ref[...],
               vh_ref, rs_ref, u_ref, f_ref, m_ref, p_ref, sums)

    @pl.when(tile == tiles - 1)
    def _():
        write_edges(scal, tiles, sums, edge_ref)
        move_present(scal, tiles, sums, sums_hbm, sem)


def second_kernel(tiles, scal, xt_ref, p0_ref, sums0_hbm, recv_ref, wout_ref, wup_ref, wdown_ref, wqb_ref, norm0_ref,
                  wfm_ref, wsb_ref, norm1_ref,
                  e_ref, vh2_ref, rs2_ref, u2_ref, gp_ref, z_ref,
                  x1_ref, vh_ref, rs_ref, u_ref, f_ref, m_ref, p_ref, sums_hbm, edge_ref,
                  wide, spread, sums, sem):
    tile = pl.program_id(0)

    @pl.when(tile == 0)
    def _():
        move_present(scal, tiles, sums0_hbm, sums, sem)
        attend_all(scal, tiles, sums, recv_ref, wqb_ref[...], wide)
        clear_present(scal, tiles, sums)

    norms = norm0_ref[...]
    spread_r = spread_tile(scal, tile, wide, p0_ref, spread)
    e_ref[...] = spread_r
    middle = xt_ref[...].astype(f32) + tn(wout_ref[...], spread_r)
    scaled_two, scale_two = norm_stats(middle)
    vh2_ref[...] = scaled_two.astype(b16)
    rs2_ref[...] = jnp.broadcast_to(scale_two, rs2_ref.shape)
    normed_two_r = (scaled_two * norms[:, 2:3] + norms[:, 3:4]).astype(b16)
    u2_ref[...] = normed_two_r
    x = middle
    for start in range(0, FF, CHUNK):
        part = slice(start, start + CHUNK)
        active, slope = gelu_pair(tn(wup_ref[:, part], normed_two_r))
        active_r = active.astype(b16)
        z_ref[part] = active_r
        gp_ref[part] = slope.astype(b16)
        x = x + tn(wdown_ref[part], active_r)
    x1_ref[...] = x
    front_tile(scal, tile, x, wfm_ref[...], wsb_ref[...], norm1_ref[...],
               vh_ref, rs_ref, u_ref, f_ref, m_ref, p_ref, sums)

    @pl.when(tile == tiles - 1)
    def _():
        write_edges(scal, tiles, sums, edge_ref)
        move_present(scal, tiles, sums, sums_hbm, sem)


def third_kernel(n_head, packed, tiles, scal, x1_ref, p_ref, sums1_hbm, recv_ref, cot_ref, wout_ref, wup_ref, wdown_ref, wqb_ref, norm_ref,
                 out_ref, d2_ref, de_ref, grads_hbm, edge_ref,
                 gn_ref, *rest):
    grad_outs, (sums, sem, grads, wide, spread, gnorm, slope_s, active_s, gup, gdown, gout) = rest[:-11], rest[-11:]
    tile = pl.program_id(0)

    @pl.when(tile == 0)
    def _():
        clear_present(scal, tiles, grads)
        gup[...] = jnp.zeros_like(gup)
        gdown[...] = jnp.zeros_like(gdown)
        gout[...] = jnp.zeros_like(gout)
        gnorm[...] = jnp.zeros_like(gnorm)
        move_present(scal, tiles, sums1_hbm, sums, sem)
        attend_all(scal, tiles, sums, recv_ref, wqb_ref[...], wide)

    norms = norm_ref[...]
    spread_r = spread_tile(scal, tile, wide, p_ref, spread)
    middle = x1_ref[...] + tn(wout_ref[...], spread_r)
    scaled_two, scale_two = norm_stats(middle)
    normed_two_r = (scaled_two * norms[:, 2:3] + norms[:, 3:4]).astype(b16)
    x = middle
    for start in range(0, FF, CHUNK):
        part = slice(start, start + CHUNK)
        active, slope = gelu_pair(tn(wup_ref[:, part], normed_two_r))
        active_r = active.astype(b16)
        active_s[part] = active_r
        slope_s[part] = slope
        x = x + tn(wdown_ref[part], active_r)
    out_ref[...] = x.T.astype(b16)
    grad = cot_ref[...].astype(f32).T
    mlp_back_tile(scal, tile, grad, lambda part: slope_s[part], lambda part: active_s[part],
                  scaled_two, scale_two, normed_two_r, spread_r, p_ref[...],
                  wout_ref[...], wup_ref, wdown_ref, norms, d2_ref, de_ref, grads,
                  gup, gdown, gout, gnorm)

    @pl.when(tile == tiles - 1)
    def _():
        write_edges(scal, tiles, grads, edge_ref)
        move_present(scal, tiles, grads, grads_hbm, sem)
        norm_rows(gnorm, (2, 3), gn_ref, 0)
        if packed:
            pack_rest(gout, gup, gdown, grad_outs[0], 0, n_head)
        else:
            for ref, total in zip(grad_outs, (gup, gdown, gout)):
                ref[...] = total[...].astype(b16)


def fourth_kernel(n_head, packed, tiles, scal, sums1_hbm, recv_ref, grads1_hbm, grad_recv_ref, de1_ref, f_ref, m_ref, p1_ref, u_ref, vh_ref, rs_ref, d21_ref,
                  wfm_ref, wsb_ref, wqb_ref, norm1_ref,
                  gp_ref, z_ref, vh2_ref, rs2_ref, u2_ref, e_ref, p0_ref, wout_ref, wup_ref, wdown_ref, norm0_ref, gn1b_ref,
                  d2_ref, de_ref, grads_hbm, edge_ref, small_ref, gn0_ref, *rest):
    grad_outs = rest[:-15]
    sums, grads, sem, both, dcount, grad_p, grad_f, gws, gqkv, gnorm, fold_s, gfm, gup, gdown, gout = rest[-15:]
    tile = pl.program_id(0)

    @pl.when(tile == 0)
    def _():
        for ref in (gfm, gws, gqkv, gup, gdown, gout, gnorm):
            ref[...] = jnp.zeros_like(ref)
        move_present(scal, tiles, sums1_hbm, sums, sem)
        move_present(scal, tiles, grads1_hbm, grads, sem)
        attend_back_all(scal, tiles, sums, recv_ref, grads, grad_recv_ref, wqb_ref[...], both, dcount, gqkv)
        clear_present(scal, tiles, grads)

    grad = attend_back_tile(scal, tile, both, dcount, de1_ref, f_ref, m_ref, p1_ref, u_ref, vh_ref, rs_ref,
                            d21_ref, wfm_ref[...], wsb_ref[...], norm1_ref[...], grad_p, grad_f, gfm, gws, gnorm)
    mlp_back_tile(scal, tile, grad, lambda part: gp_ref[part].astype(f32), lambda part: z_ref[part],
                  vh2_ref[...].astype(f32), rs2_ref[:1], u2_ref[...], e_ref[...], p0_ref[...],
                  wout_ref[...], wup_ref, wdown_ref, norm0_ref[...], d2_ref, de_ref, grads,
                  gup, gdown, gout, gnorm)

    @pl.when(tile == tiles - 1)
    def _():
        write_edges(scal, tiles, grads, edge_ref)
        move_present(scal, tiles, grads, grads_hbm, sem)
        small_rows(0, gws, gqkv, fold_s, small_ref)
        norm_rows(gnorm, (0, 1), small_ref, NORM_ROW)
        small_ref[NORM_ROW + 4 :] = gn1b_ref[...]
        norm_rows(gnorm, (2, 3), gn0_ref, 0)
        if packed:
            for head in range(n_head):
                front = pack_front(gfm, head).astype(b16)
                store_pieces(
                    grad_outs[0], head, 0, jnp.concatenate([front[: D // 2], front[D // 2 :]], axis=1)
                )
            pack_rest(gout, gup, gdown, grad_outs[0], D // 2, n_head)
        else:
            for ref, total in zip(grad_outs, (gfm, gup, gdown, gout)):
                ref[...] = total[...].astype(b16)


def fifth_kernel(n_head, packed, tiles, scal, sums0_hbm, recv_ref, grads0_hbm, grad_recv_ref, de_ref, f_ref, m_ref, p_ref, u_ref, vh_ref, rs_ref, d2_ref,
                 wfm_ref, wsb_ref, wqb_ref, norm_ref, gn0b_ref, small1_ref,
                 gin_ref, small_ref, front_ref,
                 sums, grads, sem, both, dcount, grad_p, grad_f, gws, gqkv, gnorm, fold_s, gfm):
    tile = pl.program_id(0)

    @pl.when(tile == 0)
    def _():
        for ref in (gfm, gws, gqkv, gnorm):
            ref[...] = jnp.zeros_like(ref)
        move_present(scal, tiles, sums0_hbm, sums, sem)
        move_present(scal, tiles, grads0_hbm, grads, sem)
        attend_back_all(scal, tiles, sums, recv_ref, grads, grad_recv_ref, wqb_ref[...], both, dcount, gqkv)

    grad = attend_back_tile(scal, tile, both, dcount, de_ref, f_ref, m_ref, p_ref, u_ref, vh_ref, rs_ref,
                            d2_ref, wfm_ref[...], wsb_ref[...], norm_ref[...], grad_p, grad_f, gfm, gws, gnorm)
    gin_ref[...] = grad.T

    @pl.when(tile == tiles - 1)
    def _():
        small_rows(0, gws, gqkv, fold_s, small_ref)
        norm_rows(gnorm, (0, 1), small_ref, NORM_ROW)
        small_ref[NORM_ROW + 4 : LAYER_ROWS] = gn0b_ref[...]
        small_ref[LAYER_ROWS:] = small1_ref[...]
        if packed:
            for head in range(n_head):
                front_ref[head] = pack_front(gfm, head).astype(b16)
        else:
            front_ref[...] = gfm[...].astype(b16)


def sum_parts(own, got):
    total = own.astype(f32)
    for index in range(got.shape[0]):
        total = total + got[index].astype(f32)
    return total


def total_kernel(sizes, gb_ref, gc_ref, gs_ref, tb_ref, tc_ref, ts_ref,
                 got_b, got_c, got_s, mid_c, mid_s, got_c2, got_s2, head_sem, pts_sem):
    n_pts, n_head = sizes
    pts, head = lax.axis_index("pts"), lax.axis_index("head")
    c_rows = D // n_pts
    s_rows = gs_ref.shape[0] // n_head

    def part(index, rows):
        return pl.ds(pl.multiple_of(index * rows, rows), rows)

    def over(size, which, own, to, sem, source, target):
        copies = []
        for step in range(1, size):
            peer = lax.rem(own + step, size)
            copies.append(
                pltpu.make_async_remote_copy(
                    src_ref=source(peer),
                    dst_ref=target(step - 1),
                    send_sem=sem.at[0, which, step - 1],
                    recv_sem=sem.at[1, which, step - 1],
                    device_id=to(peer),
                    device_id_type=MESH,
                )
            )
        for copy in copies:
            copy.start()
        return copies

    def over_head(which, source, target):
        return over(n_head, which, head, lambda peer: (pts, peer), head_sem, source, target)

    def over_pts(which, source, target):
        return over(n_pts, which, pts, lambda peer: (peer, head), pts_sem, source, target)

    def finish(copies):
        for copy in copies:
            copy.wait()

    barrier = pltpu.get_barrier_semaphore()
    for step in range(1, n_head):
        pl.semaphore_signal(
            barrier, inc=1, device_id=(pts, lax.rem(head + step, n_head)), device_id_type=MESH
        )
    for step in range(1, n_pts):
        pl.semaphore_signal(
            barrier, inc=1, device_id=(lax.rem(pts + step, n_pts), head), device_id_type=MESH
        )
    pl.semaphore_wait(barrier, n_head - 1 + n_pts - 1)

    first_c = over_head(0, lambda peer: gc_ref.at[peer], lambda slot: got_c.at[slot])
    first_s = over_head(1, lambda peer: gs_ref.at[part(peer, s_rows)], lambda slot: got_s.at[slot])
    first_b = over_pts(0, lambda peer: gb_ref.at[peer], lambda slot: got_b.at[slot])
    finish(first_c)
    mid_c[...] = sum_parts(gc_ref[head], got_c).astype(b16)
    next_c = over_pts(1, lambda peer: mid_c.at[part(peer, c_rows)], lambda slot: got_c2.at[slot])
    finish(first_s)
    mid_s[...] = sum_parts(gs_ref[part(head, s_rows)], got_s)
    next_s = over_pts(2, lambda peer: mid_s, lambda slot: got_s2.at[slot])
    finish(next_c)
    mine_c = part(pts, c_rows)
    tc_ref[mine_c] = sum_parts(mid_c[mine_c], got_c2).astype(b16)
    last_c = over_pts(3, lambda peer: tc_ref.at[mine_c], lambda slot: tc_ref.at[mine_c])
    finish(next_s)
    mine_s = part(head, s_rows)
    ts_ref[mine_s] = sum_parts(mid_s[...], got_s2)
    last_s = over_head(2, lambda peer: ts_ref.at[mine_s], lambda slot: ts_ref.at[mine_s])
    finish(first_b)
    tb_ref[pts] = sum_parts(gb_ref[pts], got_b).astype(b16)
    last_b = over_pts(4, lambda peer: tb_ref.at[pts], lambda slot: tb_ref.at[pts])
    finish(last_c)
    finish(last_s)
    finish(last_b)


def total_gradients(sizes, gb, gc, gs):
    n_pts, n_head = sizes
    vmem = pl.BlockSpec(memory_space=pltpu.VMEM)
    dma = pltpu.SemaphoreType.DMA
    c_rows, s_rows = D // n_pts, gs.shape[0] // n_head
    return pl.pallas_call(
        functools.partial(total_kernel, sizes),
        out_shape=(
            jax.ShapeDtypeStruct(gb.shape, b16),
            jax.ShapeDtypeStruct(gc.shape[1:], b16),
            jax.ShapeDtypeStruct(gs.shape, f32),
        ),
        in_specs=[vmem] * 3,
        out_specs=[vmem] * 3,
        scratch_shapes=[
            pltpu.VMEM((n_pts - 1,) + gb.shape[1:], b16),
            pltpu.VMEM((n_head - 1,) + gc.shape[1:], b16),
            pltpu.VMEM((n_head - 1, s_rows, 128), f32),
            pltpu.VMEM(gc.shape[1:], b16),
            pltpu.VMEM((s_rows, 128), f32),
            pltpu.VMEM((n_pts - 1, c_rows, 128), b16),
            pltpu.VMEM((n_pts - 1, s_rows, 128), f32),
            dma((2, 3, n_head - 1)),
            dma((2, 5, n_pts - 1)),
        ],
        compiler_params=pltpu.CompilerParams(
            collective_id=3, has_side_effects=True, vmem_limit_bytes=VMEM_BYTES
        ),
        name="total_gradients",
    )(gb, gc, gs)


def update_kernel(ta_ref, tb_ref, tc_ref, ts_ref, row_ref, sel_ref, m_ref, v_ref, w_ref, sm_ref, sv_ref, sw_ref,
                  nm_ref, nv_ref, nw_ref, fresh_ref, om_ref, ov_ref, ow_ref, wide, tall, front, flat):
    lane = iota((8, 128), 1)

    def place_front(base):
        for pair in range(16):
            first = front[pl.ds(2 * pair, 8, stride=32), :]
            second = front[pl.ds(2 * pair + 1, 8, stride=32), :]
            columns = slice(128 * pair, 128 * pair + 128)
            wide[base : base + 8, columns] = jnp.where(lane < 64, first, pltpu.roll(second, 64, 1))
            wide[base + 8 : base + 16, columns] = jnp.where(lane < 64, pltpu.roll(first, 64, 1), second)

    def place_rest(base):
        for part in range(8):
            for half in range(2):
                wide[base : base + 72, 256 * part + 128 * half : 256 * part + 128 * half + 128] = tall[
                    half, pl.ds(part, 72, stride=8), :
                ]

    def fill(value, base):
        size = value.shape[1]
        row = base
        while row < size * (value.shape[0] // 2):
            chunk, offset = divmod(row, size)
            for half in range(2):
                tall[half, row - base : row - base + size - offset] = value[
                    2 * chunk + half, offset:
                ].astype(f32)
            row += size - offset

    front[...] = tc_ref[...].astype(f32)
    place_front(0)
    fill(tb_ref, D // 2)
    place_rest(16)
    front[: D // 2] = tb_ref[0, : D // 2].astype(f32)
    front[D // 2 :] = tb_ref[1, : D // 2].astype(f32)
    place_front(88)
    fill(ta_ref, 0)
    place_rest(104)

    cap, blocks = m_ref.shape[0], wide.shape[0]
    mine = (iota((cap, blocks), 0) == row_ref[:1]).astype(f32)
    filled = jnp.sum(mine, axis=1, keepdims=True) > 0.5
    mine = mine.astype(b16)
    step = 512
    for start in range(0, BLOCK, step):
        part = slice(start, start + step)
        grad = wide[:, part]
        own = nn(mine, grad.astype(b16))
        old = (m_ref[:, part], v_ref[:, part], w_ref[:, part])
        new = adam_update(old[0], own, old[1], old[2], rate_large)
        for ref, before, after in zip((nm_ref, nv_ref, nw_ref), old, new):
            ref[:, part] = jnp.where(filled, after, before)
        picked = [
            sel_ref[:, which * BLOCK + start : which * BLOCK + start + step].astype(f32)
            for which in range(3)
        ]
        fresh_ref[:, part] = adam_update(picked[0], grad, picked[1], picked[2], rate_large)[0].astype(b16)
    for layer in range(2):
        for row in range(LAYER_ROWS):
            flat[layer : layer + 1, 128 * row : 128 * row + 128] = ts_ref[
                layer * LAYER_ROWS + row : layer * LAYER_ROWS + row + 1, :
            ]
    new = adam_update(sm_ref[...], flat[:2], sv_ref[...], sw_ref[...], rate_small)
    for ref, value in zip((om_ref, ov_ref, ow_ref), new):
        ref[...] = value


def update(ta, tb, tc, ts, row, sel, tables, smalls):
    vmem = pl.BlockSpec(memory_space=pltpu.VMEM)
    blocks = sel.shape[0]
    operands = (ta, tb, tc, ts, row, sel, *tables, *smalls)
    outs = [jax.ShapeDtypeStruct(table.shape, f32) for table in tables]
    outs.append(jax.ShapeDtypeStruct((blocks, BLOCK), b16))
    outs += [jax.ShapeDtypeStruct(small.shape, f32) for small in smalls]
    return pl.pallas_call(
        update_kernel,
        out_shape=outs,
        in_specs=[vmem] * len(operands),
        out_specs=[vmem] * len(outs),
        scratch_shapes=[
            pltpu.VMEM((blocks, BLOCK), f32),
            pltpu.VMEM((2, ta.shape[0] * ta.shape[1] // 2, 128), f32),
            pltpu.VMEM((D, 128), f32),
            pltpu.VMEM((8, SMALL), f32),
        ],
        compiler_params=pltpu.CompilerParams(vmem_limit_bytes=VMEM_BYTES),
        name="update",
    )(*operands)


class Args:
    def __init__(self, rows, width):
        self.rows, self.width = rows, width
        self.operands, self.in_specs, self.outs, self.out_specs = [], [], [], []

    def cols(self, *arrays):
        for array in arrays:
            self.operands.append(array)
            self.in_specs.append(
                pl.BlockSpec((array.shape[0], self.width), lambda tile, scal: (0, tile))
            )

    def points(self, *arrays):
        for array in arrays:
            self.operands.append(array)
            self.in_specs.append(
                pl.BlockSpec((self.width, array.shape[1]), lambda tile, scal: (tile, 0))
            )

    def whole(self, *arrays):
        for array in arrays:
            rank = array.ndim
            self.operands.append(array)
            self.in_specs.append(
                pl.BlockSpec(array.shape, lambda tile, scal, rank=rank: (0,) * rank)
            )

    def layer(self, index, *arrays):
        for array in arrays:
            self.operands.append(array)
            self.in_specs.append(
                pl.BlockSpec((None,) + array.shape[1:], lambda tile, scal: (index, 0, 0))
            )

    def rows_of(self, array, start, size):
        self.operands.append(array)
        self.in_specs.append(
            pl.BlockSpec((size, array.shape[1]), lambda tile, scal: (start // size, 0))
        )

    def far(self, *arrays):
        for array in arrays:
            self.operands.append(array)
            self.in_specs.append(pl.BlockSpec(memory_space=pl.ANY))

    def out_far(self, *pairs):
        for shape, dtype in pairs:
            self.outs.append(jax.ShapeDtypeStruct(shape, dtype))
            self.out_specs.append(pl.BlockSpec(memory_space=pl.ANY))

    def out_cols(self, *pairs):
        for height, dtype in pairs:
            self.outs.append(jax.ShapeDtypeStruct((height, self.rows), dtype))
            self.out_specs.append(
                pl.BlockSpec((height, self.width), lambda tile, scal: (0, tile))
            )

    def out_points(self, *dtypes):
        for dtype in dtypes:
            self.outs.append(jax.ShapeDtypeStruct((self.rows, D), dtype))
            self.out_specs.append(pl.BlockSpec((self.width, D), lambda tile, scal: (tile, 0)))

    def out_whole(self, *pairs):
        for shape, dtype in pairs:
            rank = len(shape)
            self.outs.append(jax.ShapeDtypeStruct(shape, dtype))
            self.out_specs.append(
                pl.BlockSpec(shape, lambda tile, scal, rank=rank: (0,) * rank)
            )

    def call(self, body, scal, scratch, name):
        tiles = self.rows // self.width
        return pl.pallas_call(
            functools.partial(body, tiles),
            grid_spec=pltpu.PrefetchScalarGridSpec(
                num_scalar_prefetch=1,
                grid=(tiles,),
                in_specs=self.in_specs,
                out_specs=self.out_specs,
                scratch_shapes=scratch,
            ),
            out_shape=self.outs,
            compiler_params=pltpu.CompilerParams(
                dimension_semantics=("arbitrary",), vmem_limit_bytes=VMEM_BYTES
            ),
            name=name,
        )(scal, *self.operands)


def adam_update(master, grad, first, second, rate):
    new_first = beta_one * first + (1.0 - beta_one) * grad
    new_second = beta_two * second + (1.0 - beta_two) * grad * grad
    fix_one = 1.0 - beta_one**STEP
    fix_two = 1.0 - beta_two**STEP
    direction = new_first / fix_one / (jnp.sqrt(new_second / fix_two) + adam_eps)
    return (master - rate * (direction + decay_rate * master), new_first, new_second)


def flat_blocks(n_head, gfm, gout, gup, gdown):
    def columns(grad):
        width = grad.shape[1] // n_head
        return grad.reshape(D, n_head, width).transpose(1, 0, 2).reshape(n_head, -1)

    return jnp.concatenate(
        [
            columns(gfm[:, :D]),
            columns(gfm[:, D:]),
            gout.reshape(n_head, -1),
            columns(gup),
            columns(gdown),
        ],
        axis=1,
    ).reshape(n_head, -1, BLOCK)


def on_device(
    sizes,
    tokens,
    cotangent,
    segment_ids,
    owner,
    w_fx,
    w_mid,
    w_out,
    w_up,
    w_down,
    small_master,
    small_first,
    small_second,
    master_table,
    first_table,
    second_table,
):
    n_pts, n_head = sizes
    rows = tokens.shape[0]
    width = min(512, rows)
    tiles = rows // width
    most = rows * n_pts * n_head // LARGEST
    window = (rows - 1 + most - 1) // rows
    layers = w_fx.shape[0]
    packed = (n_pts, n_head) == (8, 4)

    ids = segment_ids.reshape(-1, 128)
    w_fx = w_fx.transpose(0, 2, 1)
    w_mid = w_mid.transpose(0, 2, 1)
    tables = (master_table, first_table, second_table)
    smalls = (small_master, small_first, small_second)
    gathered, wsb, norms, scal, halves = opening(
        n_head, tiles, ids, w_fx, w_mid, small_master, tables
    )
    wfm0 = gathered.reshape(2 * D, D)

    cap = master_table.shape[0]
    if packed:
        collected = lax.all_gather(halves, "pts", axis=0, tiled=True)

    sums_shape = (MESHES, SLICES, D + 128)
    grad_sums_shape = (MESHES, SLICES, D)
    front_cols = ((D, b16), (8, f32), (D, b16), (D, b16), (D, b16), (HS, b16))
    wide_scratch = [pltpu.VMEM((MESHES, HS, D), b16), pltpu.VMEM((D, width), f32)]

    args = Args(rows, width)
    args.points(tokens)
    args.whole(wfm0)
    args.layer(0, wsb, norms)
    args.out_cols((D, b16), *front_cols)
    args.out_far((sums_shape, f32))
    args.out_whole(((2, EDGE, D), b16))
    sums_scratch = [pltpu.VMEM(sums_shape, f32), pltpu.SemaphoreType.DMA((MESHES,))]
    xt0, vh0, rs0, u0, f0, m0, p0, sums0, edge = args.call(first_kernel, scal, sums_scratch, "first")
    recv0, later, wqb0 = swap_edges_weights(
        sizes, window, 0, ((0, 1), (1, 1), (2, 0)), edge, w_fx, w_mid, w_out, small_master, 1
    )
    later = later.reshape(3 * D, D)

    args = Args(rows, width)
    args.cols(xt0, p0)
    args.far(sums0)
    args.whole(recv0)
    args.rows_of(later, 2 * D, D)
    args.layer(0, w_up, w_down)
    args.whole(wqb0)
    args.layer(0, norms)
    args.rows_of(later, 0, 2 * D)
    args.layer(1, wsb, norms)
    args.out_cols((D, b16), (D, b16), (8, f32), (D, b16), (FF, b16), (FF, b16))
    args.out_cols((D, f32), *front_cols)
    args.out_far((sums_shape, f32))
    args.out_whole(((2, EDGE, D), b16))
    (e0, vh20, rs20, u20, gp0, z0, x1, vh1, rs1, u1, f1, m1, p1, sums1, edge) = args.call(
        second_kernel, scal, wide_scratch + sums_scratch, "second"
    )
    recv1, wout1, wqb1 = swap_edges_weights(
        sizes, window, 1, ((2, 1),), edge, w_fx, w_mid, w_out, small_master, 5
    )
    wout1 = wout1.reshape(D, D)

    grad_scratch = [pltpu.VMEM((D, FF), f32), pltpu.VMEM((D, FF), f32), pltpu.VMEM((D, D), f32)]
    rest_rows = D // n_head + 2 * D

    args = Args(rows, width)
    args.cols(x1, p1)
    args.far(sums1)
    args.whole(recv1)
    args.points(cotangent)
    args.whole(wout1)
    args.layer(1, w_up, w_down)
    args.whole(wqb1)
    args.layer(1, norms)
    args.out_points(b16)
    args.out_cols((D, f32), (D, b16))
    args.out_far((grad_sums_shape, f32))
    args.out_whole(((2, EDGE, D), b16), ((4, 128), f32))
    if packed:
        args.out_whole(((n_head, n_pts, 2 * rest_rows // n_pts, 128), b16))
    else:
        args.out_whole(((D, FF), b16), ((D, FF), b16), ((D, D), b16))
    (layer_out, d21, de1, grads1, edge, gn1b, *grads_a) = args.call(
        functools.partial(third_kernel, n_head, packed),
        scal,
        sums_scratch
        + [pltpu.VMEM(grad_sums_shape, f32)]
        + wide_scratch
        + [pltpu.VMEM((4, D, 128), f32), pltpu.VMEM((FF, width), f32), pltpu.VMEM((FF, width), b16)]
        + grad_scratch,
        "third",
    )
    if packed:
        grad_recv1, chosen, row = swap_edges_pick(
            sizes, window, cap, edge, owner.reshape(1, -1), collected, 2
        )
        part_a = lax.psum_scatter(grads_a[0], "head", scatter_dimension=0, tiled=True)[0]
    else:
        grad_recv1 = swap_edges(sizes, window, edge, 4)

    back_scratch = [
        pltpu.VMEM(sums_shape, f32),
        pltpu.VMEM(grad_sums_shape, f32),
        pltpu.SemaphoreType.DMA((MESHES,)),
        pltpu.VMEM((MESHES, HS, 2 * D), b16),
        pltpu.VMEM((MESHES, HS, 128), f32),
        pltpu.VMEM((HS, width), f32),
        pltpu.VMEM((D, width), f32),
        pltpu.VMEM((D, HS), f32),
        pltpu.VMEM((D, 3 * D), f32),
        pltpu.VMEM((4, D, 128), f32),
        pltpu.VMEM((DH, 128), f32),
        pltpu.VMEM((D, 2 * D), f32),
    ]

    args = Args(rows, width)
    args.far(sums1)
    args.whole(recv1)
    args.far(grads1)
    args.whole(grad_recv1)
    args.cols(de1, f1, m1, p1, u1, vh1, rs1, d21)
    args.rows_of(later, 0, 2 * D)
    args.layer(1, wsb)
    args.whole(wqb1)
    args.layer(1, norms)
    args.cols(gp0, z0, vh20, rs20, u20, e0, p0)
    args.rows_of(later, 2 * D, D)
    args.layer(0, w_up, w_down, norms)
    args.whole(gn1b)
    args.out_cols((D, f32), (D, b16))
    args.out_far((grad_sums_shape, f32))
    args.out_whole(((2, EDGE, D), b16), ((LAYER_ROWS, 128), f32), ((4, 128), f32))
    if packed:
        args.out_whole(((n_head, n_pts, (D + 2 * rest_rows) // n_pts, 128), b16))
    else:
        args.out_whole(((D, 2 * D), b16), ((D, FF), b16), ((D, FF), b16), ((D, D), b16))
    (d20, de0, grads0, edge, small1, gn0b, *grads_b) = args.call(
        functools.partial(fourth_kernel, n_head, packed), scal, back_scratch + grad_scratch, "fourth"
    )
    if packed:
        grad_recv0, total_a = swap_edges_sums(sizes, window, edge, part_a, 6)
        mine_b = lax.psum_scatter(grads_b[0], "head", scatter_dimension=0, tiled=True)[0]
    else:
        grad_recv0 = swap_edges(sizes, window, edge, 4)

    args = Args(rows, width)
    args.far(sums0)
    args.whole(recv0)
    args.far(grads0)
    args.whole(grad_recv0)
    args.cols(de0, f0, m0, p0, u0, vh0, rs0, d20)
    args.whole(wfm0)
    args.layer(0, wsb)
    args.whole(wqb0)
    args.layer(0, norms)
    args.whole(gn0b, small1)
    args.out_points(f32)
    args.out_whole(((2 * LAYER_ROWS, 128), f32))
    args.out_whole(((n_head, D, 128), b16) if packed else ((D, 2 * D), b16))
    input_grad, small, front = args.call(
        functools.partial(fifth_kernel, n_head, packed), scal, back_scratch, "fifth"
    )

    if packed:
        total_b, total_c, total_s = total_gradients(sizes, mine_b, front, small)
        outs = update(total_a, total_b, total_c, total_s, row, chosen, tables, smalls)
        return (layer_out, input_grad, *outs)

    gup1, gdown1, gout1 = grads_a
    gfm1, gup0, gdown0, gout0 = grads_b
    small_total = lax.psum(small, ("pts", "head")).reshape(layers, -1)
    totals = []
    for parts in ((front, gout0, gup0, gdown0), (gfm1, gout1, gup1, gdown1)):
        blocks = lax.psum_scatter(
            flat_blocks(n_head, *parts), "head", scatter_dimension=0, tiled=True
        )
        totals.append(lax.psum(blocks.reshape(-1, BLOCK), "pts"))
    total_grad = jnp.concatenate(totals, axis=0).astype(f32)
    my_index = lax.axis_index("pts")
    block_ids = jnp.arange(owner.shape[0])
    same_owner = (owner[:, None] == owner[None, :]) & (block_ids[None, :] < block_ids[:, None])
    table_row = owner * cap + jnp.sum(same_owner.astype(jnp.int32), axis=1)
    place_all = (jnp.arange(n_pts * cap)[:, None] == table_row[None, :]).astype(f32)
    mine_place = lax.dynamic_slice_in_dim(place_all, my_index * cap, cap, 0)
    own_grad = jnp.dot(mine_place, total_grad, precision=HIGH)
    filled = jnp.sum(mine_place, axis=1)[:, None] > 0.5
    updated = adam_update(master_table, own_grad, first_table, second_table, rate_large)
    new_tables = [jnp.where(filled, new, old) for new, old in zip(updated, tables)]
    collected = lax.all_gather(new_tables[0].astype(b16), "pts", axis=0, tiled=True)
    pick_back = (table_row[:, None] == jnp.arange(n_pts * cap)[None, :]).astype(b16)
    fresh = jnp.dot(pick_back, collected, preferred_element_type=f32).astype(b16)
    small_outs = adam_update(small_master, small_total, small_first, small_second, rate_small)
    return (layer_out, input_grad, *new_tables, fresh, *small_outs)


def solution(mesh):
    sizes = (mesh.shape["pts"], mesh.shape["head"])
    return jax.shard_map(
        functools.partial(on_device, sizes),
        mesh=mesh,
        in_specs=(
            P(("pts", "head"), None),
            P(("pts", "head"), None),
            P("pts"),
            P(),
            P(None, None, "head"),
            P(None, None, "head"),
            P(None, "head", None),
            P(),
            P(),
            P(),
            P(),
            P(),
            P("pts", "head"),
            P("pts", "head"),
            P("pts", "head"),
        ),
        out_specs=(
            P(("pts", "head"), None),
            P(("pts", "head"), None),
            P("pts", "head"),
            P("pts", "head"),
            P("pts", "head"),
            P(None, "head"),
            P(),
            P(),
            P(),
        ),
        check_vma=False,
    )
```

```python
import functools
import math

import jax
import jax.numpy as jnp
from jax import lax
from jax.experimental import pallas as pl
from jax.experimental.pallas import tpu as pltpu
from jax.sharding import PartitionSpec as P

D = 256
HEADS = 8
DH = 32
SLICES = 64
HS = HEADS * SLICES
FF = 1024
MESHES = 24
BLOCK = 2048
SMALL = 6144
STEP = 10
LARGEST = 12
EDGE = 80
VMEM_BYTES = 58 << 20

MESH = pl.DeviceIdType.MESH
HIGH = True
norm_eps = 1e-05
beta_one = 0.9
beta_two = 0.95
adam_eps = 1e-08
decay_rate = 0.1
rate_large = 0.1
rate_small = 0.75
f32 = jnp.float32
b16 = jnp.bfloat16


def dot(a, b, contract, precise):
    dims = (contract, ((), ()))
    if not precise:
        return lax.dot_general(a, b, dims, preferred_element_type=f32)
    a_high, b_high = a.astype(b16), b.astype(b16)
    a_low = (a - a_high.astype(f32)).astype(b16)
    b_low = (b - b_high.astype(f32)).astype(b16)
    return (
        lax.dot_general(a_high, b_low, dims, preferred_element_type=f32)
        + lax.dot_general(a_low, b_high, dims, preferred_element_type=f32)
        + lax.dot_general(a_high, b_high, dims, preferred_element_type=f32)
    )


def nn(a, b, precise=False):
    return dot(a, b, ((1,), (0,)), precise)


def nt(a, b, precise=False):
    return dot(a, b, ((1,), (1,)), precise)


def tn(a, b, precise=False):
    return dot(a, b, ((0,), (0,)), precise)


def iota(shape, axis):
    return lax.broadcasted_iota(jnp.int32, shape, axis)


def pick_diag(full, per_head):
    lane_head = iota((SLICES, full.shape[1]), 1) // per_head
    total = jnp.where(lane_head == 0, full[:SLICES], 0.0)
    for head in range(1, HEADS):
        total = total + jnp.where(
            lane_head == head, full[head * SLICES : (head + 1) * SLICES], 0.0
        )
    return total


def spread_diag(small):
    lane_head = iota((SLICES, D), 1) // DH
    return jnp.concatenate(
        [jnp.where(lane_head == head, small, jnp.zeros_like(small)) for head in range(HEADS)],
        axis=0,
    )


def repeat_rows(width):
    return (iota((D, width), 0) % width == iota((D, width), 1)).astype(f32)


def slice_repeat():
    return (iota((SLICES, HS), 1) % SLICES == iota((SLICES, HS), 0)).astype(f32)


def same_head(rows_per, cols_per, shape):
    return (iota(shape, 0) // rows_per) == (iota(shape, 1) // cols_per)


def start_gather(n_head, picks, send_sem, recv_sem):
    me = lax.axis_index("head")
    copies = []
    for index, ref in enumerate(picks):
        for step in range(1, n_head):
            copy = pltpu.make_async_remote_copy(
                src_ref=ref.at[:, me],
                dst_ref=ref.at[:, me],
                send_sem=send_sem.at[index, step - 1],
                recv_sem=recv_sem.at[index, step - 1],
                device_id={"head": lax.rem(me + step, n_head)},
                device_id_type=MESH,
            )
            copy.start()
            copies.append(copy)
    return copies


def unroll_slices(row_of, out):
    lane = iota((1, 128), 1)
    for pair in range(DH // 2):
        row = row_of(pair)
        out[2 * pair : 2 * pair + 1] = jnp.where(lane < SLICES, row, 0.0)
        out[2 * pair + 1 : 2 * pair + 2] = jnp.where(
            lane < SLICES, pltpu.roll(row, 128 - SLICES, 1), 0.0
        )


def opening_kernel(n_head, tiles, ids_ref, wfx_ref, wmid_ref, sm_ref, m_ref, v_ref, w_ref,
                   out_ref, wsb_ref, norm_ref, scal_ref, tables_ref, send_sem, recv_sem, slices_s, norm_s):
    me = lax.axis_index("head")
    barrier = pltpu.get_barrier_semaphore()
    for step in range(1, n_head):
        pl.semaphore_signal(
            barrier, inc=1, device_id={"head": lax.rem(me + step, n_head)}, device_id_type=MESH
        )
    out_ref[0, me] = wfx_ref[0]
    out_ref[1, me] = wmid_ref[0]
    pl.semaphore_wait(barrier, n_head - 1)
    copies = start_gather(n_head, [out_ref], send_sem, recv_sem)
    layers = sm_ref.shape[0]
    cap, deep = m_ref.shape[0], tables_ref.shape[0]
    for which, ref in enumerate((m_ref, v_ref, w_ref)):
        value = ref[...]
        if deep > cap:
            value = jnp.concatenate([value, jnp.zeros((deep - cap, BLOCK), f32)], axis=0)
        tables_ref[:, which * BLOCK : (which + 1) * BLOCK] = value.astype(b16)
    right = (iota((128, HS), 1) % SLICES == iota((128, HS), 0)).astype(b16)
    for layer in range(layers):
        unroll_slices(lambda pair: sm_ref[layer : layer + 1, 128 * pair : 128 * pair + 128], slices_s)
        wide = nn(slices_s[...].astype(b16), right)
        tiled = jnp.concatenate([wide] * HEADS, axis=0)
        wsb_ref[layer] = jnp.where(same_head(DH, SLICES, (D, HS)), tiled, 0.0).astype(b16)
        norm_s[...] = jnp.zeros_like(norm_s)
        for row in range(4):
            start = SMALL - 4 * D + row * D
            norm_s[row : row + 1] = sm_ref[layer : layer + 1, start : start + D]
        norm_ref[layer] = norm_s[...].T
    rows = ids_ref.shape[0] // n_head
    ids = ids_ref[pl.ds(pl.multiple_of(me * rows, rows), rows), :]
    for mesh in range(MESHES + 1):
        scal_ref[mesh] = jnp.sum((ids < mesh).astype(jnp.int32))
    deep = rows // tiles
    for tile in range(tiles):
        part = ids[tile * deep : (tile + 1) * deep]
        scal_ref[MESHES + 1 + 2 * tile] = jnp.min(part)
        scal_ref[MESHES + 2 + 2 * tile] = jnp.max(part)
    for copy in copies:
        copy.wait()


def opening(n_head, tiles, ids, w_fx, w_mid, small, tables):
    layers, part, _ = w_fx.shape
    deep = -(-tables[0].shape[0] // 16) * 16
    vmem = pl.BlockSpec(memory_space=pltpu.VMEM)
    return pl.pallas_call(
        functools.partial(opening_kernel, n_head, tiles),
        out_shape=(
            jax.ShapeDtypeStruct((2, n_head, part, D), b16),
            jax.ShapeDtypeStruct((layers, D, HS), b16),
            jax.ShapeDtypeStruct((layers, D, 128), f32),
            jax.ShapeDtypeStruct((MESHES + 1 + 2 * tiles,), jnp.int32),
            jax.ShapeDtypeStruct((deep, 3 * BLOCK), b16),
        ),
        in_specs=[vmem] * 7,
        out_specs=[vmem] * 3 + [pl.BlockSpec(memory_space=pltpu.SMEM), vmem],
        scratch_shapes=[
            pltpu.SemaphoreType.DMA((1, n_head - 1)),
            pltpu.SemaphoreType.DMA((1, n_head - 1)),
            pltpu.VMEM((DH, 128), f32),
            pltpu.VMEM((128, D), f32),
        ],
        compiler_params=pltpu.CompilerParams(
            collective_id=0, has_side_effects=True, vmem_limit_bytes=VMEM_BYTES
        ),
        name="opening",
    )(ids, w_fx, w_mid, small, *tables)


def place_of(sizes, shift):
    n_pts, n_head = sizes
    total = n_pts * n_head
    me = lax.axis_index("pts") * n_head + lax.axis_index("head")
    other = lax.rem(me + (shift + total), total)
    return (other // n_head, lax.rem(other, n_head))


def greet(sizes, window):
    barrier = pltpu.get_barrier_semaphore()
    for step in range(1, window + 1):
        for shift in (step, -step):
            pl.semaphore_signal(barrier, inc=1, device_id=place_of(sizes, shift), device_id_type=MESH)
    return barrier


def start_edges(sizes, window, edge_ref, out_ref, send_sem, recv_sem):
    copies = []
    for step in range(1, window + 1):
        for side, shift in ((1, step), (0, -step)):
            slot = step - 1 if side == 1 else window + step - 1
            copy = pltpu.make_async_remote_copy(
                src_ref=edge_ref.at[side],
                dst_ref=out_ref.at[slot],
                send_sem=send_sem.at[slot],
                recv_sem=recv_sem.at[slot],
                device_id=place_of(sizes, shift),
                device_id_type=MESH,
            )
            copy.start()
            copies.append(copy)
    return copies


def edge_kernel(sizes, window, edge_ref, out_ref, send_sem, recv_sem):
    barrier = greet(sizes, window)
    pl.semaphore_wait(barrier, 2 * window)
    for copy in start_edges(sizes, window, edge_ref, out_ref, send_sem, recv_sem):
        copy.wait()


def edge_weights_kernel(sizes, window, layer, pieces, edge_ref, wfx_ref, wmid_ref, wout_ref, sm_ref,
                        out_ref, w_ref, wqb_ref,
                        send_sem, recv_sem, wsend_sem, wrecv_sem, square_s):
    n_head = sizes[1]
    me = lax.axis_index("head")
    barrier = greet(sizes, window)
    for step in range(1, n_head):
        pl.semaphore_signal(
            barrier, inc=1, device_id={"head": lax.rem(me + step, n_head)}, device_id_type=MESH
        )
    refs = (wfx_ref, wmid_ref, wout_ref)
    for index, (kind, which) in enumerate(pieces):
        w_ref[index, me] = refs[kind][which]
    pl.semaphore_wait(barrier, 2 * window + n_head - 1)
    copies = start_edges(sizes, window, edge_ref, out_ref, send_sem, recv_sem)
    copies += start_gather(n_head, [w_ref], wsend_sem, wrecv_sem)
    lane = iota((1, 128), 1)
    for part in range(3):
        start = DH * SLICES + part * DH * DH
        for group in range(DH // 4):
            row = sm_ref[layer : layer + 1, start + 128 * group : start + 128 * group + 128]
            for inner in range(4):
                moved = row if inner == 0 else pltpu.roll(row, 128 - DH * inner, 1)
                square_s[4 * group + inner : 4 * group + inner + 1] = jnp.where(
                    lane < DH, moved, 0.0
                )
        square = square_s[...]
        for turn in range(1, 128 // DH):
            square = square + pltpu.roll(square_s[...], DH * turn, 1)
        square = jnp.concatenate([square] * (D // 128), axis=1)
        square = jnp.concatenate([square] * HEADS, axis=0)
        wqb_ref[:, part * D : (part + 1) * D] = jnp.where(
            same_head(DH, DH, (D, D)), square, 0.0
        )
    for copy in copies:
        copy.wait()


def edge_pick_kernel(sizes, window, cap, edge_ref, owner_ref, tables_ref,
                     out_ref, chosen_ref, row_ref, send_sem, recv_sem, tables_s, local_sem):
    barrier = greet(sizes, window)
    load = pltpu.make_async_copy(tables_ref, tables_s, local_sem)
    load.start()
    pl.semaphore_wait(barrier, 2 * window)
    copies = start_edges(sizes, window, edge_ref, out_ref, send_sem, recv_sem)
    blocks = owner_ref.shape[1]
    deep = tables_s.shape[0] // sizes[0]
    across = jnp.broadcast_to(owner_ref[...].astype(f32), (blocks, blocks))
    down = across.T
    low, high = iota((blocks, blocks), 0), iota((blocks, blocks), 1)
    same = across == down
    slot_down = jnp.sum(jnp.where(same & (high < low), 1.0, 0.0), axis=1, keepdims=True)
    slot_across = jnp.sum(jnp.where(same & (low < high), 1.0, 0.0), axis=0, keepdims=True)
    mine = owner_ref[...] == lax.axis_index("pts")
    row_ref[...] = jnp.broadcast_to(
        jnp.where(mine, slot_across.astype(jnp.int32), -1), row_ref.shape
    )
    target = (down[:, :1] * deep + slot_down).astype(jnp.int32)
    pick = (iota((blocks, tables_s.shape[0]), 1) == target).astype(b16)
    load.wait()
    step = 1024

    def choose(part, carry):
        lanes = pl.ds(pl.multiple_of(part * step, step), step)
        chosen_ref[:, lanes] = nn(pick, tables_s[:, lanes]).astype(b16)
        return carry

    lax.fori_loop(0, tables_s.shape[1] // step, choose, 0)
    for copy in copies:
        copy.wait()


def swap_edges_pick(sizes, window, cap, edge, owner, tables, collective_id):
    _, rows, width = edge.shape
    blocks = owner.shape[1]
    vmem = pl.BlockSpec(memory_space=pltpu.VMEM)
    return pl.pallas_call(
        functools.partial(edge_pick_kernel, sizes, window, cap),
        out_shape=(
            jax.ShapeDtypeStruct((2 * window, rows, width), b16),
            jax.ShapeDtypeStruct((blocks, tables.shape[1]), b16),
            jax.ShapeDtypeStruct((8, blocks), jnp.int32),
        ),
        in_specs=[vmem, vmem, pl.BlockSpec(memory_space=pl.ANY)],
        out_specs=[vmem] * 3,
        scratch_shapes=[
            pltpu.SemaphoreType.DMA((2 * window,)),
            pltpu.SemaphoreType.DMA((2 * window,)),
            pltpu.VMEM(tables.shape, b16),
            pltpu.SemaphoreType.DMA,
        ],
        compiler_params=pltpu.CompilerParams(
            collective_id=collective_id, has_side_effects=True, vmem_limit_bytes=VMEM_BYTES
        ),
        name="swap_edges_pick",
    )(edge, owner, tables)


def edge_call(window, collective_id, rows, width, body, extra, outs, scratch, name):
    vmem = pl.BlockSpec(memory_space=pltpu.VMEM)
    outs = [jax.ShapeDtypeStruct((2 * window, rows, width), b16)] + outs
    return pl.pallas_call(
        body,
        out_shape=outs,
        in_specs=[vmem] * (1 + extra),
        out_specs=[vmem] * len(outs),
        scratch_shapes=[
            pltpu.SemaphoreType.DMA((2 * window,)),
            pltpu.SemaphoreType.DMA((2 * window,)),
        ]
        + scratch,
        compiler_params=pltpu.CompilerParams(
            collective_id=collective_id, has_side_effects=True, vmem_limit_bytes=VMEM_BYTES
        ),
        name=name,
    )


def swap_edges(sizes, window, edge, collective_id):
    _, rows, width = edge.shape
    return edge_call(
        window, collective_id, rows, width,
        functools.partial(edge_kernel, sizes, window), 0, [], [], "swap_edges",
    )(edge)[0]


def swap_edges_weights(sizes, window, layer, pieces, edge, w_fx, w_mid, w_out, small, collective_id):
    _, rows, width = edge.shape
    n_head = sizes[1]
    part = w_fx.shape[1]
    return edge_call(
        window, collective_id, rows, width,
        functools.partial(edge_weights_kernel, sizes, window, layer, pieces), 4,
        [
            jax.ShapeDtypeStruct((len(pieces), n_head, part, D), b16),
            jax.ShapeDtypeStruct((D, 3 * D), f32),
        ],
        [
            pltpu.SemaphoreType.DMA((1, n_head - 1)),
            pltpu.SemaphoreType.DMA((1, n_head - 1)),
            pltpu.VMEM((DH, 128), f32),
        ],
        "swap_edges_weights",
    )(edge, w_fx, w_mid, w_out, small)


def pts_copies(n_pts, source, target, send_sem, recv_sem):
    pts, head = lax.axis_index("pts"), lax.axis_index("head")
    copies = []
    for step in range(1, n_pts):
        peer = lax.rem(pts + step, n_pts)
        copies.append(
            pltpu.make_async_remote_copy(
                src_ref=source(step, peer),
                dst_ref=target(step, peer),
                send_sem=send_sem.at[step - 1],
                recv_sem=recv_sem.at[step - 1],
                device_id=(peer, head),
                device_id_type=MESH,
            )
        )
    return copies


def edge_sums_kernel(sizes, window, edge_ref, ga_ref, out_ref, ta_ref,
                     send_sem, recv_sem, a_send, a_recv, a_send2, a_recv2, got_a):
    n_pts, n_head = sizes
    pts, head = lax.axis_index("pts"), lax.axis_index("head")
    barrier = greet(sizes, window)
    for step in range(1, n_pts):
        pl.semaphore_signal(
            barrier, inc=1, device_id=(lax.rem(pts + step, n_pts), head), device_id_type=MESH
        )
    pl.semaphore_wait(barrier, 2 * window + n_pts - 1)
    edges = start_edges(sizes, window, edge_ref, out_ref, send_sem, recv_sem)
    gather = pts_copies(
        n_pts,
        lambda step, peer: ga_ref.at[peer],
        lambda step, peer: got_a.at[step - 1],
        a_send,
        a_recv,
    )
    for copy in gather:
        copy.start()
    for copy in gather:
        copy.wait()
    total = ga_ref[pts].astype(f32)
    for index in range(n_pts - 1):
        total = total + got_a[index].astype(f32)
    ta_ref[pts] = total.astype(b16)
    share = pts_copies(
        n_pts,
        lambda step, peer: ta_ref.at[pts],
        lambda step, peer: ta_ref.at[pts],
        a_send2,
        a_recv2,
    )
    for copy in share:
        copy.start()
    for copy in edges:
        copy.wait()
    for copy in share:
        copy.wait()


def swap_edges_sums(sizes, window, edge, ga, collective_id):
    _, rows, width = edge.shape
    n_pts = sizes[0]
    dma = pltpu.SemaphoreType.DMA
    return edge_call(
        window, collective_id, rows, width,
        functools.partial(edge_sums_kernel, sizes, window), 1,
        [jax.ShapeDtypeStruct(ga.shape, b16)],
        [dma((n_pts - 1,))] * 4 + [pltpu.VMEM((n_pts - 1,) + ga.shape[1:], b16)],
        "swap_edges_sums",
    )(edge, ga)


def norm_stats(values):
    center = jnp.mean(values, axis=0, keepdims=True)
    spread = values - center
    scale = lax.rsqrt(jnp.mean(spread * spread, axis=0, keepdims=True) + norm_eps)
    return (spread * scale, scale)


def norm_back(grad_out, scaled, scale, gain):
    inner = grad_out * gain
    return scale * (
        inner
        - jnp.mean(inner, axis=0, keepdims=True)
        - scaled * jnp.mean(inner * scaled, axis=0, keepdims=True)
    )


def group_sum(values):
    return jnp.sum(values.reshape(HEADS, SLICES, values.shape[1]), axis=1, keepdims=True)


def fold_lanes(values):
    total = values[:, :128]
    for start in range(128, values.shape[1], 128):
        total = total + values[:, start : start + 128]
    return total


def tile_mask(scal, mesh, tile, width):
    spot = iota((1, width), 1) + tile * width
    return (spot >= scal[mesh]) & (spot < scal[mesh + 1])


def tile_range(scal, tiles, tile):
    base = MESHES + 1
    ratio = (scal.shape[0] - base) // 2 // tiles
    return (scal[base + 2 * ratio * tile], scal[base + 2 * ratio * (tile + 1) - 1])


def front_tile(scal, tiles, tile, x, wfm, wsb, norms, vh_ref, rs_ref, u_ref, f_ref, m_ref, p_ref, sums):
    width = x.shape[1]
    scaled, scale = norm_stats(x)
    vh_ref[...] = scaled.astype(b16)
    rs_ref[...] = jnp.broadcast_to(scale, (8, width))
    normed = (scaled * norms[:, 0:1] + norms[:, 1:2]).astype(b16)
    u_ref[...] = normed
    joint = nn(wfm, normed)
    feats = joint[:D].astype(b16)
    middle = joint[D:].astype(b16)
    f_ref[...] = feats
    m_ref[...] = middle
    logits = tn(wsb, middle).reshape(HEADS, SLICES, width)
    top = jnp.max(logits, axis=1, keepdims=True)
    expo = jnp.exp(logits - top)
    weights = expo / jnp.sum(expo, axis=1, keepdims=True)
    weights_r = weights.reshape(HS, width).astype(b16)
    p_ref[...] = weights_r
    low, high = tile_range(scal, tiles, tile)

    def add(mesh, carry):
        keep = tile_mask(scal, mesh, tile, width).astype(b16)
        wide = jnp.concatenate(
            [feats * keep, jnp.broadcast_to(keep, (128, width))], axis=0
        )
        full = nt(weights_r, wide)
        sums[mesh, :, :D] += pick_diag(full[:, :D], DH)
        sums[mesh, :, D:] += pick_diag(full[:, D:], 16)
        return carry

    lax.fori_loop(low, high + 1, add, 0)


def present(scal, tiles, body):
    def one(mesh, carry):
        body(mesh)
        return carry

    lax.fori_loop(tile_range(scal, tiles, 0)[0], tile_range(scal, tiles, tiles - 1)[1] + 1, one, 0)


def present_pairs(scal, tiles, body):
    first = tile_range(scal, tiles, 0)[0]
    last = tile_range(scal, tiles, tiles - 1)[1]

    def pair(index, carry):
        mesh = first + 2 * index
        body(mesh, jnp.minimum(mesh + 1, last))
        return carry

    lax.fori_loop(0, lax.shift_right_logical(last - first + 2, 1), pair, 0)


def move_present(scal, tiles, source, target, sem):
    present(scal, tiles, lambda mesh: pltpu.make_async_copy(source.at[mesh], target.at[mesh], sem.at[mesh]).start())
    present(scal, tiles, lambda mesh: pltpu.make_async_copy(source.at[mesh], target.at[mesh], sem.at[mesh]).wait())


def clear_present(scal, tiles, sums):
    def clear(mesh):
        sums[mesh] = jnp.zeros(sums.shape[1:], f32)

    present(scal, tiles, clear)


def write_edges(scal, tiles, sums, edge_ref):
    first = tile_range(scal, tiles, 0)[0]
    last = tile_range(scal, tiles, tiles - 1)[1]
    extra = EDGE - SLICES
    for side, mesh in ((0, first), (1, last)):
        edge_ref[side, :SLICES] = sums[mesh, :, :D].astype(b16)
        rows = jnp.zeros((extra, D), f32)
        if sums.shape[2] > D:
            counts = jnp.concatenate(
                [sums[mesh, :, D:], jnp.zeros((D - SLICES, 128), f32)], axis=0
            )
            pick = (iota((extra, 128), 1) == 16 * iota((extra, 128), 0)).astype(f32)
            rows = nt(pick, counts, HIGH)
        edge_ref[side, SLICES:] = jnp.where(
            iota((extra, D), 0) >= HEADS, mesh.astype(f32), rows
        ).astype(b16)


def add_edges(own, mesh, recv_ref):
    wanted = mesh.astype(f32)
    total = jnp.zeros((EDGE, D), f32)
    for slot in range(recv_ref.shape[0]):
        match = recv_ref[slot, SLICES + HEADS : SLICES + HEADS + 1].astype(f32) == wanted
        total = total + jnp.where(match, recv_ref[slot].astype(f32), 0.0)
    if own.shape[1] == D:
        return own + total[:SLICES]
    extra = EDGE - SLICES
    spread = (iota((extra, 128), 1) // 16 == iota((extra, 128), 0)).astype(f32)
    counts = tn(total[SLICES:, :SLICES], spread, HIGH)
    return own + jnp.concatenate([total[:SLICES], counts], axis=1)


def attend_parts(totals, wqb):
    expand = (iota((128, D), 0) == 16 * (iota((128, D), 1) // DH)).astype(f32)
    total = jnp.concatenate(totals, axis=0)
    count = nn(total[:, D:], expand, HIGH)
    slice_tok = total[:, :D] / count
    triple = nn(slice_tok, wqb, HIGH)
    parts = []
    for index in range(len(totals)):
        rows = slice(index * SLICES, (index + 1) * SLICES)
        queries = triple[rows, :D]
        key_wide = spread_diag(triple[rows, D : 2 * D])
        value_wide = spread_diag(triple[rows, 2 * D :])
        scores = (nt(key_wide, queries, HIGH) * (1.0 / math.sqrt(DH))).reshape(
            HEADS, SLICES, SLICES
        )
        expo = jnp.exp(scores - jnp.max(scores, axis=1, keepdims=True))
        prob = (expo / jnp.sum(expo, axis=1, keepdims=True)).reshape(HS, SLICES)
        parts.append((queries, key_wide, value_wide, prob))
    return (slice_tok, count, parts)


def attend_all(scal, tiles, sums, recv_ref, wqb, attended_ref):
    def pair(*meshes):
        totals = [add_edges(sums[mesh], mesh, recv_ref) for mesh in meshes]
        _, _, parts = attend_parts(totals, wqb)
        results = [tn(prob, value_wide, HIGH).astype(b16) for _, _, value_wide, prob in parts]
        for mesh, result in zip(meshes, results):
            attended_ref[mesh] = result

    present_pairs(scal, tiles, pair)


def spread_tile(scal, tiles, tile, wide_ref, p_ref, spread):
    low, high = tile_range(scal, tiles, tile)
    weights_r = p_ref[...]
    width = weights_r.shape[1]

    def one(mesh, carry):
        keep = tile_mask(scal, mesh, tile, width)
        spread[...] = jnp.where(keep, tn(spread_diag(wide_ref[mesh]), weights_r), spread[...])
        return carry

    lax.fori_loop(low, high + 1, one, 0)
    return spread[...].astype(b16)


GELU_A = math.sqrt(2.0 / math.pi)
GELU_B = 0.044715


def gelu_pair(hidden):
    square = hidden * hidden
    bend = jnp.tanh(hidden * (GELU_A + (GELU_A * GELU_B) * square))
    half = 0.5 + 0.5 * bend
    value = hidden * half
    slope = half + (0.5 * hidden) * (1.0 - bend * bend) * (
        GELU_A + (3.0 * GELU_A * GELU_B) * square
    )
    return (value, slope)


CHUNK = 1024


def mlp_back_tile(scal, tiles, tile, grad, slopes, actives, scaled_two, scale_two, normed_two_r, spread_r,
                  weights_r, wout, wup, wdown, norms, d2_ref, de_ref, sums,
                  gup, gdown, gout, gnorm):
    width = grad.shape[1]
    grad_r = grad.astype(b16)
    grad_normed = jnp.zeros((D, width), f32)
    for start in range(0, FF, CHUNK):
        part = slice(start, start + CHUNK)
        back = (slopes(part) * nn(wdown[part], grad_r)).astype(b16)
        gup[:, part] += nt(normed_two_r, back)
        gdown[:, part] += nt(grad_r, actives(part))
        grad_normed = grad_normed + nn(wup[:, part], back)
    gnorm[2] += fold_lanes(grad_normed * scaled_two)
    gnorm[3] += fold_lanes(grad_normed)
    grad_middle = grad + norm_back(grad_normed, scaled_two, scale_two, norms[:, 2:3])
    d2_ref[...] = grad_middle
    branch_r = grad_middle.astype(b16)
    gout[...] += nt(spread_r, branch_r)
    spread_grad = nn(wout, branch_r).astype(b16)
    de_ref[...] = spread_grad
    low, high = tile_range(scal, tiles, tile)

    def add(mesh, carry):
        keep = tile_mask(scal, mesh, tile, width).astype(b16)
        sums[mesh] += pick_diag(nt(weights_r, spread_grad * keep), DH)
        return carry

    lax.fori_loop(low, high + 1, add, 0)


def attend_back_all(scal, tiles, sums, recv_ref, grads, grad_recv_ref, wqb, both, dcount, gqkv):
    root = 1.0 / math.sqrt(DH)

    def pair(*meshes):
        totals = [add_edges(sums[mesh], mesh, recv_ref) for mesh in meshes]
        outer = [add_edges(grads[mesh], mesh, grad_recv_ref) for mesh in meshes]
        slice_tok, count, parts = attend_parts(totals, wqb)
        attended, triples = [], []
        for (queries, key_wide, value_wide, prob), grad in zip(parts, outer):
            attended.append(tn(prob, value_wide, HIGH).astype(b16))
            inner = prob * nt(value_wide, grad, HIGH)
            mixed = group_sum(inner)
            grad_scores = root * (
                inner - (prob.reshape(HEADS, SLICES, SLICES) * mixed).reshape(HS, SLICES)
            )
            triples.append(
                jnp.concatenate(
                    [
                        tn(grad_scores, key_wide, HIGH),
                        pick_diag(nn(grad_scores, queries, HIGH), DH),
                        pick_diag(nn(prob, grad, HIGH), DH),
                    ],
                    axis=1,
                )
            )
        triple = jnp.concatenate(triples, axis=0)
        grad_sum = nt(triple, wqb, HIGH) / count
        grad_count = -(grad_sum * slice_tok)
        previous = recv_ref[0, SLICES + HEADS : SLICES + HEADS + 1, :1].astype(f32)
        shares = []
        for index, mesh in enumerate(meshes):
            share = 1.0 - (previous == mesh.astype(f32)).astype(f32)
            if index > 0:
                share = share * (mesh != meshes[0]).astype(f32)
            shares.append(jnp.broadcast_to(share, (SLICES, 1)))
        gqkv[...] += tn(slice_tok * jnp.concatenate(shares, axis=0), triple, HIGH)
        for index, mesh in enumerate(meshes):
            rows = slice(index * SLICES, (index + 1) * SLICES)
            both[mesh, :, :D] = spread_diag(attended[index])
            both[mesh, :, D:] = spread_diag(grad_sum[rows].astype(b16))
            column = jnp.sum(spread_diag(grad_count[rows]), axis=1, keepdims=True)
            dcount[mesh] = jnp.broadcast_to(column, (HS, 128))

    present_pairs(scal, tiles, pair)


def attend_back_tile(scal, tiles, tile, both, dcount, de_ref, f_ref, m_ref, p_ref, u_ref, vh_ref, rs_ref,
                     d2_ref, wfm, wsb, norms, grad_p, grad_f, gfm, gws, gnorm):
    low, high = tile_range(scal, tiles, tile)
    weights_r = p_ref[...]
    width = weights_r.shape[1]
    pair = jnp.concatenate([de_ref[...], f_ref[...]], axis=0)

    def one(mesh, carry):
        keep = tile_mask(scal, mesh, tile, width)
        back = nn(both[mesh], pair) + dcount[mesh][:, :1]
        grad_p[...] = jnp.where(keep, back, grad_p[...])
        grad_f[...] = jnp.where(keep, tn(both[mesh, :, D:], weights_r), grad_f[...])
        return carry

    lax.fori_loop(low, high + 1, one, 0)
    weights = weights_r.astype(f32)
    inner = weights * grad_p[...]
    mixed = group_sum(inner)
    grad_logits = (
        inner - (weights.reshape(HEADS, SLICES, width) * mixed).reshape(HS, width)
    ).astype(b16)
    gws[...] += nt(m_ref[...], grad_logits)
    grad_m = nn(wsb, grad_logits).astype(b16)
    grad_fm = jnp.concatenate([grad_f[...].astype(b16), grad_m], axis=0)
    gfm[...] += nt(u_ref[...], grad_fm)
    grad_normed = tn(wfm, grad_fm)
    scaled = vh_ref[...].astype(f32)
    gnorm[0] += fold_lanes(grad_normed * scaled)
    gnorm[1] += fold_lanes(grad_normed)
    return d2_ref[...] + norm_back(grad_normed, scaled, rs_ref[:1], norms[:, 0:1])


def small_rows(base, gws, gqkv, scratch, out_ref):
    lane = iota((1, 128), 1)
    left = repeat_rows(DH)
    fold = (iota((128, HS), 1) % SLICES == iota((128, HS), 0)).astype(f32)
    kept = jnp.where(same_head(DH, SLICES, (D, HS)), gws[...], 0.0)
    scratch[...] = nt(tn(left, kept, HIGH), fold, HIGH)
    even = scratch[pl.ds(0, DH // 2, stride=2), :]
    odd = scratch[pl.ds(1, DH // 2, stride=2), :]
    out_ref[base : base + DH // 2] = jnp.where(lane < SLICES, even, pltpu.roll(odd, SLICES, 1))
    fold = (iota((D, 128), 0) % DH == iota((D, 128), 1)).astype(f32)
    for part in range(3):
        square = jnp.where(same_head(DH, DH, (D, D)), gqkv[:, part * D : (part + 1) * D], 0.0)
        scratch[...] = nn(tn(left, square, HIGH), fold, HIGH)
        total = scratch[pl.ds(0, DH // 4, stride=4), :]
        for inner in range(1, 4):
            total = total + pltpu.roll(scratch[pl.ds(inner, DH // 4, stride=4), :], DH * inner, 1)
        start = base + DH // 2 + part * (DH // 4)
        out_ref[start : start + DH // 4] = total


NORM_ROW = (SMALL - 4 * D) // 128
LAYER_ROWS = SMALL // 128


def norm_rows(gnorm, index, out_ref, base):
    lane = iota((D, 128), 1)
    total = jnp.zeros((D, 128), f32)
    for column, row in enumerate(index):
        total = total + jnp.where(lane == column, jnp.sum(gnorm[row], axis=1, keepdims=True), 0.0)
    flat = total.T
    for column in range(len(index)):
        for half in range(D // 128):
            place = base + column * (D // 128) + half
            out_ref[place : place + 1] = flat[column : column + 1, 128 * half : 128 * half + 128]


def pack_front(gfm, head):
    lane = iota((D, 128), 1)
    start = (head // 2) * 128
    feats, middle = gfm[:, start : start + 128], gfm[:, D + start : D + start + 128]
    if head % 2 == 0:
        return jnp.where(lane < 64, feats, pltpu.roll(middle, 64, 1))
    return jnp.where(lane < 64, pltpu.roll(feats, 64, 1), middle)


def store_pieces(out_ref, head, base, value):
    size = out_ref.shape[2]
    done = 0
    while done < value.shape[0]:
        chunk, offset = divmod(base + done, size)
        count = min(size - offset, value.shape[0] - done)
        for half in range(2):
            out_ref[head, 2 * chunk + half, offset : offset + count] = value[
                done : done + count, 128 * half : 128 * half + 128
            ]
        done += count


def pack_rest(gout, gup, gdown, out_ref, base, n_head):
    for head in range(n_head):
        deep, wide = D // n_head, FF // n_head
        store_pieces(out_ref, head, base, gout[head * deep : (head + 1) * deep].astype(b16))
        start = base + deep
        store_pieces(out_ref, head, start, gup[:, head * wide : (head + 1) * wide].astype(b16))
        store_pieces(out_ref, head, start + D, gdown[:, head * wide : (head + 1) * wide].astype(b16))


def first_kernel(tiles, scal, tok_ref, wfm_ref, wsb_ref, norm_ref,
                 xt_ref, vh_ref, rs_ref, u_ref, f_ref, m_ref, p_ref, sums_hbm, edge_ref, sums, sem):
    tile = pl.program_id(0)

    @pl.when(tile == 0)
    def _():
        clear_present(scal, tiles, sums)

    x = tok_ref[...].astype(f32).T
    xt_ref[...] = x.astype(b16)
    front_tile(scal, tiles, tile, x, wfm_ref[...], wsb_ref[...], norm_ref[...],
               vh_ref, rs_ref, u_ref, f_ref, m_ref, p_ref, sums)

    @pl.when(tile == tiles - 1)
    def _():
        write_edges(scal, tiles, sums, edge_ref)
        move_present(scal, tiles, sums, sums_hbm, sem)


def second_kernel(tiles, scal, xt_ref, p0_ref, sums0_hbm, recv_ref, wout_ref, wup_ref, wdown_ref, wqb_ref, norm0_ref,
                  wfm_ref, wsb_ref, norm1_ref,
                  e_ref, vh2_ref, rs2_ref, u2_ref, gp_ref, z_ref,
                  x1_ref, vh_ref, rs_ref, u_ref, f_ref, m_ref, p_ref, sums_hbm, edge_ref,
                  wide, spread, sums, sem):
    tile = pl.program_id(0)

    @pl.when(tile == 0)
    def _():
        move_present(scal, tiles, sums0_hbm, sums, sem)
        attend_all(scal, tiles, sums, recv_ref, wqb_ref[...], wide)
        clear_present(scal, tiles, sums)

    norms = norm0_ref[...]
    spread_r = spread_tile(scal, tiles, tile, wide, p0_ref, spread)
    e_ref[...] = spread_r
    middle = xt_ref[...].astype(f32) + tn(wout_ref[...], spread_r)
    scaled_two, scale_two = norm_stats(middle)
    vh2_ref[...] = scaled_two.astype(b16)
    rs2_ref[...] = jnp.broadcast_to(scale_two, rs2_ref.shape)
    normed_two_r = (scaled_two * norms[:, 2:3] + norms[:, 3:4]).astype(b16)
    u2_ref[...] = normed_two_r
    x = middle
    for start in range(0, FF, CHUNK):
        part = slice(start, start + CHUNK)
        active, slope = gelu_pair(tn(wup_ref[:, part], normed_two_r))
        active_r = active.astype(b16)
        z_ref[part] = active_r
        gp_ref[part] = slope.astype(b16)
        x = x + tn(wdown_ref[part], active_r)
    x1_ref[...] = x
    front_tile(scal, tiles, tile, x, wfm_ref[...], wsb_ref[...], norm1_ref[...],
               vh_ref, rs_ref, u_ref, f_ref, m_ref, p_ref, sums)

    @pl.when(tile == tiles - 1)
    def _():
        write_edges(scal, tiles, sums, edge_ref)
        move_present(scal, tiles, sums, sums_hbm, sem)


def third_kernel(n_head, packed, tiles, scal, x1_ref, p_ref, sums1_hbm, recv_ref, cot_ref, wout_ref, wup_ref, wdown_ref, wqb_ref, norm_ref,
                 out_ref, d2_ref, de_ref, grads_hbm, edge_ref,
                 gn_ref, *rest):
    grad_outs, (sums, sem, grads, wide, spread, gnorm, slope_s, active_s, gup, gdown, gout) = rest[:-11], rest[-11:]
    tile = pl.program_id(0)

    @pl.when(tile == 0)
    def _():
        clear_present(scal, tiles, grads)
        gup[...] = jnp.zeros_like(gup)
        gdown[...] = jnp.zeros_like(gdown)
        gout[...] = jnp.zeros_like(gout)
        gnorm[...] = jnp.zeros_like(gnorm)
        move_present(scal, tiles, sums1_hbm, sums, sem)
        attend_all(scal, tiles, sums, recv_ref, wqb_ref[...], wide)

    norms = norm_ref[...]
    spread_r = spread_tile(scal, tiles, tile, wide, p_ref, spread)
    middle = x1_ref[...] + tn(wout_ref[...], spread_r)
    scaled_two, scale_two = norm_stats(middle)
    normed_two_r = (scaled_two * norms[:, 2:3] + norms[:, 3:4]).astype(b16)
    x = middle
    for start in range(0, FF, CHUNK):
        part = slice(start, start + CHUNK)
        active, slope = gelu_pair(tn(wup_ref[:, part], normed_two_r))
        active_r = active.astype(b16)
        active_s[part] = active_r
        slope_s[part] = slope
        x = x + tn(wdown_ref[part], active_r)
    out_ref[...] = x.T.astype(b16)
    grad = cot_ref[...].astype(f32).T
    mlp_back_tile(scal, tiles, tile, grad, lambda part: slope_s[part], lambda part: active_s[part],
                  scaled_two, scale_two, normed_two_r, spread_r, p_ref[...],
                  wout_ref[...], wup_ref, wdown_ref, norms, d2_ref, de_ref, grads,
                  gup, gdown, gout, gnorm)

    @pl.when(tile == tiles - 1)
    def _():
        write_edges(scal, tiles, grads, edge_ref)
        move_present(scal, tiles, grads, grads_hbm, sem)
        norm_rows(gnorm, (2, 3), gn_ref, 0)
        if packed:
            pack_rest(gout, gup, gdown, grad_outs[0], 0, n_head)
        else:
            for ref, total in zip(grad_outs, (gup, gdown, gout)):
                ref[...] = total[...].astype(b16)


def fourth_kernel(n_head, packed, tiles, scal, sums1_hbm, recv_ref, grads1_hbm, grad_recv_ref, de1_ref, f_ref, m_ref, p1_ref, u_ref, vh_ref, rs_ref, d21_ref,
                  wfm_ref, wsb_ref, wqb_ref, norm1_ref,
                  gp_ref, z_ref, vh2_ref, rs2_ref, u2_ref, e_ref, p0_ref, wout_ref, wup_ref, wdown_ref, norm0_ref, gn1b_ref,
                  d2_ref, de_ref, grads_hbm, edge_ref, small_ref, gn0_ref, *rest):
    grad_outs = rest[:-15]
    sums, grads, sem, both, dcount, grad_p, grad_f, gws, gqkv, gnorm, fold_s, gfm, gup, gdown, gout = rest[-15:]
    tile = pl.program_id(0)

    @pl.when(tile == 0)
    def _():
        for ref in (gfm, gws, gqkv, gup, gdown, gout, gnorm):
            ref[...] = jnp.zeros_like(ref)
        move_present(scal, tiles, sums1_hbm, sums, sem)
        move_present(scal, tiles, grads1_hbm, grads, sem)
        attend_back_all(scal, tiles, sums, recv_ref, grads, grad_recv_ref, wqb_ref[...], both, dcount, gqkv)
        clear_present(scal, tiles, grads)

    grad = attend_back_tile(scal, tiles, tile, both, dcount, de1_ref, f_ref, m_ref, p1_ref, u_ref, vh_ref, rs_ref,
                            d21_ref, wfm_ref[...], wsb_ref[...], norm1_ref[...], grad_p, grad_f, gfm, gws, gnorm)
    mlp_back_tile(scal, tiles, tile, grad, lambda part: gp_ref[part].astype(f32), lambda part: z_ref[part],
                  vh2_ref[...].astype(f32), rs2_ref[:1], u2_ref[...], e_ref[...], p0_ref[...],
                  wout_ref[...], wup_ref, wdown_ref, norm0_ref[...], d2_ref, de_ref, grads,
                  gup, gdown, gout, gnorm)

    @pl.when(tile == tiles - 1)
    def _():
        write_edges(scal, tiles, grads, edge_ref)
        move_present(scal, tiles, grads, grads_hbm, sem)
        small_rows(0, gws, gqkv, fold_s, small_ref)
        norm_rows(gnorm, (0, 1), small_ref, NORM_ROW)
        small_ref[NORM_ROW + 4 :] = gn1b_ref[...]
        norm_rows(gnorm, (2, 3), gn0_ref, 0)
        if packed:
            for head in range(n_head):
                front = pack_front(gfm, head).astype(b16)
                store_pieces(
                    grad_outs[0], head, 0, jnp.concatenate([front[: D // 2], front[D // 2 :]], axis=1)
                )
            pack_rest(gout, gup, gdown, grad_outs[0], D // 2, n_head)
        else:
            for ref, total in zip(grad_outs, (gfm, gup, gdown, gout)):
                ref[...] = total[...].astype(b16)


def fifth_kernel(n_head, packed, tiles, scal, sums0_hbm, recv_ref, grads0_hbm, grad_recv_ref, de_ref, f_ref, m_ref, p_ref, u_ref, vh_ref, rs_ref, d2_ref,
                 wfm_ref, wsb_ref, wqb_ref, norm_ref, gn0b_ref, small1_ref,
                 gin_ref, small_ref, front_ref,
                 sums, grads, sem, both, dcount, grad_p, grad_f, gws, gqkv, gnorm, fold_s, gfm):
    tile = pl.program_id(0)

    @pl.when(tile == 0)
    def _():
        for ref in (gfm, gws, gqkv, gnorm):
            ref[...] = jnp.zeros_like(ref)
        move_present(scal, tiles, sums0_hbm, sums, sem)
        move_present(scal, tiles, grads0_hbm, grads, sem)
        attend_back_all(scal, tiles, sums, recv_ref, grads, grad_recv_ref, wqb_ref[...], both, dcount, gqkv)

    grad = attend_back_tile(scal, tiles, tile, both, dcount, de_ref, f_ref, m_ref, p_ref, u_ref, vh_ref, rs_ref,
                            d2_ref, wfm_ref[...], wsb_ref[...], norm_ref[...], grad_p, grad_f, gfm, gws, gnorm)
    gin_ref[...] = grad.T

    @pl.when(tile == tiles - 1)
    def _():
        small_rows(0, gws, gqkv, fold_s, small_ref)
        norm_rows(gnorm, (0, 1), small_ref, NORM_ROW)
        small_ref[NORM_ROW + 4 : LAYER_ROWS] = gn0b_ref[...]
        small_ref[LAYER_ROWS:] = small1_ref[...]
        if packed:
            for head in range(n_head):
                front_ref[head] = pack_front(gfm, head).astype(b16)
        else:
            front_ref[...] = gfm[...].astype(b16)


def sum_parts(own, got):
    total = own.astype(f32)
    for index in range(got.shape[0]):
        total = total + got[index].astype(f32)
    return total


def total_kernel(sizes, gb_ref, gc_ref, gs_ref, tb_ref, tc_ref, ts_ref,
                 got_b, got_c, got_s, mid_c, mid_s, got_c2, got_s2, head_sem, pts_sem):
    n_pts, n_head = sizes
    pts, head = lax.axis_index("pts"), lax.axis_index("head")
    c_rows = D // n_pts
    s_rows = gs_ref.shape[0] // n_head

    def part(index, rows):
        return pl.ds(pl.multiple_of(index * rows, rows), rows)

    def over(size, which, own, to, sem, source, target):
        copies = []
        for step in range(1, size):
            peer = lax.rem(own + step, size)
            copies.append(
                pltpu.make_async_remote_copy(
                    src_ref=source(peer),
                    dst_ref=target(step - 1),
                    send_sem=sem.at[0, which, step - 1],
                    recv_sem=sem.at[1, which, step - 1],
                    device_id=to(peer),
                    device_id_type=MESH,
                )
            )
        for copy in copies:
            copy.start()
        return copies

    def over_head(which, source, target):
        return over(n_head, which, head, lambda peer: (pts, peer), head_sem, source, target)

    def over_pts(which, source, target):
        return over(n_pts, which, pts, lambda peer: (peer, head), pts_sem, source, target)

    def finish(copies):
        for copy in copies:
            copy.wait()

    barrier = pltpu.get_barrier_semaphore()
    for step in range(1, n_head):
        pl.semaphore_signal(
            barrier, inc=1, device_id=(pts, lax.rem(head + step, n_head)), device_id_type=MESH
        )
    for step in range(1, n_pts):
        pl.semaphore_signal(
            barrier, inc=1, device_id=(lax.rem(pts + step, n_pts), head), device_id_type=MESH
        )
    pl.semaphore_wait(barrier, n_head - 1 + n_pts - 1)

    first_c = over_head(0, lambda peer: gc_ref.at[peer], lambda slot: got_c.at[slot])
    first_s = over_head(1, lambda peer: gs_ref.at[part(peer, s_rows)], lambda slot: got_s.at[slot])
    first_b = over_pts(0, lambda peer: gb_ref.at[peer], lambda slot: got_b.at[slot])
    finish(first_c)
    mid_c[...] = sum_parts(gc_ref[head], got_c).astype(b16)
    next_c = over_pts(1, lambda peer: mid_c.at[part(peer, c_rows)], lambda slot: got_c2.at[slot])
    finish(first_s)
    mid_s[...] = sum_parts(gs_ref[part(head, s_rows)], got_s)
    next_s = over_pts(2, lambda peer: mid_s, lambda slot: got_s2.at[slot])
    finish(next_c)
    mine_c = part(pts, c_rows)
    tc_ref[mine_c] = sum_parts(mid_c[mine_c], got_c2).astype(b16)
    last_c = over_pts(3, lambda peer: tc_ref.at[mine_c], lambda slot: tc_ref.at[mine_c])
    finish(next_s)
    mine_s = part(head, s_rows)
    ts_ref[mine_s] = sum_parts(mid_s[...], got_s2)
    last_s = over_head(2, lambda peer: ts_ref.at[mine_s], lambda slot: ts_ref.at[mine_s])
    finish(first_b)
    tb_ref[pts] = sum_parts(gb_ref[pts], got_b).astype(b16)
    last_b = over_pts(4, lambda peer: tb_ref.at[pts], lambda slot: tb_ref.at[pts])
    finish(last_c)
    finish(last_s)
    finish(last_b)


def total_gradients(sizes, gb, gc, gs):
    n_pts, n_head = sizes
    vmem = pl.BlockSpec(memory_space=pltpu.VMEM)
    dma = pltpu.SemaphoreType.DMA
    c_rows, s_rows = D // n_pts, gs.shape[0] // n_head
    return pl.pallas_call(
        functools.partial(total_kernel, sizes),
        out_shape=(
            jax.ShapeDtypeStruct(gb.shape, b16),
            jax.ShapeDtypeStruct(gc.shape[1:], b16),
            jax.ShapeDtypeStruct(gs.shape, f32),
        ),
        in_specs=[vmem] * 3,
        out_specs=[vmem] * 3,
        scratch_shapes=[
            pltpu.VMEM((n_pts - 1,) + gb.shape[1:], b16),
            pltpu.VMEM((n_head - 1,) + gc.shape[1:], b16),
            pltpu.VMEM((n_head - 1, s_rows, 128), f32),
            pltpu.VMEM(gc.shape[1:], b16),
            pltpu.VMEM((s_rows, 128), f32),
            pltpu.VMEM((n_pts - 1, c_rows, 128), b16),
            pltpu.VMEM((n_pts - 1, s_rows, 128), f32),
            dma((2, 3, n_head - 1)),
            dma((2, 5, n_pts - 1)),
        ],
        compiler_params=pltpu.CompilerParams(
            collective_id=3, has_side_effects=True, vmem_limit_bytes=VMEM_BYTES
        ),
        name="total_gradients",
    )(gb, gc, gs)


def update_kernel(ta_ref, tb_ref, tc_ref, ts_ref, row_ref, sel_ref, m_ref, v_ref, w_ref, sm_ref, sv_ref, sw_ref,
                  nm_ref, nv_ref, nw_ref, fresh_ref, om_ref, ov_ref, ow_ref, wide, tall, front, flat):
    lane = iota((8, 128), 1)

    def place_front(base):
        for pair in range(16):
            first = front[pl.ds(2 * pair, 8, stride=32), :]
            second = front[pl.ds(2 * pair + 1, 8, stride=32), :]
            columns = slice(128 * pair, 128 * pair + 128)
            wide[base : base + 8, columns] = jnp.where(lane < 64, first, pltpu.roll(second, 64, 1))
            wide[base + 8 : base + 16, columns] = jnp.where(lane < 64, pltpu.roll(first, 64, 1), second)

    def place_rest(base):
        for part in range(8):
            for half in range(2):
                wide[base : base + 72, 256 * part + 128 * half : 256 * part + 128 * half + 128] = tall[
                    half, pl.ds(part, 72, stride=8), :
                ]

    def fill(value, base):
        size = value.shape[1]
        row = base
        while row < size * (value.shape[0] // 2):
            chunk, offset = divmod(row, size)
            for half in range(2):
                tall[half, row - base : row - base + size - offset] = value[
                    2 * chunk + half, offset:
                ].astype(f32)
            row += size - offset

    front[...] = tc_ref[...].astype(f32)
    place_front(0)
    fill(tb_ref, D // 2)
    place_rest(16)
    front[: D // 2] = tb_ref[0, : D // 2].astype(f32)
    front[D // 2 :] = tb_ref[1, : D // 2].astype(f32)
    place_front(88)
    fill(ta_ref, 0)
    place_rest(104)

    cap, blocks = m_ref.shape[0], wide.shape[0]
    mine = (iota((cap, blocks), 0) == row_ref[:1]).astype(f32)
    filled = jnp.sum(mine, axis=1, keepdims=True) > 0.5
    mine = mine.astype(b16)
    step = 512
    for start in range(0, BLOCK, step):
        part = slice(start, start + step)
        grad = wide[:, part]
        own = nn(mine, grad.astype(b16))
        old = (m_ref[:, part], v_ref[:, part], w_ref[:, part])
        new = adam_update(old[0], own, old[1], old[2], rate_large)
        for ref, before, after in zip((nm_ref, nv_ref, nw_ref), old, new):
            ref[:, part] = jnp.where(filled, after, before)
        picked = [
            sel_ref[:, which * BLOCK + start : which * BLOCK + start + step].astype(f32)
            for which in range(3)
        ]
        fresh_ref[:, part] = adam_update(picked[0], grad, picked[1], picked[2], rate_large)[0].astype(b16)
    for layer in range(2):
        for row in range(LAYER_ROWS):
            flat[layer : layer + 1, 128 * row : 128 * row + 128] = ts_ref[
                layer * LAYER_ROWS + row : layer * LAYER_ROWS + row + 1, :
            ]
    new = adam_update(sm_ref[...], flat[:2], sv_ref[...], sw_ref[...], rate_small)
    for ref, value in zip((om_ref, ov_ref, ow_ref), new):
        ref[...] = value


def update(ta, tb, tc, ts, row, sel, tables, smalls):
    vmem = pl.BlockSpec(memory_space=pltpu.VMEM)
    blocks = sel.shape[0]
    operands = (ta, tb, tc, ts, row, sel, *tables, *smalls)
    outs = [jax.ShapeDtypeStruct(table.shape, f32) for table in tables]
    outs.append(jax.ShapeDtypeStruct((blocks, BLOCK), b16))
    outs += [jax.ShapeDtypeStruct(small.shape, f32) for small in smalls]
    return pl.pallas_call(
        update_kernel,
        out_shape=outs,
        in_specs=[vmem] * len(operands),
        out_specs=[vmem] * len(outs),
        scratch_shapes=[
            pltpu.VMEM((blocks, BLOCK), f32),
            pltpu.VMEM((2, ta.shape[0] * ta.shape[1] // 2, 128), f32),
            pltpu.VMEM((D, 128), f32),
            pltpu.VMEM((8, SMALL), f32),
        ],
        compiler_params=pltpu.CompilerParams(vmem_limit_bytes=VMEM_BYTES),
        name="update",
    )(*operands)


class Args:
    def __init__(self, rows, width):
        self.rows, self.width = rows, width
        self.operands, self.in_specs, self.outs, self.out_specs = [], [], [], []

    def cols(self, *arrays):
        for array in arrays:
            self.operands.append(array)
            self.in_specs.append(
                pl.BlockSpec((array.shape[0], self.width), lambda tile, scal: (0, tile))
            )

    def points(self, *arrays):
        for array in arrays:
            self.operands.append(array)
            self.in_specs.append(
                pl.BlockSpec((self.width, array.shape[1]), lambda tile, scal: (tile, 0))
            )

    def whole(self, *arrays):
        for array in arrays:
            rank = array.ndim
            self.operands.append(array)
            self.in_specs.append(
                pl.BlockSpec(array.shape, lambda tile, scal, rank=rank: (0,) * rank)
            )

    def layer(self, index, *arrays):
        for array in arrays:
            self.operands.append(array)
            self.in_specs.append(
                pl.BlockSpec((None,) + array.shape[1:], lambda tile, scal: (index, 0, 0))
            )

    def rows_of(self, array, start, size):
        self.operands.append(array)
        self.in_specs.append(
            pl.BlockSpec((size, array.shape[1]), lambda tile, scal: (start // size, 0))
        )

    def far(self, *arrays):
        for array in arrays:
            self.operands.append(array)
            self.in_specs.append(pl.BlockSpec(memory_space=pl.ANY))

    def out_far(self, *pairs):
        for shape, dtype in pairs:
            self.outs.append(jax.ShapeDtypeStruct(shape, dtype))
            self.out_specs.append(pl.BlockSpec(memory_space=pl.ANY))

    def out_cols(self, *pairs):
        for height, dtype in pairs:
            self.outs.append(jax.ShapeDtypeStruct((height, self.rows), dtype))
            self.out_specs.append(
                pl.BlockSpec((height, self.width), lambda tile, scal: (0, tile))
            )

    def out_points(self, *dtypes):
        for dtype in dtypes:
            self.outs.append(jax.ShapeDtypeStruct((self.rows, D), dtype))
            self.out_specs.append(pl.BlockSpec((self.width, D), lambda tile, scal: (tile, 0)))

    def out_whole(self, *pairs):
        for shape, dtype in pairs:
            rank = len(shape)
            self.outs.append(jax.ShapeDtypeStruct(shape, dtype))
            self.out_specs.append(
                pl.BlockSpec(shape, lambda tile, scal, rank=rank: (0,) * rank)
            )

    def call(self, body, scal, scratch, name):
        tiles = self.rows // self.width
        return pl.pallas_call(
            functools.partial(body, tiles),
            grid_spec=pltpu.PrefetchScalarGridSpec(
                num_scalar_prefetch=1,
                grid=(tiles,),
                in_specs=self.in_specs,
                out_specs=self.out_specs,
                scratch_shapes=scratch,
            ),
            out_shape=self.outs,
            compiler_params=pltpu.CompilerParams(
                dimension_semantics=("arbitrary",), vmem_limit_bytes=VMEM_BYTES
            ),
            name=name,
        )(scal, *self.operands)


def adam_update(master, grad, first, second, rate):
    new_first = beta_one * first + (1.0 - beta_one) * grad
    new_second = beta_two * second + (1.0 - beta_two) * grad * grad
    fix_one = 1.0 - beta_one**STEP
    fix_two = 1.0 - beta_two**STEP
    direction = new_first / fix_one / (jnp.sqrt(new_second / fix_two) + adam_eps)
    return (master - rate * (direction + decay_rate * master), new_first, new_second)


def flat_blocks(n_head, gfm, gout, gup, gdown):
    def columns(grad):
        width = grad.shape[1] // n_head
        return grad.reshape(D, n_head, width).transpose(1, 0, 2).reshape(n_head, -1)

    return jnp.concatenate(
        [
            columns(gfm[:, :D]),
            columns(gfm[:, D:]),
            gout.reshape(n_head, -1),
            columns(gup),
            columns(gdown),
        ],
        axis=1,
    ).reshape(n_head, -1, BLOCK)


def on_device(
    sizes,
    tokens,
    cotangent,
    segment_ids,
    owner,
    w_fx,
    w_mid,
    w_out,
    w_up,
    w_down,
    small_master,
    small_first,
    small_second,
    master_table,
    first_table,
    second_table,
):
    n_pts, n_head = sizes
    rows = tokens.shape[0]
    width, wide = min(512, rows), min(1024, rows)
    tiles = rows // width
    most = rows * n_pts * n_head // LARGEST
    window = (rows - 1 + most - 1) // rows
    layers = w_fx.shape[0]
    packed = (n_pts, n_head) == (8, 4)

    ids = segment_ids.reshape(-1, 128)
    w_fx = w_fx.transpose(0, 2, 1)
    w_mid = w_mid.transpose(0, 2, 1)
    tables = (master_table, first_table, second_table)
    smalls = (small_master, small_first, small_second)
    gathered, wsb, norms, scal, halves = opening(
        n_head, tiles, ids, w_fx, w_mid, small_master, tables
    )
    wfm0 = gathered.reshape(2 * D, D)

    cap = master_table.shape[0]
    if packed:
        collected = lax.all_gather(halves, "pts", axis=0, tiled=True)

    sums_shape = (MESHES, SLICES, D + 128)
    grad_sums_shape = (MESHES, SLICES, D)
    front_cols = ((D, b16), (8, f32), (D, b16), (D, b16), (D, b16), (HS, b16))
    wide_scratch = [pltpu.VMEM(grad_sums_shape, b16), pltpu.VMEM((D, wide), f32)]

    args = Args(rows, wide)
    args.points(tokens)
    args.whole(wfm0)
    args.layer(0, wsb, norms)
    args.out_cols((D, b16), *front_cols)
    args.out_far((sums_shape, f32))
    args.out_whole(((2, EDGE, D), b16))
    sums_scratch = [pltpu.VMEM(sums_shape, f32), pltpu.SemaphoreType.DMA((MESHES,))]
    xt0, vh0, rs0, u0, f0, m0, p0, sums0, edge = args.call(first_kernel, scal, sums_scratch, "first")
    recv0, later, wqb0 = swap_edges_weights(
        sizes, window, 0, ((0, 1), (1, 1), (2, 0)), edge, w_fx, w_mid, w_out, small_master, 1
    )
    later = later.reshape(3 * D, D)

    args = Args(rows, wide)
    args.cols(xt0, p0)
    args.far(sums0)
    args.whole(recv0)
    args.rows_of(later, 2 * D, D)
    args.layer(0, w_up, w_down)
    args.whole(wqb0)
    args.layer(0, norms)
    args.rows_of(later, 0, 2 * D)
    args.layer(1, wsb, norms)
    args.out_cols((D, b16), (D, b16), (8, f32), (D, b16), (FF, b16), (FF, b16))
    args.out_cols((D, f32), *front_cols)
    args.out_far((sums_shape, f32))
    args.out_whole(((2, EDGE, D), b16))
    (e0, vh20, rs20, u20, gp0, z0, x1, vh1, rs1, u1, f1, m1, p1, sums1, edge) = args.call(
        second_kernel, scal, wide_scratch + sums_scratch, "second"
    )
    recv1, wout1, wqb1 = swap_edges_weights(
        sizes, window, 1, ((2, 1),), edge, w_fx, w_mid, w_out, small_master, 5
    )
    wout1 = wout1.reshape(D, D)

    grad_scratch = [pltpu.VMEM((D, FF), f32), pltpu.VMEM((D, FF), f32), pltpu.VMEM((D, D), f32)]
    rest_rows = D // n_head + 2 * D

    args = Args(rows, wide)
    args.cols(x1, p1)
    args.far(sums1)
    args.whole(recv1)
    args.points(cotangent)
    args.whole(wout1)
    args.layer(1, w_up, w_down)
    args.whole(wqb1)
    args.layer(1, norms)
    args.out_points(b16)
    args.out_cols((D, f32), (D, b16))
    args.out_far((grad_sums_shape, f32))
    args.out_whole(((2, EDGE, D), b16), ((4, 128), f32))
    if packed:
        args.out_whole(((n_head, n_pts, 2 * rest_rows // n_pts, 128), b16))
    else:
        args.out_whole(((D, FF), b16), ((D, FF), b16), ((D, D), b16))
    (layer_out, d21, de1, grads1, edge, gn1b, *grads_a) = args.call(
        functools.partial(third_kernel, n_head, packed),
        scal,
        sums_scratch
        + [pltpu.VMEM(grad_sums_shape, f32)]
        + wide_scratch
        + [pltpu.VMEM((4, D, 128), f32), pltpu.VMEM((FF, wide), f32), pltpu.VMEM((FF, wide), b16)]
        + grad_scratch,
        "third",
    )
    if packed:
        grad_recv1, chosen, row = swap_edges_pick(
            sizes, window, cap, edge, owner.reshape(1, -1), collected, 2
        )
        part_a = lax.psum_scatter(grads_a[0], "head", scatter_dimension=0, tiled=True)[0]
    else:
        grad_recv1 = swap_edges(sizes, window, edge, 4)

    back_scratch = [
        pltpu.VMEM(sums_shape, f32),
        pltpu.VMEM(grad_sums_shape, f32),
        pltpu.SemaphoreType.DMA((MESHES,)),
        pltpu.VMEM((MESHES, HS, 2 * D), b16),
        pltpu.VMEM((MESHES, HS, 128), f32),
        pltpu.VMEM((HS, width), f32),
        pltpu.VMEM((D, width), f32),
        pltpu.VMEM((D, HS), f32),
        pltpu.VMEM((D, 3 * D), f32),
        pltpu.VMEM((4, D, 128), f32),
        pltpu.VMEM((DH, 128), f32),
        pltpu.VMEM((D, 2 * D), f32),
    ]

    args = Args(rows, width)
    args.far(sums1)
    args.whole(recv1)
    args.far(grads1)
    args.whole(grad_recv1)
    args.cols(de1, f1, m1, p1, u1, vh1, rs1, d21)
    args.rows_of(later, 0, 2 * D)
    args.layer(1, wsb)
    args.whole(wqb1)
    args.layer(1, norms)
    args.cols(gp0, z0, vh20, rs20, u20, e0, p0)
    args.rows_of(later, 2 * D, D)
    args.layer(0, w_up, w_down, norms)
    args.whole(gn1b)
    args.out_cols((D, f32), (D, b16))
    args.out_far((grad_sums_shape, f32))
    args.out_whole(((2, EDGE, D), b16), ((LAYER_ROWS, 128), f32), ((4, 128), f32))
    if packed:
        args.out_whole(((n_head, n_pts, (D + 2 * rest_rows) // n_pts, 128), b16))
    else:
        args.out_whole(((D, 2 * D), b16), ((D, FF), b16), ((D, FF), b16), ((D, D), b16))
    (d20, de0, grads0, edge, small1, gn0b, *grads_b) = args.call(
        functools.partial(fourth_kernel, n_head, packed), scal, back_scratch + grad_scratch, "fourth"
    )
    if packed:
        grad_recv0, total_a = swap_edges_sums(sizes, window, edge, part_a, 6)
        mine_b = lax.psum_scatter(grads_b[0], "head", scatter_dimension=0, tiled=True)[0]
    else:
        grad_recv0 = swap_edges(sizes, window, edge, 4)

    args = Args(rows, width)
    args.far(sums0)
    args.whole(recv0)
    args.far(grads0)
    args.whole(grad_recv0)
    args.cols(de0, f0, m0, p0, u0, vh0, rs0, d20)
    args.whole(wfm0)
    args.layer(0, wsb)
    args.whole(wqb0)
    args.layer(0, norms)
    args.whole(gn0b, small1)
    args.out_points(f32)
    args.out_whole(((2 * LAYER_ROWS, 128), f32))
    args.out_whole(((n_head, D, 128), b16) if packed else ((D, 2 * D), b16))
    input_grad, small, front = args.call(
        functools.partial(fifth_kernel, n_head, packed), scal, back_scratch, "fifth"
    )

    if packed:
        total_b, total_c, total_s = total_gradients(sizes, mine_b, front, small)
        outs = update(total_a, total_b, total_c, total_s, row, chosen, tables, smalls)
        return (layer_out, input_grad, *outs)

    gup1, gdown1, gout1 = grads_a
    gfm1, gup0, gdown0, gout0 = grads_b
    small_total = lax.psum(small, ("pts", "head")).reshape(layers, -1)
    totals = []
    for parts in ((front, gout0, gup0, gdown0), (gfm1, gout1, gup1, gdown1)):
        blocks = lax.psum_scatter(
            flat_blocks(n_head, *parts), "head", scatter_dimension=0, tiled=True
        )
        totals.append(lax.psum(blocks.reshape(-1, BLOCK), "pts"))
    total_grad = jnp.concatenate(totals, axis=0).astype(f32)
    my_index = lax.axis_index("pts")
    block_ids = jnp.arange(owner.shape[0])
    same_owner = (owner[:, None] == owner[None, :]) & (block_ids[None, :] < block_ids[:, None])
    table_row = owner * cap + jnp.sum(same_owner.astype(jnp.int32), axis=1)
    place_all = (jnp.arange(n_pts * cap)[:, None] == table_row[None, :]).astype(f32)
    mine_place = lax.dynamic_slice_in_dim(place_all, my_index * cap, cap, 0)
    own_grad = jnp.dot(mine_place, total_grad, precision=lax.Precision.HIGHEST)
    filled = jnp.sum(mine_place, axis=1)[:, None] > 0.5
    updated = adam_update(master_table, own_grad, first_table, second_table, rate_large)
    new_tables = [jnp.where(filled, new, old) for new, old in zip(updated, tables)]
    collected = lax.all_gather(new_tables[0].astype(b16), "pts", axis=0, tiled=True)
    pick_back = (table_row[:, None] == jnp.arange(n_pts * cap)[None, :]).astype(b16)
    fresh = jnp.dot(pick_back, collected, preferred_element_type=f32).astype(b16)
    small_outs = adam_update(small_master, small_total, small_first, small_second, rate_small)
    return (layer_out, input_grad, *new_tables, fresh, *small_outs)


def solution(mesh):
    sizes = (mesh.shape["pts"], mesh.shape["head"])
    return jax.shard_map(
        functools.partial(on_device, sizes),
        mesh=mesh,
        in_specs=(
            P(("pts", "head"), None),
            P(("pts", "head"), None),
            P("pts"),
            P(),
            P(None, None, "head"),
            P(None, None, "head"),
            P(None, "head", None),
            P(),
            P(),
            P(),
            P(),
            P(),
            P("pts", "head"),
            P("pts", "head"),
            P("pts", "head"),
        ),
        out_specs=(
            P(("pts", "head"), None),
            P(("pts", "head"), None),
            P("pts", "head"),
            P("pts", "head"),
            P("pts", "head"),
            P(None, "head"),
            P(),
            P(),
            P(),
        ),
        check_vma=False,
    )
```

```python
import functools
import math

import jax
import jax.numpy as jnp
from jax import lax
from jax.experimental import pallas as pl
from jax.experimental.pallas import tpu as pltpu
from jax.sharding import PartitionSpec as P

D = 256
HEADS = 8
DH = 32
SLICES = 64
HS = HEADS * SLICES
FF = 1024
MESHES = 24
BLOCK = 2048
SMALL = 6144
STEP = 10
LARGEST = 12
EDGE = 80
VMEM_BYTES = 58 << 20

MESH = pl.DeviceIdType.MESH
HIGH = True
norm_eps = 1e-05
beta_one = 0.9
beta_two = 0.95
adam_eps = 1e-08
decay_rate = 0.1
rate_large = 0.1
rate_small = 0.75
f32 = jnp.float32
b16 = jnp.bfloat16


def dot(a, b, contract, precise):
    dims = (contract, ((), ()))
    if not precise:
        return lax.dot_general(a, b, dims, preferred_element_type=f32)
    a_high, b_high = a.astype(b16), b.astype(b16)
    a_low = (a - a_high.astype(f32)).astype(b16)
    b_low = (b - b_high.astype(f32)).astype(b16)
    return (
        lax.dot_general(a_high, b_low, dims, preferred_element_type=f32)
        + lax.dot_general(a_low, b_high, dims, preferred_element_type=f32)
        + lax.dot_general(a_high, b_high, dims, preferred_element_type=f32)
    )


def nn(a, b, precise=False):
    return dot(a, b, ((1,), (0,)), precise)


def nt(a, b, precise=False):
    return dot(a, b, ((1,), (1,)), precise)


def tn(a, b, precise=False):
    return dot(a, b, ((0,), (0,)), precise)


def iota(shape, axis):
    return lax.broadcasted_iota(jnp.int32, shape, axis)


def pick_diag(full, per_head):
    lane_head = iota((SLICES, full.shape[1]), 1) // per_head
    total = jnp.where(lane_head == 0, full[:SLICES], 0.0)
    for head in range(1, HEADS):
        total = total + jnp.where(
            lane_head == head, full[head * SLICES : (head + 1) * SLICES], 0.0
        )
    return total


def spread_diag(small):
    lane_head = iota((SLICES, D), 1) // DH
    return jnp.concatenate(
        [jnp.where(lane_head == head, small, jnp.zeros_like(small)) for head in range(HEADS)],
        axis=0,
    )


def repeat_rows(width):
    return (iota((D, width), 0) % width == iota((D, width), 1)).astype(f32)


def slice_repeat():
    return (iota((SLICES, HS), 1) % SLICES == iota((SLICES, HS), 0)).astype(f32)


def same_head(rows_per, cols_per, shape):
    return (iota(shape, 0) // rows_per) == (iota(shape, 1) // cols_per)


def start_gather(n_head, picks, send_sem, recv_sem):
    me = lax.axis_index("head")
    copies = []
    for index, ref in enumerate(picks):
        for step in range(1, n_head):
            copy = pltpu.make_async_remote_copy(
                src_ref=ref.at[:, me],
                dst_ref=ref.at[:, me],
                send_sem=send_sem.at[index, step - 1],
                recv_sem=recv_sem.at[index, step - 1],
                device_id={"head": lax.rem(me + step, n_head)},
                device_id_type=MESH,
            )
            copy.start()
            copies.append(copy)
    return copies


def unroll_slices(row_of, out):
    lane = iota((1, 128), 1)
    for pair in range(DH // 2):
        row = row_of(pair)
        out[2 * pair : 2 * pair + 1] = jnp.where(lane < SLICES, row, 0.0)
        out[2 * pair + 1 : 2 * pair + 2] = jnp.where(
            lane < SLICES, pltpu.roll(row, 128 - SLICES, 1), 0.0
        )


def opening_kernel(n_head, tiles, ids_ref, wfx_ref, wmid_ref, sm_ref, m_ref, v_ref, w_ref,
                   out_ref, wsb_ref, norm_ref, scal_ref, tables_ref, send_sem, recv_sem, slices_s, norm_s):
    me = lax.axis_index("head")
    barrier = pltpu.get_barrier_semaphore()
    for step in range(1, n_head):
        pl.semaphore_signal(
            barrier, inc=1, device_id={"head": lax.rem(me + step, n_head)}, device_id_type=MESH
        )
    out_ref[0, me] = wfx_ref[0]
    out_ref[1, me] = wmid_ref[0]
    pl.semaphore_wait(barrier, n_head - 1)
    copies = start_gather(n_head, [out_ref], send_sem, recv_sem)
    layers = sm_ref.shape[0]
    cap, deep = m_ref.shape[0], tables_ref.shape[0]
    for which, ref in enumerate((m_ref, v_ref, w_ref)):
        value = ref[...]
        if deep > cap:
            value = jnp.concatenate([value, jnp.zeros((deep - cap, BLOCK), f32)], axis=0)
        tables_ref[:, which * BLOCK : (which + 1) * BLOCK] = value.astype(b16)
    right = (iota((128, HS), 1) % SLICES == iota((128, HS), 0)).astype(b16)
    for layer in range(layers):
        unroll_slices(lambda pair: sm_ref[layer : layer + 1, 128 * pair : 128 * pair + 128], slices_s)
        wide = nn(slices_s[...].astype(b16), right)
        tiled = jnp.concatenate([wide] * HEADS, axis=0)
        wsb_ref[layer] = jnp.where(same_head(DH, SLICES, (D, HS)), tiled, 0.0).astype(b16)
        norm_s[...] = jnp.zeros_like(norm_s)
        for row in range(4):
            start = SMALL - 4 * D + row * D
            norm_s[row : row + 1] = sm_ref[layer : layer + 1, start : start + D]
        norm_ref[layer] = norm_s[...].T
    rows = ids_ref.shape[0] // n_head
    ids = ids_ref[pl.ds(pl.multiple_of(me * rows, rows), rows), :]
    for mesh in range(MESHES + 1):
        scal_ref[mesh] = jnp.sum((ids < mesh).astype(jnp.int32))
    deep = rows // tiles
    for tile in range(tiles):
        part = ids[tile * deep : (tile + 1) * deep]
        scal_ref[MESHES + 1 + 2 * tile] = jnp.min(part)
        scal_ref[MESHES + 2 + 2 * tile] = jnp.max(part)
    for copy in copies:
        copy.wait()


def opening(n_head, tiles, ids, w_fx, w_mid, small, tables):
    layers, part, _ = w_fx.shape
    deep = -(-tables[0].shape[0] // 16) * 16
    vmem = pl.BlockSpec(memory_space=pltpu.VMEM)
    return pl.pallas_call(
        functools.partial(opening_kernel, n_head, tiles),
        out_shape=(
            jax.ShapeDtypeStruct((2, n_head, part, D), b16),
            jax.ShapeDtypeStruct((layers, D, HS), b16),
            jax.ShapeDtypeStruct((layers, D, 128), f32),
            jax.ShapeDtypeStruct((MESHES + 1 + 2 * tiles,), jnp.int32),
            jax.ShapeDtypeStruct((deep, 3 * BLOCK), b16),
        ),
        in_specs=[vmem] * 7,
        out_specs=[vmem] * 3 + [pl.BlockSpec(memory_space=pltpu.SMEM), vmem],
        scratch_shapes=[
            pltpu.SemaphoreType.DMA((1, n_head - 1)),
            pltpu.SemaphoreType.DMA((1, n_head - 1)),
            pltpu.VMEM((DH, 128), f32),
            pltpu.VMEM((128, D), f32),
        ],
        compiler_params=pltpu.CompilerParams(
            collective_id=0, has_side_effects=True, vmem_limit_bytes=VMEM_BYTES
        ),
        name="opening",
    )(ids, w_fx, w_mid, small, *tables)


def place_of(sizes, shift):
    n_pts, n_head = sizes
    total = n_pts * n_head
    me = lax.axis_index("pts") * n_head + lax.axis_index("head")
    other = lax.rem(me + (shift + total), total)
    return (other // n_head, lax.rem(other, n_head))


def greet(sizes, window):
    barrier = pltpu.get_barrier_semaphore()
    for step in range(1, window + 1):
        for shift in (step, -step):
            pl.semaphore_signal(barrier, inc=1, device_id=place_of(sizes, shift), device_id_type=MESH)
    return barrier


def start_edges(sizes, window, edge_ref, out_ref, send_sem, recv_sem):
    copies = []
    for step in range(1, window + 1):
        for side, shift in ((1, step), (0, -step)):
            slot = step - 1 if side == 1 else window + step - 1
            copy = pltpu.make_async_remote_copy(
                src_ref=edge_ref.at[side],
                dst_ref=out_ref.at[slot],
                send_sem=send_sem.at[slot],
                recv_sem=recv_sem.at[slot],
                device_id=place_of(sizes, shift),
                device_id_type=MESH,
            )
            copy.start()
            copies.append(copy)
    return copies


def edge_kernel(sizes, window, edge_ref, out_ref, send_sem, recv_sem):
    barrier = greet(sizes, window)
    pl.semaphore_wait(barrier, 2 * window)
    for copy in start_edges(sizes, window, edge_ref, out_ref, send_sem, recv_sem):
        copy.wait()


def edge_weights_kernel(sizes, window, layer, pieces, edge_ref, wfx_ref, wmid_ref, wout_ref, sm_ref,
                        out_ref, w_ref, wqb_ref,
                        send_sem, recv_sem, wsend_sem, wrecv_sem, square_s):
    n_head = sizes[1]
    me = lax.axis_index("head")
    barrier = greet(sizes, window)
    for step in range(1, n_head):
        pl.semaphore_signal(
            barrier, inc=1, device_id={"head": lax.rem(me + step, n_head)}, device_id_type=MESH
        )
    refs = (wfx_ref, wmid_ref, wout_ref)
    for index, (kind, which) in enumerate(pieces):
        w_ref[index, me] = refs[kind][which]
    pl.semaphore_wait(barrier, 2 * window + n_head - 1)
    copies = start_edges(sizes, window, edge_ref, out_ref, send_sem, recv_sem)
    copies += start_gather(n_head, [w_ref], wsend_sem, wrecv_sem)
    lane = iota((1, 128), 1)
    for part in range(3):
        start = DH * SLICES + part * DH * DH
        for group in range(DH // 4):
            row = sm_ref[layer : layer + 1, start + 128 * group : start + 128 * group + 128]
            for inner in range(4):
                moved = row if inner == 0 else pltpu.roll(row, 128 - DH * inner, 1)
                square_s[4 * group + inner : 4 * group + inner + 1] = jnp.where(
                    lane < DH, moved, 0.0
                )
        square = square_s[...]
        for turn in range(1, 128 // DH):
            square = square + pltpu.roll(square_s[...], DH * turn, 1)
        square = jnp.concatenate([square] * (D // 128), axis=1)
        square = jnp.concatenate([square] * HEADS, axis=0)
        wqb_ref[:, part * D : (part + 1) * D] = jnp.where(
            same_head(DH, DH, (D, D)), square, 0.0
        )
    for copy in copies:
        copy.wait()


def edge_pick_kernel(sizes, window, cap, edge_ref, owner_ref, tables_ref,
                     out_ref, chosen_ref, row_ref, send_sem, recv_sem, tables_s, local_sem):
    barrier = greet(sizes, window)
    load = pltpu.make_async_copy(tables_ref, tables_s, local_sem)
    load.start()
    pl.semaphore_wait(barrier, 2 * window)
    copies = start_edges(sizes, window, edge_ref, out_ref, send_sem, recv_sem)
    blocks = owner_ref.shape[1]
    deep = tables_s.shape[0] // sizes[0]
    across = jnp.broadcast_to(owner_ref[...].astype(f32), (blocks, blocks))
    down = across.T
    low, high = iota((blocks, blocks), 0), iota((blocks, blocks), 1)
    same = across == down
    slot_down = jnp.sum(jnp.where(same & (high < low), 1.0, 0.0), axis=1, keepdims=True)
    slot_across = jnp.sum(jnp.where(same & (low < high), 1.0, 0.0), axis=0, keepdims=True)
    mine = owner_ref[...] == lax.axis_index("pts")
    row_ref[...] = jnp.broadcast_to(
        jnp.where(mine, slot_across.astype(jnp.int32), -1), row_ref.shape
    )
    target = (down[:, :1] * deep + slot_down).astype(jnp.int32)
    pick = (iota((blocks, tables_s.shape[0]), 1) == target).astype(b16)
    load.wait()
    step = 1024

    def choose(part, carry):
        lanes = pl.ds(pl.multiple_of(part * step, step), step)
        chosen_ref[:, lanes] = nn(pick, tables_s[:, lanes]).astype(b16)
        return carry

    lax.fori_loop(0, tables_s.shape[1] // step, choose, 0)
    for copy in copies:
        copy.wait()


def swap_edges_pick(sizes, window, cap, edge, owner, tables, collective_id):
    _, rows, width = edge.shape
    blocks = owner.shape[1]
    vmem = pl.BlockSpec(memory_space=pltpu.VMEM)
    return pl.pallas_call(
        functools.partial(edge_pick_kernel, sizes, window, cap),
        out_shape=(
            jax.ShapeDtypeStruct((2 * window, rows, width), b16),
            jax.ShapeDtypeStruct((blocks, tables.shape[1]), b16),
            jax.ShapeDtypeStruct((8, blocks), jnp.int32),
        ),
        in_specs=[vmem, vmem, pl.BlockSpec(memory_space=pl.ANY)],
        out_specs=[vmem] * 3,
        scratch_shapes=[
            pltpu.SemaphoreType.DMA((2 * window,)),
            pltpu.SemaphoreType.DMA((2 * window,)),
            pltpu.VMEM(tables.shape, b16),
            pltpu.SemaphoreType.DMA,
        ],
        compiler_params=pltpu.CompilerParams(
            collective_id=collective_id, has_side_effects=True, vmem_limit_bytes=VMEM_BYTES
        ),
        name="swap_edges_pick",
    )(edge, owner, tables)


def edge_call(window, collective_id, rows, width, body, extra, outs, scratch, name):
    vmem = pl.BlockSpec(memory_space=pltpu.VMEM)
    outs = [jax.ShapeDtypeStruct((2 * window, rows, width), b16)] + outs
    return pl.pallas_call(
        body,
        out_shape=outs,
        in_specs=[vmem] * (1 + extra),
        out_specs=[vmem] * len(outs),
        scratch_shapes=[
            pltpu.SemaphoreType.DMA((2 * window,)),
            pltpu.SemaphoreType.DMA((2 * window,)),
        ]
        + scratch,
        compiler_params=pltpu.CompilerParams(
            collective_id=collective_id, has_side_effects=True, vmem_limit_bytes=VMEM_BYTES
        ),
        name=name,
    )


def swap_edges(sizes, window, edge, collective_id):
    _, rows, width = edge.shape
    return edge_call(
        window, collective_id, rows, width,
        functools.partial(edge_kernel, sizes, window), 0, [], [], "swap_edges",
    )(edge)[0]


def swap_edges_weights(sizes, window, layer, pieces, edge, w_fx, w_mid, w_out, small, collective_id):
    _, rows, width = edge.shape
    n_head = sizes[1]
    part = w_fx.shape[1]
    return edge_call(
        window, collective_id, rows, width,
        functools.partial(edge_weights_kernel, sizes, window, layer, pieces), 4,
        [
            jax.ShapeDtypeStruct((len(pieces), n_head, part, D), b16),
            jax.ShapeDtypeStruct((D, 3 * D), f32),
        ],
        [
            pltpu.SemaphoreType.DMA((1, n_head - 1)),
            pltpu.SemaphoreType.DMA((1, n_head - 1)),
            pltpu.VMEM((DH, 128), f32),
        ],
        "swap_edges_weights",
    )(edge, w_fx, w_mid, w_out, small)


def pts_copies(n_pts, source, target, send_sem, recv_sem):
    pts, head = lax.axis_index("pts"), lax.axis_index("head")
    copies = []
    for step in range(1, n_pts):
        peer = lax.rem(pts + step, n_pts)
        copies.append(
            pltpu.make_async_remote_copy(
                src_ref=source(step, peer),
                dst_ref=target(step, peer),
                send_sem=send_sem.at[step - 1],
                recv_sem=recv_sem.at[step - 1],
                device_id=(peer, head),
                device_id_type=MESH,
            )
        )
    return copies


def edge_sums_kernel(sizes, window, edge_ref, ga_ref, out_ref, ta_ref,
                     send_sem, recv_sem, a_send, a_recv, a_send2, a_recv2, got_a):
    n_pts, n_head = sizes
    pts, head = lax.axis_index("pts"), lax.axis_index("head")
    barrier = greet(sizes, window)
    for step in range(1, n_pts):
        pl.semaphore_signal(
            barrier, inc=1, device_id=(lax.rem(pts + step, n_pts), head), device_id_type=MESH
        )
    pl.semaphore_wait(barrier, 2 * window + n_pts - 1)
    edges = start_edges(sizes, window, edge_ref, out_ref, send_sem, recv_sem)
    gather = pts_copies(
        n_pts,
        lambda step, peer: ga_ref.at[peer],
        lambda step, peer: got_a.at[step - 1],
        a_send,
        a_recv,
    )
    for copy in gather:
        copy.start()
    for copy in gather:
        copy.wait()
    total = ga_ref[pts].astype(f32)
    for index in range(n_pts - 1):
        total = total + got_a[index].astype(f32)
    ta_ref[pts] = total.astype(b16)
    share = pts_copies(
        n_pts,
        lambda step, peer: ta_ref.at[pts],
        lambda step, peer: ta_ref.at[pts],
        a_send2,
        a_recv2,
    )
    for copy in share:
        copy.start()
    for copy in edges:
        copy.wait()
    for copy in share:
        copy.wait()


def swap_edges_sums(sizes, window, edge, ga, collective_id):
    _, rows, width = edge.shape
    n_pts = sizes[0]
    dma = pltpu.SemaphoreType.DMA
    return edge_call(
        window, collective_id, rows, width,
        functools.partial(edge_sums_kernel, sizes, window), 1,
        [jax.ShapeDtypeStruct(ga.shape, b16)],
        [dma((n_pts - 1,))] * 4 + [pltpu.VMEM((n_pts - 1,) + ga.shape[1:], b16)],
        "swap_edges_sums",
    )(edge, ga)


def norm_stats(values):
    center = jnp.mean(values, axis=0, keepdims=True)
    spread = values - center
    scale = lax.rsqrt(jnp.mean(spread * spread, axis=0, keepdims=True) + norm_eps)
    return (spread * scale, scale)


def norm_back(grad_out, scaled, scale, gain):
    inner = grad_out * gain
    return scale * (
        inner
        - jnp.mean(inner, axis=0, keepdims=True)
        - scaled * jnp.mean(inner * scaled, axis=0, keepdims=True)
    )


def group_sum(values):
    return jnp.sum(values.reshape(HEADS, SLICES, values.shape[1]), axis=1, keepdims=True)


def fold_lanes(values):
    total = values[:, :128]
    for start in range(128, values.shape[1], 128):
        total = total + values[:, start : start + 128]
    return total


def tile_mask(scal, mesh, tile, width):
    spot = iota((1, width), 1) + tile * width
    return (spot >= scal[mesh]) & (spot < scal[mesh + 1])


def tile_range(scal, tiles, tile):
    base = MESHES + 1
    ratio = (scal.shape[0] - base) // 2 // tiles
    return (scal[base + 2 * ratio * tile], scal[base + 2 * ratio * (tile + 1) - 1])


def front_tile(scal, tiles, tile, x, wfm, wsb, norms, vh_ref, rs_ref, u_ref, f_ref, m_ref, p_ref, sums):
    width = x.shape[1]
    scaled, scale = norm_stats(x)
    vh_ref[...] = scaled.astype(b16)
    rs_ref[...] = jnp.broadcast_to(scale, (8, width))
    normed = (scaled * norms[:, 0:1] + norms[:, 1:2]).astype(b16)
    u_ref[...] = normed
    joint = nn(wfm, normed)
    feats = joint[:D].astype(b16)
    middle = joint[D:].astype(b16)
    f_ref[...] = feats
    m_ref[...] = middle
    logits = tn(wsb, middle).reshape(HEADS, SLICES, width)
    top = jnp.max(logits, axis=1, keepdims=True)
    expo = jnp.exp(logits - top)
    weights = expo / jnp.sum(expo, axis=1, keepdims=True)
    weights_r = weights.reshape(HS, width).astype(b16)
    p_ref[...] = weights_r
    low, high = tile_range(scal, tiles, tile)

    def add(mesh, carry):
        keep = tile_mask(scal, mesh, tile, width).astype(b16)
        wide = jnp.concatenate(
            [feats * keep, jnp.broadcast_to(keep, (128, width))], axis=0
        )
        full = nt(weights_r, wide)
        sums[mesh, :, :D] += pick_diag(full[:, :D], DH)
        sums[mesh, :, D:] += pick_diag(full[:, D:], 16)
        return carry

    lax.fori_loop(low, high + 1, add, 0)


def present(scal, tiles, body):
    def one(mesh, carry):
        body(mesh)
        return carry

    lax.fori_loop(tile_range(scal, tiles, 0)[0], tile_range(scal, tiles, tiles - 1)[1] + 1, one, 0)


def ends_of(scal, tiles):
    return (tile_range(scal, tiles, 0)[0], tile_range(scal, tiles, tiles - 1)[1])


def between(scal, tiles, body):
    first, last = ends_of(scal, tiles)

    def one(mesh, carry):
        body(mesh)
        return carry

    lax.fori_loop(first + 1, last, one, 0)


def fetch(source, target, sem):
    copy = pltpu.make_async_copy(source, target, sem)
    copy.start()
    copy.wait()


def clear_present(scal, tiles, sums):
    def clear(mesh):
        sums[mesh] = jnp.zeros(sums.shape[1:], f32)

    present(scal, tiles, clear)


def write_edges(scal, tiles, sums, edge_ref, ends_ref, sums_hbm, sem):
    first, last = ends_of(scal, tiles)
    extra = EDGE - SLICES
    for side, mesh in ((0, first), (1, last)):
        ends_ref[side] = sums[mesh]
        edge_ref[side, :SLICES] = sums[mesh, :, :D].astype(b16)
        rows = jnp.zeros((extra, D), f32)
        if sums.shape[2] > D:
            counts = jnp.concatenate(
                [sums[mesh, :, D:], jnp.zeros((D - SLICES, 128), f32)], axis=0
            )
            pick = (iota((extra, 128), 1) == 16 * iota((extra, 128), 0)).astype(f32)
            rows = nt(pick, counts, HIGH)
        edge_ref[side, SLICES:] = jnp.where(
            iota((extra, D), 0) >= HEADS, mesh.astype(f32), rows
        ).astype(b16)
    between(scal, tiles, lambda mesh: fetch(sums.at[mesh], sums_hbm.at[mesh], sem))


def add_edges(own, mesh, recv_ref):
    wanted = mesh.astype(f32)
    total = jnp.zeros((EDGE, D), f32)
    for slot in range(recv_ref.shape[0]):
        match = recv_ref[slot, SLICES + HEADS : SLICES + HEADS + 1].astype(f32) == wanted
        total = total + jnp.where(match, recv_ref[slot].astype(f32), 0.0)
    if own.shape[1] == D:
        return own + total[:SLICES]
    extra = EDGE - SLICES
    spread = (iota((extra, 128), 1) // 16 == iota((extra, 128), 0)).astype(f32)
    counts = tn(total[SLICES:, :SLICES], spread, HIGH)
    return own + jnp.concatenate([total[:SLICES], counts], axis=1)


def attend_parts(totals, wqb):
    expand = (iota((128, D), 0) == 16 * (iota((128, D), 1) // DH)).astype(f32)
    total = jnp.concatenate(totals, axis=0)
    count = nn(total[:, D:], expand, HIGH)
    slice_tok = total[:, :D] / count
    triple = nn(slice_tok, wqb, HIGH)
    parts = []
    for index in range(len(totals)):
        rows = slice(index * SLICES, (index + 1) * SLICES)
        queries = triple[rows, :D]
        key_wide = spread_diag(triple[rows, D : 2 * D])
        value_wide = spread_diag(triple[rows, 2 * D :])
        scores = (nt(key_wide, queries, HIGH) * (1.0 / math.sqrt(DH))).reshape(
            HEADS, SLICES, SLICES
        )
        expo = jnp.exp(scores - jnp.max(scores, axis=1, keepdims=True))
        prob = (expo / jnp.sum(expo, axis=1, keepdims=True)).reshape(HS, SLICES)
        parts.append((queries, key_wide, value_wide, prob))
    return (slice_tok, count, triple, parts)


def attend_all(scal, tiles, ends_ref, recv_ref, sums_hbm, wqb, attended_ref, kept_ref, prob_ref, spare, sem):
    ends = ends_of(scal, tiles)
    totals = [add_edges(ends_ref[side], mesh, recv_ref) for side, mesh in enumerate(ends)]
    slice_tok, count, triple, parts = attend_parts(totals, wqb)
    kept = jnp.concatenate([slice_tok, count, triple], axis=1)
    results = []
    for side, (_, _, value_wide, prob) in enumerate(parts):
        results.append(tn(prob, value_wide, HIGH).astype(b16))
        kept_ref[side] = kept[side * SLICES : (side + 1) * SLICES]
        prob_ref[side] = prob
    for mesh, result in zip(ends, results):
        attended_ref[mesh] = result

    def inner(mesh):
        fetch(sums_hbm.at[mesh], spare, sem)
        _, _, _, parts = attend_parts([spare[...]], wqb)
        attended_ref[mesh] = tn(parts[0][3], parts[0][2], HIGH).astype(b16)

    between(scal, tiles, inner)


def spread_tile(scal, tiles, tile, wide_ref, p_ref, spread):
    low, high = tile_range(scal, tiles, tile)
    weights_r = p_ref[...]
    width = weights_r.shape[1]

    def one(mesh, carry):
        keep = tile_mask(scal, mesh, tile, width)
        spread[...] = jnp.where(keep, tn(spread_diag(wide_ref[mesh]), weights_r), spread[...])
        return carry

    lax.fori_loop(low, high + 1, one, 0)
    return spread[...].astype(b16)


GELU_A = math.sqrt(2.0 / math.pi)
GELU_B = 0.044715


def gelu_pair(hidden):
    square = hidden * hidden
    bend = jnp.tanh(hidden * (GELU_A + (GELU_A * GELU_B) * square))
    half = 0.5 + 0.5 * bend
    value = hidden * half
    slope = half + (0.5 * hidden) * (1.0 - bend * bend) * (
        GELU_A + (3.0 * GELU_A * GELU_B) * square
    )
    return (value, slope)


CHUNK = 1024


def mlp_back_tile(scal, tiles, tile, grad, slopes, actives, scaled_two, scale_two, normed_two_r, spread_r,
                  weights_r, wout, wup, wdown, norms, d2_ref, de_ref, sums,
                  gup, gdown, gout, gnorm):
    width = grad.shape[1]
    grad_r = grad.astype(b16)
    grad_normed = jnp.zeros((D, width), f32)
    for start in range(0, FF, CHUNK):
        part = slice(start, start + CHUNK)
        back = (slopes(part) * nn(wdown[part], grad_r)).astype(b16)
        gup[:, part] += nt(normed_two_r, back)
        gdown[:, part] += nt(grad_r, actives(part))
        grad_normed = grad_normed + nn(wup[:, part], back)
    gnorm[2] += fold_lanes(grad_normed * scaled_two)
    gnorm[3] += fold_lanes(grad_normed)
    grad_middle = grad + norm_back(grad_normed, scaled_two, scale_two, norms[:, 2:3])
    d2_ref[...] = grad_middle
    branch_r = grad_middle.astype(b16)
    gout[...] += nt(spread_r, branch_r)
    spread_grad = nn(wout, branch_r).astype(b16)
    de_ref[...] = spread_grad
    low, high = tile_range(scal, tiles, tile)

    def add(mesh, carry):
        keep = tile_mask(scal, mesh, tile, width).astype(b16)
        sums[mesh] += pick_diag(nt(weights_r, spread_grad * keep), DH)
        return carry

    lax.fori_loop(low, high + 1, add, 0)


def attend_back(meshes, shares, slice_tok, count, parts, outer, wqb, both, dcount, gqkv):
    root = 1.0 / math.sqrt(DH)
    attended, triples = [], []
    for (queries, key_wide, value_wide, prob), grad in zip(parts, outer):
        attended.append(tn(prob, value_wide, HIGH).astype(b16))
        inner = prob * nt(value_wide, grad, HIGH)
        mixed = group_sum(inner)
        grad_scores = root * (
            inner - (prob.reshape(HEADS, SLICES, SLICES) * mixed).reshape(HS, SLICES)
        )
        triples.append(
            jnp.concatenate(
                [
                    tn(grad_scores, key_wide, HIGH),
                    pick_diag(nn(grad_scores, queries, HIGH), DH),
                    pick_diag(nn(prob, grad, HIGH), DH),
                ],
                axis=1,
            )
        )
    triple = jnp.concatenate(triples, axis=0)
    grad_sum = nt(triple, wqb, HIGH) / count
    grad_count = -(grad_sum * slice_tok)
    gqkv[...] += tn(slice_tok * jnp.concatenate(shares, axis=0), triple, HIGH)
    for index, mesh in enumerate(meshes):
        rows = slice(index * SLICES, (index + 1) * SLICES)
        both[mesh, :, :D] = spread_diag(attended[index])
        both[mesh, :, D:] = spread_diag(grad_sum[rows].astype(b16))
        column = jnp.sum(spread_diag(grad_count[rows]), axis=1, keepdims=True)
        dcount[mesh] = jnp.broadcast_to(column, (HS, 128))


def attend_back_all(scal, tiles, kept_ref, prob_ref, recv_ref, ends_ref, grad_recv_ref, sums_hbm, grads_hbm,
                    wqb, both, dcount, gqkv, spare, spare_grad, sem):
    ends = ends_of(scal, tiles)
    outer = [add_edges(ends_ref[side], mesh, grad_recv_ref) for side, mesh in enumerate(ends)]
    kept = jnp.concatenate([kept_ref[0], kept_ref[1]], axis=0)
    parts = []
    for side in range(2):
        parts.append(
            (
                kept_ref[side, :, 2 * D : 3 * D],
                spread_diag(kept_ref[side, :, 3 * D : 4 * D]),
                spread_diag(kept_ref[side, :, 4 * D :]),
                prob_ref[side],
            )
        )
    previous = recv_ref[0, SLICES + HEADS : SLICES + HEADS + 1, :1].astype(f32)
    shares = [
        jnp.broadcast_to(1.0 - (previous == ends[0].astype(f32)).astype(f32), (SLICES, 1)),
        jnp.broadcast_to((ends[1] != ends[0]).astype(f32), (SLICES, 1)),
    ]
    attend_back(ends, shares, kept[:, :D], kept[:, D : 2 * D], parts, outer, wqb, both, dcount, gqkv)

    def inner(mesh):
        fetch(sums_hbm.at[mesh], spare, sem)
        fetch(grads_hbm.at[mesh], spare_grad, sem)
        slice_tok, count, _, parts = attend_parts([spare[...]], wqb)
        attend_back(
            (mesh,), [jnp.ones((SLICES, 1), f32)], slice_tok, count, parts, [spare_grad[...]], wqb, both, dcount, gqkv
        )

    between(scal, tiles, inner)


def attend_back_tile(scal, tiles, tile, both, dcount, de_ref, f_ref, m_ref, p_ref, u_ref, vh_ref, rs_ref,
                     d2_ref, wfm, wsb, norms, grad_p, grad_f, gfm, gws, gnorm):
    low, high = tile_range(scal, tiles, tile)
    weights_r = p_ref[...]
    width = weights_r.shape[1]
    pair = jnp.concatenate([de_ref[...], f_ref[...]], axis=0)

    def one(mesh, carry):
        keep = tile_mask(scal, mesh, tile, width)
        back = nn(both[mesh], pair) + dcount[mesh][:, :1]
        grad_p[...] = jnp.where(keep, back, grad_p[...])
        grad_f[...] = jnp.where(keep, tn(both[mesh, :, D:], weights_r), grad_f[...])
        return carry

    lax.fori_loop(low, high + 1, one, 0)
    weights = weights_r.astype(f32)
    inner = weights * grad_p[...]
    mixed = group_sum(inner)
    grad_logits = (
        inner - (weights.reshape(HEADS, SLICES, width) * mixed).reshape(HS, width)
    ).astype(b16)
    gws[...] += nt(m_ref[...], grad_logits)
    grad_m = nn(wsb, grad_logits).astype(b16)
    grad_fm = jnp.concatenate([grad_f[...].astype(b16), grad_m], axis=0)
    gfm[...] += nt(u_ref[...], grad_fm)
    grad_normed = tn(wfm, grad_fm)
    scaled = vh_ref[...].astype(f32)
    gnorm[0] += fold_lanes(grad_normed * scaled)
    gnorm[1] += fold_lanes(grad_normed)
    return d2_ref[...] + norm_back(grad_normed, scaled, rs_ref[:1], norms[:, 0:1])


def small_rows(base, gws, gqkv, scratch, out_ref):
    lane = iota((1, 128), 1)
    left = repeat_rows(DH)
    fold = (iota((128, HS), 1) % SLICES == iota((128, HS), 0)).astype(f32)
    kept = jnp.where(same_head(DH, SLICES, (D, HS)), gws[...], 0.0)
    scratch[...] = nt(tn(left, kept, HIGH), fold, HIGH)
    even = scratch[pl.ds(0, DH // 2, stride=2), :]
    odd = scratch[pl.ds(1, DH // 2, stride=2), :]
    out_ref[base : base + DH // 2] = jnp.where(lane < SLICES, even, pltpu.roll(odd, SLICES, 1))
    fold = (iota((D, 128), 0) % DH == iota((D, 128), 1)).astype(f32)
    for part in range(3):
        square = jnp.where(same_head(DH, DH, (D, D)), gqkv[:, part * D : (part + 1) * D], 0.0)
        scratch[...] = nn(tn(left, square, HIGH), fold, HIGH)
        total = scratch[pl.ds(0, DH // 4, stride=4), :]
        for inner in range(1, 4):
            total = total + pltpu.roll(scratch[pl.ds(inner, DH // 4, stride=4), :], DH * inner, 1)
        start = base + DH // 2 + part * (DH // 4)
        out_ref[start : start + DH // 4] = total


NORM_ROW = (SMALL - 4 * D) // 128
LAYER_ROWS = SMALL // 128


def norm_rows(gnorm, index, out_ref, base):
    lane = iota((D, 128), 1)
    total = jnp.zeros((D, 128), f32)
    for column, row in enumerate(index):
        total = total + jnp.where(lane == column, jnp.sum(gnorm[row], axis=1, keepdims=True), 0.0)
    flat = total.T
    for column in range(len(index)):
        for half in range(D // 128):
            place = base + column * (D // 128) + half
            out_ref[place : place + 1] = flat[column : column + 1, 128 * half : 128 * half + 128]


def pack_front(gfm, head):
    lane = iota((D, 128), 1)
    start = (head // 2) * 128
    feats, middle = gfm[:, start : start + 128], gfm[:, D + start : D + start + 128]
    if head % 2 == 0:
        return jnp.where(lane < 64, feats, pltpu.roll(middle, 64, 1))
    return jnp.where(lane < 64, pltpu.roll(feats, 64, 1), middle)


def store_pieces(out_ref, head, base, value):
    size = out_ref.shape[2]
    done = 0
    while done < value.shape[0]:
        chunk, offset = divmod(base + done, size)
        count = min(size - offset, value.shape[0] - done)
        for half in range(2):
            out_ref[head, 2 * chunk + half, offset : offset + count] = value[
                done : done + count, 128 * half : 128 * half + 128
            ]
        done += count


def pack_rest(gout, gup, gdown, out_ref, base, n_head):
    for head in range(n_head):
        deep, wide = D // n_head, FF // n_head
        store_pieces(out_ref, head, base, gout[head * deep : (head + 1) * deep].astype(b16))
        start = base + deep
        store_pieces(out_ref, head, start, gup[:, head * wide : (head + 1) * wide].astype(b16))
        store_pieces(out_ref, head, start + D, gdown[:, head * wide : (head + 1) * wide].astype(b16))


def first_kernel(tiles, scal, tok_ref, wfm_ref, wsb_ref, norm_ref,
                 xt_ref, vh_ref, rs_ref, u_ref, f_ref, m_ref, p_ref, sums_hbm, edge_ref, ends_ref, sums, sem):
    tile = pl.program_id(0)

    @pl.when(tile == 0)
    def _():
        clear_present(scal, tiles, sums)

    x = tok_ref[...].astype(f32).T
    xt_ref[...] = x.astype(b16)
    front_tile(scal, tiles, tile, x, wfm_ref[...], wsb_ref[...], norm_ref[...],
               vh_ref, rs_ref, u_ref, f_ref, m_ref, p_ref, sums)

    @pl.when(tile == tiles - 1)
    def _():
        write_edges(scal, tiles, sums, edge_ref, ends_ref, sums_hbm, sem)


def second_kernel(tiles, scal, xt_ref, p0_ref, sums0_hbm, ends0_ref, recv_ref, wout_ref, wup_ref, wdown_ref, wqb_ref, norm0_ref,
                  wfm_ref, wsb_ref, norm1_ref,
                  e_ref, vh2_ref, rs2_ref, u2_ref, gp_ref, z_ref, kept_ref, prob_ref,
                  x1_ref, vh_ref, rs_ref, u_ref, f_ref, m_ref, p_ref, sums_hbm, edge_ref, ends_ref,
                  wide, spread, spare, sums, sem):
    tile = pl.program_id(0)

    @pl.when(tile == 0)
    def _():
        attend_all(scal, tiles, ends0_ref, recv_ref, sums0_hbm, wqb_ref[...], wide, kept_ref, prob_ref, spare, sem)
        clear_present(scal, tiles, sums)

    norms = norm0_ref[...]
    spread_r = spread_tile(scal, tiles, tile, wide, p0_ref, spread)
    e_ref[...] = spread_r
    middle = xt_ref[...].astype(f32) + tn(wout_ref[...], spread_r)
    scaled_two, scale_two = norm_stats(middle)
    vh2_ref[...] = scaled_two.astype(b16)
    rs2_ref[...] = jnp.broadcast_to(scale_two, rs2_ref.shape)
    normed_two_r = (scaled_two * norms[:, 2:3] + norms[:, 3:4]).astype(b16)
    u2_ref[...] = normed_two_r
    x = middle
    for start in range(0, FF, CHUNK):
        part = slice(start, start + CHUNK)
        active, slope = gelu_pair(tn(wup_ref[:, part], normed_two_r))
        active_r = active.astype(b16)
        z_ref[part] = active_r
        gp_ref[part] = slope.astype(b16)
        x = x + tn(wdown_ref[part], active_r)
    x1_ref[...] = x
    front_tile(scal, tiles, tile, x, wfm_ref[...], wsb_ref[...], norm1_ref[...],
               vh_ref, rs_ref, u_ref, f_ref, m_ref, p_ref, sums)

    @pl.when(tile == tiles - 1)
    def _():
        write_edges(scal, tiles, sums, edge_ref, ends_ref, sums_hbm, sem)


def third_kernel(n_head, packed, tiles, scal, x1_ref, p_ref, sums1_hbm, ends1_ref, recv_ref, cot_ref, wout_ref, wup_ref, wdown_ref, wqb_ref, norm_ref,
                 out_ref, d2_ref, de_ref, kept_ref, prob_ref, grads_hbm, edge_ref, ends_ref,
                 gn_ref, *rest):
    grad_outs, (wide, spread, spare, grads, sem, gnorm, slope_s, active_s, gup, gdown, gout) = rest[:-11], rest[-11:]
    tile = pl.program_id(0)

    @pl.when(tile == 0)
    def _():
        clear_present(scal, tiles, grads)
        gup[...] = jnp.zeros_like(gup)
        gdown[...] = jnp.zeros_like(gdown)
        gout[...] = jnp.zeros_like(gout)
        gnorm[...] = jnp.zeros_like(gnorm)
        attend_all(scal, tiles, ends1_ref, recv_ref, sums1_hbm, wqb_ref[...], wide, kept_ref, prob_ref, spare, sem)

    norms = norm_ref[...]
    spread_r = spread_tile(scal, tiles, tile, wide, p_ref, spread)
    middle = x1_ref[...] + tn(wout_ref[...], spread_r)
    scaled_two, scale_two = norm_stats(middle)
    normed_two_r = (scaled_two * norms[:, 2:3] + norms[:, 3:4]).astype(b16)
    x = middle
    for start in range(0, FF, CHUNK):
        part = slice(start, start + CHUNK)
        active, slope = gelu_pair(tn(wup_ref[:, part], normed_two_r))
        active_r = active.astype(b16)
        active_s[part] = active_r
        slope_s[part] = slope
        x = x + tn(wdown_ref[part], active_r)
    out_ref[...] = x.T.astype(b16)
    grad = cot_ref[...].astype(f32).T
    mlp_back_tile(scal, tiles, tile, grad, lambda part: slope_s[part], lambda part: active_s[part],
                  scaled_two, scale_two, normed_two_r, spread_r, p_ref[...],
                  wout_ref[...], wup_ref, wdown_ref, norms, d2_ref, de_ref, grads,
                  gup, gdown, gout, gnorm)

    @pl.when(tile == tiles - 1)
    def _():
        write_edges(scal, tiles, grads, edge_ref, ends_ref, grads_hbm, sem)
        norm_rows(gnorm, (2, 3), gn_ref, 0)
        if packed:
            pack_rest(gout, gup, gdown, grad_outs[0], 0, n_head)
        else:
            for ref, total in zip(grad_outs, (gup, gdown, gout)):
                ref[...] = total[...].astype(b16)


def fourth_kernel(n_head, packed, tiles, scal, sums1_hbm, kept_ref, prob_ref, recv_ref, grads1_hbm, ends1_ref, grad_recv_ref, de1_ref, f_ref, m_ref, p1_ref, u_ref, vh_ref, rs_ref, d21_ref,
                  wfm_ref, wsb_ref, wqb_ref, norm1_ref,
                  gp_ref, z_ref, vh2_ref, rs2_ref, u2_ref, e_ref, p0_ref, wout_ref, wup_ref, wdown_ref, norm0_ref, gn1b_ref,
                  d2_ref, de_ref, grads_hbm, edge_ref, ends_ref, small_ref, gn0_ref, *rest):
    grad_outs = rest[:-16]
    spare, spare_grad, sem, grads, both, dcount, grad_p, grad_f, gws, gqkv, gnorm, fold_s, gfm, gup, gdown, gout = rest[-16:]
    tile = pl.program_id(0)

    @pl.when(tile == 0)
    def _():
        for ref in (gfm, gws, gqkv, gup, gdown, gout, gnorm):
            ref[...] = jnp.zeros_like(ref)
        attend_back_all(scal, tiles, kept_ref, prob_ref, recv_ref, ends1_ref, grad_recv_ref, sums1_hbm, grads1_hbm,
                        wqb_ref[...], both, dcount, gqkv, spare, spare_grad, sem)
        clear_present(scal, tiles, grads)

    grad = attend_back_tile(scal, tiles, tile, both, dcount, de1_ref, f_ref, m_ref, p1_ref, u_ref, vh_ref, rs_ref,
                            d21_ref, wfm_ref[...], wsb_ref[...], norm1_ref[...], grad_p, grad_f, gfm, gws, gnorm)
    mlp_back_tile(scal, tiles, tile, grad, lambda part: gp_ref[part].astype(f32), lambda part: z_ref[part],
                  vh2_ref[...].astype(f32), rs2_ref[:1], u2_ref[...], e_ref[...], p0_ref[...],
                  wout_ref[...], wup_ref, wdown_ref, norm0_ref[...], d2_ref, de_ref, grads,
                  gup, gdown, gout, gnorm)

    @pl.when(tile == tiles - 1)
    def _():
        write_edges(scal, tiles, grads, edge_ref, ends_ref, grads_hbm, sem)
        small_rows(0, gws, gqkv, fold_s, small_ref)
        norm_rows(gnorm, (0, 1), small_ref, NORM_ROW)
        small_ref[NORM_ROW + 4 :] = gn1b_ref[...]
        norm_rows(gnorm, (2, 3), gn0_ref, 0)
        if packed:
            for head in range(n_head):
                front = pack_front(gfm, head).astype(b16)
                store_pieces(
                    grad_outs[0], head, 0, jnp.concatenate([front[: D // 2], front[D // 2 :]], axis=1)
                )
            pack_rest(gout, gup, gdown, grad_outs[0], D // 2, n_head)
        else:
            for ref, total in zip(grad_outs, (gfm, gup, gdown, gout)):
                ref[...] = total[...].astype(b16)


def fifth_kernel(n_head, packed, tiles, scal, sums0_hbm, kept_ref, prob_ref, recv_ref, grads0_hbm, ends0_ref, grad_recv_ref, de_ref, f_ref, m_ref, p_ref, u_ref, vh_ref, rs_ref, d2_ref,
                 wfm_ref, wsb_ref, wqb_ref, norm_ref, gn0b_ref, small1_ref,
                 gin_ref, small_ref, front_ref,
                 spare, spare_grad, sem, both, dcount, grad_p, grad_f, gws, gqkv, gnorm, fold_s, gfm):
    tile = pl.program_id(0)

    @pl.when(tile == 0)
    def _():
        for ref in (gfm, gws, gqkv, gnorm):
            ref[...] = jnp.zeros_like(ref)
        attend_back_all(scal, tiles, kept_ref, prob_ref, recv_ref, ends0_ref, grad_recv_ref, sums0_hbm, grads0_hbm,
                        wqb_ref[...], both, dcount, gqkv, spare, spare_grad, sem)

    grad = attend_back_tile(scal, tiles, tile, both, dcount, de_ref, f_ref, m_ref, p_ref, u_ref, vh_ref, rs_ref,
                            d2_ref, wfm_ref[...], wsb_ref[...], norm_ref[...], grad_p, grad_f, gfm, gws, gnorm)
    gin_ref[...] = grad.T

    @pl.when(tile == tiles - 1)
    def _():
        small_rows(0, gws, gqkv, fold_s, small_ref)
        norm_rows(gnorm, (0, 1), small_ref, NORM_ROW)
        small_ref[NORM_ROW + 4 : LAYER_ROWS] = gn0b_ref[...]
        small_ref[LAYER_ROWS:] = small1_ref[...]
        if packed:
            for head in range(n_head):
                front_ref[head] = pack_front(gfm, head).astype(b16)
        else:
            front_ref[...] = gfm[...].astype(b16)


def sum_parts(own, got):
    total = own.astype(f32)
    for index in range(got.shape[0]):
        total = total + got[index].astype(f32)
    return total


def total_kernel(sizes, gb_ref, gc_ref, gs_ref, tb_ref, tc_ref, ts_ref,
                 got_b, got_c, got_s, mid_c, mid_s, got_c2, got_s2, head_sem, pts_sem):
    n_pts, n_head = sizes
    pts, head = lax.axis_index("pts"), lax.axis_index("head")
    c_rows = D // n_pts
    s_rows = gs_ref.shape[0] // n_head

    def part(index, rows):
        return pl.ds(pl.multiple_of(index * rows, rows), rows)

    def over(size, which, own, to, sem, source, target):
        copies = []
        for step in range(1, size):
            peer = lax.rem(own + step, size)
            copies.append(
                pltpu.make_async_remote_copy(
                    src_ref=source(peer),
                    dst_ref=target(step - 1),
                    send_sem=sem.at[0, which, step - 1],
                    recv_sem=sem.at[1, which, step - 1],
                    device_id=to(peer),
                    device_id_type=MESH,
                )
            )
        for copy in copies:
            copy.start()
        return copies

    def over_head(which, source, target):
        return over(n_head, which, head, lambda peer: (pts, peer), head_sem, source, target)

    def over_pts(which, source, target):
        return over(n_pts, which, pts, lambda peer: (peer, head), pts_sem, source, target)

    def finish(copies):
        for copy in copies:
            copy.wait()

    barrier = pltpu.get_barrier_semaphore()
    for step in range(1, n_head):
        pl.semaphore_signal(
            barrier, inc=1, device_id=(pts, lax.rem(head + step, n_head)), device_id_type=MESH
        )
    for step in range(1, n_pts):
        pl.semaphore_signal(
            barrier, inc=1, device_id=(lax.rem(pts + step, n_pts), head), device_id_type=MESH
        )
    pl.semaphore_wait(barrier, n_head - 1 + n_pts - 1)

    first_c = over_head(0, lambda peer: gc_ref.at[peer], lambda slot: got_c.at[slot])
    first_s = over_head(1, lambda peer: gs_ref.at[part(peer, s_rows)], lambda slot: got_s.at[slot])
    first_b = over_pts(0, lambda peer: gb_ref.at[peer], lambda slot: got_b.at[slot])
    finish(first_c)
    mid_c[...] = sum_parts(gc_ref[head], got_c).astype(b16)
    next_c = over_pts(1, lambda peer: mid_c.at[part(peer, c_rows)], lambda slot: got_c2.at[slot])
    finish(first_s)
    mid_s[...] = sum_parts(gs_ref[part(head, s_rows)], got_s)
    next_s = over_pts(2, lambda peer: mid_s, lambda slot: got_s2.at[slot])
    finish(next_c)
    mine_c = part(pts, c_rows)
    tc_ref[mine_c] = sum_parts(mid_c[mine_c], got_c2).astype(b16)
    last_c = over_pts(3, lambda peer: tc_ref.at[mine_c], lambda slot: tc_ref.at[mine_c])
    finish(next_s)
    mine_s = part(head, s_rows)
    ts_ref[mine_s] = sum_parts(mid_s[...], got_s2)
    last_s = over_head(2, lambda peer: ts_ref.at[mine_s], lambda slot: ts_ref.at[mine_s])
    finish(first_b)
    tb_ref[pts] = sum_parts(gb_ref[pts], got_b).astype(b16)
    last_b = over_pts(4, lambda peer: tb_ref.at[pts], lambda slot: tb_ref.at[pts])
    finish(last_c)
    finish(last_s)
    finish(last_b)


def total_gradients(sizes, gb, gc, gs):
    n_pts, n_head = sizes
    vmem = pl.BlockSpec(memory_space=pltpu.VMEM)
    dma = pltpu.SemaphoreType.DMA
    c_rows, s_rows = D // n_pts, gs.shape[0] // n_head
    return pl.pallas_call(
        functools.partial(total_kernel, sizes),
        out_shape=(
            jax.ShapeDtypeStruct(gb.shape, b16),
            jax.ShapeDtypeStruct(gc.shape[1:], b16),
            jax.ShapeDtypeStruct(gs.shape, f32),
        ),
        in_specs=[vmem] * 3,
        out_specs=[vmem] * 3,
        scratch_shapes=[
            pltpu.VMEM((n_pts - 1,) + gb.shape[1:], b16),
            pltpu.VMEM((n_head - 1,) + gc.shape[1:], b16),
            pltpu.VMEM((n_head - 1, s_rows, 128), f32),
            pltpu.VMEM(gc.shape[1:], b16),
            pltpu.VMEM((s_rows, 128), f32),
            pltpu.VMEM((n_pts - 1, c_rows, 128), b16),
            pltpu.VMEM((n_pts - 1, s_rows, 128), f32),
            dma((2, 3, n_head - 1)),
            dma((2, 5, n_pts - 1)),
        ],
        compiler_params=pltpu.CompilerParams(
            collective_id=3, has_side_effects=True, vmem_limit_bytes=VMEM_BYTES
        ),
        name="total_gradients",
    )(gb, gc, gs)


def update_kernel(ta_ref, tb_ref, tc_ref, ts_ref, row_ref, sel_ref, m_ref, v_ref, w_ref, sm_ref, sv_ref, sw_ref,
                  nm_ref, nv_ref, nw_ref, fresh_ref, om_ref, ov_ref, ow_ref, wide, tall, front, flat):
    lane = iota((8, 128), 1)

    def place_front(base):
        for pair in range(16):
            first = front[pl.ds(2 * pair, 8, stride=32), :]
            second = front[pl.ds(2 * pair + 1, 8, stride=32), :]
            columns = slice(128 * pair, 128 * pair + 128)
            wide[base : base + 8, columns] = jnp.where(lane < 64, first, pltpu.roll(second, 64, 1))
            wide[base + 8 : base + 16, columns] = jnp.where(lane < 64, pltpu.roll(first, 64, 1), second)

    def place_rest(base):
        for part in range(8):
            for half in range(2):
                wide[base : base + 72, 256 * part + 128 * half : 256 * part + 128 * half + 128] = tall[
                    half, pl.ds(part, 72, stride=8), :
                ]

    def fill(value, base):
        size = value.shape[1]
        row = base
        while row < size * (value.shape[0] // 2):
            chunk, offset = divmod(row, size)
            for half in range(2):
                tall[half, row - base : row - base + size - offset] = value[
                    2 * chunk + half, offset:
                ].astype(f32)
            row += size - offset

    front[...] = tc_ref[...].astype(f32)
    place_front(0)
    fill(tb_ref, D // 2)
    place_rest(16)
    front[: D // 2] = tb_ref[0, : D // 2].astype(f32)
    front[D // 2 :] = tb_ref[1, : D // 2].astype(f32)
    place_front(88)
    fill(ta_ref, 0)
    place_rest(104)

    cap, blocks = m_ref.shape[0], wide.shape[0]
    mine = (iota((cap, blocks), 0) == row_ref[:1]).astype(f32)
    filled = jnp.sum(mine, axis=1, keepdims=True) > 0.5
    mine = mine.astype(b16)
    step = 512
    for start in range(0, BLOCK, step):
        part = slice(start, start + step)
        grad = wide[:, part]
        own = nn(mine, grad.astype(b16))
        old = (m_ref[:, part], v_ref[:, part], w_ref[:, part])
        new = adam_update(old[0], own, old[1], old[2], rate_large)
        for ref, before, after in zip((nm_ref, nv_ref, nw_ref), old, new):
            ref[:, part] = jnp.where(filled, after, before)
        picked = [
            sel_ref[:, which * BLOCK + start : which * BLOCK + start + step].astype(f32)
            for which in range(3)
        ]
        fresh_ref[:, part] = adam_update(picked[0], grad, picked[1], picked[2], rate_large)[0].astype(b16)
    for layer in range(2):
        for row in range(LAYER_ROWS):
            flat[layer : layer + 1, 128 * row : 128 * row + 128] = ts_ref[
                layer * LAYER_ROWS + row : layer * LAYER_ROWS + row + 1, :
            ]
    new = adam_update(sm_ref[...], flat[:2], sv_ref[...], sw_ref[...], rate_small)
    for ref, value in zip((om_ref, ov_ref, ow_ref), new):
        ref[...] = value


def update(ta, tb, tc, ts, row, sel, tables, smalls):
    vmem = pl.BlockSpec(memory_space=pltpu.VMEM)
    blocks = sel.shape[0]
    operands = (ta, tb, tc, ts, row, sel, *tables, *smalls)
    outs = [jax.ShapeDtypeStruct(table.shape, f32) for table in tables]
    outs.append(jax.ShapeDtypeStruct((blocks, BLOCK), b16))
    outs += [jax.ShapeDtypeStruct(small.shape, f32) for small in smalls]
    return pl.pallas_call(
        update_kernel,
        out_shape=outs,
        in_specs=[vmem] * len(operands),
        out_specs=[vmem] * len(outs),
        scratch_shapes=[
            pltpu.VMEM((blocks, BLOCK), f32),
            pltpu.VMEM((2, ta.shape[0] * ta.shape[1] // 2, 128), f32),
            pltpu.VMEM((D, 128), f32),
            pltpu.VMEM((8, SMALL), f32),
        ],
        compiler_params=pltpu.CompilerParams(vmem_limit_bytes=VMEM_BYTES),
        name="update",
    )(*operands)


class Args:
    def __init__(self, rows, width):
        self.rows, self.width = rows, width
        self.operands, self.in_specs, self.outs, self.out_specs = [], [], [], []

    def cols(self, *arrays):
        for array in arrays:
            self.operands.append(array)
            self.in_specs.append(
                pl.BlockSpec((array.shape[0], self.width), lambda tile, scal: (0, tile))
            )

    def points(self, *arrays):
        for array in arrays:
            self.operands.append(array)
            self.in_specs.append(
                pl.BlockSpec((self.width, array.shape[1]), lambda tile, scal: (tile, 0))
            )

    def whole(self, *arrays):
        for array in arrays:
            rank = array.ndim
            self.operands.append(array)
            self.in_specs.append(
                pl.BlockSpec(array.shape, lambda tile, scal, rank=rank: (0,) * rank)
            )

    def layer(self, index, *arrays):
        for array in arrays:
            self.operands.append(array)
            self.in_specs.append(
                pl.BlockSpec((None,) + array.shape[1:], lambda tile, scal: (index, 0, 0))
            )

    def rows_of(self, array, start, size):
        self.operands.append(array)
        self.in_specs.append(
            pl.BlockSpec((size, array.shape[1]), lambda tile, scal: (start // size, 0))
        )

    def far(self, *arrays):
        for array in arrays:
            self.operands.append(array)
            self.in_specs.append(pl.BlockSpec(memory_space=pl.ANY))

    def out_far(self, *pairs):
        for shape, dtype in pairs:
            self.outs.append(jax.ShapeDtypeStruct(shape, dtype))
            self.out_specs.append(pl.BlockSpec(memory_space=pl.ANY))

    def out_cols(self, *pairs):
        for height, dtype in pairs:
            self.outs.append(jax.ShapeDtypeStruct((height, self.rows), dtype))
            self.out_specs.append(
                pl.BlockSpec((height, self.width), lambda tile, scal: (0, tile))
            )

    def out_points(self, *dtypes):
        for dtype in dtypes:
            self.outs.append(jax.ShapeDtypeStruct((self.rows, D), dtype))
            self.out_specs.append(pl.BlockSpec((self.width, D), lambda tile, scal: (tile, 0)))

    def out_whole(self, *pairs):
        for shape, dtype in pairs:
            rank = len(shape)
            self.outs.append(jax.ShapeDtypeStruct(shape, dtype))
            self.out_specs.append(
                pl.BlockSpec(shape, lambda tile, scal, rank=rank: (0,) * rank)
            )

    def call(self, body, scal, scratch, name):
        tiles = self.rows // self.width
        return pl.pallas_call(
            functools.partial(body, tiles),
            grid_spec=pltpu.PrefetchScalarGridSpec(
                num_scalar_prefetch=1,
                grid=(tiles,),
                in_specs=self.in_specs,
                out_specs=self.out_specs,
                scratch_shapes=scratch,
            ),
            out_shape=self.outs,
            compiler_params=pltpu.CompilerParams(
                dimension_semantics=("arbitrary",), vmem_limit_bytes=VMEM_BYTES
            ),
            name=name,
        )(scal, *self.operands)


def adam_update(master, grad, first, second, rate):
    new_first = beta_one * first + (1.0 - beta_one) * grad
    new_second = beta_two * second + (1.0 - beta_two) * grad * grad
    fix_one = 1.0 - beta_one**STEP
    fix_two = 1.0 - beta_two**STEP
    direction = new_first / fix_one / (jnp.sqrt(new_second / fix_two) + adam_eps)
    return (master - rate * (direction + decay_rate * master), new_first, new_second)


def flat_blocks(n_head, gfm, gout, gup, gdown):
    def columns(grad):
        width = grad.shape[1] // n_head
        return grad.reshape(D, n_head, width).transpose(1, 0, 2).reshape(n_head, -1)

    return jnp.concatenate(
        [
            columns(gfm[:, :D]),
            columns(gfm[:, D:]),
            gout.reshape(n_head, -1),
            columns(gup),
            columns(gdown),
        ],
        axis=1,
    ).reshape(n_head, -1, BLOCK)


def on_device(
    sizes,
    tokens,
    cotangent,
    segment_ids,
    owner,
    w_fx,
    w_mid,
    w_out,
    w_up,
    w_down,
    small_master,
    small_first,
    small_second,
    master_table,
    first_table,
    second_table,
):
    n_pts, n_head = sizes
    rows = tokens.shape[0]
    width, wide = min(512, rows), min(1024, rows)
    tiles = rows // width
    most = rows * n_pts * n_head // LARGEST
    window = (rows - 1 + most - 1) // rows
    layers = w_fx.shape[0]
    packed = (n_pts, n_head) == (8, 4)

    ids = segment_ids.reshape(-1, 128)
    w_fx = w_fx.transpose(0, 2, 1)
    w_mid = w_mid.transpose(0, 2, 1)
    tables = (master_table, first_table, second_table)
    smalls = (small_master, small_first, small_second)
    gathered, wsb, norms, scal, halves = opening(
        n_head, tiles, ids, w_fx, w_mid, small_master, tables
    )
    wfm0 = gathered.reshape(2 * D, D)

    cap = master_table.shape[0]
    if packed:
        collected = lax.all_gather(halves, "pts", axis=0, tiled=True)

    sums_shape = (MESHES, SLICES, D + 128)
    grad_sums_shape = (MESHES, SLICES, D)
    front_cols = ((D, b16), (8, f32), (D, b16), (D, b16), (D, b16), (HS, b16))
    wide_scratch = [pltpu.VMEM(grad_sums_shape, b16), pltpu.VMEM((D, wide), f32)]

    args = Args(rows, wide)
    args.points(tokens)
    args.whole(wfm0)
    args.layer(0, wsb, norms)
    args.out_cols((D, b16), *front_cols)
    args.out_far((sums_shape, f32))
    ends_outs = (((2, EDGE, D), b16), ((2,) + sums_shape[1:], f32))
    grad_ends_outs = (((2, EDGE, D), b16), ((2,) + grad_sums_shape[1:], f32))
    kept_outs = (((2, SLICES, 5 * D), f32), ((2, HS, SLICES), f32))
    args.out_whole(*ends_outs)
    sums_scratch = [pltpu.VMEM(sums_shape, f32), pltpu.SemaphoreType.DMA]
    spare_scratch = [pltpu.VMEM(sums_shape[1:], f32)]
    xt0, vh0, rs0, u0, f0, m0, p0, sums0, edge, ends0 = args.call(first_kernel, scal, sums_scratch, "first")
    recv0, later, wqb0 = swap_edges_weights(
        sizes, window, 0, ((0, 1), (1, 1), (2, 0)), edge, w_fx, w_mid, w_out, small_master, 1
    )
    later = later.reshape(3 * D, D)

    args = Args(rows, wide)
    args.cols(xt0, p0)
    args.far(sums0)
    args.whole(ends0, recv0)
    args.rows_of(later, 2 * D, D)
    args.layer(0, w_up, w_down)
    args.whole(wqb0)
    args.layer(0, norms)
    args.rows_of(later, 0, 2 * D)
    args.layer(1, wsb, norms)
    args.out_cols((D, b16), (D, b16), (8, f32), (D, b16), (FF, b16), (FF, b16))
    args.out_whole(*kept_outs)
    args.out_cols((D, f32), *front_cols)
    args.out_far((sums_shape, f32))
    args.out_whole(*ends_outs)
    (e0, vh20, rs20, u20, gp0, z0, kept0, prob0, x1, vh1, rs1, u1, f1, m1, p1, sums1, edge, ends1) = args.call(
        second_kernel, scal, wide_scratch + spare_scratch + sums_scratch, "second"
    )
    recv1, wout1, wqb1 = swap_edges_weights(
        sizes, window, 1, ((2, 1),), edge, w_fx, w_mid, w_out, small_master, 5
    )
    wout1 = wout1.reshape(D, D)

    grad_scratch = [pltpu.VMEM((D, FF), f32), pltpu.VMEM((D, FF), f32), pltpu.VMEM((D, D), f32)]
    rest_rows = D // n_head + 2 * D

    args = Args(rows, wide)
    args.cols(x1, p1)
    args.far(sums1)
    args.whole(ends1, recv1)
    args.points(cotangent)
    args.whole(wout1)
    args.layer(1, w_up, w_down)
    args.whole(wqb1)
    args.layer(1, norms)
    args.out_points(b16)
    args.out_cols((D, f32), (D, b16))
    args.out_whole(*kept_outs)
    args.out_far((grad_sums_shape, f32))
    args.out_whole(*grad_ends_outs, ((4, 128), f32))
    if packed:
        args.out_whole(((n_head, n_pts, 2 * rest_rows // n_pts, 128), b16))
    else:
        args.out_whole(((D, FF), b16), ((D, FF), b16), ((D, D), b16))
    (layer_out, d21, de1, kept1, prob1, grads1, edge, ends1, gn1b, *grads_a) = args.call(
        functools.partial(third_kernel, n_head, packed),
        scal,
        wide_scratch
        + spare_scratch
        + [pltpu.VMEM(grad_sums_shape, f32), pltpu.SemaphoreType.DMA]
        + [pltpu.VMEM((4, D, 128), f32), pltpu.VMEM((FF, wide), f32), pltpu.VMEM((FF, wide), b16)]
        + grad_scratch,
        "third",
    )
    if packed:
        grad_recv1, chosen, row = swap_edges_pick(
            sizes, window, cap, edge, owner.reshape(1, -1), collected, 2
        )
        part_a = lax.psum_scatter(grads_a[0], "head", scatter_dimension=0, tiled=True)[0]
    else:
        grad_recv1 = swap_edges(sizes, window, edge, 4)

    back_scratch = [
        *spare_scratch,
        pltpu.VMEM(grad_sums_shape[1:], f32),
        pltpu.SemaphoreType.DMA,
        pltpu.VMEM((MESHES, HS, 2 * D), b16),
        pltpu.VMEM((MESHES, HS, 128), f32),
        pltpu.VMEM((HS, width), f32),
        pltpu.VMEM((D, width), f32),
        pltpu.VMEM((D, HS), f32),
        pltpu.VMEM((D, 3 * D), f32),
        pltpu.VMEM((4, D, 128), f32),
        pltpu.VMEM((DH, 128), f32),
        pltpu.VMEM((D, 2 * D), f32),
    ]

    args = Args(rows, width)
    args.far(sums1)
    args.whole(kept1, prob1, recv1)
    args.far(grads1)
    args.whole(ends1, grad_recv1)
    args.cols(de1, f1, m1, p1, u1, vh1, rs1, d21)
    args.rows_of(later, 0, 2 * D)
    args.layer(1, wsb)
    args.whole(wqb1)
    args.layer(1, norms)
    args.cols(gp0, z0, vh20, rs20, u20, e0, p0)
    args.rows_of(later, 2 * D, D)
    args.layer(0, w_up, w_down, norms)
    args.whole(gn1b)
    args.out_cols((D, f32), (D, b16))
    args.out_far((grad_sums_shape, f32))
    args.out_whole(*grad_ends_outs, ((LAYER_ROWS, 128), f32), ((4, 128), f32))
    if packed:
        args.out_whole(((n_head, n_pts, (D + 2 * rest_rows) // n_pts, 128), b16))
    else:
        args.out_whole(((D, 2 * D), b16), ((D, FF), b16), ((D, FF), b16), ((D, D), b16))
    (d20, de0, grads0, edge, ends0, small1, gn0b, *grads_b) = args.call(
        functools.partial(fourth_kernel, n_head, packed),
        scal,
        back_scratch[:3] + [pltpu.VMEM(grad_sums_shape, f32)] + back_scratch[3:] + grad_scratch,
        "fourth",
    )
    if packed:
        grad_recv0, total_a = swap_edges_sums(sizes, window, edge, part_a, 6)
        mine_b = lax.psum_scatter(grads_b[0], "head", scatter_dimension=0, tiled=True)[0]
    else:
        grad_recv0 = swap_edges(sizes, window, edge, 4)

    args = Args(rows, width)
    args.far(sums0)
    args.whole(kept0, prob0, recv0)
    args.far(grads0)
    args.whole(ends0, grad_recv0)
    args.cols(de0, f0, m0, p0, u0, vh0, rs0, d20)
    args.whole(wfm0)
    args.layer(0, wsb)
    args.whole(wqb0)
    args.layer(0, norms)
    args.whole(gn0b, small1)
    args.out_points(f32)
    args.out_whole(((2 * LAYER_ROWS, 128), f32))
    args.out_whole(((n_head, D, 128), b16) if packed else ((D, 2 * D), b16))
    input_grad, small, front = args.call(
        functools.partial(fifth_kernel, n_head, packed), scal, back_scratch, "fifth"
    )

    if packed:
        total_b, total_c, total_s = total_gradients(sizes, mine_b, front, small)
        outs = update(total_a, total_b, total_c, total_s, row, chosen, tables, smalls)
        return (layer_out, input_grad, *outs)

    gup1, gdown1, gout1 = grads_a
    gfm1, gup0, gdown0, gout0 = grads_b
    small_total = lax.psum(small, ("pts", "head")).reshape(layers, -1)
    totals = []
    for parts in ((front, gout0, gup0, gdown0), (gfm1, gout1, gup1, gdown1)):
        blocks = lax.psum_scatter(
            flat_blocks(n_head, *parts), "head", scatter_dimension=0, tiled=True
        )
        totals.append(lax.psum(blocks.reshape(-1, BLOCK), "pts"))
    total_grad = jnp.concatenate(totals, axis=0).astype(f32)
    my_index = lax.axis_index("pts")
    block_ids = jnp.arange(owner.shape[0])
    same_owner = (owner[:, None] == owner[None, :]) & (block_ids[None, :] < block_ids[:, None])
    table_row = owner * cap + jnp.sum(same_owner.astype(jnp.int32), axis=1)
    place_all = (jnp.arange(n_pts * cap)[:, None] == table_row[None, :]).astype(f32)
    mine_place = lax.dynamic_slice_in_dim(place_all, my_index * cap, cap, 0)
    own_grad = jnp.dot(mine_place, total_grad, precision=lax.Precision.HIGHEST)
    filled = jnp.sum(mine_place, axis=1)[:, None] > 0.5
    updated = adam_update(master_table, own_grad, first_table, second_table, rate_large)
    new_tables = [jnp.where(filled, new, old) for new, old in zip(updated, tables)]
    collected = lax.all_gather(new_tables[0].astype(b16), "pts", axis=0, tiled=True)
    pick_back = (table_row[:, None] == jnp.arange(n_pts * cap)[None, :]).astype(b16)
    fresh = jnp.dot(pick_back, collected, preferred_element_type=f32).astype(b16)
    small_outs = adam_update(small_master, small_total, small_first, small_second, rate_small)
    return (layer_out, input_grad, *new_tables, fresh, *small_outs)


def solution(mesh):
    sizes = (mesh.shape["pts"], mesh.shape["head"])
    return jax.shard_map(
        functools.partial(on_device, sizes),
        mesh=mesh,
        in_specs=(
            P(("pts", "head"), None),
            P(("pts", "head"), None),
            P("pts"),
            P(),
            P(None, None, "head"),
            P(None, None, "head"),
            P(None, "head", None),
            P(),
            P(),
            P(),
            P(),
            P(),
            P("pts", "head"),
            P("pts", "head"),
            P("pts", "head"),
        ),
        out_specs=(
            P(("pts", "head"), None),
            P(("pts", "head"), None),
            P("pts", "head"),
            P("pts", "head"),
            P("pts", "head"),
            P(None, "head"),
            P(),
            P(),
            P(),
        ),
        check_vma=False,
    )
```

```python
import functools
import math

import jax
import jax.numpy as jnp
from jax import lax
from jax.experimental import pallas as pl
from jax.experimental.pallas import tpu as pltpu
from jax.sharding import PartitionSpec as P

D = 256
HEADS = 8
DH = 32
SLICES = 64
HS = HEADS * SLICES
FF = 1024
MESHES = 24
BLOCK = 2048
SMALL = 6144
STEP = 10
LARGEST = 12
EDGE = 80
VMEM_BYTES = 58 << 20

MESH = pl.DeviceIdType.MESH
HIGH = True
norm_eps = 1e-05
beta_one = 0.9
beta_two = 0.95
adam_eps = 1e-08
decay_rate = 0.1
rate_large = 0.1
rate_small = 0.75
f32 = jnp.float32
b16 = jnp.bfloat16


def dot(a, b, contract, precise):
    dims = (contract, ((), ()))
    if not precise:
        return lax.dot_general(a, b, dims, preferred_element_type=f32)
    a_high, b_high = a.astype(b16), b.astype(b16)
    a_low = (a - a_high.astype(f32)).astype(b16)
    b_low = (b - b_high.astype(f32)).astype(b16)
    return (
        lax.dot_general(a_high, b_low, dims, preferred_element_type=f32)
        + lax.dot_general(a_low, b_high, dims, preferred_element_type=f32)
        + lax.dot_general(a_high, b_high, dims, preferred_element_type=f32)
    )


def nn(a, b, precise=False):
    return dot(a, b, ((1,), (0,)), precise)


def nt(a, b, precise=False):
    return dot(a, b, ((1,), (1,)), precise)


def tn(a, b, precise=False):
    return dot(a, b, ((0,), (0,)), precise)


def iota(shape, axis):
    return lax.broadcasted_iota(jnp.int32, shape, axis)


def pick_diag(full, per_head):
    lane_head = iota((SLICES, full.shape[1]), 1) // per_head
    total = jnp.where(lane_head == 0, full[:SLICES], 0.0)
    for head in range(1, HEADS):
        total = total + jnp.where(
            lane_head == head, full[head * SLICES : (head + 1) * SLICES], 0.0
        )
    return total


def spread_diag(small):
    lane_head = iota((SLICES, D), 1) // DH
    return jnp.concatenate(
        [jnp.where(lane_head == head, small, jnp.zeros_like(small)) for head in range(HEADS)],
        axis=0,
    )


def repeat_rows(width):
    return (iota((D, width), 0) % width == iota((D, width), 1)).astype(f32)


def slice_repeat():
    return (iota((SLICES, HS), 1) % SLICES == iota((SLICES, HS), 0)).astype(f32)


def same_head(rows_per, cols_per, shape):
    return (iota(shape, 0) // rows_per) == (iota(shape, 1) // cols_per)


def start_gather(n_head, picks, send_sem, recv_sem):
    me = lax.axis_index("head")
    copies = []
    for index, ref in enumerate(picks):
        for step in range(1, n_head):
            copy = pltpu.make_async_remote_copy(
                src_ref=ref.at[:, me],
                dst_ref=ref.at[:, me],
                send_sem=send_sem.at[index, step - 1],
                recv_sem=recv_sem.at[index, step - 1],
                device_id={"head": lax.rem(me + step, n_head)},
                device_id_type=MESH,
            )
            copy.start()
            copies.append(copy)
    return copies


def unroll_slices(row_of, out):
    lane = iota((1, 128), 1)
    for pair in range(DH // 2):
        row = row_of(pair)
        out[2 * pair : 2 * pair + 1] = jnp.where(lane < SLICES, row, 0.0)
        out[2 * pair + 1 : 2 * pair + 2] = jnp.where(
            lane < SLICES, pltpu.roll(row, 128 - SLICES, 1), 0.0
        )


def opening_kernel(n_head, tiles, ids_ref, wfx_ref, wmid_ref, sm_ref, m_ref, v_ref, w_ref,
                   out_ref, wsb_ref, norm_ref, scal_ref, tables_ref, send_sem, recv_sem, slices_s, norm_s):
    me = lax.axis_index("head")
    barrier = pltpu.get_barrier_semaphore()
    for step in range(1, n_head):
        pl.semaphore_signal(
            barrier, inc=1, device_id={"head": lax.rem(me + step, n_head)}, device_id_type=MESH
        )
    out_ref[0, me] = wfx_ref[0]
    out_ref[1, me] = wmid_ref[0]
    pl.semaphore_wait(barrier, n_head - 1)
    copies = start_gather(n_head, [out_ref], send_sem, recv_sem)
    layers = sm_ref.shape[0]
    cap, deep = m_ref.shape[0], tables_ref.shape[0]
    for which, ref in enumerate((m_ref, v_ref, w_ref)):
        value = ref[...]
        if deep > cap:
            value = jnp.concatenate([value, jnp.zeros((deep - cap, BLOCK), f32)], axis=0)
        tables_ref[:, which * BLOCK : (which + 1) * BLOCK] = value.astype(b16)
    right = (iota((128, HS), 1) % SLICES == iota((128, HS), 0)).astype(b16)
    for layer in range(layers):
        unroll_slices(lambda pair: sm_ref[layer : layer + 1, 128 * pair : 128 * pair + 128], slices_s)
        wide = nn(slices_s[...].astype(b16), right)
        tiled = jnp.concatenate([wide] * HEADS, axis=0)
        wsb_ref[layer] = jnp.where(same_head(DH, SLICES, (D, HS)), tiled, 0.0).astype(b16)
        norm_s[...] = jnp.zeros_like(norm_s)
        for row in range(4):
            start = SMALL - 4 * D + row * D
            norm_s[row : row + 1] = sm_ref[layer : layer + 1, start : start + D]
        norm_ref[layer] = norm_s[...].T
    rows = ids_ref.shape[0] // n_head
    ids = ids_ref[pl.ds(pl.multiple_of(me * rows, rows), rows), :]
    for mesh in range(MESHES + 1):
        scal_ref[mesh] = jnp.sum((ids < mesh).astype(jnp.int32))
    deep = rows // tiles
    for tile in range(tiles):
        part = ids[tile * deep : (tile + 1) * deep]
        scal_ref[MESHES + 1 + 2 * tile] = jnp.min(part)
        scal_ref[MESHES + 2 + 2 * tile] = jnp.max(part)
    for copy in copies:
        copy.wait()


def opening(n_head, tiles, ids, w_fx, w_mid, small, tables):
    layers, part, _ = w_fx.shape
    deep = -(-tables[0].shape[0] // 16) * 16
    vmem = pl.BlockSpec(memory_space=pltpu.VMEM)
    return pl.pallas_call(
        functools.partial(opening_kernel, n_head, tiles),
        out_shape=(
            jax.ShapeDtypeStruct((2, n_head, part, D), b16),
            jax.ShapeDtypeStruct((layers, D, HS), b16),
            jax.ShapeDtypeStruct((layers, D, 128), f32),
            jax.ShapeDtypeStruct((MESHES + 1 + 2 * tiles,), jnp.int32),
            jax.ShapeDtypeStruct((deep, 3 * BLOCK), b16),
        ),
        in_specs=[vmem] * 7,
        out_specs=[vmem] * 3 + [pl.BlockSpec(memory_space=pltpu.SMEM), vmem],
        scratch_shapes=[
            pltpu.SemaphoreType.DMA((1, n_head - 1)),
            pltpu.SemaphoreType.DMA((1, n_head - 1)),
            pltpu.VMEM((DH, 128), f32),
            pltpu.VMEM((128, D), f32),
        ],
        compiler_params=pltpu.CompilerParams(
            collective_id=0, has_side_effects=True, vmem_limit_bytes=VMEM_BYTES
        ),
        name="opening",
    )(ids, w_fx, w_mid, small, *tables)


def place_of(sizes, shift):
    n_pts, n_head = sizes
    total = n_pts * n_head
    me = lax.axis_index("pts") * n_head + lax.axis_index("head")
    other = lax.rem(me + (shift + total), total)
    return (other // n_head, lax.rem(other, n_head))


def greet(sizes, window):
    barrier = pltpu.get_barrier_semaphore()
    for step in range(1, window + 1):
        for shift in (step, -step):
            pl.semaphore_signal(barrier, inc=1, device_id=place_of(sizes, shift), device_id_type=MESH)
    return barrier


def start_edges(sizes, window, edge_ref, out_ref, send_sem, recv_sem):
    copies = []
    for step in range(1, window + 1):
        for side, shift in ((1, step), (0, -step)):
            slot = step - 1 if side == 1 else window + step - 1
            copy = pltpu.make_async_remote_copy(
                src_ref=edge_ref.at[side],
                dst_ref=out_ref.at[slot],
                send_sem=send_sem.at[slot],
                recv_sem=recv_sem.at[slot],
                device_id=place_of(sizes, shift),
                device_id_type=MESH,
            )
            copy.start()
            copies.append(copy)
    return copies


def edge_kernel(sizes, window, edge_ref, out_ref, send_sem, recv_sem):
    barrier = greet(sizes, window)
    pl.semaphore_wait(barrier, 2 * window)
    for copy in start_edges(sizes, window, edge_ref, out_ref, send_sem, recv_sem):
        copy.wait()


def edge_weights_kernel(sizes, window, layer, pieces, edge_ref, wfx_ref, wmid_ref, wout_ref, sm_ref,
                        out_ref, w_ref, wqb_ref,
                        send_sem, recv_sem, wsend_sem, wrecv_sem, square_s):
    n_head = sizes[1]
    me = lax.axis_index("head")
    barrier = greet(sizes, window)
    for step in range(1, n_head):
        pl.semaphore_signal(
            barrier, inc=1, device_id={"head": lax.rem(me + step, n_head)}, device_id_type=MESH
        )
    refs = (wfx_ref, wmid_ref, wout_ref)
    for index, (kind, which) in enumerate(pieces):
        w_ref[index, me] = refs[kind][which]
    pl.semaphore_wait(barrier, 2 * window + n_head - 1)
    copies = start_edges(sizes, window, edge_ref, out_ref, send_sem, recv_sem)
    copies += start_gather(n_head, [w_ref], wsend_sem, wrecv_sem)
    lane = iota((1, 128), 1)
    for part in range(3):
        start = DH * SLICES + part * DH * DH
        for group in range(DH // 4):
            row = sm_ref[layer : layer + 1, start + 128 * group : start + 128 * group + 128]
            for inner in range(4):
                moved = row if inner == 0 else pltpu.roll(row, 128 - DH * inner, 1)
                square_s[4 * group + inner : 4 * group + inner + 1] = jnp.where(
                    lane < DH, moved, 0.0
                )
        square = square_s[...]
        for turn in range(1, 128 // DH):
            square = square + pltpu.roll(square_s[...], DH * turn, 1)
        square = jnp.concatenate([square] * (D // 128), axis=1)
        square = jnp.concatenate([square] * HEADS, axis=0)
        wqb_ref[:, part * D : (part + 1) * D] = jnp.where(
            same_head(DH, DH, (D, D)), square, 0.0
        )
    for copy in copies:
        copy.wait()


def pick_rows(n_pts, owner_ref, tables_s, load, chosen_ref, row_ref):
    blocks = owner_ref.shape[1]
    deep = tables_s.shape[0] // n_pts
    across = jnp.broadcast_to(owner_ref[...].astype(f32), (blocks, blocks))
    down = across.T
    low, high = iota((blocks, blocks), 0), iota((blocks, blocks), 1)
    same = across == down
    slot_down = jnp.sum(jnp.where(same & (high < low), 1.0, 0.0), axis=1, keepdims=True)
    slot_across = jnp.sum(jnp.where(same & (low < high), 1.0, 0.0), axis=0, keepdims=True)
    mine = owner_ref[...] == lax.axis_index("pts")
    row_ref[...] = jnp.broadcast_to(
        jnp.where(mine, slot_across.astype(jnp.int32), -1), row_ref.shape
    )
    target = (down[:, :1] * deep + slot_down).astype(jnp.int32)
    pick = (iota((blocks, tables_s.shape[0]), 1) == target).astype(b16)
    load.wait()
    step = 1024

    def choose(part, carry):
        lanes = pl.ds(pl.multiple_of(part * step, step), step)
        chosen_ref[:, lanes] = nn(pick, tables_s[:, lanes]).astype(b16)
        return carry

    lax.fori_loop(0, tables_s.shape[1] // step, choose, 0)


def edge_call(window, collective_id, rows, width, body, extra, outs, scratch, name):
    vmem = pl.BlockSpec(memory_space=pltpu.VMEM)
    outs = [jax.ShapeDtypeStruct((2 * window, rows, width), b16)] + outs
    return pl.pallas_call(
        body,
        out_shape=outs,
        in_specs=[vmem] * (1 + extra),
        out_specs=[vmem] * len(outs),
        scratch_shapes=[
            pltpu.SemaphoreType.DMA((2 * window,)),
            pltpu.SemaphoreType.DMA((2 * window,)),
        ]
        + scratch,
        compiler_params=pltpu.CompilerParams(
            collective_id=collective_id, has_side_effects=True, vmem_limit_bytes=VMEM_BYTES
        ),
        name=name,
    )


def swap_edges(sizes, window, edge, collective_id):
    _, rows, width = edge.shape
    return edge_call(
        window, collective_id, rows, width,
        functools.partial(edge_kernel, sizes, window), 0, [], [], "swap_edges",
    )(edge)[0]


def swap_edges_weights(sizes, window, layer, pieces, edge, w_fx, w_mid, w_out, small, collective_id):
    _, rows, width = edge.shape
    n_head = sizes[1]
    part = w_fx.shape[1]
    return edge_call(
        window, collective_id, rows, width,
        functools.partial(edge_weights_kernel, sizes, window, layer, pieces), 4,
        [
            jax.ShapeDtypeStruct((len(pieces), n_head, part, D), b16),
            jax.ShapeDtypeStruct((D, 3 * D), f32),
        ],
        [
            pltpu.SemaphoreType.DMA((1, n_head - 1)),
            pltpu.SemaphoreType.DMA((1, n_head - 1)),
            pltpu.VMEM((DH, 128), f32),
        ],
        "swap_edges_weights",
    )(edge, w_fx, w_mid, w_out, small)


def pts_copies(n_pts, source, target, send_sem, recv_sem):
    pts, head = lax.axis_index("pts"), lax.axis_index("head")
    copies = []
    for step in range(1, n_pts):
        peer = lax.rem(pts + step, n_pts)
        copies.append(
            pltpu.make_async_remote_copy(
                src_ref=source(step, peer),
                dst_ref=target(step, peer),
                send_sem=send_sem.at[step - 1],
                recv_sem=recv_sem.at[step - 1],
                device_id=(peer, head),
                device_id_type=MESH,
            )
        )
    return copies


def edge_sums_kernel(sizes, window, edge_ref, ga_ref, owner_ref, tables_ref, out_ref, ta_ref, chosen_ref, row_ref,
                     send_sem, recv_sem, a_send, a_recv, a_send2, a_recv2, got_a, tables_s, local_sem):
    n_pts, n_head = sizes
    pts, head = lax.axis_index("pts"), lax.axis_index("head")
    barrier = greet(sizes, window)
    for step in range(1, n_pts):
        pl.semaphore_signal(
            barrier, inc=1, device_id=(lax.rem(pts + step, n_pts), head), device_id_type=MESH
        )
    load = pltpu.make_async_copy(tables_ref, tables_s, local_sem)
    load.start()
    pl.semaphore_wait(barrier, 2 * window + n_pts - 1)
    edges = start_edges(sizes, window, edge_ref, out_ref, send_sem, recv_sem)
    gather = pts_copies(
        n_pts,
        lambda step, peer: ga_ref.at[peer],
        lambda step, peer: got_a.at[step - 1],
        a_send,
        a_recv,
    )
    for copy in gather:
        copy.start()
    for copy in gather:
        copy.wait()
    total = ga_ref[pts].astype(f32)
    for index in range(n_pts - 1):
        total = total + got_a[index].astype(f32)
    ta_ref[pts] = total.astype(b16)
    share = pts_copies(
        n_pts,
        lambda step, peer: ta_ref.at[pts],
        lambda step, peer: ta_ref.at[pts],
        a_send2,
        a_recv2,
    )
    for copy in share:
        copy.start()
    pick_rows(n_pts, owner_ref, tables_s, load, chosen_ref, row_ref)
    for copy in edges:
        copy.wait()
    for copy in share:
        copy.wait()


def swap_edges_sums(sizes, window, edge, ga, owner, tables, collective_id):
    _, rows, width = edge.shape
    n_pts = sizes[0]
    blocks = owner.shape[1]
    dma = pltpu.SemaphoreType.DMA
    vmem = pl.BlockSpec(memory_space=pltpu.VMEM)
    return pl.pallas_call(
        functools.partial(edge_sums_kernel, sizes, window),
        out_shape=(
            jax.ShapeDtypeStruct((2 * window, rows, width), b16),
            jax.ShapeDtypeStruct(ga.shape, b16),
            jax.ShapeDtypeStruct((blocks, tables.shape[1]), b16),
            jax.ShapeDtypeStruct((8, blocks), jnp.int32),
        ),
        in_specs=[vmem] * 3 + [pl.BlockSpec(memory_space=pl.ANY)],
        out_specs=[vmem] * 4,
        scratch_shapes=[dma((2 * window,))] * 2
        + [dma((n_pts - 1,))] * 4
        + [
            pltpu.VMEM((n_pts - 1,) + ga.shape[1:], b16),
            pltpu.VMEM(tables.shape, b16),
            dma,
        ],
        compiler_params=pltpu.CompilerParams(
            collective_id=collective_id, has_side_effects=True, vmem_limit_bytes=VMEM_BYTES
        ),
        name="swap_edges_sums",
    )(edge, ga, owner, tables)


def norm_stats(values):
    center = jnp.mean(values, axis=0, keepdims=True)
    spread = values - center
    scale = lax.rsqrt(jnp.mean(spread * spread, axis=0, keepdims=True) + norm_eps)
    return (spread * scale, scale)


def norm_back(grad_out, scaled, scale, gain):
    inner = grad_out * gain
    return scale * (
        inner
        - jnp.mean(inner, axis=0, keepdims=True)
        - scaled * jnp.mean(inner * scaled, axis=0, keepdims=True)
    )


def group_sum(values):
    return jnp.sum(values.reshape(HEADS, SLICES, values.shape[1]), axis=1, keepdims=True)


def fold_lanes(values):
    total = values[:, :128]
    for start in range(128, values.shape[1], 128):
        total = total + values[:, start : start + 128]
    return total


def tile_mask(scal, mesh, tile, width):
    spot = iota((1, width), 1) + tile * width
    return (spot >= scal[mesh]) & (spot < scal[mesh + 1])


def tile_range(scal, tiles, tile):
    base = MESHES + 1
    ratio = (scal.shape[0] - base) // 2 // tiles
    return (scal[base + 2 * ratio * tile], scal[base + 2 * ratio * (tile + 1) - 1])


def front_tile(scal, tiles, tile, x, wfm, wsb, norms, vh_ref, rs_ref, u_ref, f_ref, m_ref, p_ref, sums):
    width = x.shape[1]
    scaled, scale = norm_stats(x)
    vh_ref[...] = scaled.astype(b16)
    rs_ref[...] = jnp.broadcast_to(scale, (8, width))
    normed = (scaled * norms[:, 0:1] + norms[:, 1:2]).astype(b16)
    u_ref[...] = normed
    joint = nn(wfm, normed)
    feats = joint[:D].astype(b16)
    middle = joint[D:].astype(b16)
    f_ref[...] = feats
    m_ref[...] = middle
    logits = tn(wsb, middle).reshape(HEADS, SLICES, width)
    top = jnp.max(logits, axis=1, keepdims=True)
    expo = jnp.exp(logits - top)
    weights = expo / jnp.sum(expo, axis=1, keepdims=True)
    weights_r = weights.reshape(HS, width).astype(b16)
    p_ref[...] = weights_r
    low, high = tile_range(scal, tiles, tile)

    def add(mesh, carry):
        keep = tile_mask(scal, mesh, tile, width).astype(b16)
        wide = jnp.concatenate(
            [feats * keep, jnp.broadcast_to(keep, (D, width))], axis=0
        )
        full = nt(weights_r, wide)
        sums[mesh, :, :D] += pick_diag(full[:, :D], DH)
        sums[mesh, :, D:] += pick_diag(full[:, D:], DH)
        return carry

    lax.fori_loop(low, high + 1, add, 0)


def present(scal, tiles, body):
    def one(mesh, carry):
        body(mesh)
        return carry

    lax.fori_loop(tile_range(scal, tiles, 0)[0], tile_range(scal, tiles, tiles - 1)[1] + 1, one, 0)


def ends_of(scal, tiles):
    return (tile_range(scal, tiles, 0)[0], tile_range(scal, tiles, tiles - 1)[1])


def between(scal, tiles, body):
    first, last = ends_of(scal, tiles)

    def one(mesh, carry):
        body(mesh)
        return carry

    lax.fori_loop(first + 1, last, one, 0)


def fetch(source, target, sem):
    copy = pltpu.make_async_copy(source, target, sem)
    copy.start()
    copy.wait()


def clear_present(scal, tiles, sums):
    def clear(mesh):
        sums[mesh] = jnp.zeros(sums.shape[1:], f32)

    present(scal, tiles, clear)


def write_edges(scal, tiles, sums, edge_ref, ends_ref, sums_hbm, sem):
    first, last = ends_of(scal, tiles)
    extra = EDGE - SLICES
    for side, mesh in ((0, first), (1, last)):
        ends_ref[side] = sums[mesh]
        edge_ref[side, :SLICES] = sums[mesh, :, :D].astype(b16)
        rows = jnp.zeros((extra, D), f32)
        if sums.shape[2] > D:
            counts = jnp.concatenate(
                [sums[mesh, :, D:], jnp.zeros((D - SLICES, D), f32)], axis=0
            )
            pick = (iota((extra, D), 1) == DH * iota((extra, D), 0)).astype(f32)
            rows = nt(pick, counts, HIGH)
        edge_ref[side, SLICES:] = jnp.where(
            iota((extra, D), 0) >= HEADS, mesh.astype(f32), rows
        ).astype(b16)
    between(scal, tiles, lambda mesh: fetch(sums.at[mesh], sums_hbm.at[mesh], sem))


def add_edges(own, mesh, recv_ref):
    wanted = mesh.astype(f32)
    total = jnp.zeros((EDGE, D), f32)
    for slot in range(recv_ref.shape[0]):
        match = recv_ref[slot, SLICES + HEADS : SLICES + HEADS + 1].astype(f32) == wanted
        total = total + jnp.where(match, recv_ref[slot].astype(f32), 0.0)
    if own.shape[1] == D:
        return own + total[:SLICES]
    extra = EDGE - SLICES
    spread = (iota((extra, D), 1) // DH == iota((extra, D), 0)).astype(f32)
    counts = tn(total[SLICES:, :SLICES], spread, HIGH)
    return own + jnp.concatenate([total[:SLICES], counts], axis=1)


def attend_parts(totals, wqb):
    total = jnp.concatenate(totals, axis=0)
    count = total[:, D:]
    slice_tok = total[:, :D] / count
    triple = nn(slice_tok, wqb, HIGH)
    parts = []
    for index in range(len(totals)):
        rows = slice(index * SLICES, (index + 1) * SLICES)
        queries = triple[rows, :D]
        key_wide = spread_diag(triple[rows, D : 2 * D])
        value_wide = spread_diag(triple[rows, 2 * D :])
        scores = (nt(key_wide, queries, HIGH) * (1.0 / math.sqrt(DH))).reshape(
            HEADS, SLICES, SLICES
        )
        expo = jnp.exp(scores - jnp.max(scores, axis=1, keepdims=True))
        prob = (expo / jnp.sum(expo, axis=1, keepdims=True)).reshape(HS, SLICES)
        parts.append((queries, key_wide, value_wide, prob))
    return (slice_tok, count, triple, parts)


def attend_all(scal, tiles, ends_ref, recv_ref, sums_hbm, wqb, attended_ref, kept_ref, prob_ref, spare, sem):
    ends = ends_of(scal, tiles)
    totals = [add_edges(ends_ref[side], mesh, recv_ref) for side, mesh in enumerate(ends)]
    slice_tok, count, triple, parts = attend_parts(totals, wqb)
    kept = jnp.concatenate([slice_tok, count, triple], axis=1)
    results = []
    for side, (_, _, value_wide, prob) in enumerate(parts):
        results.append(tn(prob, value_wide, HIGH).astype(b16))
        kept_ref[side] = kept[side * SLICES : (side + 1) * SLICES]
        prob_ref[side] = prob
    for mesh, result in zip(ends, results):
        attended_ref[mesh] = result

    def inner(mesh):
        fetch(sums_hbm.at[mesh], spare, sem)
        _, _, _, parts = attend_parts([spare[...]], wqb)
        attended_ref[mesh] = tn(parts[0][3], parts[0][2], HIGH).astype(b16)

    between(scal, tiles, inner)


def spread_tile(scal, tiles, tile, wide_ref, p_ref, spread):
    low, high = tile_range(scal, tiles, tile)
    weights_r = p_ref[...]
    width = weights_r.shape[1]

    def one(mesh, carry):
        keep = tile_mask(scal, mesh, tile, width)
        spread[...] = jnp.where(keep, tn(spread_diag(wide_ref[mesh]), weights_r), spread[...])
        return carry

    lax.fori_loop(low, high + 1, one, 0)
    return spread[...].astype(b16)


GELU_A = math.sqrt(2.0 / math.pi)
GELU_B = 0.044715


def gelu_pair(hidden):
    square = hidden * hidden
    bend = jnp.tanh(hidden * (GELU_A + (GELU_A * GELU_B) * square))
    half = 0.5 + 0.5 * bend
    value = hidden * half
    slope = half + (0.5 * hidden) * (1.0 - bend * bend) * (
        GELU_A + (3.0 * GELU_A * GELU_B) * square
    )
    return (value, slope)


CHUNK = 1024


def mlp_back_tile(scal, tiles, tile, grad, slopes, actives, scaled_two, scale_two, normed_two_r, spread_r,
                  weights_r, wout, wup, wdown, norms, d2_ref, de_ref, sums,
                  gup, gdown, gout, gnorm):
    width = grad.shape[1]
    grad_r = grad.astype(b16)
    grad_normed = jnp.zeros((D, width), f32)
    for start in range(0, FF, CHUNK):
        part = slice(start, start + CHUNK)
        back = (slopes(part) * nn(wdown[part], grad_r)).astype(b16)
        gup[:, part] += nt(normed_two_r, back)
        gdown[:, part] += nt(grad_r, actives(part))
        grad_normed = grad_normed + nn(wup[:, part], back)
    gnorm[2] += fold_lanes(grad_normed * scaled_two)
    gnorm[3] += fold_lanes(grad_normed)
    grad_middle = grad + norm_back(grad_normed, scaled_two, scale_two, norms[:, 2:3])
    d2_ref[...] = grad_middle
    branch_r = grad_middle.astype(b16)
    gout[...] += nt(spread_r, branch_r)
    spread_grad = nn(wout, branch_r).astype(b16)
    de_ref[...] = spread_grad
    low, high = tile_range(scal, tiles, tile)

    def add(mesh, carry):
        keep = tile_mask(scal, mesh, tile, width).astype(b16)
        sums[mesh] += pick_diag(nt(weights_r, spread_grad * keep), DH)
        return carry

    lax.fori_loop(low, high + 1, add, 0)


def attend_back(meshes, shares, slice_tok, count, parts, outer, wqb, both, dcount, gqkv):
    root = 1.0 / math.sqrt(DH)
    attended, triples = [], []
    for (queries, key_wide, value_wide, prob), grad in zip(parts, outer):
        attended.append(tn(prob, value_wide, HIGH).astype(b16))
        inner = prob * nt(value_wide, grad, HIGH)
        mixed = group_sum(inner)
        grad_scores = root * (
            inner - (prob.reshape(HEADS, SLICES, SLICES) * mixed).reshape(HS, SLICES)
        )
        triples.append(
            jnp.concatenate(
                [
                    tn(grad_scores, key_wide, HIGH),
                    pick_diag(nn(grad_scores, queries, HIGH), DH),
                    pick_diag(nn(prob, grad, HIGH), DH),
                ],
                axis=1,
            )
        )
    triple = jnp.concatenate(triples, axis=0)
    grad_sum = nt(triple, wqb, HIGH) / count
    grad_count = -(grad_sum * slice_tok)
    gqkv[...] += tn(slice_tok * jnp.concatenate(shares, axis=0), triple, HIGH)
    for index, mesh in enumerate(meshes):
        rows = slice(index * SLICES, (index + 1) * SLICES)
        both[mesh, :, :D] = spread_diag(attended[index])
        both[mesh, :, D:] = spread_diag(grad_sum[rows].astype(b16))
        column = jnp.sum(spread_diag(grad_count[rows]), axis=1, keepdims=True)
        dcount[mesh] = jnp.broadcast_to(column, (HS, 128))


def attend_back_all(scal, tiles, kept_ref, prob_ref, recv_ref, ends_ref, grad_recv_ref, sums_hbm, grads_hbm,
                    wqb, both, dcount, gqkv, spare, spare_grad, sem):
    ends = ends_of(scal, tiles)
    outer = [add_edges(ends_ref[side], mesh, grad_recv_ref) for side, mesh in enumerate(ends)]
    kept = jnp.concatenate([kept_ref[0], kept_ref[1]], axis=0)
    parts = []
    for side in range(2):
        parts.append(
            (
                kept_ref[side, :, 2 * D : 3 * D],
                spread_diag(kept_ref[side, :, 3 * D : 4 * D]),
                spread_diag(kept_ref[side, :, 4 * D :]),
                prob_ref[side],
            )
        )
    previous = recv_ref[0, SLICES + HEADS : SLICES + HEADS + 1, :1].astype(f32)
    shares = [
        jnp.broadcast_to(1.0 - (previous == ends[0].astype(f32)).astype(f32), (SLICES, 1)),
        jnp.broadcast_to((ends[1] != ends[0]).astype(f32), (SLICES, 1)),
    ]
    attend_back(ends, shares, kept[:, :D], kept[:, D : 2 * D], parts, outer, wqb, both, dcount, gqkv)

    def inner(mesh):
        fetch(sums_hbm.at[mesh], spare, sem)
        fetch(grads_hbm.at[mesh], spare_grad, sem)
        slice_tok, count, _, parts = attend_parts([spare[...]], wqb)
        attend_back(
            (mesh,), [jnp.ones((SLICES, 1), f32)], slice_tok, count, parts, [spare_grad[...]], wqb, both, dcount, gqkv
        )

    between(scal, tiles, inner)


def attend_back_tile(scal, tiles, tile, both, dcount, de_ref, f_ref, m_ref, p_ref, u_ref, vh_ref, rs_ref,
                     d2_ref, wfm, wsb, norms, grad_p, grad_f, gfm, gws, gnorm):
    low, high = tile_range(scal, tiles, tile)
    weights_r = p_ref[...]
    width = weights_r.shape[1]
    pair = jnp.concatenate([de_ref[...], f_ref[...]], axis=0)

    def one(mesh, carry):
        keep = tile_mask(scal, mesh, tile, width)
        back = nn(both[mesh], pair) + dcount[mesh][:, :1]
        grad_p[...] = jnp.where(keep, back, grad_p[...])
        grad_f[...] = jnp.where(keep, tn(both[mesh, :, D:], weights_r), grad_f[...])
        return carry

    lax.fori_loop(low, high + 1, one, 0)
    weights = weights_r.astype(f32)
    inner = weights * grad_p[...]
    mixed = group_sum(inner)
    grad_logits = (
        inner - (weights.reshape(HEADS, SLICES, width) * mixed).reshape(HS, width)
    ).astype(b16)
    gws[...] += nt(m_ref[...], grad_logits)
    grad_m = nn(wsb, grad_logits).astype(b16)
    grad_fm = jnp.concatenate([grad_f[...].astype(b16), grad_m], axis=0)
    gfm[...] += nt(u_ref[...], grad_fm)
    grad_normed = tn(wfm, grad_fm)
    scaled = vh_ref[...].astype(f32)
    gnorm[0] += fold_lanes(grad_normed * scaled)
    gnorm[1] += fold_lanes(grad_normed)
    return d2_ref[...] + norm_back(grad_normed, scaled, rs_ref[:1], norms[:, 0:1])


def small_rows(base, gws, gqkv, scratch, out_ref):
    lane = iota((1, 128), 1)
    left = repeat_rows(DH)
    fold = (iota((128, HS), 1) % SLICES == iota((128, HS), 0)).astype(f32)
    kept = jnp.where(same_head(DH, SLICES, (D, HS)), gws[...], 0.0)
    scratch[...] = nt(tn(left, kept, HIGH), fold, HIGH)
    even = scratch[pl.ds(0, DH // 2, stride=2), :]
    odd = scratch[pl.ds(1, DH // 2, stride=2), :]
    out_ref[base : base + DH // 2] = jnp.where(lane < SLICES, even, pltpu.roll(odd, SLICES, 1))
    fold = (iota((D, 128), 0) % DH == iota((D, 128), 1)).astype(f32)
    for part in range(3):
        square = jnp.where(same_head(DH, DH, (D, D)), gqkv[:, part * D : (part + 1) * D], 0.0)
        scratch[...] = nn(tn(left, square, HIGH), fold, HIGH)
        total = scratch[pl.ds(0, DH // 4, stride=4), :]
        for inner in range(1, 4):
            total = total + pltpu.roll(scratch[pl.ds(inner, DH // 4, stride=4), :], DH * inner, 1)
        start = base + DH // 2 + part * (DH // 4)
        out_ref[start : start + DH // 4] = total


NORM_ROW = (SMALL - 4 * D) // 128
LAYER_ROWS = SMALL // 128


def norm_rows(gnorm, index, out_ref, base):
    lane = iota((D, 128), 1)
    total = jnp.zeros((D, 128), f32)
    for column, row in enumerate(index):
        total = total + jnp.where(lane == column, jnp.sum(gnorm[row], axis=1, keepdims=True), 0.0)
    flat = total.T
    for column in range(len(index)):
        for half in range(D // 128):
            place = base + column * (D // 128) + half
            out_ref[place : place + 1] = flat[column : column + 1, 128 * half : 128 * half + 128]


def pack_front(gfm, head):
    lane = iota((D, 128), 1)
    start = (head // 2) * 128
    feats, middle = gfm[:, start : start + 128], gfm[:, D + start : D + start + 128]
    if head % 2 == 0:
        return jnp.where(lane < 64, feats, pltpu.roll(middle, 64, 1))
    return jnp.where(lane < 64, pltpu.roll(feats, 64, 1), middle)


def store_pieces(out_ref, head, base, value):
    size = out_ref.shape[2]
    done = 0
    while done < value.shape[0]:
        chunk, offset = divmod(base + done, size)
        count = min(size - offset, value.shape[0] - done)
        for half in range(2):
            out_ref[head, 2 * chunk + half, offset : offset + count] = value[
                done : done + count, 128 * half : 128 * half + 128
            ]
        done += count


def pack_rest(gout, gup, gdown, out_ref, base, n_head):
    for head in range(n_head):
        deep, wide = D // n_head, FF // n_head
        store_pieces(out_ref, head, base, gout[head * deep : (head + 1) * deep].astype(b16))
        start = base + deep
        store_pieces(out_ref, head, start, gup[:, head * wide : (head + 1) * wide].astype(b16))
        store_pieces(out_ref, head, start + D, gdown[:, head * wide : (head + 1) * wide].astype(b16))


def first_kernel(tiles, scal, tok_ref, wfm_ref, wsb_ref, norm_ref,
                 xt_ref, vh_ref, rs_ref, u_ref, f_ref, m_ref, p_ref, sums_hbm, edge_ref, ends_ref, sums, sem):
    tile = pl.program_id(0)

    @pl.when(tile == 0)
    def _():
        clear_present(scal, tiles, sums)

    x = tok_ref[...].astype(f32).T
    xt_ref[...] = x.astype(b16)
    front_tile(scal, tiles, tile, x, wfm_ref[...], wsb_ref[...], norm_ref[...],
               vh_ref, rs_ref, u_ref, f_ref, m_ref, p_ref, sums)

    @pl.when(tile == tiles - 1)
    def _():
        write_edges(scal, tiles, sums, edge_ref, ends_ref, sums_hbm, sem)


def second_kernel(tiles, scal, xt_ref, p0_ref, sums0_hbm, ends0_ref, recv_ref, wout_ref, wup_ref, wdown_ref, wqb_ref, norm0_ref,
                  wfm_ref, wsb_ref, norm1_ref,
                  e_ref, vh2_ref, rs2_ref, u2_ref, gp_ref, z_ref, kept_ref, prob_ref,
                  x1_ref, vh_ref, rs_ref, u_ref, f_ref, m_ref, p_ref, sums_hbm, edge_ref, ends_ref,
                  wide, spread, spare, sums, sem):
    tile = pl.program_id(0)

    @pl.when(tile == 0)
    def _():
        attend_all(scal, tiles, ends0_ref, recv_ref, sums0_hbm, wqb_ref[...], wide, kept_ref, prob_ref, spare, sem)
        clear_present(scal, tiles, sums)

    norms = norm0_ref[...]
    spread_r = spread_tile(scal, tiles, tile, wide, p0_ref, spread)
    e_ref[...] = spread_r
    middle = xt_ref[...].astype(f32) + tn(wout_ref[...], spread_r)
    scaled_two, scale_two = norm_stats(middle)
    vh2_ref[...] = scaled_two.astype(b16)
    rs2_ref[...] = jnp.broadcast_to(scale_two, rs2_ref.shape)
    normed_two_r = (scaled_two * norms[:, 2:3] + norms[:, 3:4]).astype(b16)
    u2_ref[...] = normed_two_r
    x = middle
    for start in range(0, FF, CHUNK):
        part = slice(start, start + CHUNK)
        active, slope = gelu_pair(tn(wup_ref[:, part], normed_two_r))
        active_r = active.astype(b16)
        z_ref[part] = active_r
        gp_ref[part] = slope.astype(b16)
        x = x + tn(wdown_ref[part], active_r)
    x1_ref[...] = x
    front_tile(scal, tiles, tile, x, wfm_ref[...], wsb_ref[...], norm1_ref[...],
               vh_ref, rs_ref, u_ref, f_ref, m_ref, p_ref, sums)

    @pl.when(tile == tiles - 1)
    def _():
        write_edges(scal, tiles, sums, edge_ref, ends_ref, sums_hbm, sem)


def third_kernel(n_head, packed, tiles, scal, x1_ref, p_ref, sums1_hbm, ends1_ref, recv_ref, cot_ref, wout_ref, wup_ref, wdown_ref, wqb_ref, norm_ref,
                 out_ref, d2_ref, de_ref, kept_ref, prob_ref, grads_hbm, edge_ref, ends_ref,
                 gn_ref, *rest):
    grad_outs, (wide, spread, spare, grads, sem, gnorm, slope_s, active_s, gup, gdown, gout) = rest[:-11], rest[-11:]
    tile = pl.program_id(0)

    @pl.when(tile == 0)
    def _():
        clear_present(scal, tiles, grads)
        gup[...] = jnp.zeros_like(gup)
        gdown[...] = jnp.zeros_like(gdown)
        gout[...] = jnp.zeros_like(gout)
        gnorm[...] = jnp.zeros_like(gnorm)
        attend_all(scal, tiles, ends1_ref, recv_ref, sums1_hbm, wqb_ref[...], wide, kept_ref, prob_ref, spare, sem)

    norms = norm_ref[...]
    spread_r = spread_tile(scal, tiles, tile, wide, p_ref, spread)
    middle = x1_ref[...] + tn(wout_ref[...], spread_r)
    scaled_two, scale_two = norm_stats(middle)
    normed_two_r = (scaled_two * norms[:, 2:3] + norms[:, 3:4]).astype(b16)
    x = middle
    for start in range(0, FF, CHUNK):
        part = slice(start, start + CHUNK)
        active, slope = gelu_pair(tn(wup_ref[:, part], normed_two_r))
        active_r = active.astype(b16)
        active_s[part] = active_r
        slope_s[part] = slope
        x = x + tn(wdown_ref[part], active_r)
    out_ref[...] = x.T.astype(b16)
    grad = cot_ref[...].astype(f32).T
    mlp_back_tile(scal, tiles, tile, grad, lambda part: slope_s[part], lambda part: active_s[part],
                  scaled_two, scale_two, normed_two_r, spread_r, p_ref[...],
                  wout_ref[...], wup_ref, wdown_ref, norms, d2_ref, de_ref, grads,
                  gup, gdown, gout, gnorm)

    @pl.when(tile == tiles - 1)
    def _():
        write_edges(scal, tiles, grads, edge_ref, ends_ref, grads_hbm, sem)
        norm_rows(gnorm, (2, 3), gn_ref, 0)
        if packed:
            pack_rest(gout, gup, gdown, grad_outs[0], 0, n_head)
        else:
            for ref, total in zip(grad_outs, (gup, gdown, gout)):
                ref[...] = total[...].astype(b16)


def fourth_kernel(n_head, packed, tiles, scal, sums1_hbm, kept_ref, prob_ref, recv_ref, grads1_hbm, ends1_ref, grad_recv_ref, de1_ref, f_ref, m_ref, p1_ref, u_ref, vh_ref, rs_ref, d21_ref,
                  wfm_ref, wsb_ref, wqb_ref, norm1_ref,
                  gp_ref, z_ref, vh2_ref, rs2_ref, u2_ref, e_ref, p0_ref, wout_ref, wup_ref, wdown_ref, norm0_ref, gn1b_ref,
                  d2_ref, de_ref, grads_hbm, edge_ref, ends_ref, small_ref, gn0_ref, *rest):
    grad_outs = rest[:-16]
    spare, spare_grad, sem, grads, both, dcount, grad_p, grad_f, gws, gqkv, gnorm, fold_s, gfm, gup, gdown, gout = rest[-16:]
    tile = pl.program_id(0)

    @pl.when(tile == 0)
    def _():
        for ref in (gfm, gws, gqkv, gup, gdown, gout, gnorm):
            ref[...] = jnp.zeros_like(ref)
        attend_back_all(scal, tiles, kept_ref, prob_ref, recv_ref, ends1_ref, grad_recv_ref, sums1_hbm, grads1_hbm,
                        wqb_ref[...], both, dcount, gqkv, spare, spare_grad, sem)
        clear_present(scal, tiles, grads)

    grad = attend_back_tile(scal, tiles, tile, both, dcount, de1_ref, f_ref, m_ref, p1_ref, u_ref, vh_ref, rs_ref,
                            d21_ref, wfm_ref[...], wsb_ref[...], norm1_ref[...], grad_p, grad_f, gfm, gws, gnorm)
    mlp_back_tile(scal, tiles, tile, grad, lambda part: gp_ref[part].astype(f32), lambda part: z_ref[part],
                  vh2_ref[...].astype(f32), rs2_ref[:1], u2_ref[...], e_ref[...], p0_ref[...],
                  wout_ref[...], wup_ref, wdown_ref, norm0_ref[...], d2_ref, de_ref, grads,
                  gup, gdown, gout, gnorm)

    @pl.when(tile == tiles - 1)
    def _():
        write_edges(scal, tiles, grads, edge_ref, ends_ref, grads_hbm, sem)
        small_rows(0, gws, gqkv, fold_s, small_ref)
        norm_rows(gnorm, (0, 1), small_ref, NORM_ROW)
        small_ref[NORM_ROW + 4 :] = gn1b_ref[...]
        norm_rows(gnorm, (2, 3), gn0_ref, 0)
        if packed:
            for head in range(n_head):
                front = pack_front(gfm, head).astype(b16)
                store_pieces(
                    grad_outs[0], head, 0, jnp.concatenate([front[: D // 2], front[D // 2 :]], axis=1)
                )
            pack_rest(gout, gup, gdown, grad_outs[0], D // 2, n_head)
        else:
            for ref, total in zip(grad_outs, (gfm, gup, gdown, gout)):
                ref[...] = total[...].astype(b16)


def fifth_kernel(n_head, packed, tiles, scal, sums0_hbm, kept_ref, prob_ref, recv_ref, grads0_hbm, ends0_ref, grad_recv_ref, de_ref, f_ref, m_ref, p_ref, u_ref, vh_ref, rs_ref, d2_ref,
                 wfm_ref, wsb_ref, wqb_ref, norm_ref, gn0b_ref, small1_ref,
                 gin_ref, small_ref, front_ref,
                 spare, spare_grad, sem, both, dcount, grad_p, grad_f, gws, gqkv, gnorm, fold_s, gfm):
    tile = pl.program_id(0)

    @pl.when(tile == 0)
    def _():
        for ref in (gfm, gws, gqkv, gnorm):
            ref[...] = jnp.zeros_like(ref)
        attend_back_all(scal, tiles, kept_ref, prob_ref, recv_ref, ends0_ref, grad_recv_ref, sums0_hbm, grads0_hbm,
                        wqb_ref[...], both, dcount, gqkv, spare, spare_grad, sem)

    grad = attend_back_tile(scal, tiles, tile, both, dcount, de_ref, f_ref, m_ref, p_ref, u_ref, vh_ref, rs_ref,
                            d2_ref, wfm_ref[...], wsb_ref[...], norm_ref[...], grad_p, grad_f, gfm, gws, gnorm)
    gin_ref[...] = grad.T

    @pl.when(tile == tiles - 1)
    def _():
        small_rows(0, gws, gqkv, fold_s, small_ref)
        norm_rows(gnorm, (0, 1), small_ref, NORM_ROW)
        small_ref[NORM_ROW + 4 : LAYER_ROWS] = gn0b_ref[...]
        small_ref[LAYER_ROWS:] = small1_ref[...]
        if packed:
            for head in range(n_head):
                front_ref[head] = pack_front(gfm, head).astype(b16)
        else:
            front_ref[...] = gfm[...].astype(b16)


def sum_parts(own, got):
    total = own.astype(f32)
    for index in range(got.shape[0]):
        total = total + got[index].astype(f32)
    return total


def total_kernel(sizes, gb_ref, gc_ref, gs_ref, tb_ref, tc_ref, ts_ref,
                 got_b, got_c, got_s, mid_c, mid_s, got_c2, got_s2, head_sem, pts_sem):
    n_pts, n_head = sizes
    pts, head = lax.axis_index("pts"), lax.axis_index("head")
    c_rows = D // n_pts
    s_rows = gs_ref.shape[0] // n_head

    def part(index, rows):
        return pl.ds(pl.multiple_of(index * rows, rows), rows)

    def over(size, which, own, to, sem, source, target):
        copies = []
        for step in range(1, size):
            peer = lax.rem(own + step, size)
            copies.append(
                pltpu.make_async_remote_copy(
                    src_ref=source(peer),
                    dst_ref=target(step - 1),
                    send_sem=sem.at[0, which, step - 1],
                    recv_sem=sem.at[1, which, step - 1],
                    device_id=to(peer),
                    device_id_type=MESH,
                )
            )
        for copy in copies:
            copy.start()
        return copies

    def over_head(which, source, target):
        return over(n_head, which, head, lambda peer: (pts, peer), head_sem, source, target)

    def over_pts(which, source, target):
        return over(n_pts, which, pts, lambda peer: (peer, head), pts_sem, source, target)

    def finish(copies):
        for copy in copies:
            copy.wait()

    barrier = pltpu.get_barrier_semaphore()
    for step in range(1, n_head):
        pl.semaphore_signal(
            barrier, inc=1, device_id=(pts, lax.rem(head + step, n_head)), device_id_type=MESH
        )
    for step in range(1, n_pts):
        pl.semaphore_signal(
            barrier, inc=1, device_id=(lax.rem(pts + step, n_pts), head), device_id_type=MESH
        )
    pl.semaphore_wait(barrier, n_head - 1 + n_pts - 1)

    first_c = over_head(0, lambda peer: gc_ref.at[peer], lambda slot: got_c.at[slot])
    first_s = over_head(1, lambda peer: gs_ref.at[part(peer, s_rows)], lambda slot: got_s.at[slot])
    first_b = over_pts(0, lambda peer: gb_ref.at[peer], lambda slot: got_b.at[slot])
    finish(first_c)
    mid_c[...] = sum_parts(gc_ref[head], got_c).astype(b16)
    next_c = over_pts(1, lambda peer: mid_c.at[part(peer, c_rows)], lambda slot: got_c2.at[slot])
    finish(first_s)
    mid_s[...] = sum_parts(gs_ref[part(head, s_rows)], got_s)
    next_s = over_pts(2, lambda peer: mid_s, lambda slot: got_s2.at[slot])
    finish(next_c)
    mine_c = part(pts, c_rows)
    tc_ref[mine_c] = sum_parts(mid_c[mine_c], got_c2).astype(b16)
    last_c = over_pts(3, lambda peer: tc_ref.at[mine_c], lambda slot: tc_ref.at[mine_c])
    finish(next_s)
    mine_s = part(head, s_rows)
    ts_ref[mine_s] = sum_parts(mid_s[...], got_s2)
    last_s = over_head(2, lambda peer: ts_ref.at[mine_s], lambda slot: ts_ref.at[mine_s])
    finish(first_b)
    tb_ref[pts] = sum_parts(gb_ref[pts], got_b).astype(b16)
    last_b = over_pts(4, lambda peer: tb_ref.at[pts], lambda slot: tb_ref.at[pts])
    finish(last_c)
    finish(last_s)
    finish(last_b)


def total_gradients(sizes, gb, gc, gs):
    n_pts, n_head = sizes
    vmem = pl.BlockSpec(memory_space=pltpu.VMEM)
    dma = pltpu.SemaphoreType.DMA
    c_rows, s_rows = D // n_pts, gs.shape[0] // n_head
    return pl.pallas_call(
        functools.partial(total_kernel, sizes),
        out_shape=(
            jax.ShapeDtypeStruct(gb.shape, b16),
            jax.ShapeDtypeStruct(gc.shape[1:], b16),
            jax.ShapeDtypeStruct(gs.shape, f32),
        ),
        in_specs=[vmem] * 3,
        out_specs=[vmem] * 3,
        scratch_shapes=[
            pltpu.VMEM((n_pts - 1,) + gb.shape[1:], b16),
            pltpu.VMEM((n_head - 1,) + gc.shape[1:], b16),
            pltpu.VMEM((n_head - 1, s_rows, 128), f32),
            pltpu.VMEM(gc.shape[1:], b16),
            pltpu.VMEM((s_rows, 128), f32),
            pltpu.VMEM((n_pts - 1, c_rows, 128), b16),
            pltpu.VMEM((n_pts - 1, s_rows, 128), f32),
            dma((2, 3, n_head - 1)),
            dma((2, 5, n_pts - 1)),
        ],
        compiler_params=pltpu.CompilerParams(
            collective_id=3, has_side_effects=True, vmem_limit_bytes=VMEM_BYTES
        ),
        name="total_gradients",
    )(gb, gc, gs)


def update_kernel(ta_ref, tb_ref, tc_ref, ts_ref, row_ref, sel_ref, m_ref, v_ref, w_ref, sm_ref, sv_ref, sw_ref,
                  nm_ref, nv_ref, nw_ref, fresh_ref, om_ref, ov_ref, ow_ref, wide, tall, front, flat):
    lane = iota((8, 128), 1)

    def place_front(base):
        for pair in range(16):
            first = front[pl.ds(2 * pair, 8, stride=32), :]
            second = front[pl.ds(2 * pair + 1, 8, stride=32), :]
            columns = slice(128 * pair, 128 * pair + 128)
            wide[base : base + 8, columns] = jnp.where(lane < 64, first, pltpu.roll(second, 64, 1))
            wide[base + 8 : base + 16, columns] = jnp.where(lane < 64, pltpu.roll(first, 64, 1), second)

    def place_rest(base):
        for part in range(8):
            for half in range(2):
                wide[base : base + 72, 256 * part + 128 * half : 256 * part + 128 * half + 128] = tall[
                    half, pl.ds(part, 72, stride=8), :
                ]

    def fill(value, base):
        size = value.shape[1]
        row = base
        while row < size * (value.shape[0] // 2):
            chunk, offset = divmod(row, size)
            for half in range(2):
                tall[half, row - base : row - base + size - offset] = value[
                    2 * chunk + half, offset:
                ].astype(f32)
            row += size - offset

    front[...] = tc_ref[...].astype(f32)
    place_front(0)
    fill(tb_ref, D // 2)
    place_rest(16)
    front[: D // 2] = tb_ref[0, : D // 2].astype(f32)
    front[D // 2 :] = tb_ref[1, : D // 2].astype(f32)
    place_front(88)
    fill(ta_ref, 0)
    place_rest(104)

    cap, blocks = m_ref.shape[0], wide.shape[0]
    mine = (iota((cap, blocks), 0) == row_ref[:1]).astype(f32)
    filled = jnp.sum(mine, axis=1, keepdims=True) > 0.5
    mine = mine.astype(b16)
    step = 512
    for start in range(0, BLOCK, step):
        part = slice(start, start + step)
        grad = wide[:, part]
        own = nn(mine, grad.astype(b16))
        old = (m_ref[:, part], v_ref[:, part], w_ref[:, part])
        new = adam_update(old[0], own, old[1], old[2], rate_large)
        for ref, before, after in zip((nm_ref, nv_ref, nw_ref), old, new):
            ref[:, part] = jnp.where(filled, after, before)
        picked = [
            sel_ref[:, which * BLOCK + start : which * BLOCK + start + step].astype(f32)
            for which in range(3)
        ]
        fresh_ref[:, part] = adam_update(picked[0], grad, picked[1], picked[2], rate_large)[0].astype(b16)
    for layer in range(2):
        for row in range(LAYER_ROWS):
            flat[layer : layer + 1, 128 * row : 128 * row + 128] = ts_ref[
                layer * LAYER_ROWS + row : layer * LAYER_ROWS + row + 1, :
            ]
    new = adam_update(sm_ref[...], flat[:2], sv_ref[...], sw_ref[...], rate_small)
    for ref, value in zip((om_ref, ov_ref, ow_ref), new):
        ref[...] = value


def update(ta, tb, tc, ts, row, sel, tables, smalls):
    vmem = pl.BlockSpec(memory_space=pltpu.VMEM)
    blocks = sel.shape[0]
    operands = (ta, tb, tc, ts, row, sel, *tables, *smalls)
    outs = [jax.ShapeDtypeStruct(table.shape, f32) for table in tables]
    outs.append(jax.ShapeDtypeStruct((blocks, BLOCK), b16))
    outs += [jax.ShapeDtypeStruct(small.shape, f32) for small in smalls]
    return pl.pallas_call(
        update_kernel,
        out_shape=outs,
        in_specs=[vmem] * len(operands),
        out_specs=[vmem] * len(outs),
        scratch_shapes=[
            pltpu.VMEM((blocks, BLOCK), f32),
            pltpu.VMEM((2, ta.shape[0] * ta.shape[1] // 2, 128), f32),
            pltpu.VMEM((D, 128), f32),
            pltpu.VMEM((8, SMALL), f32),
        ],
        compiler_params=pltpu.CompilerParams(vmem_limit_bytes=VMEM_BYTES),
        name="update",
    )(*operands)


class Args:
    def __init__(self, rows, width):
        self.rows, self.width = rows, width
        self.operands, self.in_specs, self.outs, self.out_specs = [], [], [], []

    def cols(self, *arrays):
        for array in arrays:
            self.operands.append(array)
            self.in_specs.append(
                pl.BlockSpec((array.shape[0], self.width), lambda tile, scal: (0, tile))
            )

    def points(self, *arrays):
        for array in arrays:
            self.operands.append(array)
            self.in_specs.append(
                pl.BlockSpec((self.width, array.shape[1]), lambda tile, scal: (tile, 0))
            )

    def whole(self, *arrays):
        for array in arrays:
            rank = array.ndim
            self.operands.append(array)
            self.in_specs.append(
                pl.BlockSpec(array.shape, lambda tile, scal, rank=rank: (0,) * rank)
            )

    def layer(self, index, *arrays):
        for array in arrays:
            self.operands.append(array)
            self.in_specs.append(
                pl.BlockSpec((None,) + array.shape[1:], lambda tile, scal: (index, 0, 0))
            )

    def rows_of(self, array, start, size):
        self.operands.append(array)
        self.in_specs.append(
            pl.BlockSpec((size, array.shape[1]), lambda tile, scal: (start // size, 0))
        )

    def far(self, *arrays):
        for array in arrays:
            self.operands.append(array)
            self.in_specs.append(pl.BlockSpec(memory_space=pl.ANY))

    def out_far(self, *pairs):
        for shape, dtype in pairs:
            self.outs.append(jax.ShapeDtypeStruct(shape, dtype))
            self.out_specs.append(pl.BlockSpec(memory_space=pl.ANY))

    def out_cols(self, *pairs):
        for height, dtype in pairs:
            self.outs.append(jax.ShapeDtypeStruct((height, self.rows), dtype))
            self.out_specs.append(
                pl.BlockSpec((height, self.width), lambda tile, scal: (0, tile))
            )

    def out_points(self, *dtypes):
        for dtype in dtypes:
            self.outs.append(jax.ShapeDtypeStruct((self.rows, D), dtype))
            self.out_specs.append(pl.BlockSpec((self.width, D), lambda tile, scal: (tile, 0)))

    def out_whole(self, *pairs):
        for shape, dtype in pairs:
            rank = len(shape)
            self.outs.append(jax.ShapeDtypeStruct(shape, dtype))
            self.out_specs.append(
                pl.BlockSpec(shape, lambda tile, scal, rank=rank: (0,) * rank)
            )

    def call(self, body, scal, scratch, name):
        tiles = self.rows // self.width
        return pl.pallas_call(
            functools.partial(body, tiles),
            grid_spec=pltpu.PrefetchScalarGridSpec(
                num_scalar_prefetch=1,
                grid=(tiles,),
                in_specs=self.in_specs,
                out_specs=self.out_specs,
                scratch_shapes=scratch,
            ),
            out_shape=self.outs,
            compiler_params=pltpu.CompilerParams(
                dimension_semantics=("arbitrary",), vmem_limit_bytes=VMEM_BYTES
            ),
            name=name,
        )(scal, *self.operands)


def adam_update(master, grad, first, second, rate):
    new_first = beta_one * first + (1.0 - beta_one) * grad
    new_second = beta_two * second + (1.0 - beta_two) * grad * grad
    fix_one = 1.0 - beta_one**STEP
    fix_two = 1.0 - beta_two**STEP
    direction = new_first / fix_one / (jnp.sqrt(new_second / fix_two) + adam_eps)
    return (master - rate * (direction + decay_rate * master), new_first, new_second)


def flat_blocks(n_head, gfm, gout, gup, gdown):
    def columns(grad):
        width = grad.shape[1] // n_head
        return grad.reshape(D, n_head, width).transpose(1, 0, 2).reshape(n_head, -1)

    return jnp.concatenate(
        [
            columns(gfm[:, :D]),
            columns(gfm[:, D:]),
            gout.reshape(n_head, -1),
            columns(gup),
            columns(gdown),
        ],
        axis=1,
    ).reshape(n_head, -1, BLOCK)


def on_device(
    sizes,
    tokens,
    cotangent,
    segment_ids,
    owner,
    w_fx,
    w_mid,
    w_out,
    w_up,
    w_down,
    small_master,
    small_first,
    small_second,
    master_table,
    first_table,
    second_table,
):
    n_pts, n_head = sizes
    rows = tokens.shape[0]
    width, wide = min(512, rows), min(1024, rows)
    tiles = rows // width
    most = rows * n_pts * n_head // LARGEST
    window = (rows - 1 + most - 1) // rows
    layers = w_fx.shape[0]
    packed = (n_pts, n_head) == (8, 4)

    ids = segment_ids.reshape(-1, 128)
    w_fx = w_fx.transpose(0, 2, 1)
    w_mid = w_mid.transpose(0, 2, 1)
    tables = (master_table, first_table, second_table)
    smalls = (small_master, small_first, small_second)
    gathered, wsb, norms, scal, halves = opening(
        n_head, tiles, ids, w_fx, w_mid, small_master, tables
    )
    wfm0 = gathered.reshape(2 * D, D)

    cap = master_table.shape[0]
    if packed:
        collected = lax.all_gather(halves, "pts", axis=0, tiled=True)

    sums_shape = (MESHES, SLICES, 2 * D)
    grad_sums_shape = (MESHES, SLICES, D)
    front_cols = ((D, b16), (8, f32), (D, b16), (D, b16), (D, b16), (HS, b16))
    wide_scratch = [pltpu.VMEM(grad_sums_shape, b16), pltpu.VMEM((D, wide), f32)]

    args = Args(rows, wide)
    args.points(tokens)
    args.whole(wfm0)
    args.layer(0, wsb, norms)
    args.out_cols((D, b16), *front_cols)
    args.out_far((sums_shape, f32))
    ends_outs = (((2, EDGE, D), b16), ((2,) + sums_shape[1:], f32))
    grad_ends_outs = (((2, EDGE, D), b16), ((2,) + grad_sums_shape[1:], f32))
    kept_outs = (((2, SLICES, 5 * D), f32), ((2, HS, SLICES), f32))
    args.out_whole(*ends_outs)
    sums_scratch = [pltpu.VMEM(sums_shape, f32), pltpu.SemaphoreType.DMA]
    spare_scratch = [pltpu.VMEM(sums_shape[1:], f32)]
    xt0, vh0, rs0, u0, f0, m0, p0, sums0, edge, ends0 = args.call(first_kernel, scal, sums_scratch, "first")
    recv0, later, wqb0 = swap_edges_weights(
        sizes, window, 0, ((0, 1), (1, 1), (2, 0)), edge, w_fx, w_mid, w_out, small_master, 1
    )
    later = later.reshape(3 * D, D)

    args = Args(rows, wide)
    args.cols(xt0, p0)
    args.far(sums0)
    args.whole(ends0, recv0)
    args.rows_of(later, 2 * D, D)
    args.layer(0, w_up, w_down)
    args.whole(wqb0)
    args.layer(0, norms)
    args.rows_of(later, 0, 2 * D)
    args.layer(1, wsb, norms)
    args.out_cols((D, b16), (D, b16), (8, f32), (D, b16), (FF, b16), (FF, b16))
    args.out_whole(*kept_outs)
    args.out_cols((D, f32), *front_cols)
    args.out_far((sums_shape, f32))
    args.out_whole(*ends_outs)
    (e0, vh20, rs20, u20, gp0, z0, kept0, prob0, x1, vh1, rs1, u1, f1, m1, p1, sums1, edge, ends1) = args.call(
        second_kernel, scal, wide_scratch + spare_scratch + sums_scratch, "second"
    )
    recv1, wout1, wqb1 = swap_edges_weights(
        sizes, window, 1, ((2, 1),), edge, w_fx, w_mid, w_out, small_master, 5
    )
    wout1 = wout1.reshape(D, D)

    grad_scratch = [pltpu.VMEM((D, FF), f32), pltpu.VMEM((D, FF), f32), pltpu.VMEM((D, D), f32)]
    rest_rows = D // n_head + 2 * D

    args = Args(rows, wide)
    args.cols(x1, p1)
    args.far(sums1)
    args.whole(ends1, recv1)
    args.points(cotangent)
    args.whole(wout1)
    args.layer(1, w_up, w_down)
    args.whole(wqb1)
    args.layer(1, norms)
    args.out_points(b16)
    args.out_cols((D, f32), (D, b16))
    args.out_whole(*kept_outs)
    args.out_far((grad_sums_shape, f32))
    args.out_whole(*grad_ends_outs, ((4, 128), f32))
    if packed:
        args.out_whole(((n_head, n_pts, 2 * rest_rows // n_pts, 128), b16))
    else:
        args.out_whole(((D, FF), b16), ((D, FF), b16), ((D, D), b16))
    (layer_out, d21, de1, kept1, prob1, grads1, edge, ends1, gn1b, *grads_a) = args.call(
        functools.partial(third_kernel, n_head, packed),
        scal,
        wide_scratch
        + spare_scratch
        + [pltpu.VMEM(grad_sums_shape, f32), pltpu.SemaphoreType.DMA]
        + [pltpu.VMEM((4, D, 128), f32), pltpu.VMEM((FF, wide), f32), pltpu.VMEM((FF, wide), b16)]
        + grad_scratch,
        "third",
    )
    if packed:
        grad_recv1 = swap_edges(sizes, window, edge, 4)
        grad_recv1, collected = lax.optimization_barrier((grad_recv1, collected))
        part_a = lax.psum_scatter(grads_a[0], "head", scatter_dimension=0, tiled=True)[0]
    else:
        grad_recv1 = swap_edges(sizes, window, edge, 4)

    back_scratch = [
        *spare_scratch,
        pltpu.VMEM(grad_sums_shape[1:], f32),
        pltpu.SemaphoreType.DMA,
        pltpu.VMEM((MESHES, HS, 2 * D), b16),
        pltpu.VMEM((MESHES, HS, 128), f32),
        pltpu.VMEM((HS, width), f32),
        pltpu.VMEM((D, width), f32),
        pltpu.VMEM((D, HS), f32),
        pltpu.VMEM((D, 3 * D), f32),
        pltpu.VMEM((4, D, 128), f32),
        pltpu.VMEM((DH, 128), f32),
        pltpu.VMEM((D, 2 * D), f32),
    ]

    args = Args(rows, width)
    args.far(sums1)
    args.whole(kept1, prob1, recv1)
    args.far(grads1)
    args.whole(ends1, grad_recv1)
    args.cols(de1, f1, m1, p1, u1, vh1, rs1, d21)
    args.rows_of(later, 0, 2 * D)
    args.layer(1, wsb)
    args.whole(wqb1)
    args.layer(1, norms)
    args.cols(gp0, z0, vh20, rs20, u20, e0, p0)
    args.rows_of(later, 2 * D, D)
    args.layer(0, w_up, w_down, norms)
    args.whole(gn1b)
    args.out_cols((D, f32), (D, b16))
    args.out_far((grad_sums_shape, f32))
    args.out_whole(*grad_ends_outs, ((LAYER_ROWS, 128), f32), ((4, 128), f32))
    if packed:
        args.out_whole(((n_head, n_pts, (D + 2 * rest_rows) // n_pts, 128), b16))
    else:
        args.out_whole(((D, 2 * D), b16), ((D, FF), b16), ((D, FF), b16), ((D, D), b16))
    (d20, de0, grads0, edge, ends0, small1, gn0b, *grads_b) = args.call(
        functools.partial(fourth_kernel, n_head, packed),
        scal,
        back_scratch[:3] + [pltpu.VMEM(grad_sums_shape, f32)] + back_scratch[3:] + grad_scratch,
        "fourth",
    )
    if packed:
        grad_recv0, total_a, chosen, row = swap_edges_sums(
            sizes, window, edge, part_a, owner.reshape(1, -1), collected, 6
        )
        mine_b = lax.psum_scatter(grads_b[0], "head", scatter_dimension=0, tiled=True)[0]
    else:
        grad_recv0 = swap_edges(sizes, window, edge, 4)

    args = Args(rows, width)
    args.far(sums0)
    args.whole(kept0, prob0, recv0)
    args.far(grads0)
    args.whole(ends0, grad_recv0)
    args.cols(de0, f0, m0, p0, u0, vh0, rs0, d20)
    args.whole(wfm0)
    args.layer(0, wsb)
    args.whole(wqb0)
    args.layer(0, norms)
    args.whole(gn0b, small1)
    args.out_points(f32)
    args.out_whole(((2 * LAYER_ROWS, 128), f32))
    args.out_whole(((n_head, D, 128), b16) if packed else ((D, 2 * D), b16))
    input_grad, small, front = args.call(
        functools.partial(fifth_kernel, n_head, packed), scal, back_scratch, "fifth"
    )

    if packed:
        total_b, total_c, total_s = total_gradients(sizes, mine_b, front, small)
        outs = update(total_a, total_b, total_c, total_s, row, chosen, tables, smalls)
        return (layer_out, input_grad, *outs)

    gup1, gdown1, gout1 = grads_a
    gfm1, gup0, gdown0, gout0 = grads_b
    small_total = lax.psum(small, ("pts", "head")).reshape(layers, -1)
    totals = []
    for parts in ((front, gout0, gup0, gdown0), (gfm1, gout1, gup1, gdown1)):
        blocks = lax.psum_scatter(
            flat_blocks(n_head, *parts), "head", scatter_dimension=0, tiled=True
        )
        totals.append(lax.psum(blocks.reshape(-1, BLOCK), "pts"))
    total_grad = jnp.concatenate(totals, axis=0).astype(f32)
    my_index = lax.axis_index("pts")
    block_ids = jnp.arange(owner.shape[0])
    same_owner = (owner[:, None] == owner[None, :]) & (block_ids[None, :] < block_ids[:, None])
    table_row = owner * cap + jnp.sum(same_owner.astype(jnp.int32), axis=1)
    place_all = (jnp.arange(n_pts * cap)[:, None] == table_row[None, :]).astype(f32)
    mine_place = lax.dynamic_slice_in_dim(place_all, my_index * cap, cap, 0)
    own_grad = jnp.dot(mine_place, total_grad, precision=lax.Precision.HIGHEST)
    filled = jnp.sum(mine_place, axis=1)[:, None] > 0.5
    updated = adam_update(master_table, own_grad, first_table, second_table, rate_large)
    new_tables = [jnp.where(filled, new, old) for new, old in zip(updated, tables)]
    collected = lax.all_gather(new_tables[0].astype(b16), "pts", axis=0, tiled=True)
    pick_back = (table_row[:, None] == jnp.arange(n_pts * cap)[None, :]).astype(b16)
    fresh = jnp.dot(pick_back, collected, preferred_element_type=f32).astype(b16)
    small_outs = adam_update(small_master, small_total, small_first, small_second, rate_small)
    return (layer_out, input_grad, *new_tables, fresh, *small_outs)


def solution(mesh):
    sizes = (mesh.shape["pts"], mesh.shape["head"])
    return jax.shard_map(
        functools.partial(on_device, sizes),
        mesh=mesh,
        in_specs=(
            P(("pts", "head"), None),
            P(("pts", "head"), None),
            P("pts"),
            P(),
            P(None, None, "head"),
            P(None, None, "head"),
            P(None, "head", None),
            P(),
            P(),
            P(),
            P(),
            P(),
            P("pts", "head"),
            P("pts", "head"),
            P("pts", "head"),
        ),
        out_specs=(
            P(("pts", "head"), None),
            P(("pts", "head"), None),
            P("pts", "head"),
            P("pts", "head"),
            P("pts", "head"),
            P(None, "head"),
            P(),
            P(),
            P(),
        ),
        check_vma=False,
    )
```

```python
import functools
import math

import jax
import jax.numpy as jnp
from jax import lax
from jax.experimental import pallas as pl
from jax.experimental.pallas import tpu as pltpu
from jax.sharding import PartitionSpec as P

D = 256
HEADS = 8
DH = 32
SLICES = 64
HS = HEADS * SLICES
FF = 1024
MESHES = 24
BLOCK = 2048
SMALL = 6144
STEP = 10
LARGEST = 12
EDGE = 80
VMEM_FULL = 58 << 20
VMEM_BYTES = 52 << 20

MESH = pl.DeviceIdType.MESH
HIGH = True
norm_eps = 1e-05
beta_one = 0.9
beta_two = 0.95
adam_eps = 1e-08
decay_rate = 0.1
rate_large = 0.1
rate_small = 0.75
f32 = jnp.float32
b16 = jnp.bfloat16


def dot(a, b, contract, precise):
    dims = (contract, ((), ()))
    if not precise:
        return lax.dot_general(a, b, dims, preferred_element_type=f32)
    a_high, b_high = a.astype(b16), b.astype(b16)
    a_low = (a - a_high.astype(f32)).astype(b16)
    b_low = (b - b_high.astype(f32)).astype(b16)
    return (
        lax.dot_general(a_high, b_low, dims, preferred_element_type=f32)
        + lax.dot_general(a_low, b_high, dims, preferred_element_type=f32)
        + lax.dot_general(a_high, b_high, dims, preferred_element_type=f32)
    )


def nn(a, b, precise=False):
    return dot(a, b, ((1,), (0,)), precise)


def nt(a, b, precise=False):
    return dot(a, b, ((1,), (1,)), precise)


def tn(a, b, precise=False):
    return dot(a, b, ((0,), (0,)), precise)


def iota(shape, axis):
    return lax.broadcasted_iota(jnp.int32, shape, axis)


def pick_diag(full, per_head):
    lane_head = iota((SLICES, full.shape[1]), 1) // per_head
    total = jnp.where(lane_head == 0, full[:SLICES], 0.0)
    for head in range(1, HEADS):
        total = total + jnp.where(
            lane_head == head, full[head * SLICES : (head + 1) * SLICES], 0.0
        )
    return total


def spread_diag(small):
    lane_head = iota((SLICES, D), 1) // DH
    return jnp.concatenate(
        [jnp.where(lane_head == head, small, jnp.zeros_like(small)) for head in range(HEADS)],
        axis=0,
    )


def repeat_rows(width):
    return (iota((D, width), 0) % width == iota((D, width), 1)).astype(f32)


def slice_repeat():
    return (iota((SLICES, HS), 1) % SLICES == iota((SLICES, HS), 0)).astype(f32)


def same_head(rows_per, cols_per, shape):
    return (iota(shape, 0) // rows_per) == (iota(shape, 1) // cols_per)


def start_gather(n_head, picks, send_sem, recv_sem):
    me = lax.axis_index("head")
    copies = []
    for index, ref in enumerate(picks):
        for step in range(1, n_head):
            copy = pltpu.make_async_remote_copy(
                src_ref=ref.at[:, me],
                dst_ref=ref.at[:, me],
                send_sem=send_sem.at[index, step - 1],
                recv_sem=recv_sem.at[index, step - 1],
                device_id={"head": lax.rem(me + step, n_head)},
                device_id_type=MESH,
            )
            copy.start()
            copies.append(copy)
    return copies


def unroll_slices(row_of, out):
    lane = iota((1, 128), 1)
    for pair in range(DH // 2):
        row = row_of(pair)
        out[2 * pair : 2 * pair + 1] = jnp.where(lane < SLICES, row, 0.0)
        out[2 * pair + 1 : 2 * pair + 2] = jnp.where(
            lane < SLICES, pltpu.roll(row, 128 - SLICES, 1), 0.0
        )


def opening_kernel(n_head, tiles, ids_ref, wfx_ref, wmid_ref, sm_ref, m_ref, v_ref, w_ref,
                   out_ref, wsb_ref, norm_ref, scal_ref, tables_ref, send_sem, recv_sem, slices_s, norm_s):
    me = lax.axis_index("head")
    barrier = pltpu.get_barrier_semaphore()
    for step in range(1, n_head):
        pl.semaphore_signal(
            barrier, inc=1, device_id={"head": lax.rem(me + step, n_head)}, device_id_type=MESH
        )
    out_ref[0, me] = wfx_ref[0]
    out_ref[1, me] = wmid_ref[0]
    pl.semaphore_wait(barrier, n_head - 1)
    copies = start_gather(n_head, [out_ref], send_sem, recv_sem)
    layers = sm_ref.shape[0]
    cap, deep = m_ref.shape[0], tables_ref.shape[0]
    for which, ref in enumerate((m_ref, v_ref, w_ref)):
        value = ref[...]
        if deep > cap:
            value = jnp.concatenate([value, jnp.zeros((deep - cap, BLOCK), f32)], axis=0)
        tables_ref[:, which * BLOCK : (which + 1) * BLOCK] = value.astype(b16)
    right = (iota((128, HS), 1) % SLICES == iota((128, HS), 0)).astype(b16)
    for layer in range(layers):
        unroll_slices(lambda pair: sm_ref[layer : layer + 1, 128 * pair : 128 * pair + 128], slices_s)
        wide = nn(slices_s[...].astype(b16), right)
        tiled = jnp.concatenate([wide] * HEADS, axis=0)
        wsb_ref[layer] = jnp.where(same_head(DH, SLICES, (D, HS)), tiled, 0.0).astype(b16)
        norm_s[...] = jnp.zeros_like(norm_s)
        for row in range(4):
            start = SMALL - 4 * D + row * D
            norm_s[row : row + 1] = sm_ref[layer : layer + 1, start : start + D]
        norm_ref[layer] = norm_s[...].T
    rows = ids_ref.shape[0] // n_head
    ids = ids_ref[pl.ds(pl.multiple_of(me * rows, rows), rows), :]
    for mesh in range(MESHES + 1):
        scal_ref[mesh] = jnp.sum((ids < mesh).astype(jnp.int32))
    deep = rows // tiles
    for tile in range(tiles):
        part = ids[tile * deep : (tile + 1) * deep]
        scal_ref[MESHES + 1 + 2 * tile] = jnp.min(part)
        scal_ref[MESHES + 2 + 2 * tile] = jnp.max(part)
    for copy in copies:
        copy.wait()


def opening(n_head, tiles, ids, w_fx, w_mid, small, tables):
    layers, part, _ = w_fx.shape
    deep = -(-tables[0].shape[0] // 16) * 16
    vmem = pl.BlockSpec(memory_space=pltpu.VMEM)
    return pl.pallas_call(
        functools.partial(opening_kernel, n_head, tiles),
        out_shape=(
            jax.ShapeDtypeStruct((2, n_head, part, D), b16),
            jax.ShapeDtypeStruct((layers, D, HS), b16),
            jax.ShapeDtypeStruct((layers, D, 128), f32),
            jax.ShapeDtypeStruct((MESHES + 1 + 2 * tiles,), jnp.int32),
            jax.ShapeDtypeStruct((deep, 3 * BLOCK), b16),
        ),
        in_specs=[vmem] * 7,
        out_specs=[vmem] * 3 + [pl.BlockSpec(memory_space=pltpu.SMEM), vmem],
        scratch_shapes=[
            pltpu.SemaphoreType.DMA((1, n_head - 1)),
            pltpu.SemaphoreType.DMA((1, n_head - 1)),
            pltpu.VMEM((DH, 128), f32),
            pltpu.VMEM((128, D), f32),
        ],
        cost_estimate=pl.CostEstimate(flops=0, bytes_accessed=32 << 20, transcendentals=0),
        compiler_params=pltpu.CompilerParams(
            collective_id=0, has_side_effects=True, vmem_limit_bytes=VMEM_FULL
        ),
        name="opening",
    )(ids, w_fx, w_mid, small, *tables)


def place_of(sizes, shift):
    n_pts, n_head = sizes
    total = n_pts * n_head
    me = lax.axis_index("pts") * n_head + lax.axis_index("head")
    other = lax.rem(me + (shift + total), total)
    return (other // n_head, lax.rem(other, n_head))


def greet(sizes, window):
    barrier = pltpu.get_barrier_semaphore()
    for step in range(1, window + 1):
        for shift in (step, -step):
            pl.semaphore_signal(barrier, inc=1, device_id=place_of(sizes, shift), device_id_type=MESH)
    return barrier


def start_edges(sizes, window, edge_ref, out_ref, send_sem, recv_sem):
    copies = []
    for step in range(1, window + 1):
        for side, shift in ((1, step), (0, -step)):
            slot = step - 1 if side == 1 else window + step - 1
            copy = pltpu.make_async_remote_copy(
                src_ref=edge_ref.at[side],
                dst_ref=out_ref.at[slot],
                send_sem=send_sem.at[slot],
                recv_sem=recv_sem.at[slot],
                device_id=place_of(sizes, shift),
                device_id_type=MESH,
            )
            copy.start()
            copies.append(copy)
    return copies


def edge_kernel(sizes, window, edge_ref, out_ref, send_sem, recv_sem):
    barrier = greet(sizes, window)
    pl.semaphore_wait(barrier, 2 * window)
    for copy in start_edges(sizes, window, edge_ref, out_ref, send_sem, recv_sem):
        copy.wait()


def edge_weights_kernel(sizes, window, layer, pieces, edge_ref, wfx_ref, wmid_ref, wout_ref, sm_ref,
                        out_ref, w_ref, wqb_ref,
                        send_sem, recv_sem, wsend_sem, wrecv_sem, square_s):
    n_head = sizes[1]
    me = lax.axis_index("head")
    barrier = greet(sizes, window)
    for step in range(1, n_head):
        pl.semaphore_signal(
            barrier, inc=1, device_id={"head": lax.rem(me + step, n_head)}, device_id_type=MESH
        )
    refs = (wfx_ref, wmid_ref, wout_ref)
    for index, (kind, which) in enumerate(pieces):
        w_ref[index, me] = refs[kind][which]
    pl.semaphore_wait(barrier, 2 * window + n_head - 1)
    copies = start_edges(sizes, window, edge_ref, out_ref, send_sem, recv_sem)
    copies += start_gather(n_head, [w_ref], wsend_sem, wrecv_sem)
    lane = iota((1, 128), 1)
    for part in range(3):
        start = DH * SLICES + part * DH * DH
        for group in range(DH // 4):
            row = sm_ref[layer : layer + 1, start + 128 * group : start + 128 * group + 128]
            for inner in range(4):
                moved = row if inner == 0 else pltpu.roll(row, 128 - DH * inner, 1)
                square_s[4 * group + inner : 4 * group + inner + 1] = jnp.where(
                    lane < DH, moved, 0.0
                )
        square = square_s[...]
        for turn in range(1, 128 // DH):
            square = square + pltpu.roll(square_s[...], DH * turn, 1)
        square = jnp.concatenate([square] * (D // 128), axis=1)
        square = jnp.concatenate([square] * HEADS, axis=0)
        wqb_ref[:, part * D : (part + 1) * D] = jnp.where(
            same_head(DH, DH, (D, D)), square, 0.0
        )
    for copy in copies:
        copy.wait()


def pick_rows(n_pts, owner_ref, tables_s, load, chosen_ref, row_ref):
    blocks = owner_ref.shape[1]
    deep = tables_s.shape[0] // n_pts
    across = jnp.broadcast_to(owner_ref[...].astype(f32), (blocks, blocks))
    down = across.T
    low, high = iota((blocks, blocks), 0), iota((blocks, blocks), 1)
    same = across == down
    slot_down = jnp.sum(jnp.where(same & (high < low), 1.0, 0.0), axis=1, keepdims=True)
    slot_across = jnp.sum(jnp.where(same & (low < high), 1.0, 0.0), axis=0, keepdims=True)
    mine = owner_ref[...] == lax.axis_index("pts")
    row_ref[...] = jnp.broadcast_to(
        jnp.where(mine, slot_across.astype(jnp.int32), -1), row_ref.shape
    )
    target = (down[:, :1] * deep + slot_down).astype(jnp.int32)
    pick = (iota((blocks, tables_s.shape[0]), 1) == target).astype(b16)
    load.wait()
    step = 1024

    def choose(part, carry):
        lanes = pl.ds(pl.multiple_of(part * step, step), step)
        chosen_ref[:, lanes] = nn(pick, tables_s[:, lanes]).astype(b16)
        return carry

    lax.fori_loop(0, tables_s.shape[1] // step, choose, 0)


def edge_call(window, collective_id, rows, width, body, extra, outs, scratch, name):
    vmem = pl.BlockSpec(memory_space=pltpu.VMEM)
    outs = [jax.ShapeDtypeStruct((2 * window, rows, width), b16)] + outs
    return pl.pallas_call(
        body,
        out_shape=outs,
        in_specs=[vmem] * (1 + extra),
        out_specs=[vmem] * len(outs),
        scratch_shapes=[
            pltpu.SemaphoreType.DMA((2 * window,)),
            pltpu.SemaphoreType.DMA((2 * window,)),
        ]
        + scratch,
        cost_estimate=pl.CostEstimate(flops=0, bytes_accessed=32 << 20, transcendentals=0),
        compiler_params=pltpu.CompilerParams(
            collective_id=collective_id, has_side_effects=True, vmem_limit_bytes=VMEM_BYTES
        ),
        name=name,
    )


def swap_edges(sizes, window, edge, collective_id):
    _, rows, width = edge.shape
    return edge_call(
        window, collective_id, rows, width,
        functools.partial(edge_kernel, sizes, window), 0, [], [], "swap_edges",
    )(edge)[0]


def swap_edges_weights(sizes, window, layer, pieces, edge, w_fx, w_mid, w_out, small, collective_id):
    _, rows, width = edge.shape
    n_head = sizes[1]
    part = w_fx.shape[1]
    return edge_call(
        window, collective_id, rows, width,
        functools.partial(edge_weights_kernel, sizes, window, layer, pieces), 4,
        [
            jax.ShapeDtypeStruct((len(pieces), n_head, part, D), b16),
            jax.ShapeDtypeStruct((D, 3 * D), f32),
        ],
        [
            pltpu.SemaphoreType.DMA((1, n_head - 1)),
            pltpu.SemaphoreType.DMA((1, n_head - 1)),
            pltpu.VMEM((DH, 128), f32),
        ],
        "swap_edges_weights",
    )(edge, w_fx, w_mid, w_out, small)


def pts_copies(n_pts, source, target, send_sem, recv_sem):
    pts, head = lax.axis_index("pts"), lax.axis_index("head")
    copies = []
    for step in range(1, n_pts):
        peer = lax.rem(pts + step, n_pts)
        copies.append(
            pltpu.make_async_remote_copy(
                src_ref=source(step, peer),
                dst_ref=target(step, peer),
                send_sem=send_sem.at[step - 1],
                recv_sem=recv_sem.at[step - 1],
                device_id=(peer, head),
                device_id_type=MESH,
            )
        )
    return copies


def edge_sums_kernel(sizes, window, edge_ref, ga_ref, owner_ref, tables_ref, out_ref, ta_ref, chosen_ref, row_ref,
                     send_sem, recv_sem, a_send, a_recv, a_send2, a_recv2, got_a, tables_s, local_sem):
    n_pts, n_head = sizes
    pts, head = lax.axis_index("pts"), lax.axis_index("head")
    barrier = greet(sizes, window)
    for step in range(1, n_pts):
        pl.semaphore_signal(
            barrier, inc=1, device_id=(lax.rem(pts + step, n_pts), head), device_id_type=MESH
        )
    load = pltpu.make_async_copy(tables_ref, tables_s, local_sem)
    load.start()
    pl.semaphore_wait(barrier, 2 * window + n_pts - 1)
    edges = start_edges(sizes, window, edge_ref, out_ref, send_sem, recv_sem)
    gather = pts_copies(
        n_pts,
        lambda step, peer: ga_ref.at[peer],
        lambda step, peer: got_a.at[step - 1],
        a_send,
        a_recv,
    )
    for copy in gather:
        copy.start()
    for copy in gather:
        copy.wait()
    total = ga_ref[pts].astype(f32)
    for index in range(n_pts - 1):
        total = total + got_a[index].astype(f32)
    ta_ref[pts] = total.astype(b16)
    share = pts_copies(
        n_pts,
        lambda step, peer: ta_ref.at[pts],
        lambda step, peer: ta_ref.at[pts],
        a_send2,
        a_recv2,
    )
    for copy in share:
        copy.start()
    pick_rows(n_pts, owner_ref, tables_s, load, chosen_ref, row_ref)
    for copy in edges:
        copy.wait()
    for copy in share:
        copy.wait()


def swap_edges_sums(sizes, window, edge, ga, owner, tables, collective_id):
    _, rows, width = edge.shape
    n_pts = sizes[0]
    blocks = owner.shape[1]
    dma = pltpu.SemaphoreType.DMA
    vmem = pl.BlockSpec(memory_space=pltpu.VMEM)
    return pl.pallas_call(
        functools.partial(edge_sums_kernel, sizes, window),
        out_shape=(
            jax.ShapeDtypeStruct((2 * window, rows, width), b16),
            jax.ShapeDtypeStruct(ga.shape, b16),
            jax.ShapeDtypeStruct((blocks, tables.shape[1]), b16),
            jax.ShapeDtypeStruct((8, blocks), jnp.int32),
        ),
        in_specs=[vmem] * 3 + [pl.BlockSpec(memory_space=pl.ANY)],
        out_specs=[vmem] * 4,
        scratch_shapes=[dma((2 * window,))] * 2
        + [dma((n_pts - 1,))] * 4
        + [
            pltpu.VMEM((n_pts - 1,) + ga.shape[1:], b16),
            pltpu.VMEM(tables.shape, b16),
            dma,
        ],
        cost_estimate=pl.CostEstimate(flops=0, bytes_accessed=32 << 20, transcendentals=0),
        compiler_params=pltpu.CompilerParams(
            collective_id=collective_id, has_side_effects=True, vmem_limit_bytes=VMEM_BYTES
        ),
        name="swap_edges_sums",
    )(edge, ga, owner, tables)


def norm_stats(values):
    center = jnp.mean(values, axis=0, keepdims=True)
    spread = values - center
    scale = lax.rsqrt(jnp.mean(spread * spread, axis=0, keepdims=True) + norm_eps)
    return (spread * scale, scale)


def norm_back(grad_out, scaled, scale, gain):
    inner = grad_out * gain
    return scale * (
        inner
        - jnp.mean(inner, axis=0, keepdims=True)
        - scaled * jnp.mean(inner * scaled, axis=0, keepdims=True)
    )


def group_sum(values):
    return jnp.sum(values.reshape(HEADS, SLICES, values.shape[1]), axis=1, keepdims=True)


def fold_lanes(values):
    total = values[:, :128]
    for start in range(128, values.shape[1], 128):
        total = total + values[:, start : start + 128]
    return total


def tile_mask(scal, mesh, tile, width):
    spot = iota((1, width), 1) + tile * width
    return (spot >= scal[mesh]) & (spot < scal[mesh + 1])


def tile_range(scal, tiles, tile):
    base = MESHES + 1
    ratio = (scal.shape[0] - base) // 2 // tiles
    return (scal[base + 2 * ratio * tile], scal[base + 2 * ratio * (tile + 1) - 1])


def front_tile(scal, tiles, tile, x, wfm, wsb, norms, vh_ref, rs_ref, u_ref, f_ref, m_ref, p_ref, sums):
    width = x.shape[1]
    scaled, scale = norm_stats(x)
    vh_ref[...] = scaled.astype(b16)
    rs_ref[...] = jnp.broadcast_to(scale, (8, width))
    normed = (scaled * norms[:, 0:1] + norms[:, 1:2]).astype(b16)
    u_ref[...] = normed
    joint = nn(wfm, normed)
    feats = joint[:D].astype(b16)
    middle = joint[D:].astype(b16)
    f_ref[...] = feats
    m_ref[...] = middle
    logits = tn(wsb, middle).reshape(HEADS, SLICES, width)
    top = jnp.max(logits, axis=1, keepdims=True)
    expo = jnp.exp(logits - top)
    weights = expo / jnp.sum(expo, axis=1, keepdims=True)
    weights_r = weights.reshape(HS, width).astype(b16)
    p_ref[...] = weights_r
    low, high = tile_range(scal, tiles, tile)

    def add(mesh, carry):
        keep = tile_mask(scal, mesh, tile, width).astype(b16)
        wide = jnp.concatenate(
            [feats * keep, jnp.broadcast_to(keep, (D, width))], axis=0
        )
        full = nt(weights_r, wide)
        sums[mesh, :, :D] += pick_diag(full[:, :D], DH)
        sums[mesh, :, D:] += pick_diag(full[:, D:], DH)
        return carry

    lax.fori_loop(low, high + 1, add, 0)


def present(scal, tiles, body):
    def one(mesh, carry):
        body(mesh)
        return carry

    lax.fori_loop(tile_range(scal, tiles, 0)[0], tile_range(scal, tiles, tiles - 1)[1] + 1, one, 0)


def ends_of(scal, tiles):
    return (tile_range(scal, tiles, 0)[0], tile_range(scal, tiles, tiles - 1)[1])


def between(scal, tiles, body):
    first, last = ends_of(scal, tiles)

    def one(mesh, carry):
        body(mesh)
        return carry

    lax.fori_loop(first + 1, last, one, 0)


def fetch(source, target, sem):
    copy = pltpu.make_async_copy(source, target, sem)
    copy.start()
    copy.wait()


def clear_present(scal, tiles, sums):
    def clear(mesh):
        sums[mesh] = jnp.zeros(sums.shape[1:], f32)

    present(scal, tiles, clear)


def write_edges(scal, tiles, sums, edge_ref, ends_ref, sums_hbm, sem):
    first, last = ends_of(scal, tiles)
    extra = EDGE - SLICES
    for side, mesh in ((0, first), (1, last)):
        ends_ref[side] = sums[mesh]
        edge_ref[side, :SLICES] = sums[mesh, :, :D].astype(b16)
        rows = jnp.zeros((extra, D), f32)
        if sums.shape[2] > D:
            counts = jnp.concatenate(
                [sums[mesh, :, D:], jnp.zeros((D - SLICES, D), f32)], axis=0
            )
            pick = (iota((extra, D), 1) == DH * iota((extra, D), 0)).astype(f32)
            rows = nt(pick, counts, HIGH)
        edge_ref[side, SLICES:] = jnp.where(
            iota((extra, D), 0) >= HEADS, mesh.astype(f32), rows
        ).astype(b16)
    between(scal, tiles, lambda mesh: fetch(sums.at[mesh], sums_hbm.at[mesh], sem))


def add_edges(own, mesh, recv_ref):
    wanted = mesh.astype(f32)
    total = jnp.zeros((EDGE, D), f32)
    for slot in range(recv_ref.shape[0]):
        match = recv_ref[slot, SLICES + HEADS : SLICES + HEADS + 1].astype(f32) == wanted
        total = total + jnp.where(match, recv_ref[slot].astype(f32), 0.0)
    if own.shape[1] == D:
        return own + total[:SLICES]
    extra = EDGE - SLICES
    spread = (iota((extra, D), 1) // DH == iota((extra, D), 0)).astype(f32)
    counts = tn(total[SLICES:, :SLICES], spread, HIGH)
    return own + jnp.concatenate([total[:SLICES], counts], axis=1)


def attend_parts(totals, wqb):
    total = jnp.concatenate(totals, axis=0)
    count = total[:, D:]
    slice_tok = total[:, :D] / count
    triple = nn(slice_tok, wqb, HIGH)
    parts = []
    for index in range(len(totals)):
        rows = slice(index * SLICES, (index + 1) * SLICES)
        queries = triple[rows, :D]
        key_wide = spread_diag(triple[rows, D : 2 * D])
        value_wide = spread_diag(triple[rows, 2 * D :])
        scores = (nt(key_wide, queries, HIGH) * (1.0 / math.sqrt(DH))).reshape(
            HEADS, SLICES, SLICES
        )
        expo = jnp.exp(scores - jnp.max(scores, axis=1, keepdims=True))
        prob = (expo / jnp.sum(expo, axis=1, keepdims=True)).reshape(HS, SLICES)
        parts.append((queries, key_wide, value_wide, prob))
    return (slice_tok, count, triple, parts)


def attend_all(scal, tiles, ends_ref, recv_ref, sums_hbm, wqb, attended_ref, kept_ref, prob_ref, spare, sem):
    ends = ends_of(scal, tiles)
    totals = [add_edges(ends_ref[side], mesh, recv_ref) for side, mesh in enumerate(ends)]
    slice_tok, count, triple, parts = attend_parts(totals, wqb)
    kept = jnp.concatenate([slice_tok, count, triple], axis=1)
    results = []
    for side, (_, _, value_wide, prob) in enumerate(parts):
        results.append(tn(prob, value_wide, HIGH).astype(b16))
        kept_ref[side] = kept[side * SLICES : (side + 1) * SLICES]
        prob_ref[side] = prob
    for mesh, result in zip(ends, results):
        attended_ref[mesh] = result

    def inner(mesh):
        fetch(sums_hbm.at[mesh], spare, sem)
        _, _, _, parts = attend_parts([spare[...]], wqb)
        attended_ref[mesh] = tn(parts[0][3], parts[0][2], HIGH).astype(b16)

    between(scal, tiles, inner)


def spread_tile(scal, tiles, tile, wide_ref, p_ref, spread):
    low, high = tile_range(scal, tiles, tile)
    weights_r = p_ref[...]
    width = weights_r.shape[1]

    def one(mesh, carry):
        keep = tile_mask(scal, mesh, tile, width)
        spread[...] = jnp.where(keep, tn(spread_diag(wide_ref[mesh]), weights_r), spread[...])
        return carry

    lax.fori_loop(low, high + 1, one, 0)
    return spread[...].astype(b16)


GELU_A = math.sqrt(2.0 / math.pi)
GELU_B = 0.044715


def gelu_pair(hidden):
    square = hidden * hidden
    bend = jnp.tanh(hidden * (GELU_A + (GELU_A * GELU_B) * square))
    half = 0.5 + 0.5 * bend
    value = hidden * half
    slope = half + (0.5 * hidden) * (1.0 - bend * bend) * (
        GELU_A + (3.0 * GELU_A * GELU_B) * square
    )
    return (value, slope)


CHUNK = 1024


def mlp_back_tile(scal, tiles, tile, grad, slopes, actives, scaled_two, scale_two, normed_two_r, spread_r,
                  weights_r, wout, wup, wdown, norms, d2_ref, de_ref, sums,
                  gup, gdown, gout, gnorm):
    width = grad.shape[1]
    grad_r = grad.astype(b16)
    grad_normed = jnp.zeros((D, width), f32)
    for start in range(0, FF, CHUNK):
        part = slice(start, start + CHUNK)
        back = (slopes(part) * nn(wdown[part], grad_r)).astype(b16)
        gup[:, part] += nt(normed_two_r, back)
        gdown[:, part] += nt(grad_r, actives(part))
        grad_normed = grad_normed + nn(wup[:, part], back)
    gnorm[2] += fold_lanes(grad_normed * scaled_two)
    gnorm[3] += fold_lanes(grad_normed)
    grad_middle = grad + norm_back(grad_normed, scaled_two, scale_two, norms[:, 2:3])
    d2_ref[...] = grad_middle
    branch_r = grad_middle.astype(b16)
    gout[...] += nt(spread_r, branch_r)
    spread_grad = nn(wout, branch_r).astype(b16)
    de_ref[...] = spread_grad
    low, high = tile_range(scal, tiles, tile)

    def add(mesh, carry):
        keep = tile_mask(scal, mesh, tile, width).astype(b16)
        sums[mesh] += pick_diag(nt(weights_r, spread_grad * keep), DH)
        return carry

    lax.fori_loop(low, high + 1, add, 0)


def attend_back(meshes, shares, slice_tok, count, parts, outer, wqb, both, dcount, gqkv):
    root = 1.0 / math.sqrt(DH)
    attended, triples = [], []
    for (queries, key_wide, value_wide, prob), grad in zip(parts, outer):
        attended.append(tn(prob, value_wide, HIGH).astype(b16))
        inner = prob * nt(value_wide, grad, HIGH)
        mixed = group_sum(inner)
        grad_scores = root * (
            inner - (prob.reshape(HEADS, SLICES, SLICES) * mixed).reshape(HS, SLICES)
        )
        triples.append(
            jnp.concatenate(
                [
                    tn(grad_scores, key_wide, HIGH),
                    pick_diag(nn(grad_scores, queries, HIGH), DH),
                    pick_diag(nn(prob, grad, HIGH), DH),
                ],
                axis=1,
            )
        )
    triple = jnp.concatenate(triples, axis=0)
    grad_sum = nt(triple, wqb, HIGH) / count
    grad_count = -(grad_sum * slice_tok)
    gqkv[...] += tn(slice_tok * jnp.concatenate(shares, axis=0), triple, HIGH)
    for index, mesh in enumerate(meshes):
        rows = slice(index * SLICES, (index + 1) * SLICES)
        both[mesh, :, :D] = spread_diag(attended[index])
        both[mesh, :, D:] = spread_diag(grad_sum[rows].astype(b16))
        column = jnp.sum(spread_diag(grad_count[rows]), axis=1, keepdims=True)
        dcount[mesh] = jnp.broadcast_to(column, (HS, 128))


def attend_back_all(scal, tiles, kept_ref, prob_ref, recv_ref, ends_ref, grad_recv_ref, sums_hbm, grads_hbm,
                    wqb, both, dcount, gqkv, spare, spare_grad, sem):
    ends = ends_of(scal, tiles)
    outer = [add_edges(ends_ref[side], mesh, grad_recv_ref) for side, mesh in enumerate(ends)]
    kept = jnp.concatenate([kept_ref[0], kept_ref[1]], axis=0)
    parts = []
    for side in range(2):
        parts.append(
            (
                kept_ref[side, :, 2 * D : 3 * D],
                spread_diag(kept_ref[side, :, 3 * D : 4 * D]),
                spread_diag(kept_ref[side, :, 4 * D :]),
                prob_ref[side],
            )
        )
    previous = recv_ref[0, SLICES + HEADS : SLICES + HEADS + 1, :1].astype(f32)
    shares = [
        jnp.broadcast_to(1.0 - (previous == ends[0].astype(f32)).astype(f32), (SLICES, 1)),
        jnp.broadcast_to((ends[1] != ends[0]).astype(f32), (SLICES, 1)),
    ]
    attend_back(ends, shares, kept[:, :D], kept[:, D : 2 * D], parts, outer, wqb, both, dcount, gqkv)

    def inner(mesh):
        fetch(sums_hbm.at[mesh], spare, sem)
        fetch(grads_hbm.at[mesh], spare_grad, sem)
        slice_tok, count, _, parts = attend_parts([spare[...]], wqb)
        attend_back(
            (mesh,), [jnp.ones((SLICES, 1), f32)], slice_tok, count, parts, [spare_grad[...]], wqb, both, dcount, gqkv
        )

    between(scal, tiles, inner)


def attend_back_tile(scal, tiles, tile, both, dcount, de_ref, f_ref, m_ref, p_ref, u_ref, vh_ref, rs_ref,
                     d2_ref, wfm, wsb, norms, grad_p, grad_f, gfm, gws, gnorm):
    low, high = tile_range(scal, tiles, tile)
    weights_r = p_ref[...]
    width = weights_r.shape[1]
    pair = jnp.concatenate([de_ref[...], f_ref[...]], axis=0)

    def one(mesh, carry):
        keep = tile_mask(scal, mesh, tile, width)
        back = nn(both[mesh], pair) + dcount[mesh][:, :1]
        grad_p[...] = jnp.where(keep, back, grad_p[...])
        grad_f[...] = jnp.where(keep, tn(both[mesh, :, D:], weights_r), grad_f[...])
        return carry

    lax.fori_loop(low, high + 1, one, 0)
    weights = weights_r.astype(f32)
    inner = weights * grad_p[...]
    mixed = group_sum(inner)
    grad_logits = (
        inner - (weights.reshape(HEADS, SLICES, width) * mixed).reshape(HS, width)
    ).astype(b16)
    gws[...] += nt(m_ref[...], grad_logits)
    grad_m = nn(wsb, grad_logits).astype(b16)
    grad_fm = jnp.concatenate([grad_f[...].astype(b16), grad_m], axis=0)
    gfm[...] += nt(u_ref[...], grad_fm)
    grad_normed = tn(wfm, grad_fm)
    scaled = vh_ref[...].astype(f32)
    gnorm[0] += fold_lanes(grad_normed * scaled)
    gnorm[1] += fold_lanes(grad_normed)
    return d2_ref[...] + norm_back(grad_normed, scaled, rs_ref[:1], norms[:, 0:1])


def small_rows(base, gws, gqkv, scratch, out_ref):
    lane = iota((1, 128), 1)
    left = repeat_rows(DH)
    fold = (iota((128, HS), 1) % SLICES == iota((128, HS), 0)).astype(f32)
    kept = jnp.where(same_head(DH, SLICES, (D, HS)), gws[...], 0.0)
    scratch[...] = nt(tn(left, kept, HIGH), fold, HIGH)
    even = scratch[pl.ds(0, DH // 2, stride=2), :]
    odd = scratch[pl.ds(1, DH // 2, stride=2), :]
    out_ref[base : base + DH // 2] = jnp.where(lane < SLICES, even, pltpu.roll(odd, SLICES, 1))
    fold = (iota((D, 128), 0) % DH == iota((D, 128), 1)).astype(f32)
    for part in range(3):
        square = jnp.where(same_head(DH, DH, (D, D)), gqkv[:, part * D : (part + 1) * D], 0.0)
        scratch[...] = nn(tn(left, square, HIGH), fold, HIGH)
        total = scratch[pl.ds(0, DH // 4, stride=4), :]
        for inner in range(1, 4):
            total = total + pltpu.roll(scratch[pl.ds(inner, DH // 4, stride=4), :], DH * inner, 1)
        start = base + DH // 2 + part * (DH // 4)
        out_ref[start : start + DH // 4] = total


NORM_ROW = (SMALL - 4 * D) // 128
LAYER_ROWS = SMALL // 128


def norm_rows(gnorm, index, out_ref, base):
    lane = iota((D, 128), 1)
    total = jnp.zeros((D, 128), f32)
    for column, row in enumerate(index):
        total = total + jnp.where(lane == column, jnp.sum(gnorm[row], axis=1, keepdims=True), 0.0)
    flat = total.T
    for column in range(len(index)):
        for half in range(D // 128):
            place = base + column * (D // 128) + half
            out_ref[place : place + 1] = flat[column : column + 1, 128 * half : 128 * half + 128]


def pack_front(gfm, head):
    lane = iota((D, 128), 1)
    start = (head // 2) * 128
    feats, middle = gfm[:, start : start + 128], gfm[:, D + start : D + start + 128]
    if head % 2 == 0:
        return jnp.where(lane < 64, feats, pltpu.roll(middle, 64, 1))
    return jnp.where(lane < 64, pltpu.roll(feats, 64, 1), middle)


def store_pieces(out_ref, head, base, value):
    size = out_ref.shape[2]
    done = 0
    while done < value.shape[0]:
        chunk, offset = divmod(base + done, size)
        count = min(size - offset, value.shape[0] - done)
        for half in range(2):
            out_ref[head, 2 * chunk + half, offset : offset + count] = value[
                done : done + count, 128 * half : 128 * half + 128
            ]
        done += count


def pack_rest(gout, gup, gdown, out_ref, base, n_head):
    for head in range(n_head):
        deep, wide = D // n_head, FF // n_head
        store_pieces(out_ref, head, base, gout[head * deep : (head + 1) * deep].astype(b16))
        start = base + deep
        store_pieces(out_ref, head, start, gup[:, head * wide : (head + 1) * wide].astype(b16))
        store_pieces(out_ref, head, start + D, gdown[:, head * wide : (head + 1) * wide].astype(b16))


def first_kernel(tiles, scal, tok_ref, wfm_ref, wsb_ref, norm_ref,
                 xt_ref, vh_ref, rs_ref, u_ref, f_ref, m_ref, p_ref, sums_hbm, edge_ref, ends_ref, sums, sem):
    tile = pl.program_id(0)

    @pl.when(tile == 0)
    def _():
        clear_present(scal, tiles, sums)

    turned = tok_ref[...].T
    xt_ref[...] = turned
    x = turned.astype(f32)
    front_tile(scal, tiles, tile, x, wfm_ref[...], wsb_ref[...], norm_ref[...],
               vh_ref, rs_ref, u_ref, f_ref, m_ref, p_ref, sums)

    @pl.when(tile == tiles - 1)
    def _():
        write_edges(scal, tiles, sums, edge_ref, ends_ref, sums_hbm, sem)


def second_kernel(tiles, scal, xt_ref, p0_ref, sums0_hbm, ends0_ref, recv_ref, wout_ref, wup_ref, wdown_ref, wqb_ref, norm0_ref,
                  wfm_ref, wsb_ref, norm1_ref,
                  e_ref, vh2_ref, rs2_ref, u2_ref, gp_ref, z_ref, kept_ref, prob_ref,
                  x1_ref, vh_ref, rs_ref, u_ref, f_ref, m_ref, p_ref, sums_hbm, edge_ref, ends_ref,
                  wide, spread, spare, sums, sem):
    tile = pl.program_id(0)

    @pl.when(tile == 0)
    def _():
        attend_all(scal, tiles, ends0_ref, recv_ref, sums0_hbm, wqb_ref[...], wide, kept_ref, prob_ref, spare, sem)
        clear_present(scal, tiles, sums)

    norms = norm0_ref[...]
    spread_r = spread_tile(scal, tiles, tile, wide, p0_ref, spread)
    e_ref[...] = spread_r
    middle = xt_ref[...].astype(f32) + tn(wout_ref[...], spread_r)
    scaled_two, scale_two = norm_stats(middle)
    vh2_ref[...] = scaled_two.astype(b16)
    rs2_ref[...] = jnp.broadcast_to(scale_two, rs2_ref.shape)
    normed_two_r = (scaled_two * norms[:, 2:3] + norms[:, 3:4]).astype(b16)
    u2_ref[...] = normed_two_r
    x = middle
    for start in range(0, FF, CHUNK):
        part = slice(start, start + CHUNK)
        active, slope = gelu_pair(tn(wup_ref[:, part], normed_two_r))
        active_r = active.astype(b16)
        z_ref[part] = active_r
        gp_ref[part] = slope.astype(b16)
        x = x + tn(wdown_ref[part], active_r)
    x1_ref[...] = x
    front_tile(scal, tiles, tile, x, wfm_ref[...], wsb_ref[...], norm1_ref[...],
               vh_ref, rs_ref, u_ref, f_ref, m_ref, p_ref, sums)

    @pl.when(tile == tiles - 1)
    def _():
        write_edges(scal, tiles, sums, edge_ref, ends_ref, sums_hbm, sem)


def third_kernel(n_head, packed, tiles, scal, x1_ref, p_ref, sums1_hbm, ends1_ref, recv_ref, cot_ref, wout_ref, wup_ref, wdown_ref, wqb_ref, norm_ref,
                 out_ref, d2_ref, de_ref, kept_ref, prob_ref, grads_hbm, edge_ref, ends_ref,
                 gn_ref, *rest):
    grad_outs, (wide, spread, spare, grads, sem, gnorm, slope_s, active_s, gup, gdown, gout) = rest[:-11], rest[-11:]
    tile = pl.program_id(0)

    @pl.when(tile == 0)
    def _():
        clear_present(scal, tiles, grads)
        gup[...] = jnp.zeros_like(gup)
        gdown[...] = jnp.zeros_like(gdown)
        gout[...] = jnp.zeros_like(gout)
        gnorm[...] = jnp.zeros_like(gnorm)
        attend_all(scal, tiles, ends1_ref, recv_ref, sums1_hbm, wqb_ref[...], wide, kept_ref, prob_ref, spare, sem)

    norms = norm_ref[...]
    spread_r = spread_tile(scal, tiles, tile, wide, p_ref, spread)
    middle = x1_ref[...] + tn(wout_ref[...], spread_r)
    scaled_two, scale_two = norm_stats(middle)
    normed_two_r = (scaled_two * norms[:, 2:3] + norms[:, 3:4]).astype(b16)
    x = middle
    for start in range(0, FF, CHUNK):
        part = slice(start, start + CHUNK)
        active, slope = gelu_pair(tn(wup_ref[:, part], normed_two_r))
        active_r = active.astype(b16)
        active_s[part] = active_r
        slope_s[part] = slope
        x = x + tn(wdown_ref[part], active_r)
    out_ref[...] = x.astype(b16).T
    grad = cot_ref[...].T.astype(f32)
    mlp_back_tile(scal, tiles, tile, grad, lambda part: slope_s[part], lambda part: active_s[part],
                  scaled_two, scale_two, normed_two_r, spread_r, p_ref[...],
                  wout_ref[...], wup_ref, wdown_ref, norms, d2_ref, de_ref, grads,
                  gup, gdown, gout, gnorm)

    @pl.when(tile == tiles - 1)
    def _():
        write_edges(scal, tiles, grads, edge_ref, ends_ref, grads_hbm, sem)
        norm_rows(gnorm, (2, 3), gn_ref, 0)
        if packed:
            pack_rest(gout, gup, gdown, grad_outs[0], 0, n_head)
        else:
            for ref, total in zip(grad_outs, (gup, gdown, gout)):
                ref[...] = total[...].astype(b16)


def fourth_kernel(n_head, packed, tiles, scal, sums1_hbm, kept_ref, prob_ref, recv_ref, grads1_hbm, ends1_ref, grad_recv_ref, de1_ref, f_ref, m_ref, p1_ref, u_ref, vh_ref, rs_ref, d21_ref,
                  wfm_ref, wsb_ref, wqb_ref, norm1_ref,
                  gp_ref, z_ref, vh2_ref, rs2_ref, u2_ref, e_ref, p0_ref, wout_ref, wup_ref, wdown_ref, norm0_ref, gn1b_ref,
                  d2_ref, de_ref, grads_hbm, edge_ref, ends_ref, small_ref, gn0_ref, *rest):
    grad_outs = rest[:-16]
    spare, spare_grad, sem, grads, both, dcount, grad_p, grad_f, gws, gqkv, gnorm, fold_s, gfm, gup, gdown, gout = rest[-16:]
    tile = pl.program_id(0)

    @pl.when(tile == 0)
    def _():
        for ref in (gfm, gws, gqkv, gup, gdown, gout, gnorm):
            ref[...] = jnp.zeros_like(ref)
        attend_back_all(scal, tiles, kept_ref, prob_ref, recv_ref, ends1_ref, grad_recv_ref, sums1_hbm, grads1_hbm,
                        wqb_ref[...], both, dcount, gqkv, spare, spare_grad, sem)
        clear_present(scal, tiles, grads)

    grad = attend_back_tile(scal, tiles, tile, both, dcount, de1_ref, f_ref, m_ref, p1_ref, u_ref, vh_ref, rs_ref,
                            d21_ref, wfm_ref[...], wsb_ref[...], norm1_ref[...], grad_p, grad_f, gfm, gws, gnorm)
    mlp_back_tile(scal, tiles, tile, grad, lambda part: gp_ref[part].astype(f32), lambda part: z_ref[part],
                  vh2_ref[...].astype(f32), rs2_ref[:1], u2_ref[...], e_ref[...], p0_ref[...],
                  wout_ref[...], wup_ref, wdown_ref, norm0_ref[...], d2_ref, de_ref, grads,
                  gup, gdown, gout, gnorm)

    @pl.when(tile == tiles - 1)
    def _():
        write_edges(scal, tiles, grads, edge_ref, ends_ref, grads_hbm, sem)
        small_rows(0, gws, gqkv, fold_s, small_ref)
        norm_rows(gnorm, (0, 1), small_ref, NORM_ROW)
        small_ref[NORM_ROW + 4 :] = gn1b_ref[...]
        norm_rows(gnorm, (2, 3), gn0_ref, 0)
        if packed:
            for head in range(n_head):
                front = pack_front(gfm, head).astype(b16)
                store_pieces(
                    grad_outs[0], head, 0, jnp.concatenate([front[: D // 2], front[D // 2 :]], axis=1)
                )
            pack_rest(gout, gup, gdown, grad_outs[0], D // 2, n_head)
        else:
            for ref, total in zip(grad_outs, (gfm, gup, gdown, gout)):
                ref[...] = total[...].astype(b16)


def fifth_kernel(n_head, packed, tiles, scal, sums0_hbm, kept_ref, prob_ref, recv_ref, grads0_hbm, ends0_ref, grad_recv_ref, de_ref, f_ref, m_ref, p_ref, u_ref, vh_ref, rs_ref, d2_ref,
                 wfm_ref, wsb_ref, wqb_ref, norm_ref, gn0b_ref, small1_ref,
                 gin_ref, small_ref, front_ref,
                 spare, spare_grad, sem, both, dcount, grad_p, grad_f, gws, gqkv, gnorm, fold_s, gfm):
    tile = pl.program_id(0)

    @pl.when(tile == 0)
    def _():
        for ref in (gfm, gws, gqkv, gnorm):
            ref[...] = jnp.zeros_like(ref)
        attend_back_all(scal, tiles, kept_ref, prob_ref, recv_ref, ends0_ref, grad_recv_ref, sums0_hbm, grads0_hbm,
                        wqb_ref[...], both, dcount, gqkv, spare, spare_grad, sem)

    grad = attend_back_tile(scal, tiles, tile, both, dcount, de_ref, f_ref, m_ref, p_ref, u_ref, vh_ref, rs_ref,
                            d2_ref, wfm_ref[...], wsb_ref[...], norm_ref[...], grad_p, grad_f, gfm, gws, gnorm)
    gin_ref[...] = grad.T

    @pl.when(tile == tiles - 1)
    def _():
        small_rows(0, gws, gqkv, fold_s, small_ref)
        norm_rows(gnorm, (0, 1), small_ref, NORM_ROW)
        small_ref[NORM_ROW + 4 : LAYER_ROWS] = gn0b_ref[...]
        small_ref[LAYER_ROWS:] = small1_ref[...]
        if packed:
            for head in range(n_head):
                front_ref[head] = pack_front(gfm, head).astype(b16)
        else:
            front_ref[...] = gfm[...].astype(b16)


def sum_parts(own, got):
    total = own.astype(f32)
    for index in range(got.shape[0]):
        total = total + got[index].astype(f32)
    return total


def total_kernel(sizes, gb_ref, gc_ref, gs_ref, tb_ref, tc_ref, ts_ref,
                 got_b, got_c, got_s, mid_c, mid_s, got_c2, got_s2, head_sem, pts_sem):
    n_pts, n_head = sizes
    pts, head = lax.axis_index("pts"), lax.axis_index("head")
    c_rows = D // n_pts
    s_rows = gs_ref.shape[0] // n_head

    def part(index, rows):
        return pl.ds(pl.multiple_of(index * rows, rows), rows)

    def over(size, which, own, to, sem, source, target):
        copies = []
        for step in range(1, size):
            peer = lax.rem(own + step, size)
            copies.append(
                pltpu.make_async_remote_copy(
                    src_ref=source(peer),
                    dst_ref=target(step - 1),
                    send_sem=sem.at[0, which, step - 1],
                    recv_sem=sem.at[1, which, step - 1],
                    device_id=to(peer),
                    device_id_type=MESH,
                )
            )
        for copy in copies:
            copy.start()
        return copies

    def over_head(which, source, target):
        return over(n_head, which, head, lambda peer: (pts, peer), head_sem, source, target)

    def over_pts(which, source, target):
        return over(n_pts, which, pts, lambda peer: (peer, head), pts_sem, source, target)

    def finish(copies):
        for copy in copies:
            copy.wait()

    barrier = pltpu.get_barrier_semaphore()
    for step in range(1, n_head):
        pl.semaphore_signal(
            barrier, inc=1, device_id=(pts, lax.rem(head + step, n_head)), device_id_type=MESH
        )
    for step in range(1, n_pts):
        pl.semaphore_signal(
            barrier, inc=1, device_id=(lax.rem(pts + step, n_pts), head), device_id_type=MESH
        )
    pl.semaphore_wait(barrier, n_head - 1 + n_pts - 1)

    first_c = over_head(0, lambda peer: gc_ref.at[peer], lambda slot: got_c.at[slot])
    first_s = over_head(1, lambda peer: gs_ref.at[part(peer, s_rows)], lambda slot: got_s.at[slot])
    first_b = over_pts(0, lambda peer: gb_ref.at[peer], lambda slot: got_b.at[slot])
    finish(first_c)
    mid_c[...] = sum_parts(gc_ref[head], got_c).astype(b16)
    next_c = over_pts(1, lambda peer: mid_c.at[part(peer, c_rows)], lambda slot: got_c2.at[slot])
    finish(first_s)
    mid_s[...] = sum_parts(gs_ref[part(head, s_rows)], got_s)
    next_s = over_pts(2, lambda peer: mid_s, lambda slot: got_s2.at[slot])
    finish(next_c)
    mine_c = part(pts, c_rows)
    tc_ref[mine_c] = sum_parts(mid_c[mine_c], got_c2).astype(b16)
    last_c = over_pts(3, lambda peer: tc_ref.at[mine_c], lambda slot: tc_ref.at[mine_c])
    finish(next_s)
    mine_s = part(head, s_rows)
    ts_ref[mine_s] = sum_parts(mid_s[...], got_s2)
    last_s = over_head(2, lambda peer: ts_ref.at[mine_s], lambda slot: ts_ref.at[mine_s])
    finish(first_b)
    tb_ref[pts] = sum_parts(gb_ref[pts], got_b).astype(b16)
    last_b = over_pts(4, lambda peer: tb_ref.at[pts], lambda slot: tb_ref.at[pts])
    finish(last_c)
    finish(last_s)
    finish(last_b)


def total_gradients(sizes, gb, gc, gs):
    n_pts, n_head = sizes
    vmem = pl.BlockSpec(memory_space=pltpu.VMEM)
    dma = pltpu.SemaphoreType.DMA
    c_rows, s_rows = D // n_pts, gs.shape[0] // n_head
    return pl.pallas_call(
        functools.partial(total_kernel, sizes),
        out_shape=(
            jax.ShapeDtypeStruct(gb.shape, b16),
            jax.ShapeDtypeStruct(gc.shape[1:], b16),
            jax.ShapeDtypeStruct(gs.shape, f32),
        ),
        in_specs=[vmem] * 3,
        out_specs=[vmem] * 3,
        scratch_shapes=[
            pltpu.VMEM((n_pts - 1,) + gb.shape[1:], b16),
            pltpu.VMEM((n_head - 1,) + gc.shape[1:], b16),
            pltpu.VMEM((n_head - 1, s_rows, 128), f32),
            pltpu.VMEM(gc.shape[1:], b16),
            pltpu.VMEM((s_rows, 128), f32),
            pltpu.VMEM((n_pts - 1, c_rows, 128), b16),
            pltpu.VMEM((n_pts - 1, s_rows, 128), f32),
            dma((2, 3, n_head - 1)),
            dma((2, 5, n_pts - 1)),
        ],
        cost_estimate=pl.CostEstimate(flops=0, bytes_accessed=32 << 20, transcendentals=0),
        compiler_params=pltpu.CompilerParams(
            collective_id=3, has_side_effects=True, vmem_limit_bytes=VMEM_BYTES
        ),
        name="total_gradients",
    )(gb, gc, gs)


def update_kernel(ta_ref, tb_ref, tc_ref, ts_ref, row_ref, sel_ref, m_ref, v_ref, w_ref, sm_ref, sv_ref, sw_ref,
                  nm_ref, nv_ref, nw_ref, fresh_ref, om_ref, ov_ref, ow_ref, wide, tall, front, flat):
    lane = iota((8, 128), 1)

    def place_front(base):
        for pair in range(16):
            first = front[pl.ds(2 * pair, 8, stride=32), :]
            second = front[pl.ds(2 * pair + 1, 8, stride=32), :]
            columns = slice(128 * pair, 128 * pair + 128)
            wide[base : base + 8, columns] = jnp.where(lane < 64, first, pltpu.roll(second, 64, 1))
            wide[base + 8 : base + 16, columns] = jnp.where(lane < 64, pltpu.roll(first, 64, 1), second)

    def place_rest(base):
        for part in range(8):
            for half in range(2):
                wide[base : base + 72, 256 * part + 128 * half : 256 * part + 128 * half + 128] = tall[
                    half, pl.ds(part, 72, stride=8), :
                ]

    def fill(value, base):
        size = value.shape[1]
        row = base
        while row < size * (value.shape[0] // 2):
            chunk, offset = divmod(row, size)
            for half in range(2):
                tall[half, row - base : row - base + size - offset] = value[
                    2 * chunk + half, offset:
                ].astype(f32)
            row += size - offset

    front[...] = tc_ref[...].astype(f32)
    place_front(0)
    fill(tb_ref, D // 2)
    place_rest(16)
    front[: D // 2] = tb_ref[0, : D // 2].astype(f32)
    front[D // 2 :] = tb_ref[1, : D // 2].astype(f32)
    place_front(88)
    fill(ta_ref, 0)
    place_rest(104)

    cap, blocks = m_ref.shape[0], wide.shape[0]
    mine = (iota((cap, blocks), 0) == row_ref[:1]).astype(f32)
    filled = jnp.sum(mine, axis=1, keepdims=True) > 0.5
    mine = mine.astype(b16)
    step = 512
    for start in range(0, BLOCK, step):
        part = slice(start, start + step)
        grad = wide[:, part]
        own = nn(mine, grad.astype(b16))
        old = (m_ref[:, part], v_ref[:, part], w_ref[:, part])
        new = adam_update(old[0], own, old[1], old[2], rate_large)
        for ref, before, after in zip((nm_ref, nv_ref, nw_ref), old, new):
            ref[:, part] = jnp.where(filled, after, before)
        picked = [
            sel_ref[:, which * BLOCK + start : which * BLOCK + start + step].astype(f32)
            for which in range(3)
        ]
        fresh_ref[:, part] = adam_update(picked[0], grad, picked[1], picked[2], rate_large)[0].astype(b16)
    for layer in range(2):
        for row in range(LAYER_ROWS):
            flat[layer : layer + 1, 128 * row : 128 * row + 128] = ts_ref[
                layer * LAYER_ROWS + row : layer * LAYER_ROWS + row + 1, :
            ]
    new = adam_update(sm_ref[...], flat[:2], sv_ref[...], sw_ref[...], rate_small)
    for ref, value in zip((om_ref, ov_ref, ow_ref), new):
        ref[...] = value


def update(ta, tb, tc, ts, row, sel, tables, smalls):
    vmem = pl.BlockSpec(memory_space=pltpu.VMEM)
    blocks = sel.shape[0]
    operands = (ta, tb, tc, ts, row, sel, *tables, *smalls)
    outs = [jax.ShapeDtypeStruct(table.shape, f32) for table in tables]
    outs.append(jax.ShapeDtypeStruct((blocks, BLOCK), b16))
    outs += [jax.ShapeDtypeStruct(small.shape, f32) for small in smalls]
    return pl.pallas_call(
        update_kernel,
        out_shape=outs,
        in_specs=[vmem] * len(operands),
        out_specs=[vmem] * len(outs),
        scratch_shapes=[
            pltpu.VMEM((blocks, BLOCK), f32),
            pltpu.VMEM((2, ta.shape[0] * ta.shape[1] // 2, 128), f32),
            pltpu.VMEM((D, 128), f32),
            pltpu.VMEM((8, SMALL), f32),
        ],
        compiler_params=pltpu.CompilerParams(vmem_limit_bytes=VMEM_FULL),
        name="update",
    )(*operands)


class Args:
    def __init__(self, rows, width, limit):
        self.rows, self.width, self.limit = rows, width, limit
        self.operands, self.in_specs, self.outs, self.out_specs = [], [], [], []

    def cols(self, *arrays):
        for array in arrays:
            self.operands.append(array)
            self.in_specs.append(
                pl.BlockSpec((array.shape[0], self.width), lambda tile, scal: (0, tile))
            )

    def points(self, *arrays):
        for array in arrays:
            self.operands.append(array)
            self.in_specs.append(
                pl.BlockSpec((self.width, array.shape[1]), lambda tile, scal: (tile, 0))
            )

    def whole(self, *arrays):
        for array in arrays:
            rank = array.ndim
            self.operands.append(array)
            self.in_specs.append(
                pl.BlockSpec(array.shape, lambda tile, scal, rank=rank: (0,) * rank)
            )

    def layer(self, index, *arrays):
        for array in arrays:
            self.operands.append(array)
            self.in_specs.append(
                pl.BlockSpec((None,) + array.shape[1:], lambda tile, scal: (index, 0, 0))
            )

    def rows_of(self, array, start, size):
        self.operands.append(array)
        self.in_specs.append(
            pl.BlockSpec((size, array.shape[1]), lambda tile, scal: (start // size, 0))
        )

    def far(self, *arrays):
        for array in arrays:
            self.operands.append(array)
            self.in_specs.append(pl.BlockSpec(memory_space=pl.ANY))

    def out_far(self, *pairs):
        for shape, dtype in pairs:
            self.outs.append(jax.ShapeDtypeStruct(shape, dtype))
            self.out_specs.append(pl.BlockSpec(memory_space=pl.ANY))

    def out_cols(self, *pairs):
        for height, dtype in pairs:
            self.outs.append(jax.ShapeDtypeStruct((height, self.rows), dtype))
            self.out_specs.append(
                pl.BlockSpec((height, self.width), lambda tile, scal: (0, tile))
            )

    def out_points(self, *dtypes):
        for dtype in dtypes:
            self.outs.append(jax.ShapeDtypeStruct((self.rows, D), dtype))
            self.out_specs.append(pl.BlockSpec((self.width, D), lambda tile, scal: (tile, 0)))

    def out_whole(self, *pairs):
        for shape, dtype in pairs:
            rank = len(shape)
            self.outs.append(jax.ShapeDtypeStruct(shape, dtype))
            self.out_specs.append(
                pl.BlockSpec(shape, lambda tile, scal, rank=rank: (0,) * rank)
            )

    def call(self, body, scal, scratch, name):
        tiles = self.rows // self.width
        return pl.pallas_call(
            functools.partial(body, tiles),
            grid_spec=pltpu.PrefetchScalarGridSpec(
                num_scalar_prefetch=1,
                grid=(tiles,),
                in_specs=self.in_specs,
                out_specs=self.out_specs,
                scratch_shapes=scratch,
            ),
            out_shape=self.outs,
            compiler_params=pltpu.CompilerParams(
                dimension_semantics=("arbitrary",), vmem_limit_bytes=self.limit
            ),
            cost_estimate=pl.CostEstimate(
                flops=64 * self.rows * D * D, bytes_accessed=80 * self.rows * D, transcendentals=0
            ),
            name=name,
        )(scal, *self.operands)


def adam_update(master, grad, first, second, rate):
    new_first = beta_one * first + (1.0 - beta_one) * grad
    new_second = beta_two * second + (1.0 - beta_two) * grad * grad
    fix_one = 1.0 - beta_one**STEP
    fix_two = 1.0 - beta_two**STEP
    direction = new_first / fix_one / (jnp.sqrt(new_second / fix_two) + adam_eps)
    return (master - rate * (direction + decay_rate * master), new_first, new_second)


def flat_blocks(n_head, gfm, gout, gup, gdown):
    def columns(grad):
        width = grad.shape[1] // n_head
        return grad.reshape(D, n_head, width).transpose(1, 0, 2).reshape(n_head, -1)

    return jnp.concatenate(
        [
            columns(gfm[:, :D]),
            columns(gfm[:, D:]),
            gout.reshape(n_head, -1),
            columns(gup),
            columns(gdown),
        ],
        axis=1,
    ).reshape(n_head, -1, BLOCK)


def on_device(
    sizes,
    tokens,
    cotangent,
    segment_ids,
    owner,
    w_fx,
    w_mid,
    w_out,
    w_up,
    w_down,
    small_master,
    small_first,
    small_second,
    master_table,
    first_table,
    second_table,
):
    n_pts, n_head = sizes
    rows = tokens.shape[0]
    width, wide = min(512, rows), min(1024, rows)
    tiles = rows // width
    most = rows * n_pts * n_head // LARGEST
    window = (rows - 1 + most - 1) // rows
    limit = VMEM_BYTES if window < 4 else VMEM_FULL
    layers = w_fx.shape[0]
    packed = (n_pts, n_head) == (8, 4)

    ids = segment_ids.reshape(-1, 128)
    w_fx = w_fx.transpose(0, 2, 1)
    w_mid = w_mid.transpose(0, 2, 1)
    tables = (master_table, first_table, second_table)
    smalls = (small_master, small_first, small_second)
    gathered, wsb, norms, scal, halves = opening(
        n_head, tiles, ids, w_fx, w_mid, small_master, tables
    )
    wfm0 = gathered.reshape(2 * D, D)

    cap = master_table.shape[0]
    if packed:
        collected = lax.all_gather(halves, "pts", axis=0, tiled=True)

    sums_shape = (MESHES, SLICES, 2 * D)
    grad_sums_shape = (MESHES, SLICES, D)
    front_cols = ((D, b16), (8, f32), (D, b16), (D, b16), (D, b16), (HS, b16))
    wide_scratch = [pltpu.VMEM(grad_sums_shape, b16), pltpu.VMEM((D, wide), f32)]

    args = Args(rows, wide, limit)
    args.points(tokens)
    args.whole(wfm0)
    args.layer(0, wsb, norms)
    args.out_cols((D, b16), *front_cols)
    args.out_far((sums_shape, f32))
    ends_outs = (((2, EDGE, D), b16), ((2,) + sums_shape[1:], f32))
    grad_ends_outs = (((2, EDGE, D), b16), ((2,) + grad_sums_shape[1:], f32))
    kept_outs = (((2, SLICES, 5 * D), f32), ((2, HS, SLICES), f32))
    args.out_whole(*ends_outs)
    sums_scratch = [pltpu.VMEM(sums_shape, f32), pltpu.SemaphoreType.DMA]
    spare_scratch = [pltpu.VMEM(sums_shape[1:], f32)]
    xt0, vh0, rs0, u0, f0, m0, p0, sums0, edge, ends0 = args.call(first_kernel, scal, sums_scratch, "first")
    recv0, later, wqb0 = swap_edges_weights(
        sizes, window, 0, ((0, 1), (1, 1), (2, 0)), edge, w_fx, w_mid, w_out, small_master, 1
    )
    later = later.reshape(3 * D, D)

    args = Args(rows, wide, limit)
    args.cols(xt0, p0)
    args.far(sums0)
    args.whole(ends0, recv0)
    args.rows_of(later, 2 * D, D)
    args.layer(0, w_up, w_down)
    args.whole(wqb0)
    args.layer(0, norms)
    args.rows_of(later, 0, 2 * D)
    args.layer(1, wsb, norms)
    args.out_cols((D, b16), (D, b16), (8, f32), (D, b16), (FF, b16), (FF, b16))
    args.out_whole(*kept_outs)
    args.out_cols((D, f32), *front_cols)
    args.out_far((sums_shape, f32))
    args.out_whole(*ends_outs)
    (e0, vh20, rs20, u20, gp0, z0, kept0, prob0, x1, vh1, rs1, u1, f1, m1, p1, sums1, edge, ends1) = args.call(
        second_kernel, scal, wide_scratch + spare_scratch + sums_scratch, "second"
    )
    recv1, wout1, wqb1 = swap_edges_weights(
        sizes, window, 1, ((2, 1),), edge, w_fx, w_mid, w_out, small_master, 5
    )
    wout1 = wout1.reshape(D, D)

    grad_scratch = [pltpu.VMEM((D, FF), f32), pltpu.VMEM((D, FF), f32), pltpu.VMEM((D, D), f32)]
    rest_rows = D // n_head + 2 * D

    args = Args(rows, wide, limit)
    args.cols(x1, p1)
    args.far(sums1)
    args.whole(ends1, recv1)
    args.points(cotangent)
    args.whole(wout1)
    args.layer(1, w_up, w_down)
    args.whole(wqb1)
    args.layer(1, norms)
    args.out_points(b16)
    args.out_cols((D, f32), (D, b16))
    args.out_whole(*kept_outs)
    args.out_far((grad_sums_shape, f32))
    args.out_whole(*grad_ends_outs, ((4, 128), f32))
    if packed:
        args.out_whole(((n_head, n_pts, 2 * rest_rows // n_pts, 128), b16))
    else:
        args.out_whole(((D, FF), b16), ((D, FF), b16), ((D, D), b16))
    (layer_out, d21, de1, kept1, prob1, grads1, edge, ends1, gn1b, *grads_a) = args.call(
        functools.partial(third_kernel, n_head, packed),
        scal,
        wide_scratch
        + spare_scratch
        + [pltpu.VMEM(grad_sums_shape, f32), pltpu.SemaphoreType.DMA]
        + [pltpu.VMEM((4, D, 128), f32), pltpu.VMEM((FF, wide), f32), pltpu.VMEM((FF, wide), b16)]
        + grad_scratch,
        "third",
    )
    if packed:
        grad_recv1 = swap_edges(sizes, window, edge, 4)
        grad_recv1, collected = lax.optimization_barrier((grad_recv1, collected))
        part_a = lax.psum_scatter(grads_a[0], "head", scatter_dimension=0, tiled=True)[0]
    else:
        grad_recv1 = swap_edges(sizes, window, edge, 4)

    back_scratch = [
        *spare_scratch,
        pltpu.VMEM(grad_sums_shape[1:], f32),
        pltpu.SemaphoreType.DMA,
        pltpu.VMEM((MESHES, HS, 2 * D), b16),
        pltpu.VMEM((MESHES, HS, 128), f32),
        pltpu.VMEM((HS, width), f32),
        pltpu.VMEM((D, width), f32),
        pltpu.VMEM((D, HS), f32),
        pltpu.VMEM((D, 3 * D), f32),
        pltpu.VMEM((4, D, 128), f32),
        pltpu.VMEM((DH, 128), f32),
        pltpu.VMEM((D, 2 * D), f32),
    ]

    args = Args(rows, width, limit)
    args.far(sums1)
    args.whole(kept1, prob1, recv1)
    args.far(grads1)
    args.whole(ends1, grad_recv1)
    args.cols(de1, f1, m1, p1, u1, vh1, rs1, d21)
    args.rows_of(later, 0, 2 * D)
    args.layer(1, wsb)
    args.whole(wqb1)
    args.layer(1, norms)
    args.cols(gp0, z0, vh20, rs20, u20, e0, p0)
    args.rows_of(later, 2 * D, D)
    args.layer(0, w_up, w_down, norms)
    args.whole(gn1b)
    args.out_cols((D, f32), (D, b16))
    args.out_far((grad_sums_shape, f32))
    args.out_whole(*grad_ends_outs, ((LAYER_ROWS, 128), f32), ((4, 128), f32))
    if packed:
        args.out_whole(((n_head, n_pts, (D + 2 * rest_rows) // n_pts, 128), b16))
    else:
        args.out_whole(((D, 2 * D), b16), ((D, FF), b16), ((D, FF), b16), ((D, D), b16))
    (d20, de0, grads0, edge, ends0, small1, gn0b, *grads_b) = args.call(
        functools.partial(fourth_kernel, n_head, packed),
        scal,
        back_scratch[:3] + [pltpu.VMEM(grad_sums_shape, f32)] + back_scratch[3:] + grad_scratch,
        "fourth",
    )
    if packed:
        grad_recv0, total_a, chosen, row = swap_edges_sums(
            sizes, window, edge, part_a, owner.reshape(1, -1), collected, 6
        )
        mine_b = lax.psum_scatter(grads_b[0], "head", scatter_dimension=0, tiled=True)[0]
    else:
        grad_recv0 = swap_edges(sizes, window, edge, 4)

    args = Args(rows, width, limit)
    args.far(sums0)
    args.whole(kept0, prob0, recv0)
    args.far(grads0)
    args.whole(ends0, grad_recv0)
    args.cols(de0, f0, m0, p0, u0, vh0, rs0, d20)
    args.whole(wfm0)
    args.layer(0, wsb)
    args.whole(wqb0)
    args.layer(0, norms)
    args.whole(gn0b, small1)
    args.out_points(f32)
    args.out_whole(((2 * LAYER_ROWS, 128), f32))
    args.out_whole(((n_head, D, 128), b16) if packed else ((D, 2 * D), b16))
    input_grad, small, front = args.call(
        functools.partial(fifth_kernel, n_head, packed), scal, back_scratch, "fifth"
    )

    if packed:
        total_b, total_c, total_s = total_gradients(sizes, mine_b, front, small)
        outs = update(total_a, total_b, total_c, total_s, row, chosen, tables, smalls)
        return (layer_out, input_grad, *outs)

    gup1, gdown1, gout1 = grads_a
    gfm1, gup0, gdown0, gout0 = grads_b
    small_total = lax.psum(small, ("pts", "head")).reshape(layers, -1)
    totals = []
    for parts in ((front, gout0, gup0, gdown0), (gfm1, gout1, gup1, gdown1)):
        blocks = lax.psum_scatter(
            flat_blocks(n_head, *parts), "head", scatter_dimension=0, tiled=True
        )
        totals.append(lax.psum(blocks.reshape(-1, BLOCK), "pts"))
    total_grad = jnp.concatenate(totals, axis=0).astype(f32)
    my_index = lax.axis_index("pts")
    block_ids = jnp.arange(owner.shape[0])
    same_owner = (owner[:, None] == owner[None, :]) & (block_ids[None, :] < block_ids[:, None])
    table_row = owner * cap + jnp.sum(same_owner.astype(jnp.int32), axis=1)
    place_all = (jnp.arange(n_pts * cap)[:, None] == table_row[None, :]).astype(f32)
    mine_place = lax.dynamic_slice_in_dim(place_all, my_index * cap, cap, 0)
    own_grad = jnp.dot(mine_place, total_grad, precision=lax.Precision.HIGHEST)
    filled = jnp.sum(mine_place, axis=1)[:, None] > 0.5
    updated = adam_update(master_table, own_grad, first_table, second_table, rate_large)
    new_tables = [jnp.where(filled, new, old) for new, old in zip(updated, tables)]
    collected = lax.all_gather(new_tables[0].astype(b16), "pts", axis=0, tiled=True)
    pick_back = (table_row[:, None] == jnp.arange(n_pts * cap)[None, :]).astype(b16)
    fresh = jnp.dot(pick_back, collected, preferred_element_type=f32).astype(b16)
    small_outs = adam_update(small_master, small_total, small_first, small_second, rate_small)
    return (layer_out, input_grad, *new_tables, fresh, *small_outs)


def solution(mesh):
    sizes = (mesh.shape["pts"], mesh.shape["head"])
    return jax.shard_map(
        functools.partial(on_device, sizes),
        mesh=mesh,
        in_specs=(
            P(("pts", "head"), None),
            P(("pts", "head"), None),
            P("pts"),
            P(),
            P(None, None, "head"),
            P(None, None, "head"),
            P(None, "head", None),
            P(),
            P(),
            P(),
            P(),
            P(),
            P("pts", "head"),
            P("pts", "head"),
            P("pts", "head"),
        ),
        out_specs=(
            P(("pts", "head"), None),
            P(("pts", "head"), None),
            P("pts", "head"),
            P("pts", "head"),
            P("pts", "head"),
            P(None, "head"),
            P(),
            P(),
            P(),
        ),
        check_vma=False,
    )
```

```python
import functools
import math

import jax
import jax.numpy as jnp
from jax import lax
from jax.experimental import pallas as pl
from jax.experimental.pallas import tpu as pltpu
from jax.sharding import PartitionSpec as P

D = 256
HEADS = 8
DH = 32
SLICES = 64
HS = HEADS * SLICES
FF = 1024
MESHES = 24
BLOCK = 2048
SMALL = 6144
STEP = 10
LARGEST = 12
EDGE = 80
VMEM_FULL = 58 << 20
VMEM_BYTES = 52 << 20

MESH = pl.DeviceIdType.MESH
HIGH = True
norm_eps = 1e-05
beta_one = 0.9
beta_two = 0.95
adam_eps = 1e-08
decay_rate = 0.1
rate_large = 0.1
rate_small = 0.75
f32 = jnp.float32
b16 = jnp.bfloat16


def dot(a, b, contract, precise):
    dims = (contract, ((), ()))
    if not precise:
        return lax.dot_general(a, b, dims, preferred_element_type=f32)
    a_high, b_high = a.astype(b16), b.astype(b16)
    a_low = (a - a_high.astype(f32)).astype(b16)
    b_low = (b - b_high.astype(f32)).astype(b16)
    return (
        lax.dot_general(a_high, b_low, dims, preferred_element_type=f32)
        + lax.dot_general(a_low, b_high, dims, preferred_element_type=f32)
        + lax.dot_general(a_high, b_high, dims, preferred_element_type=f32)
    )


def nn(a, b, precise=False):
    return dot(a, b, ((1,), (0,)), precise)


def nt(a, b, precise=False):
    return dot(a, b, ((1,), (1,)), precise)


def tn(a, b, precise=False):
    return dot(a, b, ((0,), (0,)), precise)


def iota(shape, axis):
    return lax.broadcasted_iota(jnp.int32, shape, axis)


def pick_diag(full, per_head):
    lane_head = iota((SLICES, full.shape[1]), 1) // per_head
    total = jnp.where(lane_head == 0, full[:SLICES], 0.0)
    for head in range(1, HEADS):
        total = total + jnp.where(
            lane_head == head, full[head * SLICES : (head + 1) * SLICES], 0.0
        )
    return total


def spread_diag(small):
    lane_head = iota((SLICES, D), 1) // DH
    return jnp.concatenate(
        [jnp.where(lane_head == head, small, jnp.zeros_like(small)) for head in range(HEADS)],
        axis=0,
    )


def repeat_rows(width):
    return (iota((D, width), 0) % width == iota((D, width), 1)).astype(f32)


def slice_repeat():
    return (iota((SLICES, HS), 1) % SLICES == iota((SLICES, HS), 0)).astype(f32)


def same_head(rows_per, cols_per, shape):
    return (iota(shape, 0) // rows_per) == (iota(shape, 1) // cols_per)


def start_gather(n_head, picks, send_sem, recv_sem):
    me = lax.axis_index("head")
    copies = []
    for index, ref in enumerate(picks):
        for step in range(1, n_head):
            copy = pltpu.make_async_remote_copy(
                src_ref=ref.at[:, me],
                dst_ref=ref.at[:, me],
                send_sem=send_sem.at[index, step - 1],
                recv_sem=recv_sem.at[index, step - 1],
                device_id={"head": lax.rem(me + step, n_head)},
                device_id_type=MESH,
            )
            copy.start()
            copies.append(copy)
    return copies


def unroll_slices(row_of, out):
    lane = iota((1, 128), 1)
    for pair in range(DH // 2):
        row = row_of(pair)
        out[2 * pair : 2 * pair + 1] = jnp.where(lane < SLICES, row, 0.0)
        out[2 * pair + 1 : 2 * pair + 2] = jnp.where(
            lane < SLICES, pltpu.roll(row, 128 - SLICES, 1), 0.0
        )


def opening_kernel(n_head, tiles, ids_ref, wfx_ref, wmid_ref, sm_ref, m_ref, v_ref, w_ref,
                   out_ref, wsb_ref, norm_ref, scal_ref, tables_ref, send_sem, recv_sem, slices_s, norm_s):
    me = lax.axis_index("head")
    barrier = pltpu.get_barrier_semaphore()
    for step in range(1, n_head):
        pl.semaphore_signal(
            barrier, inc=1, device_id={"head": lax.rem(me + step, n_head)}, device_id_type=MESH
        )
    out_ref[0, me] = wfx_ref[0]
    out_ref[1, me] = wmid_ref[0]
    pl.semaphore_wait(barrier, n_head - 1)
    copies = start_gather(n_head, [out_ref], send_sem, recv_sem)
    layers = sm_ref.shape[0]
    cap, deep = m_ref.shape[0], tables_ref.shape[0]
    for which, ref in enumerate((m_ref, v_ref, w_ref)):
        value = ref[...]
        if deep > cap:
            value = jnp.concatenate([value, jnp.zeros((deep - cap, BLOCK), f32)], axis=0)
        tables_ref[:, which * BLOCK : (which + 1) * BLOCK] = value.astype(b16)
    right = (iota((128, HS), 1) % SLICES == iota((128, HS), 0)).astype(b16)
    for layer in range(layers):
        unroll_slices(lambda pair: sm_ref[layer : layer + 1, 128 * pair : 128 * pair + 128], slices_s)
        wide = nn(slices_s[...].astype(b16), right)
        tiled = jnp.concatenate([wide] * HEADS, axis=0)
        wsb_ref[layer] = jnp.where(same_head(DH, SLICES, (D, HS)), tiled, 0.0).astype(b16)
        norm_s[...] = jnp.zeros_like(norm_s)
        for row in range(4):
            start = SMALL - 4 * D + row * D
            norm_s[row : row + 1] = sm_ref[layer : layer + 1, start : start + D]
        norm_ref[layer] = norm_s[...].T
    rows = ids_ref.shape[0] // n_head
    ids = ids_ref[pl.ds(pl.multiple_of(me * rows, rows), rows), :]
    for mesh in range(MESHES + 1):
        scal_ref[mesh] = jnp.sum((ids < mesh).astype(jnp.int32))
    deep = rows // tiles
    for tile in range(tiles):
        part = ids[tile * deep : (tile + 1) * deep]
        scal_ref[MESHES + 1 + 2 * tile] = jnp.min(part)
        scal_ref[MESHES + 2 + 2 * tile] = jnp.max(part)
    for copy in copies:
        copy.wait()


def opening(n_head, tiles, ids, w_fx, w_mid, small, tables):
    layers, part, _ = w_fx.shape
    deep = -(-tables[0].shape[0] // 16) * 16
    vmem = pl.BlockSpec(memory_space=pltpu.VMEM)
    return pl.pallas_call(
        functools.partial(opening_kernel, n_head, tiles),
        out_shape=(
            jax.ShapeDtypeStruct((2, n_head, part, D), b16),
            jax.ShapeDtypeStruct((layers, D, HS), b16),
            jax.ShapeDtypeStruct((layers, D, 128), f32),
            jax.ShapeDtypeStruct((MESHES + 1 + 2 * tiles,), jnp.int32),
            jax.ShapeDtypeStruct((deep, 3 * BLOCK), b16),
        ),
        in_specs=[vmem] * 7,
        out_specs=[vmem] * 3 + [pl.BlockSpec(memory_space=pltpu.SMEM), vmem],
        scratch_shapes=[
            pltpu.SemaphoreType.DMA((1, n_head - 1)),
            pltpu.SemaphoreType.DMA((1, n_head - 1)),
            pltpu.VMEM((DH, 128), f32),
            pltpu.VMEM((128, D), f32),
        ],
        cost_estimate=pl.CostEstimate(flops=0, bytes_accessed=32 << 20, transcendentals=0),
        compiler_params=pltpu.CompilerParams(
            collective_id=0, has_side_effects=True, vmem_limit_bytes=VMEM_FULL
        ),
        name="opening",
    )(ids, w_fx, w_mid, small, *tables)


def place_of(sizes, shift):
    n_pts, n_head = sizes
    total = n_pts * n_head
    me = lax.axis_index("pts") * n_head + lax.axis_index("head")
    other = lax.rem(me + (shift + total), total)
    return (other // n_head, lax.rem(other, n_head))


def greet(sizes, window):
    barrier = pltpu.get_barrier_semaphore()
    for step in range(1, window + 1):
        for shift in (step, -step):
            pl.semaphore_signal(barrier, inc=1, device_id=place_of(sizes, shift), device_id_type=MESH)
    return barrier


def start_edges(sizes, window, edge_ref, out_ref, send_sem, recv_sem):
    copies = []
    for step in range(1, window + 1):
        for side, shift in ((1, step), (0, -step)):
            slot = step - 1 if side == 1 else window + step - 1
            copy = pltpu.make_async_remote_copy(
                src_ref=edge_ref.at[side],
                dst_ref=out_ref.at[slot],
                send_sem=send_sem.at[slot],
                recv_sem=recv_sem.at[slot],
                device_id=place_of(sizes, shift),
                device_id_type=MESH,
            )
            copy.start()
            copies.append(copy)
    return copies


def edge_kernel(sizes, window, edge_ref, out_ref, send_sem, recv_sem):
    barrier = greet(sizes, window)
    pl.semaphore_wait(barrier, 2 * window)
    for copy in start_edges(sizes, window, edge_ref, out_ref, send_sem, recv_sem):
        copy.wait()


def edge_weights_kernel(sizes, window, layer, pieces, edge_ref, wfx_ref, wmid_ref, wout_ref, sm_ref,
                        out_ref, w_ref, wqb_ref,
                        send_sem, recv_sem, wsend_sem, wrecv_sem, square_s):
    n_head = sizes[1]
    me = lax.axis_index("head")
    barrier = greet(sizes, window)
    for step in range(1, n_head):
        pl.semaphore_signal(
            barrier, inc=1, device_id={"head": lax.rem(me + step, n_head)}, device_id_type=MESH
        )
    refs = (wfx_ref, wmid_ref, wout_ref)
    for index, (kind, which) in enumerate(pieces):
        w_ref[index, me] = refs[kind][which]
    pl.semaphore_wait(barrier, 2 * window + n_head - 1)
    copies = start_edges(sizes, window, edge_ref, out_ref, send_sem, recv_sem)
    copies += start_gather(n_head, [w_ref], wsend_sem, wrecv_sem)
    lane = iota((1, 128), 1)
    for part in range(3):
        start = DH * SLICES + part * DH * DH
        for group in range(DH // 4):
            row = sm_ref[layer : layer + 1, start + 128 * group : start + 128 * group + 128]
            for inner in range(4):
                moved = row if inner == 0 else pltpu.roll(row, 128 - DH * inner, 1)
                square_s[4 * group + inner : 4 * group + inner + 1] = jnp.where(
                    lane < DH, moved, 0.0
                )
        square = square_s[...]
        for turn in range(1, 128 // DH):
            square = square + pltpu.roll(square_s[...], DH * turn, 1)
        square = jnp.concatenate([square] * (D // 128), axis=1)
        square = jnp.concatenate([square] * HEADS, axis=0)
        wqb_ref[:, part * D : (part + 1) * D] = jnp.where(
            same_head(DH, DH, (D, D)), square, 0.0
        )
    for copy in copies:
        copy.wait()


def pick_rows(n_pts, owner_ref, tables_s, load, chosen_ref, row_ref):
    blocks = owner_ref.shape[1]
    deep = tables_s.shape[0] // n_pts
    across = jnp.broadcast_to(owner_ref[...].astype(f32), (blocks, blocks))
    down = across.T
    low, high = iota((blocks, blocks), 0), iota((blocks, blocks), 1)
    same = across == down
    slot_down = jnp.sum(jnp.where(same & (high < low), 1.0, 0.0), axis=1, keepdims=True)
    slot_across = jnp.sum(jnp.where(same & (low < high), 1.0, 0.0), axis=0, keepdims=True)
    mine = owner_ref[...] == lax.axis_index("pts")
    row_ref[...] = jnp.broadcast_to(
        jnp.where(mine, slot_across.astype(jnp.int32), -1), row_ref.shape
    )
    target = (down[:, :1] * deep + slot_down).astype(jnp.int32)
    pick = (iota((blocks, tables_s.shape[0]), 1) == target).astype(b16)
    load.wait()
    step = 1024

    def choose(part, carry):
        lanes = pl.ds(pl.multiple_of(part * step, step), step)
        chosen_ref[:, lanes] = nn(pick, tables_s[:, lanes]).astype(b16)
        return carry

    lax.fori_loop(0, tables_s.shape[1] // step, choose, 0)


def edge_call(window, collective_id, rows, width, body, extra, outs, scratch, name):
    vmem = pl.BlockSpec(memory_space=pltpu.VMEM)
    outs = [jax.ShapeDtypeStruct((2 * window, rows, width), b16)] + outs
    return pl.pallas_call(
        body,
        out_shape=outs,
        in_specs=[vmem] * (1 + extra),
        out_specs=[vmem] * len(outs),
        scratch_shapes=[
            pltpu.SemaphoreType.DMA((2 * window,)),
            pltpu.SemaphoreType.DMA((2 * window,)),
        ]
        + scratch,
        cost_estimate=pl.CostEstimate(flops=0, bytes_accessed=32 << 20, transcendentals=0),
        compiler_params=pltpu.CompilerParams(
            collective_id=collective_id, has_side_effects=True, vmem_limit_bytes=VMEM_BYTES
        ),
        name=name,
    )


def swap_edges(sizes, window, edge, collective_id):
    _, rows, width = edge.shape
    return edge_call(
        window, collective_id, rows, width,
        functools.partial(edge_kernel, sizes, window), 0, [], [], "swap_edges",
    )(edge)[0]


def swap_edges_weights(sizes, window, layer, pieces, edge, w_fx, w_mid, w_out, small, collective_id):
    _, rows, width = edge.shape
    n_head = sizes[1]
    part = w_fx.shape[1]
    return edge_call(
        window, collective_id, rows, width,
        functools.partial(edge_weights_kernel, sizes, window, layer, pieces), 4,
        [
            jax.ShapeDtypeStruct((len(pieces), n_head, part, D), b16),
            jax.ShapeDtypeStruct((D, 3 * D), f32),
        ],
        [
            pltpu.SemaphoreType.DMA((1, n_head - 1)),
            pltpu.SemaphoreType.DMA((1, n_head - 1)),
            pltpu.VMEM((DH, 128), f32),
        ],
        "swap_edges_weights",
    )(edge, w_fx, w_mid, w_out, small)


def pts_copies(n_pts, source, target, send_sem, recv_sem):
    pts, head = lax.axis_index("pts"), lax.axis_index("head")
    copies = []
    for step in range(1, n_pts):
        peer = lax.rem(pts + step, n_pts)
        copies.append(
            pltpu.make_async_remote_copy(
                src_ref=source(step, peer),
                dst_ref=target(step, peer),
                send_sem=send_sem.at[step - 1],
                recv_sem=recv_sem.at[step - 1],
                device_id=(peer, head),
                device_id_type=MESH,
            )
        )
    return copies


def edge_sums_kernel(sizes, window, edge_ref, ga_ref, owner_ref, tables_ref, out_ref, ta_ref, chosen_ref, row_ref,
                     send_sem, recv_sem, a_send, a_recv, a_send2, a_recv2, got_a, tables_s, local_sem):
    n_pts, n_head = sizes
    pts, head = lax.axis_index("pts"), lax.axis_index("head")
    barrier = greet(sizes, window)
    for step in range(1, n_pts):
        pl.semaphore_signal(
            barrier, inc=1, device_id=(lax.rem(pts + step, n_pts), head), device_id_type=MESH
        )
    load = pltpu.make_async_copy(tables_ref, tables_s, local_sem)
    load.start()
    pl.semaphore_wait(barrier, 2 * window + n_pts - 1)
    gather = pts_copies(
        n_pts,
        lambda step, peer: ga_ref.at[peer],
        lambda step, peer: got_a.at[step - 1],
        a_send,
        a_recv,
    )
    for copy in gather:
        copy.start()
    edges = start_edges(sizes, window, edge_ref, out_ref, send_sem, recv_sem)
    for copy in gather:
        copy.wait()
    total = ga_ref[pts].astype(f32)
    for index in range(n_pts - 1):
        total = total + got_a[index].astype(f32)
    ta_ref[pts] = total.astype(b16)
    share = pts_copies(
        n_pts,
        lambda step, peer: ta_ref.at[pts],
        lambda step, peer: ta_ref.at[pts],
        a_send2,
        a_recv2,
    )
    for copy in share:
        copy.start()
    pick_rows(n_pts, owner_ref, tables_s, load, chosen_ref, row_ref)
    for copy in edges:
        copy.wait()
    for copy in share:
        copy.wait()


def swap_edges_sums(sizes, window, edge, ga, owner, tables, collective_id):
    _, rows, width = edge.shape
    n_pts = sizes[0]
    blocks = owner.shape[1]
    dma = pltpu.SemaphoreType.DMA
    vmem = pl.BlockSpec(memory_space=pltpu.VMEM)
    return pl.pallas_call(
        functools.partial(edge_sums_kernel, sizes, window),
        out_shape=(
            jax.ShapeDtypeStruct((2 * window, rows, width), b16),
            jax.ShapeDtypeStruct(ga.shape, b16),
            jax.ShapeDtypeStruct((blocks, tables.shape[1]), b16),
            jax.ShapeDtypeStruct((8, blocks), jnp.int32),
        ),
        in_specs=[vmem] * 3 + [pl.BlockSpec(memory_space=pl.ANY)],
        out_specs=[vmem] * 4,
        scratch_shapes=[dma((2 * window,))] * 2
        + [dma((n_pts - 1,))] * 4
        + [
            pltpu.VMEM((n_pts - 1,) + ga.shape[1:], b16),
            pltpu.VMEM(tables.shape, b16),
            dma,
        ],
        cost_estimate=pl.CostEstimate(flops=0, bytes_accessed=32 << 20, transcendentals=0),
        compiler_params=pltpu.CompilerParams(
            collective_id=collective_id, has_side_effects=True, vmem_limit_bytes=VMEM_BYTES
        ),
        name="swap_edges_sums",
    )(edge, ga, owner, tables)


def norm_stats(values):
    center = jnp.mean(values, axis=0, keepdims=True)
    spread = values - center
    scale = lax.rsqrt(jnp.mean(spread * spread, axis=0, keepdims=True) + norm_eps)
    return (spread * scale, scale)


def norm_back(grad_out, scaled, scale, gain):
    inner = grad_out * gain
    return scale * (
        inner
        - jnp.mean(inner, axis=0, keepdims=True)
        - scaled * jnp.mean(inner * scaled, axis=0, keepdims=True)
    )


def group_sum(values):
    return jnp.sum(values.reshape(HEADS, SLICES, values.shape[1]), axis=1, keepdims=True)


def fold_lanes(values):
    total = values[:, :128]
    for start in range(128, values.shape[1], 128):
        total = total + values[:, start : start + 128]
    return total


def tile_mask(scal, mesh, tile, width):
    spot = iota((1, width), 1) + tile * width
    return (spot >= scal[mesh]) & (spot < scal[mesh + 1])


def tile_range(scal, tiles, tile):
    base = MESHES + 1
    ratio = (scal.shape[0] - base) // 2 // tiles
    return (scal[base + 2 * ratio * tile], scal[base + 2 * ratio * (tile + 1) - 1])


def front_tile(scal, tiles, tile, x, wfm, wsb, norms, vh_ref, rs_ref, u_ref, f_ref, m_ref, p_ref, sums):
    width = x.shape[1]
    scaled, scale = norm_stats(x)
    vh_ref[...] = scaled.astype(b16)
    rs_ref[...] = jnp.broadcast_to(scale, (8, width))
    normed = (scaled * norms[:, 0:1] + norms[:, 1:2]).astype(b16)
    u_ref[...] = normed
    joint = nn(wfm, normed)
    feats = joint[:D].astype(b16)
    middle = joint[D:].astype(b16)
    f_ref[...] = feats
    m_ref[...] = middle
    logits = tn(wsb, middle).reshape(HEADS, SLICES, width)
    top = jnp.max(logits, axis=1, keepdims=True)
    expo = jnp.exp(logits - top)
    weights = expo / jnp.sum(expo, axis=1, keepdims=True)
    weights_r = weights.reshape(HS, width).astype(b16)
    p_ref[...] = weights_r
    low, high = tile_range(scal, tiles, tile)

    def add(mesh, carry):
        keep = tile_mask(scal, mesh, tile, width).astype(b16)
        wide = jnp.concatenate(
            [feats * keep, jnp.broadcast_to(keep, (D, width))], axis=0
        )
        full = nt(weights_r, wide)
        sums[mesh, :, :D] += pick_diag(full[:, :D], DH)
        sums[mesh, :, D:] += pick_diag(full[:, D:], DH)
        return carry

    lax.fori_loop(low, high + 1, add, 0)


def present(scal, tiles, body):
    def one(mesh, carry):
        body(mesh)
        return carry

    lax.fori_loop(tile_range(scal, tiles, 0)[0], tile_range(scal, tiles, tiles - 1)[1] + 1, one, 0)


def ends_of(scal, tiles):
    return (tile_range(scal, tiles, 0)[0], tile_range(scal, tiles, tiles - 1)[1])


def between(scal, tiles, body):
    first, last = ends_of(scal, tiles)

    def one(mesh, carry):
        body(mesh)
        return carry

    lax.fori_loop(first + 1, last, one, 0)


def fetch(source, target, sem):
    copy = pltpu.make_async_copy(source, target, sem)
    copy.start()
    copy.wait()


def clear_present(scal, tiles, sums):
    def clear(mesh):
        sums[mesh] = jnp.zeros(sums.shape[1:], f32)

    present(scal, tiles, clear)


def write_edges(scal, tiles, sums, edge_ref, ends_ref, sums_hbm, sem):
    first, last = ends_of(scal, tiles)
    extra = EDGE - SLICES
    for side, mesh in ((0, first), (1, last)):
        ends_ref[side] = sums[mesh]
        edge_ref[side, :SLICES] = sums[mesh, :, :D].astype(b16)
        rows = jnp.zeros((extra, D), f32)
        if sums.shape[2] > D:
            counts = jnp.concatenate(
                [sums[mesh, :, D:], jnp.zeros((D - SLICES, D), f32)], axis=0
            )
            pick = (iota((extra, D), 1) == DH * iota((extra, D), 0)).astype(f32)
            rows = nt(pick, counts, HIGH)
        edge_ref[side, SLICES:] = jnp.where(
            iota((extra, D), 0) >= HEADS, mesh.astype(f32), rows
        ).astype(b16)
    between(scal, tiles, lambda mesh: fetch(sums.at[mesh], sums_hbm.at[mesh], sem))


def add_edges(own, mesh, recv_ref):
    wanted = mesh.astype(f32)
    total = jnp.zeros((EDGE, D), f32)
    for slot in range(recv_ref.shape[0]):
        match = recv_ref[slot, SLICES + HEADS : SLICES + HEADS + 1].astype(f32) == wanted
        total = total + jnp.where(match, recv_ref[slot].astype(f32), 0.0)
    if own.shape[1] == D:
        return own + total[:SLICES]
    extra = EDGE - SLICES
    spread = (iota((extra, D), 1) // DH == iota((extra, D), 0)).astype(f32)
    counts = tn(total[SLICES:, :SLICES], spread, HIGH)
    return own + jnp.concatenate([total[:SLICES], counts], axis=1)


def attend_parts(totals, wqb):
    total = jnp.concatenate(totals, axis=0)
    count = total[:, D:]
    slice_tok = total[:, :D] / count
    triple = nn(slice_tok, wqb, HIGH)
    parts = []
    for index in range(len(totals)):
        rows = slice(index * SLICES, (index + 1) * SLICES)
        queries = triple[rows, :D]
        key_wide = spread_diag(triple[rows, D : 2 * D])
        value_wide = spread_diag(triple[rows, 2 * D :])
        scores = (nt(key_wide, queries, HIGH) * (1.0 / math.sqrt(DH))).reshape(
            HEADS, SLICES, SLICES
        )
        expo = jnp.exp(scores - jnp.max(scores, axis=1, keepdims=True))
        prob = (expo / jnp.sum(expo, axis=1, keepdims=True)).reshape(HS, SLICES)
        parts.append((queries, key_wide, value_wide, prob))
    return (slice_tok, count, triple, parts)


def attend_all(scal, tiles, ends_ref, recv_ref, sums_hbm, wqb, attended_ref, kept_ref, prob_ref, spare, sem):
    ends = ends_of(scal, tiles)
    totals = [add_edges(ends_ref[side], mesh, recv_ref) for side, mesh in enumerate(ends)]
    slice_tok, count, triple, parts = attend_parts(totals, wqb)
    kept = jnp.concatenate([slice_tok, count, triple], axis=1)
    results = []
    for side, (_, _, value_wide, prob) in enumerate(parts):
        results.append(tn(prob, value_wide, HIGH).astype(b16))
        kept_ref[side] = kept[side * SLICES : (side + 1) * SLICES]
        prob_ref[side] = prob
    for mesh, result in zip(ends, results):
        attended_ref[mesh] = result

    def inner(mesh):
        fetch(sums_hbm.at[mesh], spare, sem)
        _, _, _, parts = attend_parts([spare[...]], wqb)
        attended_ref[mesh] = tn(parts[0][3], parts[0][2], HIGH).astype(b16)

    between(scal, tiles, inner)


def spread_tile(scal, tiles, tile, wide_ref, p_ref, spread):
    low, high = tile_range(scal, tiles, tile)
    weights_r = p_ref[...]
    width = weights_r.shape[1]

    def one(mesh, carry):
        keep = tile_mask(scal, mesh, tile, width)
        spread[...] = jnp.where(keep, tn(spread_diag(wide_ref[mesh]), weights_r), spread[...])
        return carry

    lax.fori_loop(low, high + 1, one, 0)
    return spread[...].astype(b16)


GELU_A = math.sqrt(2.0 / math.pi)
GELU_B = 0.044715


def gelu_pair(hidden):
    square = hidden * hidden
    bend = jnp.tanh(hidden * (GELU_A + (GELU_A * GELU_B) * square))
    half = 0.5 + 0.5 * bend
    value = hidden * half
    slope = half + (0.5 * hidden) * (1.0 - bend * bend) * (
        GELU_A + (3.0 * GELU_A * GELU_B) * square
    )
    return (value, slope)


CHUNK = 1024


def mlp_back_tile(scal, tiles, tile, grad, slopes, actives, scaled_two, scale_two, normed_two_r, spread_r,
                  weights_r, wout, wup, wdown, norms, d2_ref, de_ref, sums,
                  gup, gdown, gout, gnorm):
    width = grad.shape[1]
    grad_r = grad.astype(b16)
    grad_normed = jnp.zeros((D, width), f32)
    for start in range(0, FF, CHUNK):
        part = slice(start, start + CHUNK)
        back = (slopes(part) * nn(wdown[part], grad_r)).astype(b16)
        gup[:, part] += nt(normed_two_r, back)
        gdown[:, part] += nt(grad_r, actives(part))
        grad_normed = grad_normed + nn(wup[:, part], back)
    gnorm[2] += fold_lanes(grad_normed * scaled_two)
    gnorm[3] += fold_lanes(grad_normed)
    grad_middle = grad + norm_back(grad_normed, scaled_two, scale_two, norms[:, 2:3])
    d2_ref[...] = grad_middle
    branch_r = grad_middle.astype(b16)
    gout[...] += nt(spread_r, branch_r)
    spread_grad = nn(wout, branch_r).astype(b16)
    de_ref[...] = spread_grad
    low, high = tile_range(scal, tiles, tile)

    def add(mesh, carry):
        keep = tile_mask(scal, mesh, tile, width).astype(b16)
        sums[mesh] += pick_diag(nt(weights_r, spread_grad * keep), DH)
        return carry

    lax.fori_loop(low, high + 1, add, 0)


def attend_back(meshes, shares, slice_tok, count, parts, outer, wqb, both, dcount, gqkv):
    root = 1.0 / math.sqrt(DH)
    attended, triples = [], []
    for (queries, key_wide, value_wide, prob), grad in zip(parts, outer):
        attended.append(tn(prob, value_wide, HIGH).astype(b16))
        inner = prob * nt(value_wide, grad, HIGH)
        mixed = group_sum(inner)
        grad_scores = root * (
            inner - (prob.reshape(HEADS, SLICES, SLICES) * mixed).reshape(HS, SLICES)
        )
        triples.append(
            jnp.concatenate(
                [
                    tn(grad_scores, key_wide, HIGH),
                    pick_diag(nn(grad_scores, queries, HIGH), DH),
                    pick_diag(nn(prob, grad, HIGH), DH),
                ],
                axis=1,
            )
        )
    triple = jnp.concatenate(triples, axis=0)
    grad_sum = nt(triple, wqb, HIGH) / count
    grad_count = -(grad_sum * slice_tok)
    gqkv[...] += tn(slice_tok * jnp.concatenate(shares, axis=0), triple, HIGH)
    for index, mesh in enumerate(meshes):
        rows = slice(index * SLICES, (index + 1) * SLICES)
        both[mesh, :, :D] = spread_diag(attended[index])
        both[mesh, :, D:] = spread_diag(grad_sum[rows].astype(b16))
        column = jnp.sum(spread_diag(grad_count[rows]), axis=1, keepdims=True)
        dcount[mesh] = jnp.broadcast_to(column, (HS, 128))


def attend_back_all(scal, tiles, kept_ref, prob_ref, recv_ref, ends_ref, grad_recv_ref, sums_hbm, grads_hbm,
                    wqb, both, dcount, gqkv, spare, spare_grad, sem):
    ends = ends_of(scal, tiles)
    outer = [add_edges(ends_ref[side], mesh, grad_recv_ref) for side, mesh in enumerate(ends)]
    kept = jnp.concatenate([kept_ref[0], kept_ref[1]], axis=0)
    parts = []
    for side in range(2):
        parts.append(
            (
                kept_ref[side, :, 2 * D : 3 * D],
                spread_diag(kept_ref[side, :, 3 * D : 4 * D]),
                spread_diag(kept_ref[side, :, 4 * D :]),
                prob_ref[side],
            )
        )
    previous = recv_ref[0, SLICES + HEADS : SLICES + HEADS + 1, :1].astype(f32)
    shares = [
        jnp.broadcast_to(1.0 - (previous == ends[0].astype(f32)).astype(f32), (SLICES, 1)),
        jnp.broadcast_to((ends[1] != ends[0]).astype(f32), (SLICES, 1)),
    ]
    attend_back(ends, shares, kept[:, :D], kept[:, D : 2 * D], parts, outer, wqb, both, dcount, gqkv)

    def inner(mesh):
        fetch(sums_hbm.at[mesh], spare, sem)
        fetch(grads_hbm.at[mesh], spare_grad, sem)
        slice_tok, count, _, parts = attend_parts([spare[...]], wqb)
        attend_back(
            (mesh,), [jnp.ones((SLICES, 1), f32)], slice_tok, count, parts, [spare_grad[...]], wqb, both, dcount, gqkv
        )

    between(scal, tiles, inner)


def attend_back_tile(scal, tiles, tile, both, dcount, de_ref, f_ref, m_ref, p_ref, u_ref, vh_ref, rs_ref,
                     d2_ref, wfm, wsb, norms, grad_p, grad_f, gfm, gws, gnorm):
    low, high = tile_range(scal, tiles, tile)
    weights_r = p_ref[...]
    width = weights_r.shape[1]
    pair = jnp.concatenate([de_ref[...], f_ref[...]], axis=0)

    def one(mesh, carry):
        keep = tile_mask(scal, mesh, tile, width)
        back = nn(both[mesh], pair) + dcount[mesh][:, :1]
        grad_p[...] = jnp.where(keep, back, grad_p[...])
        grad_f[...] = jnp.where(keep, tn(both[mesh, :, D:], weights_r), grad_f[...])
        return carry

    lax.fori_loop(low, high + 1, one, 0)
    weights = weights_r.astype(f32)
    inner = weights * grad_p[...]
    mixed = group_sum(inner)
    grad_logits = (
        inner - (weights.reshape(HEADS, SLICES, width) * mixed).reshape(HS, width)
    ).astype(b16)
    gws[...] += nt(m_ref[...], grad_logits)
    grad_m = nn(wsb, grad_logits).astype(b16)
    grad_fm = jnp.concatenate([grad_f[...].astype(b16), grad_m], axis=0)
    gfm[...] += nt(u_ref[...], grad_fm)
    grad_normed = tn(wfm, grad_fm)
    scaled = vh_ref[...].astype(f32)
    gnorm[0] += fold_lanes(grad_normed * scaled)
    gnorm[1] += fold_lanes(grad_normed)
    return d2_ref[...] + norm_back(grad_normed, scaled, rs_ref[:1], norms[:, 0:1])


def small_rows(base, gws, gqkv, scratch, out_ref):
    lane = iota((1, 128), 1)
    left = repeat_rows(DH)
    fold = (iota((128, HS), 1) % SLICES == iota((128, HS), 0)).astype(f32)
    kept = jnp.where(same_head(DH, SLICES, (D, HS)), gws[...], 0.0)
    scratch[...] = nt(tn(left, kept, HIGH), fold, HIGH)
    even = scratch[pl.ds(0, DH // 2, stride=2), :]
    odd = scratch[pl.ds(1, DH // 2, stride=2), :]
    out_ref[base : base + DH // 2] = jnp.where(lane < SLICES, even, pltpu.roll(odd, SLICES, 1))
    fold = (iota((D, 128), 0) % DH == iota((D, 128), 1)).astype(f32)
    for part in range(3):
        square = jnp.where(same_head(DH, DH, (D, D)), gqkv[:, part * D : (part + 1) * D], 0.0)
        scratch[...] = nn(tn(left, square, HIGH), fold, HIGH)
        total = scratch[pl.ds(0, DH // 4, stride=4), :]
        for inner in range(1, 4):
            total = total + pltpu.roll(scratch[pl.ds(inner, DH // 4, stride=4), :], DH * inner, 1)
        start = base + DH // 2 + part * (DH // 4)
        out_ref[start : start + DH // 4] = total


NORM_ROW = (SMALL - 4 * D) // 128
LAYER_ROWS = SMALL // 128


def norm_rows(gnorm, index, out_ref, base):
    lane = iota((D, 128), 1)
    total = jnp.zeros((D, 128), f32)
    for column, row in enumerate(index):
        total = total + jnp.where(lane == column, jnp.sum(gnorm[row], axis=1, keepdims=True), 0.0)
    flat = total.T
    for column in range(len(index)):
        for half in range(D // 128):
            place = base + column * (D // 128) + half
            out_ref[place : place + 1] = flat[column : column + 1, 128 * half : 128 * half + 128]


def pack_front(gfm, head):
    lane = iota((D, 128), 1)
    start = (head // 2) * 128
    feats, middle = gfm[:, start : start + 128], gfm[:, D + start : D + start + 128]
    if head % 2 == 0:
        return jnp.where(lane < 64, feats, pltpu.roll(middle, 64, 1))
    return jnp.where(lane < 64, pltpu.roll(feats, 64, 1), middle)


def store_pieces(out_ref, head, base, value):
    size = out_ref.shape[2]
    done = 0
    while done < value.shape[0]:
        chunk, offset = divmod(base + done, size)
        count = min(size - offset, value.shape[0] - done)
        for half in range(2):
            out_ref[head, 2 * chunk + half, offset : offset + count] = value[
                done : done + count, 128 * half : 128 * half + 128
            ]
        done += count


def pack_rest(gout, gup, gdown, out_ref, base, n_head):
    for head in range(n_head):
        deep, wide = D // n_head, FF // n_head
        store_pieces(out_ref, head, base, gout[head * deep : (head + 1) * deep].astype(b16))
        start = base + deep
        store_pieces(out_ref, head, start, gup[:, head * wide : (head + 1) * wide].astype(b16))
        store_pieces(out_ref, head, start + D, gdown[:, head * wide : (head + 1) * wide].astype(b16))


def first_kernel(tiles, scal, tok_ref, wfm_ref, wsb_ref, norm_ref,
                 xt_ref, vh_ref, rs_ref, u_ref, f_ref, m_ref, p_ref, sums_hbm, edge_ref, ends_ref, sums, sem):
    tile = pl.program_id(0)

    @pl.when(tile == 0)
    def _():
        clear_present(scal, tiles, sums)

    turned = tok_ref[...].T
    xt_ref[...] = turned
    x = turned.astype(f32)
    front_tile(scal, tiles, tile, x, wfm_ref[...], wsb_ref[...], norm_ref[...],
               vh_ref, rs_ref, u_ref, f_ref, m_ref, p_ref, sums)

    @pl.when(tile == tiles - 1)
    def _():
        write_edges(scal, tiles, sums, edge_ref, ends_ref, sums_hbm, sem)


def second_kernel(tiles, scal, xt_ref, p0_ref, sums0_hbm, ends0_ref, recv_ref, wout_ref, wup_ref, wdown_ref, wqb_ref, norm0_ref,
                  wfm_ref, wsb_ref, norm1_ref,
                  e_ref, vh2_ref, rs2_ref, u2_ref, gp_ref, z_ref, kept_ref, prob_ref,
                  x1_ref, vh_ref, rs_ref, u_ref, f_ref, m_ref, p_ref, sums_hbm, edge_ref, ends_ref,
                  wide, spread, spare, sums, sem):
    tile = pl.program_id(0)

    @pl.when(tile == 0)
    def _():
        attend_all(scal, tiles, ends0_ref, recv_ref, sums0_hbm, wqb_ref[...], wide, kept_ref, prob_ref, spare, sem)
        clear_present(scal, tiles, sums)

    norms = norm0_ref[...]
    spread_r = spread_tile(scal, tiles, tile, wide, p0_ref, spread)
    e_ref[...] = spread_r
    middle = xt_ref[...].astype(f32) + tn(wout_ref[...], spread_r)
    scaled_two, scale_two = norm_stats(middle)
    vh2_ref[...] = scaled_two.astype(b16)
    rs2_ref[...] = jnp.broadcast_to(scale_two, rs2_ref.shape)
    normed_two_r = (scaled_two * norms[:, 2:3] + norms[:, 3:4]).astype(b16)
    u2_ref[...] = normed_two_r
    x = middle
    for start in range(0, FF, CHUNK):
        part = slice(start, start + CHUNK)
        active, slope = gelu_pair(tn(wup_ref[:, part], normed_two_r))
        active_r = active.astype(b16)
        z_ref[part] = active_r
        gp_ref[part] = slope.astype(b16)
        x = x + tn(wdown_ref[part], active_r)
    x1_ref[...] = x
    front_tile(scal, tiles, tile, x, wfm_ref[...], wsb_ref[...], norm1_ref[...],
               vh_ref, rs_ref, u_ref, f_ref, m_ref, p_ref, sums)

    @pl.when(tile == tiles - 1)
    def _():
        write_edges(scal, tiles, sums, edge_ref, ends_ref, sums_hbm, sem)


def third_kernel(n_head, packed, tiles, scal, x1_ref, p_ref, sums1_hbm, ends1_ref, recv_ref, cot_ref, wout_ref, wup_ref, wdown_ref, wqb_ref, norm_ref,
                 out_ref, d2_ref, de_ref, kept_ref, prob_ref, grads_hbm, edge_ref, ends_ref,
                 gn_ref, *rest):
    grad_outs, (wide, spread, spare, grads, sem, gnorm, slope_s, active_s, gup, gdown, gout) = rest[:-11], rest[-11:]
    tile = pl.program_id(0)

    @pl.when(tile == 0)
    def _():
        clear_present(scal, tiles, grads)
        gup[...] = jnp.zeros_like(gup)
        gdown[...] = jnp.zeros_like(gdown)
        gout[...] = jnp.zeros_like(gout)
        gnorm[...] = jnp.zeros_like(gnorm)
        attend_all(scal, tiles, ends1_ref, recv_ref, sums1_hbm, wqb_ref[...], wide, kept_ref, prob_ref, spare, sem)

    norms = norm_ref[...]
    spread_r = spread_tile(scal, tiles, tile, wide, p_ref, spread)
    middle = x1_ref[...] + tn(wout_ref[...], spread_r)
    scaled_two, scale_two = norm_stats(middle)
    normed_two_r = (scaled_two * norms[:, 2:3] + norms[:, 3:4]).astype(b16)
    x = middle
    for start in range(0, FF, CHUNK):
        part = slice(start, start + CHUNK)
        active, slope = gelu_pair(tn(wup_ref[:, part], normed_two_r))
        active_r = active.astype(b16)
        active_s[part] = active_r
        slope_s[part] = slope
        x = x + tn(wdown_ref[part], active_r)
    out_ref[...] = x.astype(b16).T
    grad = cot_ref[...].T.astype(f32)
    mlp_back_tile(scal, tiles, tile, grad, lambda part: slope_s[part], lambda part: active_s[part],
                  scaled_two, scale_two, normed_two_r, spread_r, p_ref[...],
                  wout_ref[...], wup_ref, wdown_ref, norms, d2_ref, de_ref, grads,
                  gup, gdown, gout, gnorm)

    @pl.when(tile == tiles - 1)
    def _():
        write_edges(scal, tiles, grads, edge_ref, ends_ref, grads_hbm, sem)
        norm_rows(gnorm, (2, 3), gn_ref, 0)
        if packed:
            pack_rest(gout, gup, gdown, grad_outs[0], 0, n_head)
        else:
            for ref, total in zip(grad_outs, (gup, gdown, gout)):
                ref[...] = total[...].astype(b16)


def fourth_kernel(n_head, packed, tiles, scal, sums1_hbm, kept_ref, prob_ref, recv_ref, grads1_hbm, ends1_ref, grad_recv_ref, de1_ref, f_ref, m_ref, p1_ref, u_ref, vh_ref, rs_ref, d21_ref,
                  wfm_ref, wsb_ref, wqb_ref, norm1_ref,
                  gp_ref, z_ref, vh2_ref, rs2_ref, u2_ref, e_ref, p0_ref, wout_ref, wup_ref, wdown_ref, norm0_ref, gn1b_ref,
                  d2_ref, de_ref, grads_hbm, edge_ref, ends_ref, small_ref, gn0_ref, *rest):
    grad_outs = rest[:-16]
    spare, spare_grad, sem, grads, both, dcount, grad_p, grad_f, gws, gqkv, gnorm, fold_s, gfm, gup, gdown, gout = rest[-16:]
    tile = pl.program_id(0)

    @pl.when(tile == 0)
    def _():
        for ref in (gfm, gws, gqkv, gup, gdown, gout, gnorm):
            ref[...] = jnp.zeros_like(ref)
        attend_back_all(scal, tiles, kept_ref, prob_ref, recv_ref, ends1_ref, grad_recv_ref, sums1_hbm, grads1_hbm,
                        wqb_ref[...], both, dcount, gqkv, spare, spare_grad, sem)
        clear_present(scal, tiles, grads)

    grad = attend_back_tile(scal, tiles, tile, both, dcount, de1_ref, f_ref, m_ref, p1_ref, u_ref, vh_ref, rs_ref,
                            d21_ref, wfm_ref[...], wsb_ref[...], norm1_ref[...], grad_p, grad_f, gfm, gws, gnorm)
    mlp_back_tile(scal, tiles, tile, grad, lambda part: gp_ref[part].astype(f32), lambda part: z_ref[part],
                  vh2_ref[...].astype(f32), rs2_ref[:1], u2_ref[...], e_ref[...], p0_ref[...],
                  wout_ref[...], wup_ref, wdown_ref, norm0_ref[...], d2_ref, de_ref, grads,
                  gup, gdown, gout, gnorm)

    @pl.when(tile == tiles - 1)
    def _():
        write_edges(scal, tiles, grads, edge_ref, ends_ref, grads_hbm, sem)
        small_rows(0, gws, gqkv, fold_s, small_ref)
        norm_rows(gnorm, (0, 1), small_ref, NORM_ROW)
        small_ref[NORM_ROW + 4 :] = gn1b_ref[...]
        norm_rows(gnorm, (2, 3), gn0_ref, 0)
        if packed:
            for head in range(n_head):
                front = pack_front(gfm, head).astype(b16)
                store_pieces(
                    grad_outs[0], head, 0, jnp.concatenate([front[: D // 2], front[D // 2 :]], axis=1)
                )
            pack_rest(gout, gup, gdown, grad_outs[0], D // 2, n_head)
        else:
            for ref, total in zip(grad_outs, (gfm, gup, gdown, gout)):
                ref[...] = total[...].astype(b16)


def fifth_kernel(n_head, packed, tiles, scal, sums0_hbm, kept_ref, prob_ref, recv_ref, grads0_hbm, ends0_ref, grad_recv_ref, de_ref, f_ref, m_ref, p_ref, u_ref, vh_ref, rs_ref, d2_ref,
                 wfm_ref, wsb_ref, wqb_ref, norm_ref, gn0b_ref, small1_ref,
                 gin_ref, small_ref, front_ref,
                 spare, spare_grad, sem, both, dcount, grad_p, grad_f, gws, gqkv, gnorm, fold_s, gfm):
    tile = pl.program_id(0)

    @pl.when(tile == 0)
    def _():
        for ref in (gfm, gws, gqkv, gnorm):
            ref[...] = jnp.zeros_like(ref)
        attend_back_all(scal, tiles, kept_ref, prob_ref, recv_ref, ends0_ref, grad_recv_ref, sums0_hbm, grads0_hbm,
                        wqb_ref[...], both, dcount, gqkv, spare, spare_grad, sem)

    grad = attend_back_tile(scal, tiles, tile, both, dcount, de_ref, f_ref, m_ref, p_ref, u_ref, vh_ref, rs_ref,
                            d2_ref, wfm_ref[...], wsb_ref[...], norm_ref[...], grad_p, grad_f, gfm, gws, gnorm)
    gin_ref[...] = grad.T

    @pl.when(tile == tiles - 1)
    def _():
        small_rows(0, gws, gqkv, fold_s, small_ref)
        norm_rows(gnorm, (0, 1), small_ref, NORM_ROW)
        small_ref[NORM_ROW + 4 : LAYER_ROWS] = gn0b_ref[...]
        small_ref[LAYER_ROWS:] = small1_ref[...]
        if packed:
            for head in range(n_head):
                front_ref[head] = pack_front(gfm, head).astype(b16)
        else:
            front_ref[...] = gfm[...].astype(b16)


def sum_parts(own, got):
    total = own.astype(f32)
    for index in range(got.shape[0]):
        total = total + got[index].astype(f32)
    return total


def total_kernel(sizes, gb_ref, gc_ref, gs_ref, tb_ref, tc_ref, ts_ref,
                 got_b, got_c, got_s, mid_c, mid_s, got_c2, got_s2, head_sem, pts_sem):
    n_pts, n_head = sizes
    pts, head = lax.axis_index("pts"), lax.axis_index("head")
    c_rows = D // n_pts
    s_rows = gs_ref.shape[0] // n_head

    def part(index, rows):
        return pl.ds(pl.multiple_of(index * rows, rows), rows)

    def over(size, which, own, to, sem, source, target):
        copies = []
        for step in range(1, size):
            peer = lax.rem(own + step, size)
            copies.append(
                pltpu.make_async_remote_copy(
                    src_ref=source(peer),
                    dst_ref=target(step - 1),
                    send_sem=sem.at[0, which, step - 1],
                    recv_sem=sem.at[1, which, step - 1],
                    device_id=to(peer),
                    device_id_type=MESH,
                )
            )
        for copy in copies:
            copy.start()
        return copies

    def over_head(which, source, target):
        return over(n_head, which, head, lambda peer: (pts, peer), head_sem, source, target)

    def over_pts(which, source, target):
        return over(n_pts, which, pts, lambda peer: (peer, head), pts_sem, source, target)

    def finish(copies):
        for copy in copies:
            copy.wait()

    barrier = pltpu.get_barrier_semaphore()
    for step in range(1, n_head):
        pl.semaphore_signal(
            barrier, inc=1, device_id=(pts, lax.rem(head + step, n_head)), device_id_type=MESH
        )
    for step in range(1, n_pts):
        pl.semaphore_signal(
            barrier, inc=1, device_id=(lax.rem(pts + step, n_pts), head), device_id_type=MESH
        )
    pl.semaphore_wait(barrier, n_head - 1 + n_pts - 1)

    first_b = over_pts(0, lambda peer: gb_ref.at[peer], lambda slot: got_b.at[slot])
    first_c = over_head(0, lambda peer: gc_ref.at[peer], lambda slot: got_c.at[slot])
    first_s = over_head(1, lambda peer: gs_ref.at[part(peer, s_rows)], lambda slot: got_s.at[slot])
    finish(first_c)
    mid_c[...] = sum_parts(gc_ref[head], got_c).astype(b16)
    next_c = over_pts(1, lambda peer: mid_c.at[part(peer, c_rows)], lambda slot: got_c2.at[slot])
    finish(first_s)
    mid_s[...] = sum_parts(gs_ref[part(head, s_rows)], got_s)
    next_s = over_pts(2, lambda peer: mid_s, lambda slot: got_s2.at[slot])
    finish(next_c)
    mine_c = part(pts, c_rows)
    tc_ref[mine_c] = sum_parts(mid_c[mine_c], got_c2).astype(b16)
    last_c = over_pts(3, lambda peer: tc_ref.at[mine_c], lambda slot: tc_ref.at[mine_c])
    finish(next_s)
    mine_s = part(head, s_rows)
    ts_ref[mine_s] = sum_parts(mid_s[...], got_s2)
    last_s = over_head(2, lambda peer: ts_ref.at[mine_s], lambda slot: ts_ref.at[mine_s])
    finish(first_b)
    tb_ref[pts] = sum_parts(gb_ref[pts], got_b).astype(b16)
    last_b = over_pts(4, lambda peer: tb_ref.at[pts], lambda slot: tb_ref.at[pts])
    finish(last_c)
    finish(last_s)
    finish(last_b)


def total_gradients(sizes, gb, gc, gs):
    n_pts, n_head = sizes
    vmem = pl.BlockSpec(memory_space=pltpu.VMEM)
    dma = pltpu.SemaphoreType.DMA
    c_rows, s_rows = D // n_pts, gs.shape[0] // n_head
    return pl.pallas_call(
        functools.partial(total_kernel, sizes),
        out_shape=(
            jax.ShapeDtypeStruct(gb.shape, b16),
            jax.ShapeDtypeStruct(gc.shape[1:], b16),
            jax.ShapeDtypeStruct(gs.shape, f32),
        ),
        in_specs=[vmem] * 3,
        out_specs=[vmem] * 3,
        scratch_shapes=[
            pltpu.VMEM((n_pts - 1,) + gb.shape[1:], b16),
            pltpu.VMEM((n_head - 1,) + gc.shape[1:], b16),
            pltpu.VMEM((n_head - 1, s_rows, 128), f32),
            pltpu.VMEM(gc.shape[1:], b16),
            pltpu.VMEM((s_rows, 128), f32),
            pltpu.VMEM((n_pts - 1, c_rows, 128), b16),
            pltpu.VMEM((n_pts - 1, s_rows, 128), f32),
            dma((2, 3, n_head - 1)),
            dma((2, 5, n_pts - 1)),
        ],
        cost_estimate=pl.CostEstimate(flops=0, bytes_accessed=32 << 20, transcendentals=0),
        compiler_params=pltpu.CompilerParams(
            collective_id=3, has_side_effects=True, vmem_limit_bytes=VMEM_BYTES
        ),
        name="total_gradients",
    )(gb, gc, gs)


def update_kernel(ta_ref, tb_ref, tc_ref, ts_ref, row_ref, sel_ref, m_ref, v_ref, w_ref, sm_ref, sv_ref, sw_ref,
                  nm_ref, nv_ref, nw_ref, fresh_ref, om_ref, ov_ref, ow_ref, wide, tall, front, flat):
    lane = iota((8, 128), 1)

    def place_front(base):
        for pair in range(16):
            first = front[pl.ds(2 * pair, 8, stride=32), :]
            second = front[pl.ds(2 * pair + 1, 8, stride=32), :]
            columns = slice(128 * pair, 128 * pair + 128)
            wide[base : base + 8, columns] = jnp.where(lane < 64, first, pltpu.roll(second, 64, 1))
            wide[base + 8 : base + 16, columns] = jnp.where(lane < 64, pltpu.roll(first, 64, 1), second)

    def place_rest(base):
        for part in range(8):
            for half in range(2):
                wide[base : base + 72, 256 * part + 128 * half : 256 * part + 128 * half + 128] = tall[
                    half, pl.ds(part, 72, stride=8), :
                ]

    def fill(value, base):
        size = value.shape[1]
        row = base
        while row < size * (value.shape[0] // 2):
            chunk, offset = divmod(row, size)
            for half in range(2):
                tall[half, row - base : row - base + size - offset] = value[
                    2 * chunk + half, offset:
                ].astype(f32)
            row += size - offset

    front[...] = tc_ref[...].astype(f32)
    place_front(0)
    fill(tb_ref, D // 2)
    place_rest(16)
    front[: D // 2] = tb_ref[0, : D // 2].astype(f32)
    front[D // 2 :] = tb_ref[1, : D // 2].astype(f32)
    place_front(88)
    fill(ta_ref, 0)
    place_rest(104)

    cap, blocks = m_ref.shape[0], wide.shape[0]
    mine = (iota((cap, blocks), 0) == row_ref[:1]).astype(f32)
    filled = jnp.sum(mine, axis=1, keepdims=True) > 0.5
    mine = mine.astype(b16)
    step = 512
    for start in range(0, BLOCK, step):
        part = slice(start, start + step)
        grad = wide[:, part]
        own = nn(mine, grad.astype(b16))
        old = (m_ref[:, part], v_ref[:, part], w_ref[:, part])
        new = adam_update(old[0], own, old[1], old[2], rate_large)
        for ref, before, after in zip((nm_ref, nv_ref, nw_ref), old, new):
            ref[:, part] = jnp.where(filled, after, before)
        picked = [
            sel_ref[:, which * BLOCK + start : which * BLOCK + start + step].astype(f32)
            for which in range(3)
        ]
        fresh_ref[:, part] = adam_update(picked[0], grad, picked[1], picked[2], rate_large)[0].astype(b16)
    for layer in range(2):
        for row in range(LAYER_ROWS):
            flat[layer : layer + 1, 128 * row : 128 * row + 128] = ts_ref[
                layer * LAYER_ROWS + row : layer * LAYER_ROWS + row + 1, :
            ]
    new = adam_update(sm_ref[...], flat[:2], sv_ref[...], sw_ref[...], rate_small)
    for ref, value in zip((om_ref, ov_ref, ow_ref), new):
        ref[...] = value


def update(ta, tb, tc, ts, row, sel, tables, smalls):
    vmem = pl.BlockSpec(memory_space=pltpu.VMEM)
    blocks = sel.shape[0]
    operands = (ta, tb, tc, ts, row, sel, *tables, *smalls)
    outs = [jax.ShapeDtypeStruct(table.shape, f32) for table in tables]
    outs.append(jax.ShapeDtypeStruct((blocks, BLOCK), b16))
    outs += [jax.ShapeDtypeStruct(small.shape, f32) for small in smalls]
    return pl.pallas_call(
        update_kernel,
        out_shape=outs,
        in_specs=[vmem] * len(operands),
        out_specs=[vmem] * len(outs),
        scratch_shapes=[
            pltpu.VMEM((blocks, BLOCK), f32),
            pltpu.VMEM((2, ta.shape[0] * ta.shape[1] // 2, 128), f32),
            pltpu.VMEM((D, 128), f32),
            pltpu.VMEM((8, SMALL), f32),
        ],
        compiler_params=pltpu.CompilerParams(vmem_limit_bytes=VMEM_FULL),
        name="update",
    )(*operands)


class Args:
    def __init__(self, rows, width, limit):
        self.rows, self.width, self.limit = rows, width, limit
        self.operands, self.in_specs, self.outs, self.out_specs = [], [], [], []

    def cols(self, *arrays):
        for array in arrays:
            self.operands.append(array)
            self.in_specs.append(
                pl.BlockSpec((array.shape[0], self.width), lambda tile, scal: (0, tile))
            )

    def points(self, *arrays):
        for array in arrays:
            self.operands.append(array)
            self.in_specs.append(
                pl.BlockSpec((self.width, array.shape[1]), lambda tile, scal: (tile, 0))
            )

    def whole(self, *arrays):
        for array in arrays:
            rank = array.ndim
            self.operands.append(array)
            self.in_specs.append(
                pl.BlockSpec(array.shape, lambda tile, scal, rank=rank: (0,) * rank)
            )

    def layer(self, index, *arrays):
        for array in arrays:
            self.operands.append(array)
            self.in_specs.append(
                pl.BlockSpec((None,) + array.shape[1:], lambda tile, scal: (index, 0, 0))
            )

    def rows_of(self, array, start, size):
        self.operands.append(array)
        self.in_specs.append(
            pl.BlockSpec((size, array.shape[1]), lambda tile, scal: (start // size, 0))
        )

    def far(self, *arrays):
        for array in arrays:
            self.operands.append(array)
            self.in_specs.append(pl.BlockSpec(memory_space=pl.ANY))

    def out_far(self, *pairs):
        for shape, dtype in pairs:
            self.outs.append(jax.ShapeDtypeStruct(shape, dtype))
            self.out_specs.append(pl.BlockSpec(memory_space=pl.ANY))

    def out_cols(self, *pairs):
        for height, dtype in pairs:
            self.outs.append(jax.ShapeDtypeStruct((height, self.rows), dtype))
            self.out_specs.append(
                pl.BlockSpec((height, self.width), lambda tile, scal: (0, tile))
            )

    def out_points(self, *dtypes):
        for dtype in dtypes:
            self.outs.append(jax.ShapeDtypeStruct((self.rows, D), dtype))
            self.out_specs.append(pl.BlockSpec((self.width, D), lambda tile, scal: (tile, 0)))

    def out_whole(self, *pairs):
        for shape, dtype in pairs:
            rank = len(shape)
            self.outs.append(jax.ShapeDtypeStruct(shape, dtype))
            self.out_specs.append(
                pl.BlockSpec(shape, lambda tile, scal, rank=rank: (0,) * rank)
            )

    def call(self, body, scal, scratch, name):
        tiles = self.rows // self.width
        return pl.pallas_call(
            functools.partial(body, tiles),
            grid_spec=pltpu.PrefetchScalarGridSpec(
                num_scalar_prefetch=1,
                grid=(tiles,),
                in_specs=self.in_specs,
                out_specs=self.out_specs,
                scratch_shapes=scratch,
            ),
            out_shape=self.outs,
            compiler_params=pltpu.CompilerParams(
                dimension_semantics=("arbitrary",), vmem_limit_bytes=self.limit
            ),
            cost_estimate=pl.CostEstimate(
                flops=64 * self.rows * D * D, bytes_accessed=80 * self.rows * D, transcendentals=0
            ),
            name=name,
        )(scal, *self.operands)


def adam_update(master, grad, first, second, rate):
    new_first = beta_one * first + (1.0 - beta_one) * grad
    new_second = beta_two * second + (1.0 - beta_two) * grad * grad
    fix_one = 1.0 - beta_one**STEP
    fix_two = 1.0 - beta_two**STEP
    direction = new_first / fix_one / (jnp.sqrt(new_second / fix_two) + adam_eps)
    return (master - rate * (direction + decay_rate * master), new_first, new_second)


def flat_blocks(n_head, gfm, gout, gup, gdown):
    def columns(grad):
        width = grad.shape[1] // n_head
        return grad.reshape(D, n_head, width).transpose(1, 0, 2).reshape(n_head, -1)

    return jnp.concatenate(
        [
            columns(gfm[:, :D]),
            columns(gfm[:, D:]),
            gout.reshape(n_head, -1),
            columns(gup),
            columns(gdown),
        ],
        axis=1,
    ).reshape(n_head, -1, BLOCK)


def on_device(
    sizes,
    tokens,
    cotangent,
    segment_ids,
    owner,
    w_fx,
    w_mid,
    w_out,
    w_up,
    w_down,
    small_master,
    small_first,
    small_second,
    master_table,
    first_table,
    second_table,
):
    n_pts, n_head = sizes
    rows = tokens.shape[0]
    width, wide = min(512, rows), min(1024, rows)
    tiles = rows // width
    most = rows * n_pts * n_head // LARGEST
    window = (rows - 1 + most - 1) // rows
    limit = VMEM_BYTES if window < 4 else VMEM_FULL
    layers = w_fx.shape[0]
    packed = (n_pts, n_head) == (8, 4)

    ids = segment_ids.reshape(-1, 128)
    w_fx = w_fx.transpose(0, 2, 1)
    w_mid = w_mid.transpose(0, 2, 1)
    tables = (master_table, first_table, second_table)
    smalls = (small_master, small_first, small_second)
    gathered, wsb, norms, scal, halves = opening(
        n_head, tiles, ids, w_fx, w_mid, small_master, tables
    )
    wfm0 = gathered.reshape(2 * D, D)

    cap = master_table.shape[0]
    if packed:
        collected = lax.all_gather(halves, "pts", axis=0, tiled=True)

    sums_shape = (MESHES, SLICES, 2 * D)
    grad_sums_shape = (MESHES, SLICES, D)
    front_cols = ((D, b16), (8, f32), (D, b16), (D, b16), (D, b16), (HS, b16))
    wide_scratch = [pltpu.VMEM(grad_sums_shape, b16), pltpu.VMEM((D, wide), f32)]

    args = Args(rows, wide, limit)
    args.points(tokens)
    args.whole(wfm0)
    args.layer(0, wsb, norms)
    args.out_cols((D, b16), *front_cols)
    args.out_far((sums_shape, f32))
    ends_outs = (((2, EDGE, D), b16), ((2,) + sums_shape[1:], f32))
    grad_ends_outs = (((2, EDGE, D), b16), ((2,) + grad_sums_shape[1:], f32))
    kept_outs = (((2, SLICES, 5 * D), f32), ((2, HS, SLICES), f32))
    args.out_whole(*ends_outs)
    sums_scratch = [pltpu.VMEM(sums_shape, f32), pltpu.SemaphoreType.DMA]
    spare_scratch = [pltpu.VMEM(sums_shape[1:], f32)]
    xt0, vh0, rs0, u0, f0, m0, p0, sums0, edge, ends0 = args.call(first_kernel, scal, sums_scratch, "first")
    recv0, later, wqb0 = swap_edges_weights(
        sizes, window, 0, ((0, 1), (1, 1), (2, 0)), edge, w_fx, w_mid, w_out, small_master, 1
    )
    later = later.reshape(3 * D, D)

    args = Args(rows, wide, limit)
    args.cols(xt0, p0)
    args.far(sums0)
    args.whole(ends0, recv0)
    args.rows_of(later, 2 * D, D)
    args.layer(0, w_up, w_down)
    args.whole(wqb0)
    args.layer(0, norms)
    args.rows_of(later, 0, 2 * D)
    args.layer(1, wsb, norms)
    args.out_cols((D, b16), (D, b16), (8, f32), (D, b16), (FF, b16), (FF, b16))
    args.out_whole(*kept_outs)
    args.out_cols((D, f32), *front_cols)
    args.out_far((sums_shape, f32))
    args.out_whole(*ends_outs)
    (e0, vh20, rs20, u20, gp0, z0, kept0, prob0, x1, vh1, rs1, u1, f1, m1, p1, sums1, edge, ends1) = args.call(
        second_kernel, scal, wide_scratch + spare_scratch + sums_scratch, "second"
    )
    recv1, wout1, wqb1 = swap_edges_weights(
        sizes, window, 1, ((2, 1),), edge, w_fx, w_mid, w_out, small_master, 5
    )
    wout1 = wout1.reshape(D, D)

    grad_scratch = [pltpu.VMEM((D, FF), f32), pltpu.VMEM((D, FF), f32), pltpu.VMEM((D, D), f32)]
    rest_rows = D // n_head + 2 * D

    args = Args(rows, wide, limit)
    args.cols(x1, p1)
    args.far(sums1)
    args.whole(ends1, recv1)
    args.points(cotangent)
    args.whole(wout1)
    args.layer(1, w_up, w_down)
    args.whole(wqb1)
    args.layer(1, norms)
    args.out_points(b16)
    args.out_cols((D, f32), (D, b16))
    args.out_whole(*kept_outs)
    args.out_far((grad_sums_shape, f32))
    args.out_whole(*grad_ends_outs, ((4, 128), f32))
    if packed:
        args.out_whole(((n_head, n_pts, 2 * rest_rows // n_pts, 128), b16))
    else:
        args.out_whole(((D, FF), b16), ((D, FF), b16), ((D, D), b16))
    (layer_out, d21, de1, kept1, prob1, grads1, edge, ends1, gn1b, *grads_a) = args.call(
        functools.partial(third_kernel, n_head, packed),
        scal,
        wide_scratch
        + spare_scratch
        + [pltpu.VMEM(grad_sums_shape, f32), pltpu.SemaphoreType.DMA]
        + [pltpu.VMEM((4, D, 128), f32), pltpu.VMEM((FF, wide), f32), pltpu.VMEM((FF, wide), b16)]
        + grad_scratch,
        "third",
    )
    if packed:
        grad_recv1 = swap_edges(sizes, window, edge, 4)
        grad_recv1, collected = lax.optimization_barrier((grad_recv1, collected))
        part_a = lax.psum_scatter(grads_a[0], "head", scatter_dimension=0, tiled=True)[0]
    else:
        grad_recv1 = swap_edges(sizes, window, edge, 4)

    back_scratch = [
        *spare_scratch,
        pltpu.VMEM(grad_sums_shape[1:], f32),
        pltpu.SemaphoreType.DMA,
        pltpu.VMEM((MESHES, HS, 2 * D), b16),
        pltpu.VMEM((MESHES, HS, 128), f32),
        pltpu.VMEM((HS, width), f32),
        pltpu.VMEM((D, width), f32),
        pltpu.VMEM((D, HS), f32),
        pltpu.VMEM((D, 3 * D), f32),
        pltpu.VMEM((4, D, 128), f32),
        pltpu.VMEM((DH, 128), f32),
        pltpu.VMEM((D, 2 * D), f32),
    ]

    args = Args(rows, width, limit)
    args.far(sums1)
    args.whole(kept1, prob1, recv1)
    args.far(grads1)
    args.whole(ends1, grad_recv1)
    args.cols(de1, f1, m1, p1, u1, vh1, rs1, d21)
    args.rows_of(later, 0, 2 * D)
    args.layer(1, wsb)
    args.whole(wqb1)
    args.layer(1, norms)
    args.cols(gp0, z0, vh20, rs20, u20, e0, p0)
    args.rows_of(later, 2 * D, D)
    args.layer(0, w_up, w_down, norms)
    args.whole(gn1b)
    args.out_cols((D, f32), (D, b16))
    args.out_far((grad_sums_shape, f32))
    args.out_whole(*grad_ends_outs, ((LAYER_ROWS, 128), f32), ((4, 128), f32))
    if packed:
        args.out_whole(((n_head, n_pts, (D + 2 * rest_rows) // n_pts, 128), b16))
    else:
        args.out_whole(((D, 2 * D), b16), ((D, FF), b16), ((D, FF), b16), ((D, D), b16))
    (d20, de0, grads0, edge, ends0, small1, gn0b, *grads_b) = args.call(
        functools.partial(fourth_kernel, n_head, packed),
        scal,
        back_scratch[:3] + [pltpu.VMEM(grad_sums_shape, f32)] + back_scratch[3:] + grad_scratch,
        "fourth",
    )
    if packed:
        grad_recv0, total_a, chosen, row = swap_edges_sums(
            sizes, window, edge, part_a, owner.reshape(1, -1), collected, 6
        )
        mine_b = lax.psum_scatter(grads_b[0], "head", scatter_dimension=0, tiled=True)[0]
    else:
        grad_recv0 = swap_edges(sizes, window, edge, 4)

    args = Args(rows, width, limit)
    args.far(sums0)
    args.whole(kept0, prob0, recv0)
    args.far(grads0)
    args.whole(ends0, grad_recv0)
    args.cols(de0, f0, m0, p0, u0, vh0, rs0, d20)
    args.whole(wfm0)
    args.layer(0, wsb)
    args.whole(wqb0)
    args.layer(0, norms)
    args.whole(gn0b, small1)
    args.out_points(f32)
    args.out_whole(((2 * LAYER_ROWS, 128), f32))
    args.out_whole(((n_head, D, 128), b16) if packed else ((D, 2 * D), b16))
    input_grad, small, front = args.call(
        functools.partial(fifth_kernel, n_head, packed), scal, back_scratch, "fifth"
    )

    if packed:
        total_b, total_c, total_s = total_gradients(sizes, mine_b, front, small)
        outs = update(total_a, total_b, total_c, total_s, row, chosen, tables, smalls)
        return (layer_out, input_grad, *outs)

    gup1, gdown1, gout1 = grads_a
    gfm1, gup0, gdown0, gout0 = grads_b
    small_total = lax.psum(small, ("pts", "head")).reshape(layers, -1)
    totals = []
    for parts in ((front, gout0, gup0, gdown0), (gfm1, gout1, gup1, gdown1)):
        blocks = lax.psum_scatter(
            flat_blocks(n_head, *parts), "head", scatter_dimension=0, tiled=True
        )
        totals.append(lax.psum(blocks.reshape(-1, BLOCK), "pts"))
    total_grad = jnp.concatenate(totals, axis=0).astype(f32)
    my_index = lax.axis_index("pts")
    block_ids = jnp.arange(owner.shape[0])
    same_owner = (owner[:, None] == owner[None, :]) & (block_ids[None, :] < block_ids[:, None])
    table_row = owner * cap + jnp.sum(same_owner.astype(jnp.int32), axis=1)
    place_all = (jnp.arange(n_pts * cap)[:, None] == table_row[None, :]).astype(f32)
    mine_place = lax.dynamic_slice_in_dim(place_all, my_index * cap, cap, 0)
    own_grad = jnp.dot(mine_place, total_grad, precision=lax.Precision.HIGHEST)
    filled = jnp.sum(mine_place, axis=1)[:, None] > 0.5
    updated = adam_update(master_table, own_grad, first_table, second_table, rate_large)
    new_tables = [jnp.where(filled, new, old) for new, old in zip(updated, tables)]
    collected = lax.all_gather(new_tables[0].astype(b16), "pts", axis=0, tiled=True)
    pick_back = (table_row[:, None] == jnp.arange(n_pts * cap)[None, :]).astype(b16)
    fresh = jnp.dot(pick_back, collected, preferred_element_type=f32).astype(b16)
    small_outs = adam_update(small_master, small_total, small_first, small_second, rate_small)
    return (layer_out, input_grad, *new_tables, fresh, *small_outs)


def solution(mesh):
    sizes = (mesh.shape["pts"], mesh.shape["head"])
    return jax.shard_map(
        functools.partial(on_device, sizes),
        mesh=mesh,
        in_specs=(
            P(("pts", "head"), None),
            P(("pts", "head"), None),
            P("pts"),
            P(),
            P(None, None, "head"),
            P(None, None, "head"),
            P(None, "head", None),
            P(),
            P(),
            P(),
            P(),
            P(),
            P("pts", "head"),
            P("pts", "head"),
            P("pts", "head"),
        ),
        out_specs=(
            P(("pts", "head"), None),
            P(("pts", "head"), None),
            P("pts", "head"),
            P("pts", "head"),
            P("pts", "head"),
            P(None, "head"),
            P(),
            P(),
            P(),
        ),
        check_vma=False,
    )
```

```python
import functools
import math

import jax
import jax.numpy as jnp
from jax import lax
from jax.experimental import pallas as pl
from jax.experimental.pallas import tpu as pltpu
from jax.sharding import PartitionSpec as P

D = 256
HEADS = 8
DH = 32
SLICES = 64
HS = HEADS * SLICES
FF = 1024
MESHES = 24
BLOCK = 2048
SMALL = 6144
STEP = 10
LARGEST = 12
EDGE = 80
VMEM_FULL = 58 << 20
VMEM_BYTES = 52 << 20

MESH = pl.DeviceIdType.MESH
HIGH = True
norm_eps = 1e-05
beta_one = 0.9
beta_two = 0.95
adam_eps = 1e-08
decay_rate = 0.1
rate_large = 0.1
rate_small = 0.75
f32 = jnp.float32
b16 = jnp.bfloat16


def dot(a, b, contract, precise):
    dims = (contract, ((), ()))
    if not precise:
        return lax.dot_general(a, b, dims, preferred_element_type=f32)
    a_high, b_high = a.astype(b16), b.astype(b16)
    a_low = (a - a_high.astype(f32)).astype(b16)
    b_low = (b - b_high.astype(f32)).astype(b16)
    return (
        lax.dot_general(a_high, b_low, dims, preferred_element_type=f32)
        + lax.dot_general(a_low, b_high, dims, preferred_element_type=f32)
        + lax.dot_general(a_high, b_high, dims, preferred_element_type=f32)
    )


def nn(a, b, precise=False):
    return dot(a, b, ((1,), (0,)), precise)


def nt(a, b, precise=False):
    return dot(a, b, ((1,), (1,)), precise)


def tn(a, b, precise=False):
    return dot(a, b, ((0,), (0,)), precise)


def iota(shape, axis):
    return lax.broadcasted_iota(jnp.int32, shape, axis)


def pick_diag(full, per_head):
    lane_head = iota((SLICES, full.shape[1]), 1) // per_head
    total = jnp.where(lane_head == 0, full[:SLICES], 0.0)
    for head in range(1, HEADS):
        total = total + jnp.where(
            lane_head == head, full[head * SLICES : (head + 1) * SLICES], 0.0
        )
    return total


def spread_diag(small):
    lane_head = iota((SLICES, D), 1) // DH
    return jnp.concatenate(
        [jnp.where(lane_head == head, small, jnp.zeros_like(small)) for head in range(HEADS)],
        axis=0,
    )


def repeat_rows(width):
    return (iota((D, width), 0) % width == iota((D, width), 1)).astype(f32)


def slice_repeat():
    return (iota((SLICES, HS), 1) % SLICES == iota((SLICES, HS), 0)).astype(f32)


def same_head(rows_per, cols_per, shape):
    return (iota(shape, 0) // rows_per) == (iota(shape, 1) // cols_per)


def start_gather(n_head, picks, send_sem, recv_sem):
    me = lax.axis_index("head")
    copies = []
    for index, ref in enumerate(picks):
        for step in range(1, n_head):
            copy = pltpu.make_async_remote_copy(
                src_ref=ref.at[:, me],
                dst_ref=ref.at[:, me],
                send_sem=send_sem.at[index, step - 1],
                recv_sem=recv_sem.at[index, step - 1],
                device_id={"head": lax.rem(me + step, n_head)},
                device_id_type=MESH,
            )
            copy.start()
            copies.append(copy)
    return copies


def unroll_slices(row_of, out):
    lane = iota((1, 128), 1)
    for pair in range(DH // 2):
        row = row_of(pair)
        out[2 * pair : 2 * pair + 1] = jnp.where(lane < SLICES, row, 0.0)
        out[2 * pair + 1 : 2 * pair + 2] = jnp.where(
            lane < SLICES, pltpu.roll(row, 128 - SLICES, 1), 0.0
        )


def opening_kernel(n_head, tiles, ids_ref, wfx_ref, wmid_ref, sm_ref, m_ref, v_ref, w_ref,
                   out_ref, wsb_ref, norm_ref, scal_ref, tables_ref, send_sem, recv_sem, slices_s, norm_s):
    me = lax.axis_index("head")
    barrier = pltpu.get_barrier_semaphore()
    for step in range(1, n_head):
        pl.semaphore_signal(
            barrier, inc=1, device_id={"head": lax.rem(me + step, n_head)}, device_id_type=MESH
        )
    out_ref[0, me] = wfx_ref[0]
    out_ref[1, me] = wmid_ref[0]
    pl.semaphore_wait(barrier, n_head - 1)
    copies = start_gather(n_head, [out_ref], send_sem, recv_sem)
    layers = sm_ref.shape[0]
    cap, deep = m_ref.shape[0], tables_ref.shape[0]
    for which, ref in enumerate((m_ref, v_ref, w_ref)):
        value = ref[...]
        if deep > cap:
            value = jnp.concatenate([value, jnp.zeros((deep - cap, BLOCK), f32)], axis=0)
        tables_ref[:, which * BLOCK : (which + 1) * BLOCK] = value.astype(b16)
    right = (iota((128, HS), 1) % SLICES == iota((128, HS), 0)).astype(b16)
    for layer in range(layers):
        unroll_slices(lambda pair: sm_ref[layer : layer + 1, 128 * pair : 128 * pair + 128], slices_s)
        wide = nn(slices_s[...].astype(b16), right)
        tiled = jnp.concatenate([wide] * HEADS, axis=0)
        wsb_ref[layer] = jnp.where(same_head(DH, SLICES, (D, HS)), tiled, 0.0).astype(b16)
        norm_s[...] = jnp.zeros_like(norm_s)
        for row in range(4):
            start = SMALL - 4 * D + row * D
            norm_s[row : row + 1] = sm_ref[layer : layer + 1, start : start + D]
        norm_ref[layer] = norm_s[...].T
    rows = ids_ref.shape[0] // n_head
    ids = ids_ref[pl.ds(pl.multiple_of(me * rows, rows), rows), :]
    for mesh in range(MESHES + 1):
        scal_ref[mesh] = jnp.sum((ids < mesh).astype(jnp.int32))
    deep = rows // tiles
    for tile in range(tiles):
        part = ids[tile * deep : (tile + 1) * deep]
        scal_ref[MESHES + 1 + 2 * tile] = jnp.min(part)
        scal_ref[MESHES + 2 + 2 * tile] = jnp.max(part)
    for copy in copies:
        copy.wait()


def opening(n_head, tiles, ids, w_fx, w_mid, small, tables):
    layers, part, _ = w_fx.shape
    deep = -(-tables[0].shape[0] // 16) * 16
    vmem = pl.BlockSpec(memory_space=pltpu.VMEM)
    return pl.pallas_call(
        functools.partial(opening_kernel, n_head, tiles),
        out_shape=(
            jax.ShapeDtypeStruct((2, n_head, part, D), b16),
            jax.ShapeDtypeStruct((layers, D, HS), b16),
            jax.ShapeDtypeStruct((layers, D, 128), f32),
            jax.ShapeDtypeStruct((MESHES + 1 + 2 * tiles,), jnp.int32),
            jax.ShapeDtypeStruct((deep, 3 * BLOCK), b16),
        ),
        in_specs=[vmem] * 7,
        out_specs=[vmem] * 3 + [pl.BlockSpec(memory_space=pltpu.SMEM), vmem],
        scratch_shapes=[
            pltpu.SemaphoreType.DMA((1, n_head - 1)),
            pltpu.SemaphoreType.DMA((1, n_head - 1)),
            pltpu.VMEM((DH, 128), f32),
            pltpu.VMEM((128, D), f32),
        ],
        cost_estimate=pl.CostEstimate(flops=0, bytes_accessed=32 << 20, transcendentals=0),
        compiler_params=pltpu.CompilerParams(
            collective_id=0, has_side_effects=True, vmem_limit_bytes=VMEM_FULL
        ),
        name="opening",
    )(ids, w_fx, w_mid, small, *tables)


def place_of(sizes, shift):
    n_pts, n_head = sizes
    total = n_pts * n_head
    me = lax.axis_index("pts") * n_head + lax.axis_index("head")
    other = lax.rem(me + (shift + total), total)
    return (other // n_head, lax.rem(other, n_head))


def greet(sizes, window):
    barrier = pltpu.get_barrier_semaphore()
    for step in range(1, window + 1):
        for shift in (step, -step):
            pl.semaphore_signal(barrier, inc=1, device_id=place_of(sizes, shift), device_id_type=MESH)
    return barrier


def start_edges(sizes, window, edge_ref, out_ref, send_sem, recv_sem):
    copies = []
    for step in range(1, window + 1):
        for side, shift in ((1, step), (0, -step)):
            slot = step - 1 if side == 1 else window + step - 1
            copy = pltpu.make_async_remote_copy(
                src_ref=edge_ref.at[side],
                dst_ref=out_ref.at[slot],
                send_sem=send_sem.at[slot],
                recv_sem=recv_sem.at[slot],
                device_id=place_of(sizes, shift),
                device_id_type=MESH,
            )
            copy.start()
            copies.append(copy)
    return copies


def edge_kernel(sizes, window, edge_ref, out_ref, send_sem, recv_sem):
    barrier = greet(sizes, window)
    pl.semaphore_wait(barrier, 2 * window)
    for copy in start_edges(sizes, window, edge_ref, out_ref, send_sem, recv_sem):
        copy.wait()


def edge_weights_kernel(sizes, window, layer, pieces, edge_ref, wfx_ref, wmid_ref, wout_ref, sm_ref,
                        out_ref, w_ref, wqb_ref,
                        send_sem, recv_sem, wsend_sem, wrecv_sem, square_s):
    n_head = sizes[1]
    me = lax.axis_index("head")
    barrier = greet(sizes, window)
    for step in range(1, n_head):
        pl.semaphore_signal(
            barrier, inc=1, device_id={"head": lax.rem(me + step, n_head)}, device_id_type=MESH
        )
    refs = (wfx_ref, wmid_ref, wout_ref)
    for index, (kind, which) in enumerate(pieces):
        w_ref[index, me] = refs[kind][which]
    pl.semaphore_wait(barrier, 2 * window + n_head - 1)
    copies = start_edges(sizes, window, edge_ref, out_ref, send_sem, recv_sem)
    copies += start_gather(n_head, [w_ref], wsend_sem, wrecv_sem)
    lane = iota((1, 128), 1)
    for part in range(3):
        start = DH * SLICES + part * DH * DH
        for group in range(DH // 4):
            row = sm_ref[layer : layer + 1, start + 128 * group : start + 128 * group + 128]
            for inner in range(4):
                moved = row if inner == 0 else pltpu.roll(row, 128 - DH * inner, 1)
                square_s[4 * group + inner : 4 * group + inner + 1] = jnp.where(
                    lane < DH, moved, 0.0
                )
        square = square_s[...]
        for turn in range(1, 128 // DH):
            square = square + pltpu.roll(square_s[...], DH * turn, 1)
        square = jnp.concatenate([square] * (D // 128), axis=1)
        square = jnp.concatenate([square] * HEADS, axis=0)
        wqb_ref[:, part * D : (part + 1) * D] = jnp.where(
            same_head(DH, DH, (D, D)), square, 0.0
        )
    for copy in copies:
        copy.wait()


def pick_rows(n_pts, owner_ref, tables_s, load, chosen_ref, row_ref):
    blocks = owner_ref.shape[1]
    deep = tables_s.shape[0] // n_pts
    across = jnp.broadcast_to(owner_ref[...].astype(f32), (blocks, blocks))
    down = across.T
    low, high = iota((blocks, blocks), 0), iota((blocks, blocks), 1)
    same = across == down
    slot_down = jnp.sum(jnp.where(same & (high < low), 1.0, 0.0), axis=1, keepdims=True)
    slot_across = jnp.sum(jnp.where(same & (low < high), 1.0, 0.0), axis=0, keepdims=True)
    mine = owner_ref[...] == lax.axis_index("pts")
    row_ref[...] = jnp.broadcast_to(
        jnp.where(mine, slot_across.astype(jnp.int32), -1), row_ref.shape
    )
    target = (down[:, :1] * deep + slot_down).astype(jnp.int32)
    pick = (iota((blocks, tables_s.shape[0]), 1) == target).astype(b16)
    load.wait()
    step = 1024

    def choose(part, carry):
        lanes = pl.ds(pl.multiple_of(part * step, step), step)
        chosen_ref[:, lanes] = nn(pick, tables_s[:, lanes]).astype(b16)
        return carry

    lax.fori_loop(0, tables_s.shape[1] // step, choose, 0)


def edge_call(window, collective_id, rows, width, body, extra, outs, scratch, name):
    vmem = pl.BlockSpec(memory_space=pltpu.VMEM)
    outs = [jax.ShapeDtypeStruct((2 * window, rows, width), b16)] + outs
    return pl.pallas_call(
        body,
        out_shape=outs,
        in_specs=[vmem] * (1 + extra),
        out_specs=[vmem] * len(outs),
        scratch_shapes=[
            pltpu.SemaphoreType.DMA((2 * window,)),
            pltpu.SemaphoreType.DMA((2 * window,)),
        ]
        + scratch,
        cost_estimate=pl.CostEstimate(flops=0, bytes_accessed=32 << 20, transcendentals=0),
        compiler_params=pltpu.CompilerParams(
            collective_id=collective_id, has_side_effects=True, vmem_limit_bytes=VMEM_BYTES
        ),
        name=name,
    )


def swap_edges(sizes, window, edge, collective_id):
    _, rows, width = edge.shape
    return edge_call(
        window, collective_id, rows, width,
        functools.partial(edge_kernel, sizes, window), 0, [], [], "swap_edges",
    )(edge)[0]


def swap_edges_weights(sizes, window, layer, pieces, edge, w_fx, w_mid, w_out, small, collective_id):
    _, rows, width = edge.shape
    n_head = sizes[1]
    part = w_fx.shape[1]
    return edge_call(
        window, collective_id, rows, width,
        functools.partial(edge_weights_kernel, sizes, window, layer, pieces), 4,
        [
            jax.ShapeDtypeStruct((len(pieces), n_head, part, D), b16),
            jax.ShapeDtypeStruct((D, 3 * D), f32),
        ],
        [
            pltpu.SemaphoreType.DMA((1, n_head - 1)),
            pltpu.SemaphoreType.DMA((1, n_head - 1)),
            pltpu.VMEM((DH, 128), f32),
        ],
        "swap_edges_weights",
    )(edge, w_fx, w_mid, w_out, small)


def pts_copies(n_pts, source, target, send_sem, recv_sem):
    pts, head = lax.axis_index("pts"), lax.axis_index("head")
    copies = []
    for step in range(1, n_pts):
        peer = lax.rem(pts + step, n_pts)
        copies.append(
            pltpu.make_async_remote_copy(
                src_ref=source(step, peer),
                dst_ref=target(step, peer),
                send_sem=send_sem.at[step - 1],
                recv_sem=recv_sem.at[step - 1],
                device_id=(peer, head),
                device_id_type=MESH,
            )
        )
    return copies


def edge_sums_kernel(sizes, window, edge_ref, ga_ref, owner_ref, tables_ref, out_ref, ta_ref, chosen_ref, row_ref,
                     send_sem, recv_sem, a_send, a_recv, a_send2, a_recv2, got_a, tables_s, local_sem):
    n_pts, n_head = sizes
    pts, head = lax.axis_index("pts"), lax.axis_index("head")
    barrier = greet(sizes, window)
    for step in range(1, n_pts):
        pl.semaphore_signal(
            barrier, inc=1, device_id=(lax.rem(pts + step, n_pts), head), device_id_type=MESH
        )
    load = pltpu.make_async_copy(tables_ref, tables_s, local_sem)
    load.start()
    pl.semaphore_wait(barrier, 2 * window + n_pts - 1)
    gather = pts_copies(
        n_pts,
        lambda step, peer: ga_ref.at[peer],
        lambda step, peer: got_a.at[step - 1],
        a_send,
        a_recv,
    )
    for copy in gather:
        copy.start()
    edges = start_edges(sizes, window, edge_ref, out_ref, send_sem, recv_sem)
    for copy in gather:
        copy.wait()
    total = ga_ref[pts].astype(f32)
    for index in range(n_pts - 1):
        total = total + got_a[index].astype(f32)
    ta_ref[pts] = total.astype(b16)
    share = pts_copies(
        n_pts,
        lambda step, peer: ta_ref.at[pts],
        lambda step, peer: ta_ref.at[pts],
        a_send2,
        a_recv2,
    )
    for copy in share:
        copy.start()
    pick_rows(n_pts, owner_ref, tables_s, load, chosen_ref, row_ref)
    for copy in edges:
        copy.wait()
    for copy in share:
        copy.wait()


def swap_edges_sums(sizes, window, edge, ga, owner, tables, collective_id):
    _, rows, width = edge.shape
    n_pts = sizes[0]
    blocks = owner.shape[1]
    dma = pltpu.SemaphoreType.DMA
    vmem = pl.BlockSpec(memory_space=pltpu.VMEM)
    return pl.pallas_call(
        functools.partial(edge_sums_kernel, sizes, window),
        out_shape=(
            jax.ShapeDtypeStruct((2 * window, rows, width), b16),
            jax.ShapeDtypeStruct(ga.shape, b16),
            jax.ShapeDtypeStruct((blocks, tables.shape[1]), b16),
            jax.ShapeDtypeStruct((8, blocks), jnp.int32),
        ),
        in_specs=[vmem] * 3 + [pl.BlockSpec(memory_space=pl.ANY)],
        out_specs=[vmem] * 4,
        scratch_shapes=[dma((2 * window,))] * 2
        + [dma((n_pts - 1,))] * 4
        + [
            pltpu.VMEM((n_pts - 1,) + ga.shape[1:], b16),
            pltpu.VMEM(tables.shape, b16),
            dma,
        ],
        cost_estimate=pl.CostEstimate(flops=0, bytes_accessed=32 << 20, transcendentals=0),
        compiler_params=pltpu.CompilerParams(
            collective_id=collective_id, has_side_effects=True, vmem_limit_bytes=VMEM_BYTES
        ),
        name="swap_edges_sums",
    )(edge, ga, owner, tables)


def norm_stats(values):
    center = jnp.mean(values, axis=0, keepdims=True)
    spread = values - center
    scale = lax.rsqrt(jnp.mean(spread * spread, axis=0, keepdims=True) + norm_eps)
    return (spread * scale, scale)


def norm_back(grad_out, scaled, scale, gain):
    inner = grad_out * gain
    return scale * (
        inner
        - jnp.mean(inner, axis=0, keepdims=True)
        - scaled * jnp.mean(inner * scaled, axis=0, keepdims=True)
    )


def group_sum(values):
    return jnp.sum(values.reshape(HEADS, SLICES, values.shape[1]), axis=1, keepdims=True)


def fold_lanes(values):
    total = values[:, :128]
    for start in range(128, values.shape[1], 128):
        total = total + values[:, start : start + 128]
    return total


def tile_mask(scal, mesh, tile, width):
    spot = iota((1, width), 1) + tile * width
    return (spot >= scal[mesh]) & (spot < scal[mesh + 1])


def tile_range(scal, tiles, tile):
    base = MESHES + 1
    ratio = (scal.shape[0] - base) // 2 // tiles
    return (scal[base + 2 * ratio * tile], scal[base + 2 * ratio * (tile + 1) - 1])


def front_tile(scal, tiles, tile, x, wfm, wsb, norms, vh_ref, rs_ref, u_ref, f_ref, m_ref, p_ref, sums):
    width = x.shape[1]
    scaled, scale = norm_stats(x)
    vh_ref[...] = scaled.astype(b16)
    rs_ref[...] = jnp.broadcast_to(scale, (8, width))
    normed = (scaled * norms[:, 0:1] + norms[:, 1:2]).astype(b16)
    u_ref[...] = normed
    joint = nn(wfm, normed)
    feats = joint[:D].astype(b16)
    middle = joint[D:].astype(b16)
    f_ref[...] = feats
    m_ref[...] = middle
    logits = tn(wsb, middle).reshape(HEADS, SLICES, width)
    top = jnp.max(logits, axis=1, keepdims=True)
    expo = jnp.exp(logits - top)
    weights = expo / jnp.sum(expo, axis=1, keepdims=True)
    weights_r = weights.reshape(HS, width).astype(b16)
    p_ref[...] = weights_r
    low, high = tile_range(scal, tiles, tile)

    def add(mesh, carry):
        keep = tile_mask(scal, mesh, tile, width).astype(b16)
        wide = jnp.concatenate(
            [feats * keep, jnp.broadcast_to(keep, (D, width))], axis=0
        )
        full = nt(weights_r, wide)
        sums[mesh, :, :D] += pick_diag(full[:, :D], DH)
        sums[mesh, :, D:] += pick_diag(full[:, D:], DH)
        return carry

    lax.fori_loop(low, high + 1, add, 0)


def present(scal, tiles, body):
    def one(mesh, carry):
        body(mesh)
        return carry

    lax.fori_loop(tile_range(scal, tiles, 0)[0], tile_range(scal, tiles, tiles - 1)[1] + 1, one, 0)


def ends_of(scal, tiles):
    return (tile_range(scal, tiles, 0)[0], tile_range(scal, tiles, tiles - 1)[1])


def between(scal, tiles, body):
    first, last = ends_of(scal, tiles)

    def one(mesh, carry):
        body(mesh)
        return carry

    lax.fori_loop(first + 1, last, one, 0)


def fetch(source, target, sem):
    copy = pltpu.make_async_copy(source, target, sem)
    copy.start()
    copy.wait()


def clear_present(scal, tiles, sums):
    def clear(mesh):
        sums[mesh] = jnp.zeros(sums.shape[1:], f32)

    present(scal, tiles, clear)


def write_edges(scal, tiles, sums, edge_ref, ends_ref, sums_hbm, sem):
    first, last = ends_of(scal, tiles)
    extra = EDGE - SLICES
    for side, mesh in ((0, first), (1, last)):
        ends_ref[side] = sums[mesh]
        edge_ref[side, :SLICES] = sums[mesh, :, :D].astype(b16)
        rows = jnp.zeros((extra, D), f32)
        if sums.shape[2] > D:
            counts = jnp.concatenate(
                [sums[mesh, :, D:], jnp.zeros((D - SLICES, D), f32)], axis=0
            )
            pick = (iota((extra, D), 1) == DH * iota((extra, D), 0)).astype(f32)
            rows = nt(pick, counts, HIGH)
        edge_ref[side, SLICES:] = jnp.where(
            iota((extra, D), 0) >= HEADS, mesh.astype(f32), rows
        ).astype(b16)
    between(scal, tiles, lambda mesh: fetch(sums.at[mesh], sums_hbm.at[mesh], sem))


def add_edges(own, mesh, recv_ref):
    wanted = mesh.astype(f32)
    total = jnp.zeros((EDGE, D), f32)
    for slot in range(recv_ref.shape[0]):
        match = recv_ref[slot, SLICES + HEADS : SLICES + HEADS + 1].astype(f32) == wanted
        total = total + jnp.where(match, recv_ref[slot].astype(f32), 0.0)
    if own.shape[1] == D:
        return own + total[:SLICES]
    extra = EDGE - SLICES
    spread = (iota((extra, D), 1) // DH == iota((extra, D), 0)).astype(f32)
    counts = tn(total[SLICES:, :SLICES], spread, HIGH)
    return own + jnp.concatenate([total[:SLICES], counts], axis=1)


def attend_parts(totals, wqb):
    total = jnp.concatenate(totals, axis=0)
    count = total[:, D:]
    slice_tok = total[:, :D] / count
    triple = nn(slice_tok, wqb, HIGH)
    parts = []
    for index in range(len(totals)):
        rows = slice(index * SLICES, (index + 1) * SLICES)
        queries = triple[rows, :D]
        key_wide = spread_diag(triple[rows, D : 2 * D])
        value_wide = spread_diag(triple[rows, 2 * D :])
        scores = (nt(key_wide, queries, HIGH) * (1.0 / math.sqrt(DH))).reshape(
            HEADS, SLICES, SLICES
        )
        expo = jnp.exp(scores - jnp.max(scores, axis=1, keepdims=True))
        prob = (expo / jnp.sum(expo, axis=1, keepdims=True)).reshape(HS, SLICES)
        parts.append((queries, key_wide, value_wide, prob))
    return (slice_tok, count, triple, parts)


def attend_all(scal, tiles, ends_ref, recv_ref, sums_hbm, wqb, attended_ref, kept_ref, prob_ref, spare, sem):
    ends = ends_of(scal, tiles)
    totals = [add_edges(ends_ref[side], mesh, recv_ref) for side, mesh in enumerate(ends)]
    slice_tok, count, triple, parts = attend_parts(totals, wqb)
    kept = jnp.concatenate([slice_tok, count, triple], axis=1)
    results = []
    for side, (_, _, value_wide, prob) in enumerate(parts):
        results.append(tn(prob, value_wide, HIGH).astype(b16))
        kept_ref[side] = kept[side * SLICES : (side + 1) * SLICES]
        prob_ref[side] = prob
    for mesh, result in zip(ends, results):
        attended_ref[mesh] = result

    def inner(mesh):
        fetch(sums_hbm.at[mesh], spare, sem)
        _, _, _, parts = attend_parts([spare[...]], wqb)
        attended_ref[mesh] = tn(parts[0][3], parts[0][2], HIGH).astype(b16)

    between(scal, tiles, inner)


def spread_tile(scal, tiles, tile, wide_ref, p_ref, spread):
    low, high = tile_range(scal, tiles, tile)
    weights_r = p_ref[...]
    width = weights_r.shape[1]

    def one(mesh, carry):
        keep = tile_mask(scal, mesh, tile, width)
        spread[...] = jnp.where(keep, tn(spread_diag(wide_ref[mesh]), weights_r), spread[...])
        return carry

    lax.fori_loop(low, high + 1, one, 0)
    return spread[...].astype(b16)


GELU_A = math.sqrt(2.0 / math.pi)
GELU_B = 0.044715


def gelu_pair(hidden):
    square = hidden * hidden
    bend = jnp.tanh(hidden * (GELU_A + (GELU_A * GELU_B) * square))
    half = 0.5 + 0.5 * bend
    value = hidden * half
    slope = half + (0.5 * hidden) * (1.0 - bend * bend) * (
        GELU_A + (3.0 * GELU_A * GELU_B) * square
    )
    return (value, slope)


CHUNK = 1024


def mlp_back_tile(scal, tiles, tile, grad, slopes, actives, scaled_two, scale_two, normed_two_r, spread_r,
                  weights_r, wout, wup, wdown, norms, d2_ref, de_ref, sums,
                  gup, gdown, gout, gnorm):
    width = grad.shape[1]
    grad_r = grad.astype(b16)
    grad_normed = jnp.zeros((D, width), f32)
    for start in range(0, FF, CHUNK):
        part = slice(start, start + CHUNK)
        back = (slopes(part) * nn(wdown[part], grad_r)).astype(b16)
        gup[:, part] += nt(normed_two_r, back)
        gdown[:, part] += nt(grad_r, actives(part))
        grad_normed = grad_normed + nn(wup[:, part], back)
    gnorm[2] += fold_lanes(grad_normed * scaled_two)
    gnorm[3] += fold_lanes(grad_normed)
    grad_middle = grad + norm_back(grad_normed, scaled_two, scale_two, norms[:, 2:3])
    d2_ref[...] = grad_middle
    branch_r = grad_middle.astype(b16)
    gout[...] += nt(spread_r, branch_r)
    spread_grad = nn(wout, branch_r).astype(b16)
    de_ref[...] = spread_grad
    low, high = tile_range(scal, tiles, tile)

    def add(mesh, carry):
        keep = tile_mask(scal, mesh, tile, width).astype(b16)
        sums[mesh] += pick_diag(nt(weights_r, spread_grad * keep), DH)
        return carry

    lax.fori_loop(low, high + 1, add, 0)


def attend_back(meshes, shares, slice_tok, count, parts, outer, wqb, both, dcount, gqkv):
    root = 1.0 / math.sqrt(DH)
    attended, triples = [], []
    for (queries, key_wide, value_wide, prob), grad in zip(parts, outer):
        attended.append(tn(prob, value_wide, HIGH).astype(b16))
        inner = prob * nt(value_wide, grad, HIGH)
        mixed = group_sum(inner)
        grad_scores = root * (
            inner - (prob.reshape(HEADS, SLICES, SLICES) * mixed).reshape(HS, SLICES)
        )
        triples.append(
            jnp.concatenate(
                [
                    tn(grad_scores, key_wide, HIGH),
                    pick_diag(nn(grad_scores, queries, HIGH), DH),
                    pick_diag(nn(prob, grad, HIGH), DH),
                ],
                axis=1,
            )
        )
    triple = jnp.concatenate(triples, axis=0)
    grad_sum = nt(triple, wqb, HIGH) / count
    grad_count = -(grad_sum * slice_tok)
    gqkv[...] += tn(slice_tok * jnp.concatenate(shares, axis=0), triple, HIGH)
    for index, mesh in enumerate(meshes):
        rows = slice(index * SLICES, (index + 1) * SLICES)
        both[mesh, :, :D] = spread_diag(attended[index])
        both[mesh, :, D:] = spread_diag(grad_sum[rows].astype(b16))
        column = jnp.sum(spread_diag(grad_count[rows]), axis=1, keepdims=True)
        dcount[mesh] = jnp.broadcast_to(column, (HS, 128))


def attend_back_all(scal, tiles, kept_ref, prob_ref, recv_ref, ends_ref, grad_recv_ref, sums_hbm, grads_hbm,
                    wqb, both, dcount, gqkv, spare, spare_grad, sem):
    ends = ends_of(scal, tiles)
    outer = [add_edges(ends_ref[side], mesh, grad_recv_ref) for side, mesh in enumerate(ends)]
    kept = jnp.concatenate([kept_ref[0], kept_ref[1]], axis=0)
    parts = []
    for side in range(2):
        parts.append(
            (
                kept_ref[side, :, 2 * D : 3 * D],
                spread_diag(kept_ref[side, :, 3 * D : 4 * D]),
                spread_diag(kept_ref[side, :, 4 * D :]),
                prob_ref[side],
            )
        )
    previous = recv_ref[0, SLICES + HEADS : SLICES + HEADS + 1, :1].astype(f32)
    shares = [
        jnp.broadcast_to(1.0 - (previous == ends[0].astype(f32)).astype(f32), (SLICES, 1)),
        jnp.broadcast_to((ends[1] != ends[0]).astype(f32), (SLICES, 1)),
    ]
    attend_back(ends, shares, kept[:, :D], kept[:, D : 2 * D], parts, outer, wqb, both, dcount, gqkv)

    def inner(mesh):
        fetch(sums_hbm.at[mesh], spare, sem)
        fetch(grads_hbm.at[mesh], spare_grad, sem)
        slice_tok, count, _, parts = attend_parts([spare[...]], wqb)
        attend_back(
            (mesh,), [jnp.ones((SLICES, 1), f32)], slice_tok, count, parts, [spare_grad[...]], wqb, both, dcount, gqkv
        )

    between(scal, tiles, inner)


def attend_back_tile(scal, tiles, tile, both, dcount, de_ref, f_ref, m_ref, p_ref, u_ref, vh_ref, rs_ref,
                     d2_ref, wfm, wsb, norms, grad_p, grad_f, gfm, gws, gnorm):
    low, high = tile_range(scal, tiles, tile)
    weights_r = p_ref[...]
    width = weights_r.shape[1]
    pair = jnp.concatenate([de_ref[...], f_ref[...]], axis=0)

    def one(mesh, carry):
        keep = tile_mask(scal, mesh, tile, width)
        back = nn(both[mesh], pair) + dcount[mesh][:, :1]
        grad_p[...] = jnp.where(keep, back, grad_p[...])
        grad_f[...] = jnp.where(keep, tn(both[mesh, :, D:], weights_r), grad_f[...])
        return carry

    lax.fori_loop(low, high + 1, one, 0)
    weights = weights_r.astype(f32)
    inner = weights * grad_p[...]
    mixed = group_sum(inner)
    grad_logits = (
        inner - (weights.reshape(HEADS, SLICES, width) * mixed).reshape(HS, width)
    ).astype(b16)
    gws[...] += nt(m_ref[...], grad_logits)
    grad_m = nn(wsb, grad_logits).astype(b16)
    grad_fm = jnp.concatenate([grad_f[...].astype(b16), grad_m], axis=0)
    gfm[...] += nt(u_ref[...], grad_fm)
    grad_normed = tn(wfm, grad_fm)
    scaled = vh_ref[...].astype(f32)
    gnorm[0] += fold_lanes(grad_normed * scaled)
    gnorm[1] += fold_lanes(grad_normed)
    return d2_ref[...] + norm_back(grad_normed, scaled, rs_ref[:1], norms[:, 0:1])


def small_rows(base, gws, gqkv, scratch, out_ref):
    lane = iota((1, 128), 1)
    left = repeat_rows(DH)
    fold = (iota((128, HS), 1) % SLICES == iota((128, HS), 0)).astype(f32)
    kept = jnp.where(same_head(DH, SLICES, (D, HS)), gws[...], 0.0)
    scratch[...] = nt(tn(left, kept, HIGH), fold, HIGH)
    even = scratch[pl.ds(0, DH // 2, stride=2), :]
    odd = scratch[pl.ds(1, DH // 2, stride=2), :]
    out_ref[base : base + DH // 2] = jnp.where(lane < SLICES, even, pltpu.roll(odd, SLICES, 1))
    fold = (iota((D, 128), 0) % DH == iota((D, 128), 1)).astype(f32)
    for part in range(3):
        square = jnp.where(same_head(DH, DH, (D, D)), gqkv[:, part * D : (part + 1) * D], 0.0)
        scratch[...] = nn(tn(left, square, HIGH), fold, HIGH)
        total = scratch[pl.ds(0, DH // 4, stride=4), :]
        for inner in range(1, 4):
            total = total + pltpu.roll(scratch[pl.ds(inner, DH // 4, stride=4), :], DH * inner, 1)
        start = base + DH // 2 + part * (DH // 4)
        out_ref[start : start + DH // 4] = total


NORM_ROW = (SMALL - 4 * D) // 128
LAYER_ROWS = SMALL // 128


def norm_rows(gnorm, index, out_ref, base):
    lane = iota((D, 128), 1)
    total = jnp.zeros((D, 128), f32)
    for column, row in enumerate(index):
        total = total + jnp.where(lane == column, jnp.sum(gnorm[row], axis=1, keepdims=True), 0.0)
    flat = total.T
    for column in range(len(index)):
        for half in range(D // 128):
            place = base + column * (D // 128) + half
            out_ref[place : place + 1] = flat[column : column + 1, 128 * half : 128 * half + 128]


def pack_front(gfm, head):
    lane = iota((D, 128), 1)
    start = (head // 2) * 128
    feats, middle = gfm[:, start : start + 128], gfm[:, D + start : D + start + 128]
    if head % 2 == 0:
        return jnp.where(lane < 64, feats, pltpu.roll(middle, 64, 1))
    return jnp.where(lane < 64, pltpu.roll(feats, 64, 1), middle)


def store_pieces(out_ref, head, base, value):
    size = out_ref.shape[2]
    done = 0
    while done < value.shape[0]:
        chunk, offset = divmod(base + done, size)
        count = min(size - offset, value.shape[0] - done)
        for half in range(2):
            out_ref[head, 2 * chunk + half, offset : offset + count] = value[
                done : done + count, 128 * half : 128 * half + 128
            ]
        done += count


def pack_rest(gout, gup, gdown, out_ref, base, n_head):
    for head in range(n_head):
        deep, wide = D // n_head, FF // n_head
        store_pieces(out_ref, head, base, gout[head * deep : (head + 1) * deep].astype(b16))
        start = base + deep
        store_pieces(out_ref, head, start, gup[:, head * wide : (head + 1) * wide].astype(b16))
        store_pieces(out_ref, head, start + D, gdown[:, head * wide : (head + 1) * wide].astype(b16))


def first_kernel(tiles, scal, tok_ref, wfm_ref, wsb_ref, norm_ref,
                 xt_ref, vh_ref, rs_ref, u_ref, f_ref, m_ref, p_ref, sums_hbm, edge_ref, ends_ref, sums, sem):
    tile = pl.program_id(0)

    @pl.when(tile == 0)
    def _():
        clear_present(scal, tiles, sums)

    turned = tok_ref[...].T
    xt_ref[...] = turned
    x = turned.astype(f32)
    front_tile(scal, tiles, tile, x, wfm_ref[...], wsb_ref[...], norm_ref[...],
               vh_ref, rs_ref, u_ref, f_ref, m_ref, p_ref, sums)

    @pl.when(tile == tiles - 1)
    def _():
        write_edges(scal, tiles, sums, edge_ref, ends_ref, sums_hbm, sem)


def second_kernel(tiles, scal, xt_ref, p0_ref, sums0_hbm, ends0_ref, recv_ref, wout_ref, wup_ref, wdown_ref, wqb_ref, norm0_ref,
                  wfm_ref, wsb_ref, norm1_ref,
                  e_ref, vh2_ref, rs2_ref, u2_ref, gp_ref, z_ref, kept_ref, prob_ref,
                  x1_ref, vh_ref, rs_ref, u_ref, f_ref, m_ref, p_ref, sums_hbm, edge_ref, ends_ref,
                  wide, spread, spare, sums, sem):
    tile = pl.program_id(0)

    @pl.when(tile == 0)
    def _():
        attend_all(scal, tiles, ends0_ref, recv_ref, sums0_hbm, wqb_ref[...], wide, kept_ref, prob_ref, spare, sem)
        clear_present(scal, tiles, sums)

    norms = norm0_ref[...]
    spread_r = spread_tile(scal, tiles, tile, wide, p0_ref, spread)
    e_ref[...] = spread_r
    middle = xt_ref[...].astype(f32) + tn(wout_ref[...], spread_r)
    scaled_two, scale_two = norm_stats(middle)
    vh2_ref[...] = scaled_two.astype(b16)
    rs2_ref[...] = jnp.broadcast_to(scale_two, rs2_ref.shape)
    normed_two_r = (scaled_two * norms[:, 2:3] + norms[:, 3:4]).astype(b16)
    u2_ref[...] = normed_two_r
    x = middle
    for start in range(0, FF, CHUNK):
        part = slice(start, start + CHUNK)
        active, slope = gelu_pair(tn(wup_ref[:, part], normed_two_r))
        active_r = active.astype(b16)
        z_ref[part] = active_r
        gp_ref[part] = slope.astype(b16)
        x = x + tn(wdown_ref[part], active_r)
    x1_ref[...] = x
    front_tile(scal, tiles, tile, x, wfm_ref[...], wsb_ref[...], norm1_ref[...],
               vh_ref, rs_ref, u_ref, f_ref, m_ref, p_ref, sums)

    @pl.when(tile == tiles - 1)
    def _():
        write_edges(scal, tiles, sums, edge_ref, ends_ref, sums_hbm, sem)


def third_kernel(n_head, packed, tiles, scal, x1_ref, p_ref, sums1_hbm, ends1_ref, recv_ref, cot_ref, wout_ref, wup_ref, wdown_ref, wqb_ref, norm_ref,
                 out_ref, d2_ref, de_ref, kept_ref, prob_ref, grads_hbm, edge_ref, ends_ref,
                 gn_ref, *rest):
    grad_outs, (wide, spread, spare, grads, sem, gnorm, slope_s, active_s, gup, gdown, gout) = rest[:-11], rest[-11:]
    tile = pl.program_id(0)

    @pl.when(tile == 0)
    def _():
        clear_present(scal, tiles, grads)
        gup[...] = jnp.zeros_like(gup)
        gdown[...] = jnp.zeros_like(gdown)
        gout[...] = jnp.zeros_like(gout)
        gnorm[...] = jnp.zeros_like(gnorm)
        attend_all(scal, tiles, ends1_ref, recv_ref, sums1_hbm, wqb_ref[...], wide, kept_ref, prob_ref, spare, sem)

    norms = norm_ref[...]
    spread_r = spread_tile(scal, tiles, tile, wide, p_ref, spread)
    middle = x1_ref[...] + tn(wout_ref[...], spread_r)
    scaled_two, scale_two = norm_stats(middle)
    normed_two_r = (scaled_two * norms[:, 2:3] + norms[:, 3:4]).astype(b16)
    x = middle
    for start in range(0, FF, CHUNK):
        part = slice(start, start + CHUNK)
        active, slope = gelu_pair(tn(wup_ref[:, part], normed_two_r))
        active_r = active.astype(b16)
        active_s[part] = active_r
        slope_s[part] = slope
        x = x + tn(wdown_ref[part], active_r)
    out_ref[...] = x.astype(b16).T
    grad = cot_ref[...].T.astype(f32)
    mlp_back_tile(scal, tiles, tile, grad, lambda part: slope_s[part], lambda part: active_s[part],
                  scaled_two, scale_two, normed_two_r, spread_r, p_ref[...],
                  wout_ref[...], wup_ref, wdown_ref, norms, d2_ref, de_ref, grads,
                  gup, gdown, gout, gnorm)

    @pl.when(tile == tiles - 1)
    def _():
        write_edges(scal, tiles, grads, edge_ref, ends_ref, grads_hbm, sem)
        norm_rows(gnorm, (2, 3), gn_ref, 0)
        if packed:
            pack_rest(gout, gup, gdown, grad_outs[0], 0, n_head)
        else:
            for ref, total in zip(grad_outs, (gup, gdown, gout)):
                ref[...] = total[...].astype(b16)


def fourth_kernel(n_head, packed, tiles, scal, sums1_hbm, kept_ref, prob_ref, recv_ref, grads1_hbm, ends1_ref, grad_recv_ref, de1_ref, f_ref, m_ref, p1_ref, u_ref, vh_ref, rs_ref, d21_ref,
                  wfm_ref, wsb_ref, wqb_ref, norm1_ref,
                  gp_ref, z_ref, vh2_ref, rs2_ref, u2_ref, e_ref, p0_ref, wout_ref, wup_ref, wdown_ref, norm0_ref, gn1b_ref,
                  d2_ref, de_ref, grads_hbm, edge_ref, ends_ref, small_ref, gn0_ref, *rest):
    grad_outs = rest[:-16]
    spare, spare_grad, sem, grads, both, dcount, grad_p, grad_f, gws, gqkv, gnorm, fold_s, gfm, gup, gdown, gout = rest[-16:]
    tile = pl.program_id(0)

    @pl.when(tile == 0)
    def _():
        for ref in (gfm, gws, gqkv, gup, gdown, gout, gnorm):
            ref[...] = jnp.zeros_like(ref)
        attend_back_all(scal, tiles, kept_ref, prob_ref, recv_ref, ends1_ref, grad_recv_ref, sums1_hbm, grads1_hbm,
                        wqb_ref[...], both, dcount, gqkv, spare, spare_grad, sem)
        clear_present(scal, tiles, grads)

    grad = attend_back_tile(scal, tiles, tile, both, dcount, de1_ref, f_ref, m_ref, p1_ref, u_ref, vh_ref, rs_ref,
                            d21_ref, wfm_ref[...], wsb_ref[...], norm1_ref[...], grad_p, grad_f, gfm, gws, gnorm)
    mlp_back_tile(scal, tiles, tile, grad, lambda part: gp_ref[part].astype(f32), lambda part: z_ref[part],
                  vh2_ref[...].astype(f32), rs2_ref[:1], u2_ref[...], e_ref[...], p0_ref[...],
                  wout_ref[...], wup_ref, wdown_ref, norm0_ref[...], d2_ref, de_ref, grads,
                  gup, gdown, gout, gnorm)

    @pl.when(tile == tiles - 1)
    def _():
        write_edges(scal, tiles, grads, edge_ref, ends_ref, grads_hbm, sem)
        small_rows(0, gws, gqkv, fold_s, small_ref)
        norm_rows(gnorm, (0, 1), small_ref, NORM_ROW)
        small_ref[NORM_ROW + 4 :] = gn1b_ref[...]
        norm_rows(gnorm, (2, 3), gn0_ref, 0)
        if packed:
            for head in range(n_head):
                front = pack_front(gfm, head).astype(b16)
                store_pieces(
                    grad_outs[0], head, 0, jnp.concatenate([front[: D // 2], front[D // 2 :]], axis=1)
                )
            pack_rest(gout, gup, gdown, grad_outs[0], D // 2, n_head)
        else:
            for ref, total in zip(grad_outs, (gfm, gup, gdown, gout)):
                ref[...] = total[...].astype(b16)


def fifth_kernel(n_head, packed, tiles, scal, sums0_hbm, kept_ref, prob_ref, recv_ref, grads0_hbm, ends0_ref, grad_recv_ref, de_ref, f_ref, m_ref, p_ref, u_ref, vh_ref, rs_ref, d2_ref,
                 wfm_ref, wsb_ref, wqb_ref, norm_ref, gn0b_ref, small1_ref,
                 gin_ref, small_ref, front_ref,
                 spare, spare_grad, sem, both, dcount, grad_p, grad_f, gws, gqkv, gnorm, fold_s, gfm):
    tile = pl.program_id(0)

    @pl.when(tile == 0)
    def _():
        for ref in (gfm, gws, gqkv, gnorm):
            ref[...] = jnp.zeros_like(ref)
        attend_back_all(scal, tiles, kept_ref, prob_ref, recv_ref, ends0_ref, grad_recv_ref, sums0_hbm, grads0_hbm,
                        wqb_ref[...], both, dcount, gqkv, spare, spare_grad, sem)

    grad = attend_back_tile(scal, tiles, tile, both, dcount, de_ref, f_ref, m_ref, p_ref, u_ref, vh_ref, rs_ref,
                            d2_ref, wfm_ref[...], wsb_ref[...], norm_ref[...], grad_p, grad_f, gfm, gws, gnorm)
    gin_ref[...] = grad.T

    @pl.when(tile == tiles - 1)
    def _():
        small_rows(0, gws, gqkv, fold_s, small_ref)
        norm_rows(gnorm, (0, 1), small_ref, NORM_ROW)
        small_ref[NORM_ROW + 4 : LAYER_ROWS] = gn0b_ref[...]
        small_ref[LAYER_ROWS:] = small1_ref[...]
        if packed:
            for head in range(n_head):
                front_ref[head] = pack_front(gfm, head).astype(b16)
        else:
            front_ref[...] = gfm[...].astype(b16)


def sum_parts(own, got):
    total = own.astype(f32)
    for index in range(got.shape[0]):
        total = total + got[index].astype(f32)
    return total


def total_kernel(sizes, gb_ref, gc_ref, gs_ref, tb_ref, tc_ref, ts_ref,
                 got_b, got_c, got_s, mid_c, mid_s, got_c2, got_s2, head_sem, pts_sem):
    n_pts, n_head = sizes
    pts, head = lax.axis_index("pts"), lax.axis_index("head")
    c_rows = D // n_pts
    s_rows = gs_ref.shape[0] // n_head

    def part(index, rows):
        return pl.ds(pl.multiple_of(index * rows, rows), rows)

    def over(size, which, own, to, sem, source, target):
        copies = []
        for step in range(1, size):
            peer = lax.rem(own + step, size)
            copies.append(
                pltpu.make_async_remote_copy(
                    src_ref=source(peer),
                    dst_ref=target(step - 1),
                    send_sem=sem.at[0, which, step - 1],
                    recv_sem=sem.at[1, which, step - 1],
                    device_id=to(peer),
                    device_id_type=MESH,
                )
            )
        for copy in copies:
            copy.start()
        return copies

    def over_head(which, source, target):
        return over(n_head, which, head, lambda peer: (pts, peer), head_sem, source, target)

    def over_pts(which, source, target):
        return over(n_pts, which, pts, lambda peer: (peer, head), pts_sem, source, target)

    def finish(copies):
        for copy in copies:
            copy.wait()

    barrier = pltpu.get_barrier_semaphore()
    for step in range(1, n_head):
        pl.semaphore_signal(
            barrier, inc=1, device_id=(pts, lax.rem(head + step, n_head)), device_id_type=MESH
        )
    for step in range(1, n_pts):
        pl.semaphore_signal(
            barrier, inc=1, device_id=(lax.rem(pts + step, n_pts), head), device_id_type=MESH
        )
    pl.semaphore_wait(barrier, n_head - 1 + n_pts - 1)

    first_c = over_head(0, lambda peer: gc_ref.at[peer], lambda slot: got_c.at[slot])
    first_s = over_head(1, lambda peer: gs_ref.at[part(peer, s_rows)], lambda slot: got_s.at[slot])
    first_b = over_pts(0, lambda peer: gb_ref.at[peer], lambda slot: got_b.at[slot])
    finish(first_c)
    mid_c[...] = sum_parts(gc_ref[head], got_c).astype(b16)
    next_c = over_pts(1, lambda peer: mid_c.at[part(peer, c_rows)], lambda slot: got_c2.at[slot])
    finish(first_s)
    mid_s[...] = sum_parts(gs_ref[part(head, s_rows)], got_s)
    next_s = over_pts(2, lambda peer: mid_s, lambda slot: got_s2.at[slot])
    finish(next_c)
    mine_c = part(pts, c_rows)
    tc_ref[mine_c] = sum_parts(mid_c[mine_c], got_c2).astype(b16)
    last_c = over_pts(3, lambda peer: tc_ref.at[mine_c], lambda slot: tc_ref.at[mine_c])
    finish(next_s)
    mine_s = part(head, s_rows)
    ts_ref[mine_s] = sum_parts(mid_s[...], got_s2)
    last_s = over_head(2, lambda peer: ts_ref.at[mine_s], lambda slot: ts_ref.at[mine_s])
    finish(first_b)
    tb_ref[pts] = sum_parts(gb_ref[pts], got_b).astype(b16)
    last_b = over_pts(4, lambda peer: tb_ref.at[pts], lambda slot: tb_ref.at[pts])
    finish(last_c)
    finish(last_s)
    finish(last_b)


def total_gradients(sizes, gb, gc, gs):
    n_pts, n_head = sizes
    vmem = pl.BlockSpec(memory_space=pltpu.VMEM)
    dma = pltpu.SemaphoreType.DMA
    c_rows, s_rows = D // n_pts, gs.shape[0] // n_head
    return pl.pallas_call(
        functools.partial(total_kernel, sizes),
        out_shape=(
            jax.ShapeDtypeStruct(gb.shape, b16),
            jax.ShapeDtypeStruct(gc.shape[1:], b16),
            jax.ShapeDtypeStruct(gs.shape, f32),
        ),
        in_specs=[vmem] * 3,
        out_specs=[vmem] * 3,
        scratch_shapes=[
            pltpu.VMEM((n_pts - 1,) + gb.shape[1:], b16),
            pltpu.VMEM((n_head - 1,) + gc.shape[1:], b16),
            pltpu.VMEM((n_head - 1, s_rows, 128), f32),
            pltpu.VMEM(gc.shape[1:], b16),
            pltpu.VMEM((s_rows, 128), f32),
            pltpu.VMEM((n_pts - 1, c_rows, 128), b16),
            pltpu.VMEM((n_pts - 1, s_rows, 128), f32),
            dma((2, 3, n_head - 1)),
            dma((2, 5, n_pts - 1)),
        ],
        cost_estimate=pl.CostEstimate(flops=0, bytes_accessed=32 << 20, transcendentals=0),
        compiler_params=pltpu.CompilerParams(
            collective_id=3, has_side_effects=True, vmem_limit_bytes=VMEM_BYTES
        ),
        name="total_gradients",
    )(gb, gc, gs)


def update_kernel(ta_ref, tb_ref, tc_ref, ts_ref, row_ref, sel_ref, m_ref, v_ref, w_ref, sm_ref, sv_ref, sw_ref,
                  nm_ref, nv_ref, nw_ref, fresh_ref, om_ref, ov_ref, ow_ref, wide, tall, front, flat):
    lane = iota((8, 128), 1)

    def place_front(base):
        for pair in range(16):
            first = front[pl.ds(2 * pair, 8, stride=32), :]
            second = front[pl.ds(2 * pair + 1, 8, stride=32), :]
            columns = slice(128 * pair, 128 * pair + 128)
            wide[base : base + 8, columns] = jnp.where(lane < 64, first, pltpu.roll(second, 64, 1))
            wide[base + 8 : base + 16, columns] = jnp.where(lane < 64, pltpu.roll(first, 64, 1), second)

    def place_rest(base):
        for part in range(8):
            for half in range(2):
                wide[base : base + 72, 256 * part + 128 * half : 256 * part + 128 * half + 128] = tall[
                    half, pl.ds(part, 72, stride=8), :
                ]

    def fill(value, base):
        size = value.shape[1]
        row = base
        while row < size * (value.shape[0] // 2):
            chunk, offset = divmod(row, size)
            for half in range(2):
                tall[half, row - base : row - base + size - offset] = value[
                    2 * chunk + half, offset:
                ].astype(f32)
            row += size - offset

    front[...] = tc_ref[...].astype(f32)
    place_front(0)
    fill(tb_ref, D // 2)
    place_rest(16)
    front[: D // 2] = tb_ref[0, : D // 2].astype(f32)
    front[D // 2 :] = tb_ref[1, : D // 2].astype(f32)
    place_front(88)
    fill(ta_ref, 0)
    place_rest(104)

    cap, blocks = m_ref.shape[0], wide.shape[0]
    mine = (iota((cap, blocks), 0) == row_ref[:1]).astype(f32)
    filled = jnp.sum(mine, axis=1, keepdims=True) > 0.5
    mine = mine.astype(b16)
    step = 512
    for start in range(0, BLOCK, step):
        part = slice(start, start + step)
        grad = wide[:, part]
        own = nn(mine, grad.astype(b16))
        old = (m_ref[:, part], v_ref[:, part], w_ref[:, part])
        new = adam_update(old[0], own, old[1], old[2], rate_large)
        for ref, before, after in zip((nm_ref, nv_ref, nw_ref), old, new):
            ref[:, part] = jnp.where(filled, after, before)
        picked = [
            sel_ref[:, which * BLOCK + start : which * BLOCK + start + step].astype(f32)
            for which in range(3)
        ]
        fresh_ref[:, part] = adam_update(picked[0], grad, picked[1], picked[2], rate_large)[0].astype(b16)
    for layer in range(2):
        for row in range(LAYER_ROWS):
            flat[layer : layer + 1, 128 * row : 128 * row + 128] = ts_ref[
                layer * LAYER_ROWS + row : layer * LAYER_ROWS + row + 1, :
            ]
    new = adam_update(sm_ref[...], flat[:2], sv_ref[...], sw_ref[...], rate_small)
    for ref, value in zip((om_ref, ov_ref, ow_ref), new):
        ref[...] = value


def update(ta, tb, tc, ts, row, sel, tables, smalls):
    vmem = pl.BlockSpec(memory_space=pltpu.VMEM)
    blocks = sel.shape[0]
    operands = (ta, tb, tc, ts, row, sel, *tables, *smalls)
    outs = [jax.ShapeDtypeStruct(table.shape, f32) for table in tables]
    outs.append(jax.ShapeDtypeStruct((blocks, BLOCK), b16))
    outs += [jax.ShapeDtypeStruct(small.shape, f32) for small in smalls]
    return pl.pallas_call(
        update_kernel,
        out_shape=outs,
        in_specs=[vmem] * len(operands),
        out_specs=[vmem] * len(outs),
        scratch_shapes=[
            pltpu.VMEM((blocks, BLOCK), f32),
            pltpu.VMEM((2, ta.shape[0] * ta.shape[1] // 2, 128), f32),
            pltpu.VMEM((D, 128), f32),
            pltpu.VMEM((8, SMALL), f32),
        ],
        compiler_params=pltpu.CompilerParams(vmem_limit_bytes=VMEM_FULL),
        name="update",
    )(*operands)


class Args:
    def __init__(self, rows, width, limit):
        self.rows, self.width, self.limit = rows, width, limit
        self.operands, self.in_specs, self.outs, self.out_specs = [], [], [], []

    def cols(self, *arrays):
        for array in arrays:
            self.operands.append(array)
            self.in_specs.append(
                pl.BlockSpec((array.shape[0], self.width), lambda tile, scal: (0, tile))
            )

    def points(self, *arrays):
        for array in arrays:
            self.operands.append(array)
            self.in_specs.append(
                pl.BlockSpec((self.width, array.shape[1]), lambda tile, scal: (tile, 0))
            )

    def whole(self, *arrays):
        for array in arrays:
            rank = array.ndim
            self.operands.append(array)
            self.in_specs.append(
                pl.BlockSpec(array.shape, lambda tile, scal, rank=rank: (0,) * rank)
            )

    def layer(self, index, *arrays):
        for array in arrays:
            self.operands.append(array)
            self.in_specs.append(
                pl.BlockSpec((None,) + array.shape[1:], lambda tile, scal: (index, 0, 0))
            )

    def rows_of(self, array, start, size):
        self.operands.append(array)
        self.in_specs.append(
            pl.BlockSpec((size, array.shape[1]), lambda tile, scal: (start // size, 0))
        )

    def far(self, *arrays):
        for array in arrays:
            self.operands.append(array)
            self.in_specs.append(pl.BlockSpec(memory_space=pl.ANY))

    def out_far(self, *pairs):
        for shape, dtype in pairs:
            self.outs.append(jax.ShapeDtypeStruct(shape, dtype))
            self.out_specs.append(pl.BlockSpec(memory_space=pl.ANY))

    def out_cols(self, *pairs):
        for height, dtype in pairs:
            self.outs.append(jax.ShapeDtypeStruct((height, self.rows), dtype))
            self.out_specs.append(
                pl.BlockSpec((height, self.width), lambda tile, scal: (0, tile))
            )

    def out_points(self, *dtypes):
        for dtype in dtypes:
            self.outs.append(jax.ShapeDtypeStruct((self.rows, D), dtype))
            self.out_specs.append(pl.BlockSpec((self.width, D), lambda tile, scal: (tile, 0)))

    def out_whole(self, *pairs):
        for shape, dtype in pairs:
            rank = len(shape)
            self.outs.append(jax.ShapeDtypeStruct(shape, dtype))
            self.out_specs.append(
                pl.BlockSpec(shape, lambda tile, scal, rank=rank: (0,) * rank)
            )

    def call(self, body, scal, scratch, name):
        tiles = self.rows // self.width
        return pl.pallas_call(
            functools.partial(body, tiles),
            grid_spec=pltpu.PrefetchScalarGridSpec(
                num_scalar_prefetch=1,
                grid=(tiles,),
                in_specs=self.in_specs,
                out_specs=self.out_specs,
                scratch_shapes=scratch,
            ),
            out_shape=self.outs,
            compiler_params=pltpu.CompilerParams(
                dimension_semantics=("arbitrary",), vmem_limit_bytes=self.limit
            ),
            cost_estimate=pl.CostEstimate(
                flops=64 * self.rows * D * D, bytes_accessed=80 * self.rows * D, transcendentals=0
            ),
            name=name,
        )(scal, *self.operands)


def adam_update(master, grad, first, second, rate):
    new_first = beta_one * first + (1.0 - beta_one) * grad
    new_second = beta_two * second + (1.0 - beta_two) * grad * grad
    fix_one = 1.0 - beta_one**STEP
    fix_two = 1.0 - beta_two**STEP
    direction = new_first / fix_one / (jnp.sqrt(new_second / fix_two) + adam_eps)
    return (master - rate * (direction + decay_rate * master), new_first, new_second)


def flat_blocks(n_head, gfm, gout, gup, gdown):
    def columns(grad):
        width = grad.shape[1] // n_head
        return grad.reshape(D, n_head, width).transpose(1, 0, 2).reshape(n_head, -1)

    return jnp.concatenate(
        [
            columns(gfm[:, :D]),
            columns(gfm[:, D:]),
            gout.reshape(n_head, -1),
            columns(gup),
            columns(gdown),
        ],
        axis=1,
    ).reshape(n_head, -1, BLOCK)


def on_device(
    sizes,
    tokens,
    cotangent,
    segment_ids,
    owner,
    w_fx,
    w_mid,
    w_out,
    w_up,
    w_down,
    small_master,
    small_first,
    small_second,
    master_table,
    first_table,
    second_table,
):
    n_pts, n_head = sizes
    rows = tokens.shape[0]
    width, wide = min(512, rows), min(1024, rows)
    tiles = rows // width
    most = rows * n_pts * n_head // LARGEST
    window = (rows - 1 + most - 1) // rows
    limit = VMEM_BYTES if window < 4 else VMEM_FULL
    layers = w_fx.shape[0]
    packed = (n_pts, n_head) == (8, 4)

    ids = segment_ids.reshape(-1, 128)
    w_fx = w_fx.transpose(0, 2, 1)
    w_mid = w_mid.transpose(0, 2, 1)
    tables = (master_table, first_table, second_table)
    smalls = (small_master, small_first, small_second)
    gathered, wsb, norms, scal, halves = opening(
        n_head, tiles, ids, w_fx, w_mid, small_master, tables
    )
    wfm0 = gathered.reshape(2 * D, D)

    cap = master_table.shape[0]
    if packed:
        collected = lax.all_gather(halves, "pts", axis=0, tiled=True)

    sums_shape = (MESHES, SLICES, 2 * D)
    grad_sums_shape = (MESHES, SLICES, D)
    front_cols = ((D, b16), (8, f32), (D, b16), (D, b16), (D, b16), (HS, b16))
    wide_scratch = [pltpu.VMEM(grad_sums_shape, b16), pltpu.VMEM((D, wide), f32)]

    args = Args(rows, wide, limit)
    args.points(tokens)
    args.whole(wfm0)
    args.layer(0, wsb, norms)
    args.out_cols((D, b16), *front_cols)
    args.out_far((sums_shape, f32))
    ends_outs = (((2, EDGE, D), b16), ((2,) + sums_shape[1:], f32))
    grad_ends_outs = (((2, EDGE, D), b16), ((2,) + grad_sums_shape[1:], f32))
    kept_outs = (((2, SLICES, 5 * D), f32), ((2, HS, SLICES), f32))
    args.out_whole(*ends_outs)
    sums_scratch = [pltpu.VMEM(sums_shape, f32), pltpu.SemaphoreType.DMA]
    spare_scratch = [pltpu.VMEM(sums_shape[1:], f32)]
    xt0, vh0, rs0, u0, f0, m0, p0, sums0, edge, ends0 = args.call(first_kernel, scal, sums_scratch, "first")
    recv0, later, wqb0 = swap_edges_weights(
        sizes, window, 0, ((0, 1), (1, 1), (2, 0)), edge, w_fx, w_mid, w_out, small_master, 1
    )
    later = later.reshape(3 * D, D)

    args = Args(rows, wide, limit)
    args.cols(xt0, p0)
    args.far(sums0)
    args.whole(ends0, recv0)
    args.rows_of(later, 2 * D, D)
    args.layer(0, w_up, w_down)
    args.whole(wqb0)
    args.layer(0, norms)
    args.rows_of(later, 0, 2 * D)
    args.layer(1, wsb, norms)
    args.out_cols((D, b16), (D, b16), (8, f32), (D, b16), (FF, b16), (FF, b16))
    args.out_whole(*kept_outs)
    args.out_cols((D, f32), *front_cols)
    args.out_far((sums_shape, f32))
    args.out_whole(*ends_outs)
    (e0, vh20, rs20, u20, gp0, z0, kept0, prob0, x1, vh1, rs1, u1, f1, m1, p1, sums1, edge, ends1) = args.call(
        second_kernel, scal, wide_scratch + spare_scratch + sums_scratch, "second"
    )
    recv1, wout1, wqb1 = swap_edges_weights(
        sizes, window, 1, ((2, 1),), edge, w_fx, w_mid, w_out, small_master, 5
    )
    wout1 = wout1.reshape(D, D)

    grad_scratch = [pltpu.VMEM((D, FF), f32), pltpu.VMEM((D, FF), f32), pltpu.VMEM((D, D), f32)]
    rest_rows = D // n_head + 2 * D

    args = Args(rows, wide, limit)
    args.cols(x1, p1)
    args.far(sums1)
    args.whole(ends1, recv1)
    args.points(cotangent)
    args.whole(wout1)
    args.layer(1, w_up, w_down)
    args.whole(wqb1)
    args.layer(1, norms)
    args.out_points(b16)
    args.out_cols((D, f32), (D, b16))
    args.out_whole(*kept_outs)
    args.out_far((grad_sums_shape, f32))
    args.out_whole(*grad_ends_outs, ((4, 128), f32))
    if packed:
        args.out_whole(((n_head, n_pts, 2 * rest_rows // n_pts, 128), b16))
    else:
        args.out_whole(((D, FF), b16), ((D, FF), b16), ((D, D), b16))
    (layer_out, d21, de1, kept1, prob1, grads1, edge, ends1, gn1b, *grads_a) = args.call(
        functools.partial(third_kernel, n_head, packed),
        scal,
        wide_scratch
        + spare_scratch
        + [pltpu.VMEM(grad_sums_shape, f32), pltpu.SemaphoreType.DMA]
        + [pltpu.VMEM((4, D, 128), f32), pltpu.VMEM((FF, wide), f32), pltpu.VMEM((FF, wide), b16)]
        + grad_scratch,
        "third",
    )
    if packed:
        grad_recv1 = swap_edges(sizes, window, edge, 4)
        grad_recv1, collected = lax.optimization_barrier((grad_recv1, collected))
        part_a = lax.psum_scatter(grads_a[0], "head", scatter_dimension=0, tiled=True)[0]
    else:
        grad_recv1 = swap_edges(sizes, window, edge, 4)

    back_scratch = [
        *spare_scratch,
        pltpu.VMEM(grad_sums_shape[1:], f32),
        pltpu.SemaphoreType.DMA,
        pltpu.VMEM((MESHES, HS, 2 * D), b16),
        pltpu.VMEM((MESHES, HS, 128), f32),
        pltpu.VMEM((HS, width), f32),
        pltpu.VMEM((D, width), f32),
        pltpu.VMEM((D, HS), f32),
        pltpu.VMEM((D, 3 * D), f32),
        pltpu.VMEM((4, D, 128), f32),
        pltpu.VMEM((DH, 128), f32),
        pltpu.VMEM((D, 2 * D), f32),
    ]

    args = Args(rows, width, limit)
    args.far(sums1)
    args.whole(kept1, prob1, recv1)
    args.far(grads1)
    args.whole(ends1, grad_recv1)
    args.cols(de1, f1, m1, p1, u1, vh1, rs1, d21)
    args.rows_of(later, 0, 2 * D)
    args.layer(1, wsb)
    args.whole(wqb1)
    args.layer(1, norms)
    args.cols(gp0, z0, vh20, rs20, u20, e0, p0)
    args.rows_of(later, 2 * D, D)
    args.layer(0, w_up, w_down, norms)
    args.whole(gn1b)
    args.out_cols((D, f32), (D, b16))
    args.out_far((grad_sums_shape, f32))
    args.out_whole(*grad_ends_outs, ((LAYER_ROWS, 128), f32), ((4, 128), f32))
    if packed:
        args.out_whole(((n_head, n_pts, (D + 2 * rest_rows) // n_pts, 128), b16))
    else:
        args.out_whole(((D, 2 * D), b16), ((D, FF), b16), ((D, FF), b16), ((D, D), b16))
    (d20, de0, grads0, edge, ends0, small1, gn0b, *grads_b) = args.call(
        functools.partial(fourth_kernel, n_head, packed),
        scal,
        back_scratch[:3] + [pltpu.VMEM(grad_sums_shape, f32)] + back_scratch[3:] + grad_scratch,
        "fourth",
    )
    if packed:
        grad_recv0, total_a, chosen, row = swap_edges_sums(
            sizes, window, edge, part_a, owner.reshape(1, -1), collected, 6
        )
        mine_b = lax.psum_scatter(grads_b[0], "head", scatter_dimension=0, tiled=True)[0]
    else:
        grad_recv0 = swap_edges(sizes, window, edge, 4)

    args = Args(rows, width, limit)
    args.far(sums0)
    args.whole(kept0, prob0, recv0)
    args.far(grads0)
    args.whole(ends0, grad_recv0)
    args.cols(de0, f0, m0, p0, u0, vh0, rs0, d20)
    args.whole(wfm0)
    args.layer(0, wsb)
    args.whole(wqb0)
    args.layer(0, norms)
    args.whole(gn0b, small1)
    args.out_points(f32)
    args.out_whole(((2 * LAYER_ROWS, 128), f32))
    args.out_whole(((n_head, D, 128), b16) if packed else ((D, 2 * D), b16))
    input_grad, small, front = args.call(
        functools.partial(fifth_kernel, n_head, packed), scal, back_scratch, "fifth"
    )

    if packed:
        total_b, total_c, total_s = total_gradients(sizes, mine_b, front, small)
        outs = update(total_a, total_b, total_c, total_s, row, chosen, tables, smalls)
        return (layer_out, input_grad, *outs)

    gup1, gdown1, gout1 = grads_a
    gfm1, gup0, gdown0, gout0 = grads_b
    small_total = lax.psum(small, ("pts", "head")).reshape(layers, -1)
    totals = []
    for parts in ((front, gout0, gup0, gdown0), (gfm1, gout1, gup1, gdown1)):
        blocks = lax.psum_scatter(
            flat_blocks(n_head, *parts), "head", scatter_dimension=0, tiled=True
        )
        totals.append(lax.psum(blocks.reshape(-1, BLOCK), "pts"))
    total_grad = jnp.concatenate(totals, axis=0).astype(f32)
    my_index = lax.axis_index("pts")
    block_ids = jnp.arange(owner.shape[0])
    same_owner = (owner[:, None] == owner[None, :]) & (block_ids[None, :] < block_ids[:, None])
    table_row = owner * cap + jnp.sum(same_owner.astype(jnp.int32), axis=1)
    place_all = (jnp.arange(n_pts * cap)[:, None] == table_row[None, :]).astype(f32)
    mine_place = lax.dynamic_slice_in_dim(place_all, my_index * cap, cap, 0)
    own_grad = jnp.dot(mine_place, total_grad, precision=lax.Precision.HIGHEST)
    filled = jnp.sum(mine_place, axis=1)[:, None] > 0.5
    updated = adam_update(master_table, own_grad, first_table, second_table, rate_large)
    new_tables = [jnp.where(filled, new, old) for new, old in zip(updated, tables)]
    collected = lax.all_gather(new_tables[0].astype(b16), "pts", axis=0, tiled=True)
    pick_back = (table_row[:, None] == jnp.arange(n_pts * cap)[None, :]).astype(b16)
    fresh = jnp.dot(pick_back, collected, preferred_element_type=f32).astype(b16)
    small_outs = adam_update(small_master, small_total, small_first, small_second, rate_small)
    return (layer_out, input_grad, *new_tables, fresh, *small_outs)


def solution(mesh):
    sizes = (mesh.shape["pts"], mesh.shape["head"])
    return jax.shard_map(
        functools.partial(on_device, sizes),
        mesh=mesh,
        in_specs=(
            P(("pts", "head"), None),
            P(("pts", "head"), None),
            P("pts"),
            P(),
            P(None, None, "head"),
            P(None, None, "head"),
            P(None, "head", None),
            P(),
            P(),
            P(),
            P(),
            P(),
            P("pts", "head"),
            P("pts", "head"),
            P("pts", "head"),
        ),
        out_specs=(
            P(("pts", "head"), None),
            P(("pts", "head"), None),
            P("pts", "head"),
            P("pts", "head"),
            P("pts", "head"),
            P(None, "head"),
            P(),
            P(),
            P(),
        ),
        check_vma=False,
    )
```
